32 devices in a mesh: seq: 8 (over z, core), head: 2 (over y), batch: 2 (over x).
Axes of the slice: x: 2, y: 2, z: 4, core: 2. Of those that a mesh axis runs over, the one named last changes fastest.
Arguments:
- queries: bfloat16 [4096, 1024], P(('batch', 'seq'), 'head'), parts along dimension 0, may hold values from -16 to 16, as said below
- key_rows: bfloat16 [4096, 256], P(('batch', 'seq'), 'head'), parts along dimension 0, may hold values from -16 to 16
- value_rows: bfloat16 [4096, 256], P(('batch', 'seq'), 'head'), parts along dimension 0, may hold values from -6 to 6
- out_grad: bfloat16 [4096, 1024], P(('batch', 'seq'), 'head'), parts along dimension 0, may hold values from -6 to 6
- tile_ids: int32 [32], P('batch'), parts along dimension 0, may hold values from 0 to 15, each once
- tile_mask: int32 [32, 16], P('batch'), parts along dimension 0, may hold values from 0 to 1, as said below
Outputs:
- attended: bfloat16 [4096, 1024], P(('batch', 'seq'), 'head'), parts along dimension 0
- query_grad: float32 [4096, 1024], P(('batch', 'seq'), 'head'), parts along dimension 0
- key_grad: float32 [4096, 256], P(('batch', 'seq'), 'head'), parts along dimension 0
- value_grad: float32 [4096, 256], P(('batch', 'seq'), 'head'), parts along dimension 0
The draws below stay inside these ranges and needn't reach their ends.
There are 2 independent parts, one for each index of `batch`. The reference program is written for one: setup_inputs(seed, part) draws one part's arguments, and reference() takes and returns one part's arrays. A program takes and returns all parts, laid end to end along the dimension named above; each array names one. Nothing has to cross between parts.
Inputs may be any that keep to these rules, and one draw needn't show every extreme that they name: `queries`: in the hidden draw a few query rows equal scaled key rows of the same tile. `tile_mask`: 1 only where the key tile's index is at most the query tile's; 1 on the diagonal.
All inputs are finite; a program needn't handle non-finite values.
Results may differ from the reference program's by a relative error of at most 0.03.
Values may be sent and summed in bfloat16 or wider, within the bound.
No kernel may reach another device: no remote copies, remote signals or barrier semaphores. Data moves between devices by JAX's collectives and lax.ppermute only.
A program may use at most 64 MiB of HBM per device.

```python
import jax
import jax.numpy as jnp
from jax import lax

NH = 4
HD = 128
TILE = 128
KVH = 2
TOKENS = 2048
NT = 16


def draw_queries(key, part):
    base = jnp.clip(jax.random.normal(jax.random.fold_in(key, 1), (TOKENS, KVH * NH * HD), jnp.float32), -4.0, 4.0)
    return base.astype(jnp.bfloat16)


def draw_key_rows(key, part):
    base = jnp.clip(jax.random.normal(jax.random.fold_in(key, 2), (TOKENS, KVH * HD), jnp.float32), -4.0, 4.0)
    return base.astype(jnp.bfloat16)


def draw_tile_mask(key, part):
    tiles = TOKENS // TILE
    prompt = max(1, tiles // 8)
    answers = min(16, tiles - prompt)
    room = tiles - prompt - 1
    cuts = jnp.sort(jax.random.permutation(jax.random.fold_in(key, 5), room)[:answers - 1]).astype(jnp.int32)
    bounds = jnp.concatenate([jnp.array([-1], jnp.int32), cuts, jnp.array([room], jnp.int32)])
    lengths = bounds[1:] - bounds[:-1]
    ends = prompt + jnp.cumsum(lengths)
    places = jnp.arange(tiles, dtype=jnp.int32)
    segment = jnp.where(places < prompt, 0, 1 + jnp.sum((places[:, None] >= ends[None, :answers - 1]).astype(jnp.int32), axis=1))
    allowed = (places[None, :] <= places[:, None]) & ((segment[None, :] == 0) | (segment[None, :] == segment[:, None]))
    return allowed.astype(jnp.int32)


def level_of(stream_key, shape, split, least, top_value):
    def one(position, blocks):
        draws = jax.random.uniform(jax.random.fold_in(jax.random.fold_in(stream_key, 6), position), (blocks,), jnp.float32, least / len(split), top_value / len(split))
        return jnp.repeat(jnp.exp(draws), shape[position] // blocks).reshape((-1,) + (1,) * (len(shape) - position - 1))

    factor_of = one(*split[0])
    for cut in split[1:]:
        factor_of = factor_of * one(*cut)
    return factor_of


def scatter_about(key, dims, width, bound, pieces=(), kind=jnp.bfloat16):
    gain = level_of(key, dims, pieces, -0.22, 0.18) if pieces else 1.0
    entries = jax.random.normal(key, dims, jnp.float32) * width * gain
    return jnp.minimum(jnp.maximum(entries, -bound), bound).astype(kind)


def setup_inputs(seed: int = 0, part: int = 0) -> dict:
    key_of = jax.random.split(jax.random.key(seed), 7)
    part_splits = jax.random.split(jax.random.fold_in(key_of[6], part), 7)
    queries = draw_queries(jax.random.fold_in(jax.random.fold_in(key_of[6], part), 71), part)
    key_rows = draw_key_rows(jax.random.fold_in(jax.random.fold_in(key_of[6], part), 71), part)
    value_rows = scatter_about(part_splits[2], (TOKENS, KVH * HD), 1.0, 6.0, ((0, 8), (1, 2)))
    out_grad = scatter_about(part_splits[3], (TOKENS, KVH * NH * HD), 1.0, 6.0, ((0, 8), (1, 2)))
    tile_ids = jax.random.permutation(part_splits[4], NT).astype(jnp.int32)
    tile_mask = draw_tile_mask(jax.random.fold_in(jax.random.fold_in(key_of[6], part), 71), part)
    return dict(queries=queries, key_rows=key_rows, value_rows=value_rows, out_grad=out_grad, tile_ids=tile_ids, tile_mask=tile_mask)


far_below = -1.0e30


def rounded(values):
    return lax.optimization_barrier(values.astype(jnp.bfloat16)).astype(jnp.float32)


def tile_allowed(tile_mask, query_tiles, key_tiles):
    table = jnp.take(jnp.take(tile_mask, query_tiles, axis=0), key_tiles, axis=1) == 1
    same_tile = query_tiles[:, None] == key_tiles[None, :]
    inside = lax.broadcasted_iota(jnp.int32, (TILE, TILE), 0) >= lax.broadcasted_iota(jnp.int32, (TILE, TILE), 1)
    full = table[:, None, :, None] & (jnp.logical_not(same_tile)[:, None, :, None] | inside[None, :, None, :])
    return full.reshape(query_tiles.shape[0] * TILE, key_tiles.shape[0] * TILE)


def one_group(queries, key_rows, value_rows, out_grad, tile_ids, tile_mask):
    factor = HD ** -0.5
    block_rows = min(512, TOKENS)
    block_count = TOKENS // block_rows
    query_blocks = queries.reshape(block_count, block_rows, NH, HD)
    grad_blocks = out_grad.reshape(block_count, block_rows, NH, HD)
    tile_blocks = tile_ids.reshape(block_count, block_rows // TILE)
    keys_wide = key_rows.astype(jnp.float32)
    values_wide = value_rows.astype(jnp.float32)

    def scores_for(query_block, tile_block):
        allowed = tile_allowed(tile_mask, tile_block, tile_ids)[None]
        scores = jnp.einsum('qhd,kd->hqk', query_block.astype(jnp.float32), keys_wide) * factor
        return allowed, jnp.where(allowed, scores, far_below)

    def forward(inputs):
        query_block, tile_block = inputs
        allowed, scores = scores_for(query_block, tile_block)
        row_max = jnp.max(scores, axis=-1)
        softmax_terms = jnp.where(allowed, jnp.exp(scores - row_max[..., None]), 0.0)
        denominator = jnp.sum(softmax_terms, axis=-1)
        weighted = jnp.einsum('hqk,kd->qhd', rounded(softmax_terms), values_wide)
        output = (weighted / denominator.T[:, :, None]).astype(jnp.bfloat16)
        return output, row_max + jnp.log(denominator)

    outputs, log_totals = lax.map(forward, (query_blocks, tile_blocks))

    def backward(carry, inputs):
        key_sum, value_sum = carry
        query_block, out_block, grad_block, log_total, tile_block = inputs
        allowed, scores = scores_for(query_block, tile_block)
        softmax_terms = jnp.where(allowed, jnp.exp(scores - log_total[..., None]), 0.0)
        row_delta = jnp.sum(grad_block.astype(jnp.float32) * out_block.astype(jnp.float32), axis=-1).T
        dprobs = jnp.einsum('qhd,kd->hqk', grad_block.astype(jnp.float32), values_wide)
        dscores = rounded(softmax_terms * (dprobs - row_delta[..., None]))
        query_part = jnp.einsum('hqk,kd->qhd', dscores, keys_wide) * factor
        key_sum = key_sum + jnp.einsum('hqk,qhd->kd', dscores, query_block.astype(jnp.float32)) * factor
        value_sum = value_sum + jnp.einsum('hqk,qhd->kd', rounded(softmax_terms), grad_block.astype(jnp.float32))
        return (key_sum, value_sum), query_part

    zeros_wide = jnp.zeros((TOKENS, HD), jnp.float32)
    (key_grad, value_grad), query_parts = lax.scan(backward, (zeros_wide, zeros_wide), (query_blocks, outputs, grad_blocks, log_totals, tile_blocks))
    return outputs.reshape(TOKENS, NH, HD), query_parts.reshape(TOKENS, NH, HD), key_grad, value_grad


def reference(queries, key_rows, value_rows, out_grad, tile_ids, tile_mask):
    query_groups = jnp.transpose(queries.reshape(TOKENS, KVH, NH, HD), (1, 0, 2, 3))
    grad_groups = jnp.transpose(out_grad.reshape(TOKENS, KVH, NH, HD), (1, 0, 2, 3))
    key_groups = jnp.transpose(key_rows.reshape(TOKENS, KVH, HD), (1, 0, 2))
    value_groups = jnp.transpose(value_rows.reshape(TOKENS, KVH, HD), (1, 0, 2))

    def per_group(inputs):
        return one_group(inputs[0], inputs[1], inputs[2], inputs[3], tile_ids, tile_mask)

    outputs, query_parts, key_parts, value_parts = lax.map(per_group, (query_groups, key_groups, value_groups, grad_groups))
    attended = jnp.transpose(outputs, (1, 0, 2, 3)).reshape(TOKENS, KVH * NH * HD)
    query_grad = jnp.transpose(query_parts, (1, 0, 2, 3)).reshape(TOKENS, KVH * NH * HD)
    key_grad = jnp.transpose(key_parts, (1, 0, 2)).reshape(TOKENS, KVH * HD)
    value_grad = jnp.transpose(value_parts, (1, 0, 2)).reshape(TOKENS, KVH * HD)
    return attended, query_grad, key_grad, value_grad
```

```python
import functools
import math

import jax
import jax.numpy as jnp
from jax import lax
from jax.experimental import pallas as pl
from jax.experimental.pallas import tpu as pltpu
from jax.sharding import PartitionSpec as P

HD = 128
TILE = 128
UNIT = 16
FAR_BELOW = -1e30
LOG2E = 1.4426950408889634
NT_DIMS = (((1,), (1,)), ((), ()))
VMEM_LIMIT = 48 * 1024 * 1024

SMEM_SPEC = pl.BlockSpec(memory_space=pltpu.SMEM)
VMEM_SPEC = pl.BlockSpec(memory_space=pltpu.VMEM)
ANY_SPEC = pl.BlockSpec(memory_space=pl.ANY)


def call(kernel, in_specs, out_shape, out_specs, scratch=(), flops=0, moved=0):
    return pl.pallas_call(
        kernel,
        in_specs=in_specs,
        out_shape=out_shape,
        out_specs=out_specs,
        scratch_shapes=list(scratch),
        compiler_params=pltpu.CompilerParams(vmem_limit_bytes=VMEM_LIMIT),
        cost_estimate=pl.CostEstimate(flops=flops, bytes_accessed=moved, transcendentals=0),
    )


def unit_places(pieces):
    per_piece = 2 * (TILE // UNIT) // pieces
    return [(g // per_piece, g % per_piece, g // 2, g % 2) for g in range(2 * (TILE // UNIT))]


def pack_kernel(pieces, tiles, key_ref, value_ref, out_ref):
    for tile in range(tiles):
        for piece, place, block, kind in unit_places(pieces):
            source = value_ref if kind else key_ref
            out_ref[piece, tile, place] = source[pl.ds(tile * TILE + block * UNIT, UNIT), :]


def shared_kernel(tile_total, tiles, ids_ref, mask_ref, info_ref, spare_ref):
    del spare_ref

    def one(position, count):
        key_tile = ids_ref[position]
        home = position // tiles
        wanted = jnp.int32(0)
        for other in range(tile_total):
            away = jnp.where(home == other // tiles, 0, 1)
            wanted = wanted | (mask_ref[ids_ref[other], key_tile] & away)
        info_ref[1 + count] = position
        return count + wanted

    for place in range(1, tile_total + 2):
        info_ref[place] = 0
    info_ref[0] = lax.fori_loop(0, tile_total, one, jnp.int32(0))


def select_kernel(pieces, slots, info_ref, held_ref, out_ref):
    for slot in range(slots):
        chosen = held_ref[info_ref[1 + slot]]
        for piece in range(pieces):
            out_ref[piece, slot] = chosen


def reduce_kernel(pieces, slots, info_ref, terms_ref, out_ref):
    out_ref[...] = jnp.zeros_like(out_ref)
    for slot in range(slots):
        total = terms_ref[0, slot].astype(jnp.float32)
        for piece in range(1, pieces):
            total = total + terms_ref[piece, slot].astype(jnp.float32)

        @pl.when(slot < info_ref[0])
        def _():
            out_ref[info_ref[1 + slot]] = total.astype(jnp.bfloat16)


def final_kernel(pieces, tiles, key_ref, value_ref, sums_ref, key_out, value_out):
    for tile in range(tiles):
        for piece, place, block, kind in unit_places(pieces):
            source, target = (value_ref, value_out) if kind else (key_ref, key_out)
            rows = pl.ds(tile * TILE + block * UNIT, UNIT)
            target[rows, :] = source[rows, :] + sums_ref[piece, tile, place].astype(jnp.float32)


def attention_kernel(
    pieces,
    tiles,
    slots,
    heads,
    rounds,
    rank_ref,
    ids_ref,
    mask_ref,
    info_ref,
    query_ref,
    grad_ref,
    key_ref,
    value_ref,
    first_ref,
    more_ref,
    attended_ref,
    query_out,
    key_out,
    value_out,
    first_out,
    more_out,
    bias_ref,
    keys_ref,
    values_ref,
    key_sum,
    value_sum,
    score_ref,
    staged_ref,
    copy_sem,
):
    rank = rank_ref[0]
    rows = tiles * TILE
    chunk = slots * TILE
    factor = HD**-0.5
    scale = factor * LOG2E
    needed = info_ref[0]
    my_tiles = [ids_ref[rank * tiles + b] for b in range(tiles)]
    triangle = jnp.where(
        lax.broadcasted_iota(jnp.int32, (TILE, TILE), 0)
        <= lax.broadcasted_iota(jnp.int32, (TILE, TILE), 1),
        0.0,
        FAR_BELOW,
    )

    def block_bias(allowed):
        return jnp.full((TILE, TILE), jnp.where(allowed, 0.0, FAR_BELOW), jnp.float32)

    for a in range(tiles):
        for b in range(tiles):
            own = triangle if a == b else block_bias(mask_ref[my_tiles[b], my_tiles[a]] == 1)
            bias_ref[pl.ds(a * TILE, TILE), pl.ds(b * TILE, TILE)] = own

    def slot_bias(slot, first_row):
        position = info_ref[1 + slot]
        usable = (slot < needed) & (position // tiles != rank)
        tile = ids_ref[position]
        for b in range(tiles):
            bias_ref[pl.ds(first_row, TILE), pl.ds(b * TILE, TILE)] = block_bias(
                usable & (mask_ref[my_tiles[b], tile] == 1)
            )

    for slot in range(slots):
        slot_bias(jnp.int32(slot), rows + slot * TILE)

    keys_ref[pl.ds(0, rows), :] = key_ref[...]
    values_ref[pl.ds(0, rows), :] = value_ref[...]

    def unpack(source, first_row):
        for slot in range(slots):
            for piece, place, block, kind in unit_places(pieces):
                target = values_ref if kind else keys_ref
                target[pl.ds(first_row + slot * TILE + block * UNIT, UNIT), :] = source[
                    piece, slot, place
                ]

    def repack(target, first_row):
        for slot in range(slots):
            for piece, place, block, kind in unit_places(pieces):
                source = value_sum if kind else key_sum
                unit = source[pl.ds(first_row + slot * TILE + block * UNIT, UNIT), :]
                if kind == 0:
                    unit = unit * factor
                target[piece, slot, place] = unit.astype(jnp.bfloat16)

    unpack(first_ref, rows)
    head_columns = [pl.ds(h * HD, HD) for h in range(heads)]
    both = rows + chunk

    @pl.when(needed <= slots)
    def _():
        keys = keys_ref[pl.ds(0, both), :]
        values = values_ref[pl.ds(0, both), :]
        keys_t = keys.T
        values_t = values.T
        for h in range(heads):
            query = query_ref[:, head_columns[h]]
            grad = grad_ref[:, head_columns[h]]
            scores = (
                lax.dot_general(keys, query, NT_DIMS, preferred_element_type=jnp.float32) * scale
                + bias_ref[pl.ds(0, both), :]
            )
            row_max = jnp.max(scores, axis=0, keepdims=True)
            terms = jnp.exp2(scores - row_max)
            inverse = 1.0 / jnp.sum(terms, axis=0, keepdims=True)
            weighted = jnp.dot(
                values_t, terms.astype(jnp.bfloat16), preferred_element_type=jnp.float32
            )
            out = (weighted * inverse).astype(jnp.bfloat16)
            attended_ref[:, head_columns[h]] = out.T
            delta = jnp.sum(
                grad.T.astype(jnp.float32) * out.astype(jnp.float32), axis=0, keepdims=True
            )
            probs = terms * inverse
            dprobs = lax.dot_general(values, grad, NT_DIMS, preferred_element_type=jnp.float32)
            dscores = (probs * (dprobs - delta)).astype(jnp.bfloat16)
            query_t = jnp.dot(keys_t, dscores, preferred_element_type=jnp.float32) * factor
            query_out[:, head_columns[h]] = query_t.T
            key_part = jnp.dot(dscores, query, preferred_element_type=jnp.float32)
            value_part = jnp.dot(
                probs.astype(jnp.bfloat16), grad, preferred_element_type=jnp.float32
            )
            if h == 0:
                key_sum[pl.ds(0, both), :] = key_part
                value_sum[pl.ds(0, both), :] = value_part
            else:
                key_sum[pl.ds(0, both), :] += key_part
                value_sum[pl.ds(0, both), :] += value_part

    @pl.when(needed > slots)
    def _():
        used = (needed + slots - 1) // slots

        def fetch(index, carry):
            copy = pltpu.make_async_copy(more_ref.at[index], staged_ref, copy_sem)
            copy.start()
            copy.wait()
            first_row = pl.multiple_of(both + index * chunk, chunk)
            unpack(staged_ref, first_row)
            for slot in range(slots):
                slot_bias((index + 1) * slots + slot, first_row + slot * TILE)
            return carry

        lax.fori_loop(0, used - 1, fetch, 0)
        key_sum[...] = jnp.zeros_like(key_sum)
        value_sum[...] = jnp.zeros_like(value_sum)
        blocks = (rows + used * chunk) // TILE

        def block_rows(index):
            return pl.ds(pl.multiple_of(index * TILE, TILE), TILE)

        for h in range(heads):
            query = query_ref[:, head_columns[h]]
            grad = grad_ref[:, head_columns[h]]

            def score(index, row_max):
                at = block_rows(index)
                scores = (
                    lax.dot_general(
                        keys_ref[at, :], query, NT_DIMS, preferred_element_type=jnp.float32
                    )
                    * scale
                    + bias_ref[at, :]
                )
                score_ref[at, :] = scores
                return jnp.maximum(row_max, jnp.max(scores, axis=0, keepdims=True))

            row_max = lax.fori_loop(
                0, blocks, score, jnp.full((1, rows), FAR_BELOW, jnp.float32)
            )

            def forward(index, carry):
                total, weighted = carry
                at = block_rows(index)
                terms = jnp.exp2(score_ref[at, :] - row_max)
                score_ref[at, :] = terms
                weighted = weighted + jnp.dot(
                    values_ref[at, :].T,
                    terms.astype(jnp.bfloat16),
                    preferred_element_type=jnp.float32,
                )
                return total + jnp.sum(terms, axis=0, keepdims=True), weighted

            total, weighted = lax.fori_loop(
                0,
                blocks,
                forward,
                (jnp.zeros((1, rows), jnp.float32), jnp.zeros((HD, rows), jnp.float32)),
            )
            inverse = 1.0 / total
            out = (weighted * inverse).astype(jnp.bfloat16)
            attended_ref[:, head_columns[h]] = out.T
            delta = jnp.sum(
                grad.T.astype(jnp.float32) * out.astype(jnp.float32), axis=0, keepdims=True
            )

            def backward(index, query_t):
                at = block_rows(index)
                probs = score_ref[at, :] * inverse
                dprobs = lax.dot_general(
                    values_ref[at, :], grad, NT_DIMS, preferred_element_type=jnp.float32
                )
                dscores = (probs * (dprobs - delta)).astype(jnp.bfloat16)
                key_sum[at, :] += jnp.dot(dscores, query, preferred_element_type=jnp.float32)
                value_sum[at, :] += jnp.dot(
                    probs.astype(jnp.bfloat16), grad, preferred_element_type=jnp.float32
                )
                return query_t + jnp.dot(
                    keys_ref[at, :].T, dscores, preferred_element_type=jnp.float32
                )

            query_t = lax.fori_loop(0, blocks, backward, jnp.zeros((HD, rows), jnp.float32))
            query_out[:, head_columns[h]] = (query_t * factor).T

        def store(index, carry):
            repack(staged_ref, pl.multiple_of(both + index * chunk, chunk))
            copy = pltpu.make_async_copy(staged_ref, more_out.at[index], copy_sem)
            copy.start()
            copy.wait()
            return carry

        lax.fori_loop(0, used - 1, store, 0)

    key_out[...] = key_sum[pl.ds(0, rows), :] * factor
    value_out[...] = value_sum[pl.ds(0, rows), :]
    repack(first_out, rows)


def exchange(values):
    return lax.all_to_all(values, "seq", split_axis=0, concat_axis=0, tiled=True)


def per_device(queries, key_rows, value_rows, out_grad, tile_ids, tile_mask):
    row_count = queries.shape[0]
    heads = queries.shape[1] // HD
    pieces = lax.axis_size("seq")
    tiles = row_count // TILE
    tile_total = tile_ids.shape[0]
    slots = tiles
    units = 2 * (TILE // UNIT)
    assert key_rows.shape[1] == HD and units % pieces == 0
    per_piece = units // pieces
    rounds = math.ceil(tile_total / slots)
    rank = lax.axis_index("seq").astype(jnp.int32).reshape(1)
    message = (pieces, tiles, per_piece, UNIT, HD)
    buffer = (rounds - 1,) + message
    held_shape = (tile_total, per_piece, UNIT, HD)
    shape = jax.ShapeDtypeStruct
    bf16, f32 = jnp.bfloat16, jnp.float32

    packed = call(
        functools.partial(pack_kernel, pieces, tiles),
        [VMEM_SPEC] * 2,
        shape(message, bf16),
        VMEM_SPEC,
        moved=4 * row_count * HD * 2,
    )(key_rows, value_rows)
    info, spare = call(
        functools.partial(shared_kernel, tile_total, tiles),
        [SMEM_SPEC] * 2,
        (shape((tile_total + 2,), jnp.int32), shape(buffer, bf16)),
        (SMEM_SPEC, ANY_SPEC),
        moved=4096,
    )(tile_ids, tile_mask)
    held = exchange(packed).reshape(held_shape)
    used = (info[0] + slots - 1) // slots

    chosen = call(
        functools.partial(select_kernel, pieces, slots),
        [SMEM_SPEC, VMEM_SPEC],
        shape(message, bf16),
        VMEM_SPEC,
        moved=2 * row_count * HD * 2,
    )(info, held)
    first = exchange(chosen)

    def gather_more(index, buffered):
        places = lax.dynamic_slice_in_dim(info, 1 + index * slots, slots)
        picked = jnp.take(held, places, axis=0)
        arrived = exchange(jnp.broadcast_to(picked[None], message))
        return lax.dynamic_update_index_in_dim(buffered, arrived, index - 1, 0)

    more = lax.fori_loop(1, used, gather_more, spare)

    all_rows = row_count + rounds * slots * TILE
    attended, query_grad, key_own, value_own, first_terms, more_terms = call(
        functools.partial(attention_kernel, pieces, tiles, slots, heads, rounds),
        [SMEM_SPEC] * 4 + [VMEM_SPEC] * 5 + [ANY_SPEC],
        (
            shape(queries.shape, bf16),
            shape(queries.shape, f32),
            shape(key_rows.shape, f32),
            shape(value_rows.shape, f32),
            shape(message, bf16),
            shape(buffer, bf16),
        ),
        (VMEM_SPEC,) * 5 + (ANY_SPEC,),
        scratch=(
            pltpu.VMEM((all_rows, row_count), f32),
            pltpu.VMEM((all_rows, HD), bf16),
            pltpu.VMEM((all_rows, HD), bf16),
            pltpu.VMEM((all_rows, HD), f32),
            pltpu.VMEM((all_rows, HD), f32),
            pltpu.VMEM((all_rows, row_count), f32),
            pltpu.VMEM(message, bf16),
            pltpu.SemaphoreType.DMA,
        ),
        flops=12 * heads * row_count * 2 * row_count * HD,
        moved=12 * row_count * heads * HD,
    )(rank, tile_ids, tile_mask, info, queries, out_grad, key_rows, value_rows, first, more)

    summed = call(
        functools.partial(reduce_kernel, pieces, slots),
        [SMEM_SPEC, VMEM_SPEC],
        shape(held_shape, bf16),
        VMEM_SPEC,
        moved=2 * row_count * HD * 2,
    )(info, exchange(first_terms))

    def reduce_more(index, totals):
        places = lax.dynamic_slice_in_dim(info, 1 + index * slots, slots)
        arrived = exchange(lax.dynamic_index_in_dim(more_terms, index - 1, 0, keepdims=False))
        pieces_sum = jnp.sum(arrived.astype(f32), axis=0).astype(bf16)
        live = index * slots + jnp.arange(slots) < info[0]
        places = jnp.where(live, places, tile_total)
        return totals.at[places].set(pieces_sum, mode="drop")

    summed = lax.fori_loop(1, used, reduce_more, summed)
    returned = exchange(summed.reshape(message))
    key_grad, value_grad = call(
        functools.partial(final_kernel, pieces, tiles),
        [VMEM_SPEC] * 3,
        (shape(key_rows.shape, f32), shape(value_rows.shape, f32)),
        (VMEM_SPEC,) * 2,
        moved=5 * row_count * HD * 4,
    )(key_own, value_own, returned)
    return attended, query_grad, key_grad, value_grad


def solution(mesh):
    return jax.shard_map(
        per_device,
        mesh=mesh,
        in_specs=(
            P(("batch", "seq"), "head"),
            P(("batch", "seq"), "head"),
            P(("batch", "seq"), "head"),
            P(("batch", "seq"), "head"),
            P("batch"),
            P("batch", None),
        ),
        out_specs=(P(("batch", "seq"), "head"),) * 4,
        check_vma=False,
    )
```

```python
import functools
import math

import jax
import jax.numpy as jnp
from jax import lax
from jax.experimental import pallas as pl
from jax.experimental.pallas import tpu as pltpu
from jax.sharding import PartitionSpec as P

HD = 128
TILE = 128
UNIT = 16
FAR_BELOW = -1e30
LOG2E = 1.4426950408889634
NT_DIMS = (((1,), (1,)), ((), ()))
VMEM_LIMIT = 48 * 1024 * 1024

SMEM_SPEC = pl.BlockSpec(memory_space=pltpu.SMEM)
VMEM_SPEC = pl.BlockSpec(memory_space=pltpu.VMEM)
ANY_SPEC = pl.BlockSpec(memory_space=pl.ANY)


def call(kernel, in_specs, out_shape, out_specs, scratch=(), flops=0, moved=0):
    return pl.pallas_call(
        kernel,
        in_specs=in_specs,
        out_shape=out_shape,
        out_specs=out_specs,
        scratch_shapes=list(scratch),
        compiler_params=pltpu.CompilerParams(vmem_limit_bytes=VMEM_LIMIT),
        cost_estimate=pl.CostEstimate(flops=flops, bytes_accessed=moved, transcendentals=0),
    )


def unit_at(piece, place, pieces):
    per_piece = 2 * (TILE // UNIT) // pieces
    if per_piece % 2 == 0:
        return piece * (per_piece // 2) + place // 2, place % 2
    return (piece * per_piece + place) // 2, (piece * per_piece + place) % 2


def unit_rows(first_row, block):
    return pl.ds(pl.multiple_of(first_row + block * UNIT, UNIT), UNIT)


def pack_kernel(pieces, tiles, key_ref, value_ref, *refs):
    outs, (held_ref, key_sem, value_sem) = refs[:pieces], refs[pieces:]
    copies = [
        pltpu.make_async_copy(key_ref, held_ref.at[0], key_sem),
        pltpu.make_async_copy(value_ref, held_ref.at[1], value_sem),
    ]
    for copy in copies:
        copy.start()
    for copy in copies:
        copy.wait()
    rank = lax.axis_index("seq")
    for step, out_ref in enumerate(outs):
        for tile in range(tiles):
            for place in range(out_ref.shape[1]):
                block, kind = unit_at(rank ^ step, place, pieces)
                out_ref[tile, place] = held_ref[kind, unit_rows(tile * TILE, block), :]


def shared_kernel(tile_total, tiles, ids_ref, mask_ref, info_ref, spare_ref, spare_sums_ref):
    del spare_ref, spare_sums_ref
    for place in range(1, tile_total + 2):
        info_ref[place] = 0

    def one(position, count):
        key_tile = ids_ref[position]
        home = position // tiles
        wanted = jnp.int32(0)
        for other in range(tile_total):
            away = jnp.where(home == other // tiles, 0, 1)
            wanted = wanted | (mask_ref[ids_ref[other], key_tile] & away)
        info_ref[1 + count] = position
        info_ref[tile_total + 2 + position] = jnp.where(wanted == 1, count, -1)
        return count + wanted

    info_ref[0] = lax.fori_loop(0, tile_total, one, jnp.int32(0))


def select_kernel(pieces, tiles, slots, info_ref, *refs):
    arrived, (out_ref, all_ref, held_ref, copy_sem) = refs[:pieces], refs[pieces:]
    rank = lax.axis_index("seq")
    for step, source in enumerate(arrived):
        held_ref[pl.ds((rank ^ step) * tiles, tiles)] = source[...]
    for slot in range(slots):
        out_ref[slot] = held_ref[info_ref[1 + slot]]

    @pl.when(info_ref[0] > slots)
    def _():
        copy = pltpu.make_async_copy(held_ref, all_ref, copy_sem)
        copy.start()
        copy.wait()


def reduce_kernel(pieces, tiles, slots, tile_total, info_ref, extra_ref, *refs):
    terms, outs = refs[:pieces], refs[pieces : 2 * pieces]
    totals_ref, copy_sem = refs[2 * pieces :]
    rank = lax.axis_index("seq")

    @pl.when(info_ref[0] > slots)
    def _():
        copy = pltpu.make_async_copy(extra_ref, totals_ref, copy_sem)
        copy.start()
        copy.wait()

    for slot in range(slots):
        total = terms[0][slot].astype(jnp.float32)
        for source in terms[1:]:
            total = total + source[slot].astype(jnp.float32)
        totals_ref[slot] = total.astype(jnp.bfloat16)
    for step, out_ref in enumerate(outs):
        for tile in range(tiles):
            slot = info_ref[tile_total + 2 + (rank ^ step) * tiles + tile]
            total = totals_ref[jnp.maximum(slot, 0)]
            out_ref[tile] = jnp.where(slot >= 0, total, jnp.zeros_like(total))


def final_kernel(pieces, tiles, key_ref, value_ref, *refs):
    sums, (key_out, value_out, total_ref) = refs[:pieces], refs[pieces:]
    rank = lax.axis_index("seq")
    total_ref[0] = key_ref[...]
    total_ref[1] = value_ref[...]
    for step, source in enumerate(sums):
        for tile in range(tiles):
            for place in range(source.shape[1]):
                block, kind = unit_at(rank ^ step, place, pieces)
                total_ref[kind, unit_rows(tile * TILE, block), :] += source[tile, place].astype(
                    jnp.float32
                )
    key_out[...] = total_ref[0]
    value_out[...] = total_ref[1]


def attention_kernel(
    pieces,
    tiles,
    slots,
    heads,
    ids_ref,
    mask_ref,
    info_ref,
    query_ref,
    grad_ref,
    key_ref,
    value_ref,
    more_ref,
    *refs,
):
    first_refs, refs = refs[:pieces], refs[pieces:]
    attended_ref, query_out, key_out, value_out, more_out = refs[:5]
    first_outs, refs = refs[5 : 5 + pieces], refs[5 + pieces :]
    bias_ref, held_ref, sum_ref, score_ref, staged_ref, copy_sem = refs
    keys_ref, values_ref = held_ref.at[0], held_ref.at[1]
    key_sum, value_sum = sum_ref.at[0], sum_ref.at[1]
    rank = lax.axis_index("seq")
    rows = tiles * TILE
    chunk = slots * TILE
    factor = HD**-0.5
    scale = factor * LOG2E
    needed = info_ref[0]
    my_tiles = [ids_ref[rank * tiles + b] for b in range(tiles)]
    triangle = jnp.where(
        lax.broadcasted_iota(jnp.int32, (TILE, TILE), 0)
        <= lax.broadcasted_iota(jnp.int32, (TILE, TILE), 1),
        0.0,
        FAR_BELOW,
    )

    def block_bias(allowed):
        return jnp.full((TILE, TILE), jnp.where(allowed, 0.0, FAR_BELOW), jnp.float32)

    for a in range(tiles):
        for b in range(tiles):
            own = triangle if a == b else block_bias(mask_ref[my_tiles[b], my_tiles[a]] == 1)
            bias_ref[pl.ds(a * TILE, TILE), pl.ds(b * TILE, TILE)] = own

    def slot_bias(slot, first_row):
        position = info_ref[1 + slot]
        usable = (slot < needed) & (position // tiles != rank)
        tile = ids_ref[position]
        for b in range(tiles):
            bias_ref[pl.ds(first_row, TILE), pl.ds(b * TILE, TILE)] = block_bias(
                usable & (mask_ref[my_tiles[b], tile] == 1)
            )

    for slot in range(slots):
        slot_bias(jnp.int32(slot), rows + slot * TILE)

    keys_ref[pl.ds(0, rows), :] = key_ref[...]
    values_ref[pl.ds(0, rows), :] = value_ref[...]

    def unpack(source, piece, first_row):
        for slot in range(slots):
            for place in range(source.shape[1]):
                block, kind = unit_at(piece, place, pieces)
                held_ref[kind, unit_rows(first_row + slot * TILE, block), :] = source[slot, place]

    def repack(target, piece, first_row):
        for slot in range(slots):
            for place in range(target.shape[1]):
                block, kind = unit_at(piece, place, pieces)
                unit = sum_ref[kind, unit_rows(first_row + slot * TILE, block), :]
                unit = unit * jnp.where(kind == 0, factor, 1.0)
                target[slot, place] = unit.astype(jnp.bfloat16)

    for step, source in enumerate(first_refs):
        unpack(source, rank ^ step, rows)
    head_columns = [pl.ds(h * HD, HD) for h in range(heads)]
    both = rows + chunk

    @pl.when(needed <= slots)
    def _():
        keys = keys_ref[pl.ds(0, both), :]
        values = values_ref[pl.ds(0, both), :]
        keys_t = keys.T
        values_t = values.T
        for h in range(heads):
            query = query_ref[:, head_columns[h]]
            grad = grad_ref[:, head_columns[h]]
            scores = (
                lax.dot_general(keys, query, NT_DIMS, preferred_element_type=jnp.float32) * scale
                + bias_ref[pl.ds(0, both), :]
            )
            row_max = jnp.max(scores, axis=0, keepdims=True)
            terms = jnp.exp2(scores - row_max)
            inverse = 1.0 / jnp.sum(terms, axis=0, keepdims=True)
            weighted = jnp.dot(
                values_t, terms.astype(jnp.bfloat16), preferred_element_type=jnp.float32
            )
            out = (weighted * inverse).astype(jnp.bfloat16)
            attended_ref[:, head_columns[h]] = out.T
            delta = jnp.sum(
                grad.T.astype(jnp.float32) * out.astype(jnp.float32), axis=0, keepdims=True
            )
            probs = terms * inverse
            dprobs = lax.dot_general(values, grad, NT_DIMS, preferred_element_type=jnp.float32)
            dscores = (probs * (dprobs - delta)).astype(jnp.bfloat16)
            query_t = jnp.dot(keys_t, dscores, preferred_element_type=jnp.float32) * factor
            query_out[:, head_columns[h]] = query_t.T
            key_part = jnp.dot(dscores, query, preferred_element_type=jnp.float32)
            value_part = jnp.dot(
                probs.astype(jnp.bfloat16), grad, preferred_element_type=jnp.float32
            )
            if h == 0:
                key_sum[pl.ds(0, both), :] = key_part
                value_sum[pl.ds(0, both), :] = value_part
            else:
                key_sum[pl.ds(0, both), :] += key_part
                value_sum[pl.ds(0, both), :] += value_part

    @pl.when(needed > slots)
    def _():
        used = (needed + slots - 1) // slots

        def fetch(index, carry):
            copy = pltpu.make_async_copy(more_ref.at[index], staged_ref, copy_sem)
            copy.start()
            copy.wait()
            first_row = pl.multiple_of(both + index * chunk, chunk)
            for piece in range(pieces):
                unpack(staged_ref.at[piece], piece, first_row)
            for slot in range(slots):
                slot_bias((index + 1) * slots + slot, first_row + slot * TILE)
            return carry

        lax.fori_loop(0, used - 1, fetch, 0)
        key_sum[...] = jnp.zeros_like(key_sum)
        value_sum[...] = jnp.zeros_like(value_sum)
        blocks = (rows + used * chunk) // TILE

        def block_rows(index):
            return pl.ds(pl.multiple_of(index * TILE, TILE), TILE)

        for h in range(heads):
            query = query_ref[:, head_columns[h]]
            grad = grad_ref[:, head_columns[h]]

            def score(index, row_max):
                at = block_rows(index)
                scores = (
                    lax.dot_general(
                        keys_ref[at, :], query, NT_DIMS, preferred_element_type=jnp.float32
                    )
                    * scale
                    + bias_ref[at, :]
                )
                score_ref[at, :] = scores
                return jnp.maximum(row_max, jnp.max(scores, axis=0, keepdims=True))

            row_max = lax.fori_loop(
                0, blocks, score, jnp.full((1, rows), FAR_BELOW, jnp.float32)
            )

            def forward(index, carry):
                total, weighted = carry
                at = block_rows(index)
                terms = jnp.exp2(score_ref[at, :] - row_max)
                score_ref[at, :] = terms
                weighted = weighted + jnp.dot(
                    values_ref[at, :].T,
                    terms.astype(jnp.bfloat16),
                    preferred_element_type=jnp.float32,
                )
                return total + jnp.sum(terms, axis=0, keepdims=True), weighted

            total, weighted = lax.fori_loop(
                0,
                blocks,
                forward,
                (jnp.zeros((1, rows), jnp.float32), jnp.zeros((HD, rows), jnp.float32)),
            )
            inverse = 1.0 / total
            out = (weighted * inverse).astype(jnp.bfloat16)
            attended_ref[:, head_columns[h]] = out.T
            delta = jnp.sum(
                grad.T.astype(jnp.float32) * out.astype(jnp.float32), axis=0, keepdims=True
            )

            def backward(index, query_t):
                at = block_rows(index)
                probs = score_ref[at, :] * inverse
                dprobs = lax.dot_general(
                    values_ref[at, :], grad, NT_DIMS, preferred_element_type=jnp.float32
                )
                dscores = (probs * (dprobs - delta)).astype(jnp.bfloat16)
                key_sum[at, :] += jnp.dot(dscores, query, preferred_element_type=jnp.float32)
                value_sum[at, :] += jnp.dot(
                    probs.astype(jnp.bfloat16), grad, preferred_element_type=jnp.float32
                )
                return query_t + jnp.dot(
                    keys_ref[at, :].T, dscores, preferred_element_type=jnp.float32
                )

            query_t = lax.fori_loop(0, blocks, backward, jnp.zeros((HD, rows), jnp.float32))
            query_out[:, head_columns[h]] = (query_t * factor).T

        def store(index, carry):
            for piece in range(pieces):
                repack(staged_ref.at[piece], piece, both + index * chunk)
            copy = pltpu.make_async_copy(staged_ref, more_out.at[index], copy_sem)
            copy.start()
            copy.wait()
            return carry

        lax.fori_loop(0, used - 1, store, 0)

    key_out[...] = key_sum[pl.ds(0, rows), :] * factor
    value_out[...] = value_sum[pl.ds(0, rows), :]
    for step, target in enumerate(first_outs):
        repack(target, rank ^ step, rows)


def swap(values, pieces):
    arrived = [values[0]]
    for step in range(1, pieces):
        pairs = [(source, source ^ step) for source in range(pieces)]
        arrived.append(lax.ppermute(values[step], "seq", pairs))
    return arrived


def exchange(values):
    return lax.all_to_all(values, "seq", split_axis=0, concat_axis=0, tiled=True)


def per_device(queries, key_rows, value_rows, out_grad, tile_ids, tile_mask):
    row_count = queries.shape[0]
    heads = queries.shape[1] // HD
    pieces = lax.axis_size("seq")
    tiles = row_count // TILE
    tile_total = tile_ids.shape[0]
    slots = tiles
    units = 2 * (TILE // UNIT)
    assert key_rows.shape[1] == HD and units % pieces == 0
    per_piece = units // pieces
    rounds = math.ceil(tile_total / slots)
    message = (tiles, per_piece, UNIT, HD)
    whole = (pieces,) + message
    buffer = (rounds - 1,) + whole
    held_shape = (tile_total, per_piece, UNIT, HD)
    total_shape = (rounds * slots, per_piece, UNIT, HD)
    shape = jax.ShapeDtypeStruct
    bf16, f32 = jnp.bfloat16, jnp.float32

    packed = call(
        functools.partial(pack_kernel, pieces, tiles),
        [ANY_SPEC] * 2,
        (shape(message, bf16),) * pieces,
        (VMEM_SPEC,) * pieces,
        scratch=(
            pltpu.VMEM((2, row_count, HD), bf16),
            pltpu.SemaphoreType.DMA,
            pltpu.SemaphoreType.DMA,
        ),
        moved=4 * row_count * HD * 2,
    )(key_rows, value_rows)
    arrived = swap(packed, pieces)
    info, spare, spare_sums = call(
        functools.partial(shared_kernel, tile_total, tiles),
        [SMEM_SPEC] * 2,
        (
            shape((2 * tile_total + 2,), jnp.int32),
            shape(buffer, bf16),
            shape(total_shape, bf16),
        ),
        (SMEM_SPEC, ANY_SPEC, ANY_SPEC),
        moved=8 * 1024 * 1024,
    )(tile_ids, tile_mask)
    used = (info[0] + slots - 1) // slots

    chosen, held = call(
        functools.partial(select_kernel, pieces, tiles, slots),
        [SMEM_SPEC] + [VMEM_SPEC] * pieces,
        (shape(message, bf16), shape(held_shape, bf16)),
        (VMEM_SPEC, ANY_SPEC),
        scratch=(pltpu.VMEM(held_shape, bf16), pltpu.SemaphoreType.DMA),
        moved=2 * row_count * HD * 2,
    )(info, *arrived)
    firsts = swap([chosen] * pieces, pieces)

    def gather_more(index, buffered):
        places = lax.dynamic_slice_in_dim(info, 1 + index * slots, slots)
        picked = jnp.take(held, places, axis=0)
        gathered = exchange(jnp.broadcast_to(picked[None], whole))
        return lax.dynamic_update_index_in_dim(buffered, gathered, index - 1, 0)

    more = lax.fori_loop(1, used, gather_more, spare)

    all_rows = row_count + rounds * slots * TILE
    attended, query_grad, key_own, value_own, more_terms, *terms = call(
        functools.partial(attention_kernel, pieces, tiles, slots, heads),
        [SMEM_SPEC] * 3 + [VMEM_SPEC] * 4 + [ANY_SPEC] + [VMEM_SPEC] * pieces,
        (
            shape(queries.shape, bf16),
            shape(queries.shape, f32),
            shape(key_rows.shape, f32),
            shape(value_rows.shape, f32),
            shape(buffer, bf16),
        )
        + (shape(message, bf16),) * pieces,
        (VMEM_SPEC,) * 4 + (ANY_SPEC,) + (VMEM_SPEC,) * pieces,
        scratch=(
            pltpu.VMEM((all_rows, row_count), f32),
            pltpu.VMEM((2, all_rows, HD), bf16),
            pltpu.VMEM((2, all_rows, HD), f32),
            pltpu.VMEM((all_rows, row_count), f32),
            pltpu.VMEM(whole, bf16),
            pltpu.SemaphoreType.DMA,
        ),
        flops=12 * heads * row_count * 2 * row_count * HD,
        moved=12 * row_count * heads * HD,
    )(tile_ids, tile_mask, info, queries, out_grad, key_rows, value_rows, more, *firsts)
    terms = swap(terms, pieces)

    def reduce_more(index, totals):
        got = exchange(lax.dynamic_index_in_dim(more_terms, index - 1, 0, keepdims=False))
        total = jnp.sum(got.astype(f32), axis=0).astype(bf16)
        return lax.dynamic_update_slice_in_dim(totals, total, index * slots, 0)

    extra = lax.fori_loop(1, used, reduce_more, spare_sums)
    returned = call(
        functools.partial(reduce_kernel, pieces, tiles, slots, tile_total),
        [SMEM_SPEC, ANY_SPEC] + [VMEM_SPEC] * pieces,
        (shape(message, bf16),) * pieces,
        (VMEM_SPEC,) * pieces,
        scratch=(pltpu.VMEM(total_shape, bf16), pltpu.SemaphoreType.DMA),
        moved=2 * row_count * HD * 2,
    )(info, extra, *terms)
    key_grad, value_grad = call(
        functools.partial(final_kernel, pieces, tiles),
        [VMEM_SPEC] * (2 + pieces),
        (shape(key_rows.shape, f32), shape(value_rows.shape, f32)),
        (VMEM_SPEC,) * 2,
        scratch=(pltpu.VMEM((2, row_count, HD), f32),),
        moved=5 * row_count * HD * 4,
    )(key_own, value_own, *swap(returned, pieces))
    return attended, query_grad, key_grad, value_grad


def solution(mesh):
    return jax.shard_map(
        per_device,
        mesh=mesh,
        in_specs=(
            P(("batch", "seq"), "head"),
            P(("batch", "seq"), "head"),
            P(("batch", "seq"), "head"),
            P(("batch", "seq"), "head"),
            P("batch"),
            P("batch", None),
        ),
        out_specs=(P(("batch", "seq"), "head"),) * 4,
        check_vma=False,
    )
```

```python
import functools
import math

import jax
import jax.numpy as jnp
from jax import lax
from jax.experimental import pallas as pl
from jax.experimental.pallas import tpu as pltpu
from jax.sharding import PartitionSpec as P

HD = 128
TILE = 128
FAR_BELOW = -1e30
LOG2E = 1.4426950408889634
NT_DIMS = (((1,), (1,)), ((), ()))
VMEM_LIMIT = 48 * 1024 * 1024

SMEM_SPEC = pl.BlockSpec(memory_space=pltpu.SMEM)
VMEM_SPEC = pl.BlockSpec(memory_space=pltpu.VMEM)
ANY_SPEC = pl.BlockSpec(memory_space=pl.ANY)


def call(kernel, in_specs, out_shape, out_specs, scratch=(), flops=0, moved=0):
    return pl.pallas_call(
        kernel,
        in_specs=in_specs,
        out_shape=out_shape,
        out_specs=out_specs,
        scratch_shapes=list(scratch),
        compiler_params=pltpu.CompilerParams(vmem_limit_bytes=VMEM_LIMIT),
        cost_estimate=pl.CostEstimate(flops=flops, bytes_accessed=moved, transcendentals=0),
    )


def tile_rows(first_row, tile):
    return pl.ds(pl.multiple_of(first_row + tile * TILE, TILE), TILE)


def shared_kernel(tile_total, tiles, ids_ref, mask_ref, info_ref, spare_ref, spare_sums_ref, any_ref):
    del spare_ref, spare_sums_ref
    for place in range(1, tile_total + 2):
        info_ref[place] = 0
    for tile in range(tile_total):
        users = mask_ref[0, tile]
        for other in range(1, tile_total):
            users = users + mask_ref[other, tile]
        any_ref[tile] = users
    count = jnp.int32(0)
    for position in range(tile_total):
        key_tile = ids_ref[position]
        away = any_ref[key_tile]
        for local in range(tiles):
            away = away - mask_ref[ids_ref[position // tiles * tiles + local], key_tile]
        info_ref[1 + count] = position
        info_ref[tile_total + 2 + position] = jnp.where(away > 0, count, -1)
        count = count + jnp.where(away > 0, 1, 0)
    info_ref[0] = count


def select_kernel(tiles, slots, base, info_ref, *refs):
    if base is None:
        base_ref, *refs = refs
        base = base_ref[0] * slots
    key_ref, value_ref, key_other, value_other, out_ref = refs
    rank = lax.axis_index("seq")
    odd = rank % 2
    out_ref[...] = jnp.zeros_like(out_ref)
    for slot in range(slots):
        position = info_ref[1 + base + slot]
        home = position // tiles
        rows = tile_rows(0, position % tiles)
        for kind, own, other in ((0, key_ref, key_other), (1, value_ref, value_other)):

            @pl.when((odd == kind) & (home == rank))
            def _():
                out_ref[slot] = own[rows, :]

            @pl.when((odd == kind) & (home == rank ^ 1))
            def _():
                out_ref[slot] = other[rows, :]


def final_kernel(tiles, slots, chips, tile_total, info_ref, extra_ref, key_ref, value_ref, *refs):
    sums, refs = refs[: 2 * chips], refs[2 * chips :]
    key_out, value_out, total_ref, staged_ref, copy_sem = refs
    rank = lax.axis_index("seq")
    odd = rank % 2
    total_ref[0] = key_ref[...]
    total_ref[1] = value_ref[...]
    for tile in range(tiles):
        slot = info_ref[tile_total + 2 + rank * tiles + tile]
        rows = tile_rows(0, tile)

        @pl.when((slot >= 0) & (slot < slots))
        def _():
            for part in range(2):
                terms = sums[part * chips : (part + 1) * chips]
                total = terms[0][slot].astype(jnp.float32)
                for source in terms[1:]:
                    total = total + source[slot].astype(jnp.float32)
                total_ref[odd ^ part, rows, :] += total

        @pl.when(slot >= slots)
        def _():
            for part in range(2):
                copy = pltpu.make_async_copy(
                    extra_ref.at[slot // slots - 1, part, slot % slots], staged_ref, copy_sem
                )
                copy.start()
                copy.wait()
                total_ref[odd ^ part, rows, :] += staged_ref[...].astype(jnp.float32)

    key_out[...] = total_ref[0]
    value_out[...] = total_ref[1]


def attention_kernel(
    chips,
    tiles,
    slots,
    heads,
    ids_ref,
    mask_ref,
    info_ref,
    query_ref,
    grad_ref,
    key_ref,
    value_ref,
    key_other,
    value_other,
    more_ref,
    *refs,
):
    arrived, handed, refs = refs[: chips - 1], refs[chips - 1 : 2 * chips - 2], refs[2 * chips - 2 :]
    attended_ref, query_out, key_out, value_out, keep_ref, give_ref, more_out, *refs = refs
    bias_ref, held_ref, sum_ref, score_ref, staged_ref, copy_sem = refs
    keys_ref, values_ref = held_ref.at[0], held_ref.at[1]
    key_sum, value_sum = sum_ref.at[0], sum_ref.at[1]
    rank = lax.axis_index("seq")
    odd = rank % 2
    rows = tiles * TILE
    chunk = slots * TILE
    factor = HD**-0.5
    scale = factor * LOG2E
    needed = info_ref[0]
    my_tiles = [ids_ref[rank * tiles + b] for b in range(tiles)]
    triangle = jnp.where(
        lax.broadcasted_iota(jnp.int32, (TILE, TILE), 0)
        <= lax.broadcasted_iota(jnp.int32, (TILE, TILE), 1),
        0.0,
        FAR_BELOW,
    )

    def block_bias(allowed):
        return jnp.full((TILE, TILE), jnp.where(allowed, 0.0, FAR_BELOW), jnp.float32)

    for a in range(tiles):
        for b in range(tiles):
            own = triangle if a == b else block_bias(mask_ref[my_tiles[b], my_tiles[a]] == 1)
            bias_ref[pl.ds(a * TILE, TILE), pl.ds(b * TILE, TILE)] = own

    def slot_bias(slot, first_row):
        position = info_ref[1 + slot]
        usable = (slot < needed) & (position // tiles != rank)
        tile = ids_ref[position]
        for b in range(tiles):
            bias_ref[pl.ds(first_row, TILE), pl.ds(b * TILE, TILE)] = block_bias(
                usable & (mask_ref[my_tiles[b], tile] == 1)
            )

    for slot in range(slots):
        slot_bias(jnp.int32(slot), rows + slot * TILE)

    keys_ref[pl.ds(0, rows), :] = key_ref[...]
    values_ref[pl.ds(0, rows), :] = value_ref[...]

    def repack(target, part, first_row):
        kind = odd ^ part
        for slot in range(slots):
            total = sum_ref[kind, tile_rows(first_row, slot), :]
            target[slot] = (total * jnp.where(kind == 0, factor, 1.0)).astype(jnp.bfloat16)

    for slot in range(slots):
        position = info_ref[1 + slot]
        away = (position // (2 * tiles)) ^ (rank // 2)
        at = tile_rows(rows, slot)

        @pl.when(away == 0)
        def _():
            source = tile_rows(0, position % tiles)
            keys_ref[at, :] = key_other[source, :]
            values_ref[at, :] = value_other[source, :]

        for step in range(1, chips):

            @pl.when(away == step)
            def _():
                held_ref[odd, at, :] = arrived[step - 1][slot]
                held_ref[odd ^ 1, at, :] = handed[step - 1][slot]

    head_columns = [pl.ds(h * HD, HD) for h in range(heads)]
    both = rows + chunk

    @pl.when(needed <= slots)
    def _():
        keys = keys_ref[pl.ds(0, both), :]
        values = values_ref[pl.ds(0, both), :]
        keys_t = keys.T
        values_t = values.T
        for h in range(heads):
            query = query_ref[:, head_columns[h]]
            grad = grad_ref[:, head_columns[h]]
            scores = (
                lax.dot_general(keys, query, NT_DIMS, preferred_element_type=jnp.float32) * scale
                + bias_ref[pl.ds(0, both), :]
            )
            row_max = jnp.max(scores, axis=0, keepdims=True)
            terms = jnp.exp2(scores - row_max)
            inverse = 1.0 / jnp.sum(terms, axis=0, keepdims=True)
            weighted = jnp.dot(
                values_t, terms.astype(jnp.bfloat16), preferred_element_type=jnp.float32
            )
            out = (weighted * inverse).astype(jnp.bfloat16)
            attended_ref[:, head_columns[h]] = out.T
            delta = jnp.sum(
                grad.T.astype(jnp.float32) * out.astype(jnp.float32), axis=0, keepdims=True
            )
            probs = terms * inverse
            dprobs = lax.dot_general(values, grad, NT_DIMS, preferred_element_type=jnp.float32)
            dscores = (probs * (dprobs - delta)).astype(jnp.bfloat16)
            query_t = jnp.dot(keys_t, dscores, preferred_element_type=jnp.float32) * factor
            query_out[:, head_columns[h]] = query_t.T
            key_part = jnp.dot(dscores, query, preferred_element_type=jnp.float32)
            value_part = jnp.dot(
                probs.astype(jnp.bfloat16), grad, preferred_element_type=jnp.float32
            )
            if h == 0:
                key_sum[pl.ds(0, both), :] = key_part
                value_sum[pl.ds(0, both), :] = value_part
            else:
                key_sum[pl.ds(0, both), :] += key_part
                value_sum[pl.ds(0, both), :] += value_part

    @pl.when(needed > slots)
    def _():
        used = (needed + slots - 1) // slots

        def fetch(index, carry):
            copy = pltpu.make_async_copy(more_ref.at[index], staged_ref, copy_sem)
            copy.start()
            copy.wait()
            first_row = pl.multiple_of(both + index * chunk, chunk)
            for slot in range(slots):
                for part in range(2):
                    held_ref[odd ^ part, tile_rows(first_row, slot), :] = staged_ref[part, slot]
                slot_bias((index + 1) * slots + slot, first_row + slot * TILE)
            return carry

        lax.fori_loop(0, used - 1, fetch, 0)
        key_sum[...] = jnp.zeros_like(key_sum)
        value_sum[...] = jnp.zeros_like(value_sum)
        blocks = (rows + used * chunk) // TILE

        def block_rows(index):
            return pl.ds(pl.multiple_of(index * TILE, TILE), TILE)

        for h in range(heads):
            query = query_ref[:, head_columns[h]]
            grad = grad_ref[:, head_columns[h]]

            def score(index, row_max):
                at = block_rows(index)
                scores = (
                    lax.dot_general(
                        keys_ref[at, :], query, NT_DIMS, preferred_element_type=jnp.float32
                    )
                    * scale
                    + bias_ref[at, :]
                )
                score_ref[at, :] = scores
                return jnp.maximum(row_max, jnp.max(scores, axis=0, keepdims=True))

            row_max = lax.fori_loop(
                0, blocks, score, jnp.full((1, rows), FAR_BELOW, jnp.float32)
            )

            def forward(index, carry):
                total, weighted = carry
                at = block_rows(index)
                terms = jnp.exp2(score_ref[at, :] - row_max)
                score_ref[at, :] = terms
                weighted = weighted + jnp.dot(
                    values_ref[at, :].T,
                    terms.astype(jnp.bfloat16),
                    preferred_element_type=jnp.float32,
                )
                return total + jnp.sum(terms, axis=0, keepdims=True), weighted

            total, weighted = lax.fori_loop(
                0,
                blocks,
                forward,
                (jnp.zeros((1, rows), jnp.float32), jnp.zeros((HD, rows), jnp.float32)),
            )
            inverse = 1.0 / total
            out = (weighted * inverse).astype(jnp.bfloat16)
            attended_ref[:, head_columns[h]] = out.T
            delta = jnp.sum(
                grad.T.astype(jnp.float32) * out.astype(jnp.float32), axis=0, keepdims=True
            )

            def backward(index, query_t):
                at = block_rows(index)
                probs = score_ref[at, :] * inverse
                dprobs = lax.dot_general(
                    values_ref[at, :], grad, NT_DIMS, preferred_element_type=jnp.float32
                )
                dscores = (probs * (dprobs - delta)).astype(jnp.bfloat16)
                key_sum[at, :] += jnp.dot(dscores, query, preferred_element_type=jnp.float32)
                value_sum[at, :] += jnp.dot(
                    probs.astype(jnp.bfloat16), grad, preferred_element_type=jnp.float32
                )
                return query_t + jnp.dot(
                    keys_ref[at, :].T, dscores, preferred_element_type=jnp.float32
                )

            query_t = lax.fori_loop(0, blocks, backward, jnp.zeros((HD, rows), jnp.float32))
            query_out[:, head_columns[h]] = (query_t * factor).T

        def store(index, carry):
            for part in range(2):
                repack(staged_ref.at[part], part, both + index * chunk)
            copy = pltpu.make_async_copy(staged_ref, more_out.at[index], copy_sem)
            copy.start()
            copy.wait()
            return carry

        lax.fori_loop(0, used - 1, store, 0)

    key_out[...] = key_sum[pl.ds(0, rows), :] * factor
    value_out[...] = value_sum[pl.ds(0, rows), :]
    repack(keep_ref, 0, rows)
    repack(give_ref, 1, rows)


def per_device(queries, key_rows, value_rows, out_grad, tile_ids, tile_mask):
    row_count = queries.shape[0]
    heads = queries.shape[1] // HD
    ranks = lax.axis_size("seq")
    chips = ranks // 2
    assert key_rows.shape[1] == HD and ranks > 1 and ranks & (ranks - 1) == 0
    tiles = row_count // TILE
    tile_total = tile_ids.shape[0]
    slots = tiles
    rounds = math.ceil(tile_total / slots)
    slot_shape = (slots, TILE, HD)
    buffer = (rounds - 1, 2) + slot_shape
    shape = jax.ShapeDtypeStruct
    bf16, f32 = jnp.bfloat16, jnp.float32

    def swap(values, step):
        return lax.ppermute(values, "seq", [(source, source ^ step) for source in range(ranks)])

    def across(values):
        return [swap(values, 2 * step) for step in range(1, chips)]

    def add(*values):
        total = values[0].astype(f32)
        for value in values[1:]:
            total = total + value.astype(f32)
        return total.astype(bf16)

    key_other, value_other = swap(key_rows, 1), swap(value_rows, 1)
    info, spare, spare_sums = call(
        functools.partial(shared_kernel, tile_total, tiles),
        [SMEM_SPEC] * 2,
        (shape((2 * tile_total + 2,), jnp.int32), shape(buffer, bf16), shape(buffer, bf16)),
        (SMEM_SPEC, ANY_SPEC, ANY_SPEC),
        scratch=(pltpu.SMEM((tile_total,), jnp.int32),),
        moved=4 * 1024 * 1024,
    )(tile_ids, tile_mask)
    used = (info[0] + slots - 1) // slots
    chip_rows = (key_rows, value_rows, key_other, value_other)

    def select(base, *lead):
        return call(
            functools.partial(select_kernel, tiles, slots, base),
            [SMEM_SPEC] * (1 + len(lead)) + [VMEM_SPEC] * 4,
            shape(slot_shape, bf16),
            VMEM_SPEC,
            moved=5 * row_count * HD * 2,
        )(info, *lead, *chip_rows)

    arrived = across(select(0))
    handed = [swap(values, 1) for values in arrived]

    def gather_more(index, buffered):
        chosen = select(None, index.reshape(1))
        total = add(chosen, *across(chosen))
        pair = jnp.stack([total, swap(total, 1)])
        return lax.dynamic_update_index_in_dim(buffered, pair, index - 1, 0)

    more = lax.fori_loop(1, used, gather_more, spare)

    all_rows = row_count + rounds * slots * TILE
    attended, query_grad, key_own, value_own, keep, give, more_terms = call(
        functools.partial(attention_kernel, chips, tiles, slots, heads),
        [SMEM_SPEC] * 3 + [VMEM_SPEC] * 6 + [ANY_SPEC] + [VMEM_SPEC] * (2 * chips - 2),
        (
            shape(queries.shape, bf16),
            shape(queries.shape, f32),
            shape(key_rows.shape, f32),
            shape(value_rows.shape, f32),
            shape(slot_shape, bf16),
            shape(slot_shape, bf16),
            shape(buffer, bf16),
        ),
        (VMEM_SPEC,) * 6 + (ANY_SPEC,),
        scratch=(
            pltpu.VMEM((all_rows, row_count), f32),
            pltpu.VMEM((2, all_rows, HD), bf16),
            pltpu.VMEM((2, all_rows, HD), f32),
            pltpu.VMEM((all_rows, row_count), f32),
            pltpu.VMEM((2,) + slot_shape, bf16),
            pltpu.SemaphoreType.DMA,
        ),
        flops=12 * heads * row_count * 2 * row_count * HD,
        moved=12 * row_count * heads * HD,
    )(tile_ids, tile_mask, info, queries, out_grad, *chip_rows, more, *arrived, *handed)

    chip_sum = add(keep, swap(give, 1))
    sums = [chip_sum] + across(chip_sum)
    sums = sums + [swap(values, 1) for values in sums]

    def reduce_more(index, totals):
        terms = lax.dynamic_index_in_dim(more_terms, index - 1, 0, keepdims=False)
        part = add(terms[0], swap(terms[1], 1))
        total = add(part, *across(part))
        pair = jnp.stack([total, swap(total, 1)])
        return lax.dynamic_update_index_in_dim(totals, pair, index - 1, 0)

    extra = lax.fori_loop(1, used, reduce_more, spare_sums)
    key_grad, value_grad = call(
        functools.partial(final_kernel, tiles, slots, chips, tile_total),
        [SMEM_SPEC, ANY_SPEC] + [VMEM_SPEC] * (2 + 2 * chips),
        (shape(key_rows.shape, f32), shape(value_rows.shape, f32)),
        (VMEM_SPEC,) * 2,
        scratch=(
            pltpu.VMEM((2, row_count, HD), f32),
            pltpu.VMEM((TILE, HD), bf16),
            pltpu.SemaphoreType.DMA,
        ),
        moved=5 * row_count * HD * 4,
    )(info, extra, key_own, value_own, *sums)
    return attended, query_grad, key_grad, value_grad


def solution(mesh):
    return jax.shard_map(
        per_device,
        mesh=mesh,
        in_specs=(
            P(("batch", "seq"), "head"),
            P(("batch", "seq"), "head"),
            P(("batch", "seq"), "head"),
            P(("batch", "seq"), "head"),
            P("batch"),
            P("batch", None),
        ),
        out_specs=(P(("batch", "seq"), "head"),) * 4,
        check_vma=False,
    )
```

```python
import functools
import math

import jax
import jax.numpy as jnp
from jax import lax
from jax.experimental import pallas as pl
from jax.experimental.pallas import tpu as pltpu
from jax.sharding import PartitionSpec as P

HD = 128
TILE = 128
FAR_BELOW = -1e30
LOG2E = 1.4426950408889634
NT_DIMS = (((1,), (1,)), ((), ()))
VMEM_LIMIT = 48 * 1024 * 1024

SMEM_SPEC = pl.BlockSpec(memory_space=pltpu.SMEM)
VMEM_SPEC = pl.BlockSpec(memory_space=pltpu.VMEM)
ANY_SPEC = pl.BlockSpec(memory_space=pl.ANY)


def call(kernel, in_specs, out_shape, out_specs, scratch=(), flops=0, moved=0):
    return pl.pallas_call(
        kernel,
        in_specs=in_specs,
        out_shape=out_shape,
        out_specs=out_specs,
        scratch_shapes=list(scratch),
        compiler_params=pltpu.CompilerParams(vmem_limit_bytes=VMEM_LIMIT),
        cost_estimate=pl.CostEstimate(flops=flops, bytes_accessed=moved, transcendentals=0),
    )


def tile_rows(first_row, tile):
    return pl.ds(pl.multiple_of(first_row + tile * TILE, TILE), TILE)


def holders(tile_total, info_ref):
    return info_ref[2 * tile_total + 2], info_ref[2 * tile_total + 3]


def route_parts(first, second, chips):
    third, fourth = [chip for chip in range(chips) if chip not in (first, second)]
    return [
        [(first, second), (second, first)],
        [(first, third), (second, fourth)],
        [(first, fourth), (second, third)],
    ]


def shared_kernel(tile_total, tiles, ids_ref, mask_ref, info_ref, spare_ref, spare_sums_ref, any_ref):
    del spare_ref, spare_sums_ref
    for place in range(1, tile_total + 2):
        info_ref[place] = 0
    for tile in range(tile_total):
        users = mask_ref[0, tile]
        for other in range(1, tile_total):
            users = users + mask_ref[other, tile]
        any_ref[tile] = users
    count = jnp.int32(0)
    for position in range(tile_total):
        key_tile = ids_ref[position]
        away = any_ref[key_tile]
        for local in range(tiles):
            away = away - mask_ref[ids_ref[position // tiles * tiles + local], key_tile]
        info_ref[1 + count] = position
        info_ref[tile_total + 2 + position] = jnp.where(away > 0, count, -1)
        count = count + jnp.where(away > 0, 1, 0)
    info_ref[0] = count
    first = jnp.where(count > 0, info_ref[1] // (2 * tiles), 0)
    second = jnp.where(count > 1, info_ref[2] // (2 * tiles), first)
    info_ref[2 * tile_total + 2] = first
    info_ref[2 * tile_total + 3] = second
    info_ref[2 * tile_total + 4] = second * (second + 1) // 2 + first


def select_kernel(tiles, slots, base, info_ref, *refs):
    if base is None:
        base_ref, *refs = refs
        base = base_ref[0] * slots
    key_ref, value_ref, key_other, value_other, out_ref, *single = refs
    rank = lax.axis_index("seq")
    odd = rank % 2
    out_ref[...] = jnp.zeros_like(out_ref)
    for slot in range(slots):
        position = info_ref[1 + base + slot]
        home = position // tiles
        rows = tile_rows(0, position % tiles)
        for kind, own, other in ((0, key_ref, key_other), (1, value_ref, value_other)):

            @pl.when((odd == kind) & (home == rank))
            def _():
                out_ref[slot] = own[rows, :]

            @pl.when((odd == kind) & (home == rank ^ 1))
            def _():
                out_ref[slot] = other[rows, :]

    if single:
        held = info_ref[1 + base] // (2 * tiles) == rank // 2
        single[0][...] = jnp.where(held, out_ref[0], out_ref[1])


def final_kernel(tiles, slots, chips, tile_total, routed, info_ref, extra_ref, key_ref, value_ref, *refs):
    sums, refs = refs[: 2 * chips], refs[2 * chips :]
    key_out, value_out, total_ref, staged_ref, copy_sem = refs
    rank = lax.axis_index("seq")
    odd = rank % 2
    total_ref[0] = key_ref[...]
    total_ref[1] = value_ref[...]
    for tile in range(tiles):
        slot = info_ref[tile_total + 2 + rank * tiles + tile]
        rows = tile_rows(0, tile)

        @pl.when((slot >= 0) & (slot < slots))
        def _():
            for part in range(2):
                own, *terms = sums[part * chips : (part + 1) * chips]
                if not routed:
                    total = own[slot].astype(jnp.float32)
                    for source in terms:
                        total = total + source[slot].astype(jnp.float32)
                    total_ref[odd ^ part, rows, :] += total
                    continue
                first, second = holders(tile_total, info_ref)

                @pl.when(first == second)
                def _():
                    total_ref[odd ^ part, rows, :] += own[slot].astype(jnp.float32)

                    @pl.when(slot == 0)
                    def _():
                        total_ref[odd ^ part, rows, :] += terms[1][...].astype(jnp.float32)

                    @pl.when(slot == 1)
                    def _():
                        total_ref[odd ^ part, rows, :] += terms[2][...].astype(jnp.float32)

                @pl.when(first != second)
                def _():
                    total = own[1].astype(jnp.float32)
                    for source in terms:
                        total = total + source[...].astype(jnp.float32)
                    total_ref[odd ^ part, rows, :] += total

        @pl.when(slot >= slots)
        def _():
            for part in range(2):
                copy = pltpu.make_async_copy(
                    extra_ref.at[slot // slots - 1, part, slot % slots], staged_ref, copy_sem
                )
                copy.start()
                copy.wait()
                total_ref[odd ^ part, rows, :] += staged_ref[...].astype(jnp.float32)

    key_out[...] = total_ref[0]
    value_out[...] = total_ref[1]


def attention_kernel(
    chips,
    tiles,
    slots,
    heads,
    routed,
    ids_ref,
    mask_ref,
    info_ref,
    query_ref,
    grad_ref,
    key_ref,
    value_ref,
    key_other,
    value_other,
    more_ref,
    *refs,
):
    arrived, handed, refs = refs[: chips - 1], refs[chips - 1 : 2 * chips - 2], refs[2 * chips - 2 :]
    attended_ref, query_out, key_out, value_out, keep_ref, give_ref, more_out, *refs = refs
    bias_ref, held_ref, sum_ref, score_ref, staged_ref, copy_sem = refs
    keys_ref, values_ref = held_ref.at[0], held_ref.at[1]
    key_sum, value_sum = sum_ref.at[0], sum_ref.at[1]
    rank = lax.axis_index("seq")
    odd = rank % 2
    rows = tiles * TILE
    chunk = slots * TILE
    factor = HD**-0.5
    scale = factor * LOG2E
    needed = info_ref[0]
    chip = rank // 2
    first, second = holders(ids_ref.shape[0], info_ref)
    apart = first != second
    place = chip - (first < chip).astype(jnp.int32) - (second < chip).astype(jnp.int32)
    turned = apart & (chip != first) & (chip != second) & (place == 1)
    my_tiles = [ids_ref[rank * tiles + b] for b in range(tiles)]
    triangle = jnp.where(
        lax.broadcasted_iota(jnp.int32, (TILE, TILE), 0)
        <= lax.broadcasted_iota(jnp.int32, (TILE, TILE), 1),
        0.0,
        FAR_BELOW,
    )

    def block_bias(allowed):
        return jnp.full((TILE, TILE), jnp.where(allowed, 0.0, FAR_BELOW), jnp.float32)

    for a in range(tiles):
        for b in range(tiles):
            own = triangle if a == b else block_bias(mask_ref[my_tiles[b], my_tiles[a]] == 1)
            bias_ref[pl.ds(a * TILE, TILE), pl.ds(b * TILE, TILE)] = own

    def slot_bias(slot, first_row):
        position = info_ref[1 + slot]
        usable = (slot < needed) & (position // tiles != rank)
        tile = ids_ref[position]
        for b in range(tiles):
            bias_ref[pl.ds(first_row, TILE), pl.ds(b * TILE, TILE)] = block_bias(
                usable & (mask_ref[my_tiles[b], tile] == 1)
            )

    for slot in range(slots):
        slot_bias(jnp.int32(slot), rows + slot * TILE)

    keys_ref[pl.ds(0, rows), :] = key_ref[...]
    values_ref[pl.ds(0, rows), :] = value_ref[...]

    def repack(target, part, first_row, swapped=0):
        kind = odd ^ part
        for slot in range(slots):
            total = sum_ref[kind, tile_rows(first_row, slot ^ swapped), :]
            target[slot] = (total * jnp.where(kind == 0, factor, 1.0)).astype(jnp.bfloat16)

    for slot in range(slots):
        position = info_ref[1 + slot]
        away = (position // (2 * tiles)) ^ chip
        at = tile_rows(rows, slot)
        if routed:
            holder = second if slot else first
            relayed = jnp.where(turned, 3 - slot, 2 + slot)
            away = jnp.where(apart & ((chip == first) | (chip == second)), 1, relayed)
            away = jnp.where(holder == chip, 0, away)

        @pl.when(away == 0)
        def _():
            source = tile_rows(0, position % tiles)
            keys_ref[at, :] = key_other[source, :]
            values_ref[at, :] = value_other[source, :]

        for step in range(1, chips):

            @pl.when(away == step)
            def _():
                which = ... if routed else slot
                held_ref[odd, at, :] = arrived[step - 1][which]
                held_ref[odd ^ 1, at, :] = handed[step - 1][which]

    head_columns = [pl.ds(h * HD, HD) for h in range(heads)]
    both = rows + chunk

    @pl.when(needed <= slots)
    def _():
        keys = keys_ref[pl.ds(0, both), :]
        values = values_ref[pl.ds(0, both), :]
        keys_t = keys.T
        values_t = values.T
        for h in range(heads):
            query = query_ref[:, head_columns[h]]
            grad = grad_ref[:, head_columns[h]]
            scores = (
                lax.dot_general(keys, query, NT_DIMS, preferred_element_type=jnp.float32) * scale
                + bias_ref[pl.ds(0, both), :]
            )
            row_max = jnp.max(scores, axis=0, keepdims=True)
            terms = jnp.exp2(scores - row_max)
            inverse = 1.0 / jnp.sum(terms, axis=0, keepdims=True)
            weighted = jnp.dot(
                values_t, terms.astype(jnp.bfloat16), preferred_element_type=jnp.float32
            )
            out = (weighted * inverse).astype(jnp.bfloat16)
            attended_ref[:, head_columns[h]] = out.T
            delta = jnp.sum(
                grad.T.astype(jnp.float32) * out.astype(jnp.float32), axis=0, keepdims=True
            )
            probs = terms * inverse
            dprobs = lax.dot_general(values, grad, NT_DIMS, preferred_element_type=jnp.float32)
            dscores = (probs * (dprobs - delta)).astype(jnp.bfloat16)
            query_t = jnp.dot(keys_t, dscores, preferred_element_type=jnp.float32) * factor
            query_out[:, head_columns[h]] = query_t.T
            key_part = jnp.dot(dscores, query, preferred_element_type=jnp.float32)
            value_part = jnp.dot(
                probs.astype(jnp.bfloat16), grad, preferred_element_type=jnp.float32
            )
            if h == 0:
                key_sum[pl.ds(0, both), :] = key_part
                value_sum[pl.ds(0, both), :] = value_part
            else:
                key_sum[pl.ds(0, both), :] += key_part
                value_sum[pl.ds(0, both), :] += value_part

    @pl.when(needed > slots)
    def _():
        used = (needed + slots - 1) // slots

        def fetch(index, carry):
            copy = pltpu.make_async_copy(more_ref.at[index], staged_ref, copy_sem)
            copy.start()
            copy.wait()
            first_row = pl.multiple_of(both + index * chunk, chunk)
            for slot in range(slots):
                for part in range(2):
                    held_ref[odd ^ part, tile_rows(first_row, slot), :] = staged_ref[part, slot]
                slot_bias((index + 1) * slots + slot, first_row + slot * TILE)
            return carry

        lax.fori_loop(0, used - 1, fetch, 0)
        key_sum[...] = jnp.zeros_like(key_sum)
        value_sum[...] = jnp.zeros_like(value_sum)
        blocks = (rows + used * chunk) // TILE

        def block_rows(index):
            return pl.ds(pl.multiple_of(index * TILE, TILE), TILE)

        for h in range(heads):
            query = query_ref[:, head_columns[h]]
            grad = grad_ref[:, head_columns[h]]

            def score(index, row_max):
                at = block_rows(index)
                scores = (
                    lax.dot_general(
                        keys_ref[at, :], query, NT_DIMS, preferred_element_type=jnp.float32
                    )
                    * scale
                    + bias_ref[at, :]
                )
                score_ref[at, :] = scores
                return jnp.maximum(row_max, jnp.max(scores, axis=0, keepdims=True))

            row_max = lax.fori_loop(
                0, blocks, score, jnp.full((1, rows), FAR_BELOW, jnp.float32)
            )

            def forward(index, carry):
                total, weighted = carry
                at = block_rows(index)
                terms = jnp.exp2(score_ref[at, :] - row_max)
                score_ref[at, :] = terms
                weighted = weighted + jnp.dot(
                    values_ref[at, :].T,
                    terms.astype(jnp.bfloat16),
                    preferred_element_type=jnp.float32,
                )
                return total + jnp.sum(terms, axis=0, keepdims=True), weighted

            total, weighted = lax.fori_loop(
                0,
                blocks,
                forward,
                (jnp.zeros((1, rows), jnp.float32), jnp.zeros((HD, rows), jnp.float32)),
            )
            inverse = 1.0 / total
            out = (weighted * inverse).astype(jnp.bfloat16)
            attended_ref[:, head_columns[h]] = out.T
            delta = jnp.sum(
                grad.T.astype(jnp.float32) * out.astype(jnp.float32), axis=0, keepdims=True
            )

            def backward(index, query_t):
                at = block_rows(index)
                probs = score_ref[at, :] * inverse
                dprobs = lax.dot_general(
                    values_ref[at, :], grad, NT_DIMS, preferred_element_type=jnp.float32
                )
                dscores = (probs * (dprobs - delta)).astype(jnp.bfloat16)
                key_sum[at, :] += jnp.dot(dscores, query, preferred_element_type=jnp.float32)
                value_sum[at, :] += jnp.dot(
                    probs.astype(jnp.bfloat16), grad, preferred_element_type=jnp.float32
                )
                return query_t + jnp.dot(
                    keys_ref[at, :].T, dscores, preferred_element_type=jnp.float32
                )

            query_t = lax.fori_loop(0, blocks, backward, jnp.zeros((HD, rows), jnp.float32))
            query_out[:, head_columns[h]] = (query_t * factor).T

        def store(index, carry):
            for part in range(2):
                repack(staged_ref.at[part], part, both + index * chunk)
            copy = pltpu.make_async_copy(staged_ref, more_out.at[index], copy_sem)
            copy.start()
            copy.wait()
            return carry

        lax.fori_loop(0, used - 1, store, 0)

    key_out[...] = key_sum[pl.ds(0, rows), :] * factor
    value_out[...] = value_sum[pl.ds(0, rows), :]
    swapped = 0
    if routed:
        swapped = ((apart & (chip == first)) | turned).astype(jnp.int32)
    repack(keep_ref, 0, rows, swapped)
    repack(give_ref, 1, rows, swapped)


def per_device(queries, key_rows, value_rows, out_grad, tile_ids, tile_mask):
    row_count = queries.shape[0]
    heads = queries.shape[1] // HD
    ranks = lax.axis_size("seq")
    chips = ranks // 2
    assert key_rows.shape[1] == HD and ranks > 1 and ranks & (ranks - 1) == 0
    tiles = row_count // TILE
    tile_total = tile_ids.shape[0]
    slots = tiles
    rounds = math.ceil(tile_total / slots)
    slot_shape = (slots, TILE, HD)
    buffer = (rounds - 1, 2) + slot_shape
    shape = jax.ShapeDtypeStruct
    bf16, f32 = jnp.bfloat16, jnp.float32

    def swap(values, step):
        return lax.ppermute(values, "seq", [(source, source ^ step) for source in range(ranks)])

    def across(values):
        return [swap(values, 2 * step) for step in range(1, chips)]

    def add(*values):
        total = values[0].astype(f32)
        for value in values[1:]:
            total = total + value.astype(f32)
        return total.astype(bf16)

    key_other, value_other = swap(key_rows, 1), swap(value_rows, 1)
    routed = chips == 4 and slots == 2

    def route_switch(branch_index, build, *operands):
        branches = [
            functools.partial(build, first, second)
            for second in range(chips)
            for first in range(second + 1)
        ]
        return lax.switch(branch_index, branches, *operands)

    def chip_permute(values, pairs):
        return lax.ppermute(
            values, "seq", [(2 * a + core, 2 * b + core) for a, b in pairs for core in range(2)]
        )

    def spread(first, second, pair, single):
        if first == second:
            others = [chip for chip in range(chips) if chip != first]
            total = add(*[chip_permute(pair, [(first, other)]) for other in others])
            return total[0], total[0], total[1]
        return tuple(chip_permute(single, part) for part in route_parts(first, second, chips))

    def collect(first, second, pair):
        if first == second:
            others = [chip for chip in range(chips) if chip != first]
            total = add(*[chip_permute(pair, [(other, first)]) for other in others])
            return total[0], total[0], total[1]
        out = []
        for place, part in enumerate(route_parts(first, second, chips)):
            back = [(target, source) for source, target in part]
            out.append(chip_permute(pair[place // 2], back))
        return tuple(out)

    info, spare, spare_sums = call(
        functools.partial(shared_kernel, tile_total, tiles),
        [SMEM_SPEC] * 2,
        (shape((2 * tile_total + 5,), jnp.int32), shape(buffer, bf16), shape(buffer, bf16)),
        (SMEM_SPEC, ANY_SPEC, ANY_SPEC),
        scratch=(pltpu.SMEM((tile_total,), jnp.int32),),
        moved=4 * 1024 * 1024,
    )(tile_ids, tile_mask)
    used = (info[0] + slots - 1) // slots
    chip_rows = (key_rows, value_rows, key_other, value_other)

    def select(base, *lead):
        single = routed and base == 0
        return call(
            functools.partial(select_kernel, tiles, slots, base),
            [SMEM_SPEC] * (1 + len(lead)) + [VMEM_SPEC] * 4,
            (shape(slot_shape, bf16),) + (shape((TILE, HD), bf16),) * single,
            (VMEM_SPEC,) * (1 + single),
            moved=5 * row_count * HD * 2,
        )(info, *lead, *chip_rows)

    branch_index = info[2 * tile_total + 4]
    if routed:
        arrived = route_switch(branch_index, spread, *select(0))
    else:
        arrived = across(*select(0))
    handed = [swap(values, 1) for values in arrived]

    def gather_more(index, buffered):
        (chosen,) = select(None, index.reshape(1))
        total = add(chosen, *across(chosen))
        pair = jnp.stack([total, swap(total, 1)])
        return lax.dynamic_update_index_in_dim(buffered, pair, index - 1, 0)

    more = lax.fori_loop(1, used, gather_more, spare)

    all_rows = row_count + rounds * slots * TILE
    attended, query_grad, key_own, value_own, keep, give, more_terms = call(
        functools.partial(attention_kernel, chips, tiles, slots, heads, routed),
        [SMEM_SPEC] * 3 + [VMEM_SPEC] * 6 + [ANY_SPEC] + [VMEM_SPEC] * (2 * chips - 2),
        (
            shape(queries.shape, bf16),
            shape(queries.shape, f32),
            shape(key_rows.shape, f32),
            shape(value_rows.shape, f32),
            shape(slot_shape, bf16),
            shape(slot_shape, bf16),
            shape(buffer, bf16),
        ),
        (VMEM_SPEC,) * 6 + (ANY_SPEC,),
        scratch=(
            pltpu.VMEM((all_rows, row_count), f32),
            pltpu.VMEM((2, all_rows, HD), bf16),
            pltpu.VMEM((2, all_rows, HD), f32),
            pltpu.VMEM((all_rows, row_count), f32),
            pltpu.VMEM((2,) + slot_shape, bf16),
            pltpu.SemaphoreType.DMA,
        ),
        flops=12 * heads * row_count * 2 * row_count * HD,
        moved=12 * row_count * heads * HD,
    )(tile_ids, tile_mask, info, queries, out_grad, *chip_rows, more, *arrived, *handed)

    chip_sum = add(keep, swap(give, 1))
    if routed:
        sums = [chip_sum, *route_switch(branch_index, collect, chip_sum)]
    else:
        sums = [chip_sum] + across(chip_sum)
    sums = sums + [swap(values, 1) for values in sums]

    def reduce_more(index, totals):
        terms = lax.dynamic_index_in_dim(more_terms, index - 1, 0, keepdims=False)
        part = add(terms[0], swap(terms[1], 1))
        total = add(part, *across(part))
        pair = jnp.stack([total, swap(total, 1)])
        return lax.dynamic_update_index_in_dim(totals, pair, index - 1, 0)

    extra = lax.fori_loop(1, used, reduce_more, spare_sums)
    key_grad, value_grad = call(
        functools.partial(final_kernel, tiles, slots, chips, tile_total, routed),
        [SMEM_SPEC, ANY_SPEC] + [VMEM_SPEC] * (2 + 2 * chips),
        (shape(key_rows.shape, f32), shape(value_rows.shape, f32)),
        (VMEM_SPEC,) * 2,
        scratch=(
            pltpu.VMEM((2, row_count, HD), f32),
            pltpu.VMEM((TILE, HD), bf16),
            pltpu.SemaphoreType.DMA,
        ),
        moved=5 * row_count * HD * 4,
    )(info, extra, key_own, value_own, *sums)
    return attended, query_grad, key_grad, value_grad


def solution(mesh):
    return jax.shard_map(
        per_device,
        mesh=mesh,
        in_specs=(
            P(("batch", "seq"), "head"),
            P(("batch", "seq"), "head"),
            P(("batch", "seq"), "head"),
            P(("batch", "seq"), "head"),
            P("batch"),
            P("batch", None),
        ),
        out_specs=(P(("batch", "seq"), "head"),) * 4,
        check_vma=False,
    )
```

```python
import functools
import math

import jax
import jax.numpy as jnp
from jax import lax
from jax.experimental import pallas as pl
from jax.experimental.pallas import tpu as pltpu
from jax.sharding import PartitionSpec as P

HD = 128
TILE = 128
FAR_BELOW = -1e30
LOG2E = 1.4426950408889634
NT_DIMS = (((1,), (1,)), ((), ()))
VMEM_LIMIT = 48 * 1024 * 1024

SMEM_SPEC = pl.BlockSpec(memory_space=pltpu.SMEM)
VMEM_SPEC = pl.BlockSpec(memory_space=pltpu.VMEM)
ANY_SPEC = pl.BlockSpec(memory_space=pl.ANY)


def call(kernel, in_specs, out_shape, out_specs, scratch=(), flops=0, moved=0):
    return pl.pallas_call(
        kernel,
        in_specs=in_specs,
        out_shape=out_shape,
        out_specs=out_specs,
        scratch_shapes=list(scratch),
        compiler_params=pltpu.CompilerParams(vmem_limit_bytes=VMEM_LIMIT),
        cost_estimate=pl.CostEstimate(flops=flops, bytes_accessed=moved, transcendentals=0),
    )


def tile_rows(first_row, tile):
    return pl.ds(pl.multiple_of(first_row + tile * TILE, TILE), TILE)


def shared_kernel(tile_total, tiles, ids_any, mask_any, info_ref, spare_ref, spare_sums_ref, *refs):
    del spare_ref, spare_sums_ref
    any_ref, ids_ref, mask_ref, ids_sem, mask_sem = refs
    copies = [
        pltpu.make_async_copy(ids_any, ids_ref, ids_sem),
        pltpu.make_async_copy(mask_any, mask_ref, mask_sem),
    ]
    for copy in copies:
        copy.start()
    for copy in copies:
        copy.wait()
    for place in range(1, tile_total + 2):
        info_ref[place] = 0
    for tile in range(tile_total):
        users = mask_ref[0, tile]
        for other in range(1, tile_total):
            users = users + mask_ref[other, tile]
        any_ref[tile] = users
    count = jnp.int32(0)
    for position in range(tile_total):
        key_tile = ids_ref[position]
        away = any_ref[key_tile]
        for local in range(tiles):
            away = away - mask_ref[ids_ref[position // tiles * tiles + local], key_tile]
        info_ref[1 + count] = position
        info_ref[tile_total + 2 + position] = jnp.where(away > 0, count, -1)
        count = count + jnp.where(away > 0, 1, 0)
    info_ref[0] = count


def select_kernel(tiles, slots, base, info_ref, *refs):
    if base is None:
        base_ref, *refs = refs
        base = base_ref[0] * slots
    key_ref, value_ref, key_other, value_other, out_ref = refs
    rank = lax.axis_index("seq")
    odd = rank % 2
    out_ref[...] = jnp.zeros_like(out_ref)
    for slot in range(slots):
        position = info_ref[1 + base + slot]
        home = position // tiles
        rows = tile_rows(0, position % tiles)
        for kind, own, other in ((0, key_ref, key_other), (1, value_ref, value_other)):

            @pl.when((odd == kind) & (home == rank))
            def _():
                out_ref[slot] = own[rows, :]

            @pl.when((odd == kind) & (home == rank ^ 1))
            def _():
                out_ref[slot] = other[rows, :]


def final_kernel(tiles, slots, tile_total, info_ref, extra_ref, key_ref, value_ref, *refs):
    own_sums, other_sums, key_out, value_out, staged_ref, copy_sem = refs
    rank = lax.axis_index("seq")
    odd = rank % 2
    outs = (key_out, value_out)
    key_out[...] = key_ref[...]
    value_out[...] = value_ref[...]
    for tile in range(tiles):
        slot = info_ref[tile_total + 2 + rank * tiles + tile]
        rows = tile_rows(0, tile)
        for kind, out in enumerate(outs):
            for part, source in enumerate((own_sums, other_sums)):

                @pl.when((slot >= 0) & (slot < slots) & (odd ^ part == kind))
                def _():
                    out[rows, :] += source[slot].astype(jnp.float32)

                @pl.when((slot >= slots) & (odd ^ part == kind))
                def _():
                    copy = pltpu.make_async_copy(
                        extra_ref.at[slot // slots - 1, part, slot % slots], staged_ref, copy_sem
                    )
                    copy.start()
                    copy.wait()
                    out[rows, :] += staged_ref[...].astype(jnp.float32)


def attention_kernel(
    tiles,
    slots,
    heads,
    ids_ref,
    mask_ref,
    info_ref,
    query_ref,
    grad_ref,
    key_ref,
    value_ref,
    own_slots,
    other_slots,
    more_ref,
    attended_ref,
    query_out,
    key_out,
    value_out,
    keep_ref,
    give_ref,
    more_out,
    bias_ref,
    held_ref,
    sum_ref,
    score_ref,
    staged_ref,
    copy_sem,
):
    keys_ref, values_ref = held_ref.at[0], held_ref.at[1]
    key_sum, value_sum = sum_ref.at[0], sum_ref.at[1]
    rank = lax.axis_index("seq")
    odd = rank % 2
    rows = tiles * TILE
    chunk = slots * TILE
    factor = HD**-0.5
    scale = factor * LOG2E
    needed = info_ref[0]
    my_tiles = [ids_ref[rank * tiles + b] for b in range(tiles)]
    triangle = jnp.where(
        lax.broadcasted_iota(jnp.int32, (TILE, TILE), 0)
        <= lax.broadcasted_iota(jnp.int32, (TILE, TILE), 1),
        0.0,
        FAR_BELOW,
    )

    def block_bias(allowed):
        return jnp.full((TILE, TILE), jnp.where(allowed, 0.0, FAR_BELOW), jnp.float32)

    for a in range(tiles):
        for b in range(tiles):
            own = triangle if a == b else block_bias(mask_ref[my_tiles[b], my_tiles[a]] == 1)
            bias_ref[pl.ds(a * TILE, TILE), pl.ds(b * TILE, TILE)] = own

    def slot_bias(slot, first_row):
        position = info_ref[1 + slot]
        usable = (slot < needed) & (position // tiles != rank)
        tile = ids_ref[position]
        for b in range(tiles):
            bias_ref[pl.ds(first_row, TILE), pl.ds(b * TILE, TILE)] = block_bias(
                usable & (mask_ref[my_tiles[b], tile] == 1)
            )

    for slot in range(slots):
        slot_bias(jnp.int32(slot), rows + slot * TILE)

    keys_ref[pl.ds(0, rows), :] = key_ref[...]
    values_ref[pl.ds(0, rows), :] = value_ref[...]

    def repack(target, part, first_row):
        kind = odd ^ part
        for slot in range(slots):
            total = sum_ref[kind, tile_rows(first_row, slot), :]
            target[slot] = (total * jnp.where(kind == 0, factor, 1.0)).astype(jnp.bfloat16)

    for slot in range(slots):
        at = tile_rows(rows, slot)
        held_ref[odd, at, :] = own_slots[slot]
        held_ref[odd ^ 1, at, :] = other_slots[slot]

    head_columns = [pl.ds(h * HD, HD) for h in range(heads)]
    both = rows + chunk

    @pl.when(needed <= slots)
    def _():
        keys = keys_ref[pl.ds(0, both), :]
        values = values_ref[pl.ds(0, both), :]
        keys_t = keys.T
        values_t = values.T
        for h in range(heads):
            query = query_ref[:, head_columns[h]]
            grad = grad_ref[:, head_columns[h]]
            scores = (
                lax.dot_general(keys, query, NT_DIMS, preferred_element_type=jnp.float32) * scale
                + bias_ref[pl.ds(0, both), :]
            )
            row_max = jnp.max(scores, axis=0, keepdims=True)
            terms = jnp.exp2(scores - row_max)
            inverse = 1.0 / jnp.sum(terms, axis=0, keepdims=True)
            weighted = jnp.dot(
                values_t, terms.astype(jnp.bfloat16), preferred_element_type=jnp.float32
            )
            out = (weighted * inverse).astype(jnp.bfloat16)
            attended_ref[:, head_columns[h]] = out.T
            delta = jnp.sum(
                grad.T.astype(jnp.float32) * out.astype(jnp.float32), axis=0, keepdims=True
            )
            probs = terms * inverse
            dprobs = lax.dot_general(values, grad, NT_DIMS, preferred_element_type=jnp.float32)
            dscores = (probs * (dprobs - delta)).astype(jnp.bfloat16)
            query_t = jnp.dot(keys_t, dscores, preferred_element_type=jnp.float32) * factor
            query_out[:, head_columns[h]] = query_t.T
            key_part = jnp.dot(dscores, query, preferred_element_type=jnp.float32)
            value_part = jnp.dot(
                probs.astype(jnp.bfloat16), grad, preferred_element_type=jnp.float32
            )
            if h == 0:
                key_sum[pl.ds(0, both), :] = key_part
                value_sum[pl.ds(0, both), :] = value_part
            else:
                key_sum[pl.ds(0, both), :] += key_part
                value_sum[pl.ds(0, both), :] += value_part

    @pl.when(needed > slots)
    def _():
        used = (needed + slots - 1) // slots

        def fetch(index, carry):
            copy = pltpu.make_async_copy(more_ref.at[index], staged_ref, copy_sem)
            copy.start()
            copy.wait()
            first_row = pl.multiple_of(both + index * chunk, chunk)
            for slot in range(slots):
                for part in range(2):
                    held_ref[odd ^ part, tile_rows(first_row, slot), :] = staged_ref[part, slot]
                slot_bias((index + 1) * slots + slot, first_row + slot * TILE)
            return carry

        lax.fori_loop(0, used - 1, fetch, 0)
        key_sum[...] = jnp.zeros_like(key_sum)
        value_sum[...] = jnp.zeros_like(value_sum)
        blocks = (rows + used * chunk) // TILE

        def block_rows(index):
            return pl.ds(pl.multiple_of(index * TILE, TILE), TILE)

        for h in range(heads):
            query = query_ref[:, head_columns[h]]
            grad = grad_ref[:, head_columns[h]]

            def score(index, row_max):
                at = block_rows(index)
                scores = (
                    lax.dot_general(
                        keys_ref[at, :], query, NT_DIMS, preferred_element_type=jnp.float32
                    )
                    * scale
                    + bias_ref[at, :]
                )
                score_ref[at, :] = scores
                return jnp.maximum(row_max, jnp.max(scores, axis=0, keepdims=True))

            row_max = lax.fori_loop(
                0, blocks, score, jnp.full((1, rows), FAR_BELOW, jnp.float32)
            )

            def forward(index, carry):
                total, weighted = carry
                at = block_rows(index)
                terms = jnp.exp2(score_ref[at, :] - row_max)
                score_ref[at, :] = terms
                weighted = weighted + jnp.dot(
                    values_ref[at, :].T,
                    terms.astype(jnp.bfloat16),
                    preferred_element_type=jnp.float32,
                )
                return total + jnp.sum(terms, axis=0, keepdims=True), weighted

            total, weighted = lax.fori_loop(
                0,
                blocks,
                forward,
                (jnp.zeros((1, rows), jnp.float32), jnp.zeros((HD, rows), jnp.float32)),
            )
            inverse = 1.0 / total
            out = (weighted * inverse).astype(jnp.bfloat16)
            attended_ref[:, head_columns[h]] = out.T
            delta = jnp.sum(
                grad.T.astype(jnp.float32) * out.astype(jnp.float32), axis=0, keepdims=True
            )

            def backward(index, query_t):
                at = block_rows(index)
                probs = score_ref[at, :] * inverse
                dprobs = lax.dot_general(
                    values_ref[at, :], grad, NT_DIMS, preferred_element_type=jnp.float32
                )
                dscores = (probs * (dprobs - delta)).astype(jnp.bfloat16)
                key_sum[at, :] += jnp.dot(dscores, query, preferred_element_type=jnp.float32)
                value_sum[at, :] += jnp.dot(
                    probs.astype(jnp.bfloat16), grad, preferred_element_type=jnp.float32
                )
                return query_t + jnp.dot(
                    keys_ref[at, :].T, dscores, preferred_element_type=jnp.float32
                )

            query_t = lax.fori_loop(0, blocks, backward, jnp.zeros((HD, rows), jnp.float32))
            query_out[:, head_columns[h]] = (query_t * factor).T

        def store(index, carry):
            for part in range(2):
                repack(staged_ref.at[part], part, both + index * chunk)
            copy = pltpu.make_async_copy(staged_ref, more_out.at[index], copy_sem)
            copy.start()
            copy.wait()
            return carry

        lax.fori_loop(0, used - 1, store, 0)

    key_out[...] = key_sum[pl.ds(0, rows), :] * factor
    value_out[...] = value_sum[pl.ds(0, rows), :]
    repack(keep_ref, 0, rows)
    repack(give_ref, 1, rows)


def per_device(queries, key_rows, value_rows, out_grad, tile_ids, tile_mask):
    row_count = queries.shape[0]
    heads = queries.shape[1] // HD
    ranks = lax.axis_size("seq")
    assert key_rows.shape[1] == HD and ranks > 1 and ranks & (ranks - 1) == 0
    tiles = row_count // TILE
    tile_total = tile_ids.shape[0]
    slots = tiles
    rounds = math.ceil(tile_total / slots)
    slot_shape = (slots, TILE, HD)
    buffer = (rounds - 1, 2) + slot_shape
    shape = jax.ShapeDtypeStruct
    bf16, f32 = jnp.bfloat16, jnp.float32

    def swap(values, step):
        return lax.ppermute(values, "seq", [(source, source ^ step) for source in range(ranks)])

    def add(one, other):
        return (one.astype(f32) + other.astype(f32)).astype(bf16)

    def chip_total(values):
        step = ranks // 2
        while step > 1:
            values = add(values, swap(values, step))
            step //= 2
        return values, swap(values, 1)

    key_other, value_other = swap(key_rows, 1), swap(value_rows, 1)
    info, spare, spare_sums = call(
        functools.partial(shared_kernel, tile_total, tiles),
        [ANY_SPEC] * 2,
        (shape((2 * tile_total + 2,), jnp.int32), shape(buffer, bf16), shape(buffer, bf16)),
        (SMEM_SPEC, ANY_SPEC, ANY_SPEC),
        scratch=(
            pltpu.SMEM((tile_total,), jnp.int32),
            pltpu.SMEM(tile_ids.shape, jnp.int32),
            pltpu.SMEM(tile_mask.shape, jnp.int32),
            pltpu.SemaphoreType.DMA,
            pltpu.SemaphoreType.DMA,
        ),
        moved=4 * 1024 * 1024,
    )(tile_ids, tile_mask)
    used = (info[0] + slots - 1) // slots
    chip_rows = (key_rows, value_rows, key_other, value_other)

    def select(base, *lead):
        return call(
            functools.partial(select_kernel, tiles, slots, base),
            [SMEM_SPEC] * (1 + len(lead)) + [VMEM_SPEC] * 4,
            shape(slot_shape, bf16),
            VMEM_SPEC,
            moved=5 * row_count * HD * 2,
        )(info, *lead, *chip_rows)

    own_slots, other_slots = chip_total(select(0))

    def gather_more(index, buffered):
        pair = jnp.stack(chip_total(select(None, index.reshape(1))))
        return lax.dynamic_update_index_in_dim(buffered, pair, index - 1, 0)

    more = lax.fori_loop(1, used, gather_more, spare)

    all_rows = row_count + rounds * slots * TILE
    attended, query_grad, key_own, value_own, keep, give, more_terms = call(
        functools.partial(attention_kernel, tiles, slots, heads),
        [SMEM_SPEC] * 3 + [VMEM_SPEC] * 6 + [ANY_SPEC],
        (
            shape(queries.shape, bf16),
            shape(queries.shape, f32),
            shape(key_rows.shape, f32),
            shape(value_rows.shape, f32),
            shape(slot_shape, bf16),
            shape(slot_shape, bf16),
            shape(buffer, bf16),
        ),
        (VMEM_SPEC,) * 6 + (ANY_SPEC,),
        scratch=(
            pltpu.VMEM((all_rows, row_count), f32),
            pltpu.VMEM((2, all_rows, HD), bf16),
            pltpu.VMEM((2, all_rows, HD), f32),
            pltpu.VMEM((all_rows, row_count), f32),
            pltpu.VMEM((2,) + slot_shape, bf16),
            pltpu.SemaphoreType.DMA,
        ),
        flops=12 * heads * row_count * 2 * row_count * HD,
        moved=12 * row_count * heads * HD,
    )(tile_ids, tile_mask, info, queries, out_grad, key_rows, value_rows, own_slots, other_slots, more)

    own_sums, other_sums = chip_total(add(keep, swap(give, 1)))

    def reduce_more(index, totals):
        terms = lax.dynamic_index_in_dim(more_terms, index - 1, 0, keepdims=False)
        pair = jnp.stack(chip_total(add(terms[0], swap(terms[1], 1))))
        return lax.dynamic_update_index_in_dim(totals, pair, index - 1, 0)

    extra = lax.fori_loop(1, used, reduce_more, spare_sums)
    key_grad, value_grad = call(
        functools.partial(final_kernel, tiles, slots, tile_total),
        [SMEM_SPEC, ANY_SPEC] + [VMEM_SPEC] * 4,
        (shape(key_rows.shape, f32), shape(value_rows.shape, f32)),
        (VMEM_SPEC,) * 2,
        scratch=(
            pltpu.VMEM((TILE, HD), bf16),
            pltpu.SemaphoreType.DMA,
        ),
        moved=5 * row_count * HD * 4,
    )(info, extra, key_own, value_own, own_sums, other_sums)
    return attended, query_grad, key_grad, value_grad


def solution(mesh):
    return jax.shard_map(
        per_device,
        mesh=mesh,
        in_specs=(
            P(("batch", "seq"), "head"),
            P(("batch", "seq"), "head"),
            P(("batch", "seq"), "head"),
            P(("batch", "seq"), "head"),
            P("batch"),
            P("batch", None),
        ),
        out_specs=(P(("batch", "seq"), "head"),) * 4,
        check_vma=False,
    )
```

```python
import functools
import math

import jax
import jax.numpy as jnp
from jax import lax
from jax.experimental import pallas as pl
from jax.experimental.pallas import tpu as pltpu
from jax.sharding import PartitionSpec as P

HD = 128
TILE = 128
FAR_BELOW = -1e30
LOG2E = 1.4426950408889634
NT_DIMS = (((1,), (1,)), ((), ()))
VMEM_LIMIT = 40 * 1024 * 1024

SMEM_SPEC = pl.BlockSpec(memory_space=pltpu.SMEM)
VMEM_SPEC = pl.BlockSpec(memory_space=pltpu.VMEM)
ANY_SPEC = pl.BlockSpec(memory_space=pl.ANY)
HBM_SPEC = pl.BlockSpec(memory_space=pltpu.HBM)


def call(kernel, in_specs, out_shape, out_specs, scratch=(), flops=0, moved=0):
    return pl.pallas_call(
        kernel,
        in_specs=in_specs,
        out_shape=out_shape,
        out_specs=out_specs,
        scratch_shapes=list(scratch),
        compiler_params=pltpu.CompilerParams(vmem_limit_bytes=VMEM_LIMIT),
        cost_estimate=pl.CostEstimate(flops=flops, bytes_accessed=moved, transcendentals=0),
    )


def tile_rows(first_row, tile):
    return pl.ds(pl.multiple_of(first_row + tile * TILE, TILE), TILE)


def shared_kernel(tile_total, tiles, ids_hbm, mask_hbm, info_ref, spare_ref, spare_sums_ref, *refs):
    del spare_ref, spare_sums_ref
    any_ref, ids_ref, mask_ref, ids_sem, mask_sem = refs
    copies = [
        pltpu.make_async_copy(ids_hbm, ids_ref, ids_sem),
        pltpu.make_async_copy(mask_hbm, mask_ref, mask_sem),
    ]
    for copy in copies:
        copy.start()
    for copy in copies:
        copy.wait()
    for place in range(1, tile_total + 2):
        info_ref[place] = 0
    for tile in range(tile_total):
        users = mask_ref[0, tile]
        for other in range(1, tile_total):
            users = users + mask_ref[other, tile]
        any_ref[tile] = users
    count = jnp.int32(0)
    for position in range(tile_total):
        key_tile = ids_ref[position]
        away = any_ref[key_tile]
        for local in range(tiles):
            away = away - mask_ref[ids_ref[position // tiles * tiles + local], key_tile]
        info_ref[1 + count] = position
        info_ref[tile_total + 2 + position] = jnp.where(away > 0, count, -1)
        count = count + jnp.where(away > 0, 1, 0)
    info_ref[0] = count


def select_kernel(tiles, slots, base, info_ref, *refs):
    if base is None:
        base_ref, *refs = refs
        base = base_ref[0] * slots
    key_ref, value_ref, key_other, value_other, out_ref = refs
    rank = lax.axis_index("seq")
    odd = rank % 2
    out_ref[...] = jnp.zeros_like(out_ref)
    for slot in range(slots):
        position = info_ref[1 + base + slot]
        home = position // tiles
        rows = tile_rows(0, position % tiles)
        for kind, own, other in ((0, key_ref, key_other), (1, value_ref, value_other)):

            @pl.when((odd == kind) & (home == rank))
            def _():
                out_ref[slot] = own[rows, :]

            @pl.when((odd == kind) & (home == rank ^ 1))
            def _():
                out_ref[slot] = other[rows, :]


def final_kernel(tiles, slots, chips, tile_total, info_ref, extra_ref, key_ref, value_ref, *refs):
    sums, refs = refs[: 2 * chips], refs[2 * chips :]
    key_out, value_out, total_ref, staged_ref, copy_sem = refs
    rank = lax.axis_index("seq")
    odd = rank % 2
    total_ref[0] = key_ref[...]
    total_ref[1] = value_ref[...]
    for tile in range(tiles):
        slot = info_ref[tile_total + 2 + rank * tiles + tile]
        rows = tile_rows(0, tile)

        @pl.when((slot >= 0) & (slot < slots))
        def _():
            for part in range(2):
                terms = sums[part * chips : (part + 1) * chips]
                total = terms[0][slot].astype(jnp.float32)
                for source in terms[1:]:
                    total = total + source[slot].astype(jnp.float32)
                total_ref[odd ^ part, rows, :] += total

        @pl.when(slot >= slots)
        def _():
            for part in range(2):
                copy = pltpu.make_async_copy(
                    extra_ref.at[slot // slots - 1, part, slot % slots], staged_ref, copy_sem
                )
                copy.start()
                copy.wait()
                total_ref[odd ^ part, rows, :] += staged_ref[...].astype(jnp.float32)

    key_out[...] = total_ref[0]
    value_out[...] = total_ref[1]


def causal_bias():
    later = lax.broadcasted_iota(jnp.int32, (TILE, TILE), 1)
    return jnp.where(lax.broadcasted_iota(jnp.int32, (TILE, TILE), 0) <= later, 0.0, FAR_BELOW)


def block_bias(allowed):
    return jnp.full((TILE, TILE), jnp.where(allowed, 0.0, FAR_BELOW), jnp.float32)


def own_bias(tiles, bias_ref, my_tiles, mask_ref):
    for a in range(tiles):
        for b in range(tiles):
            allowed = mask_ref[my_tiles[b], my_tiles[a]] == 1
            bias = causal_bias() if a == b else block_bias(allowed)
            bias_ref[pl.ds(a * TILE, TILE), pl.ds(b * TILE, TILE)] = bias


def dot(one, other):
    return jnp.dot(one, other, preferred_element_type=jnp.float32)


def dot_t(one, other):
    return lax.dot_general(one, other, NT_DIMS, preferred_element_type=jnp.float32)


def own_kernel(
    tiles,
    heads,
    ids_hbm,
    mask_hbm,
    query_ref,
    grad_ref,
    key_ref,
    value_ref,
    order_ref,
    terms_ref,
    dprobs_ref,
    max_ref,
    total_ref,
    weighted_ref,
    grad_t_ref,
    bias_ref,
    ids_ref,
    mask_ref,
    ids_sem,
    mask_sem,
):
    del order_ref
    copies = [
        pltpu.make_async_copy(ids_hbm, ids_ref, ids_sem),
        pltpu.make_async_copy(mask_hbm, mask_ref, mask_sem),
    ]
    for copy in copies:
        copy.start()
    for copy in copies:
        copy.wait()
    rank = lax.axis_index("seq")
    scale = HD**-0.5 * LOG2E
    my_tiles = [ids_ref[rank * tiles + b] for b in range(tiles)]
    own_bias(tiles, bias_ref, my_tiles, mask_ref)
    keys = key_ref[...]
    values = value_ref[...]
    values_t = values.T
    for h in range(heads):
        columns = pl.ds(h * HD, HD)
        query = query_ref[:, columns]
        grad = grad_ref[:, columns]
        scores = dot_t(keys, query) * scale + bias_ref[...]
        row_max = jnp.max(scores, axis=0, keepdims=True)
        terms = jnp.exp2(scores - row_max)
        terms_ref[h] = terms
        max_ref[h] = row_max
        total_ref[h] = jnp.sum(terms, axis=0, keepdims=True)
        weighted_ref[h] = dot(values_t, terms.astype(jnp.bfloat16))
        dprobs_ref[h] = dot_t(values, grad)
        grad_t_ref[h] = grad.T


def gathered_kernel(
    chips,
    tiles,
    slots,
    heads,
    ids_ref,
    mask_ref,
    info_ref,
    query_ref,
    grad_ref,
    key_ref,
    value_ref,
    key_other,
    value_other,
    max_own,
    total_own,
    weighted_own,
    grad_t_ref,
    more_ref,
    *refs,
):
    arrived, handed, refs = refs[: chips - 1], refs[chips - 1 : 2 * chips - 2], refs[2 * chips - 2 :]
    keep_ref, give_ref, scale_out, delta_out, out_t_ref, dscores_ref, slot_keys, *refs = refs
    more_out, attended_full, query_full, key_full, value_full, *refs = refs
    bias_ref, held_ref, sum_ref, score_ref, staged_ref, attended_ref, query_out, copy_sem = refs
    keys_ref, values_ref = held_ref.at[0], held_ref.at[1]
    key_sum, value_sum = sum_ref.at[0], sum_ref.at[1]
    rank = lax.axis_index("seq")
    odd = rank % 2
    rows = tiles * TILE
    chunk = slots * TILE
    factor = HD**-0.5
    scale = factor * LOG2E
    needed = info_ref[0]
    my_tiles = [ids_ref[rank * tiles + b] for b in range(tiles)]
    columns = [pl.ds(h * HD, HD) for h in range(heads)]

    def slot_bias(slot, first_row):
        position = info_ref[1 + slot]
        usable = (slot < needed) & (position // tiles != rank)
        tile = ids_ref[position]
        for b in range(tiles):
            bias_ref[pl.ds(first_row, TILE), pl.ds(b * TILE, TILE)] = block_bias(
                usable & (mask_ref[my_tiles[b], tile] == 1)
            )

    def repack(target, part, first_row):
        kind = odd ^ part
        for slot in range(slots):
            total = sum_ref[kind, tile_rows(first_row, slot), :]
            target[slot] = (total * jnp.where(kind == 0, factor, 1.0)).astype(jnp.bfloat16)

    for slot in range(slots):
        slot_bias(jnp.int32(slot), slot * TILE)
        position = info_ref[1 + slot]
        away = (position // (2 * tiles)) ^ (rank // 2)
        at = tile_rows(0, slot)

        @pl.when(away == 0)
        def _():
            source = tile_rows(0, position % tiles)
            keys_ref[at, :] = key_other[source, :]
            values_ref[at, :] = value_other[source, :]

        for step in range(1, chips):

            @pl.when(away == step)
            def _():
                held_ref[odd, at, :] = arrived[step - 1][slot]
                held_ref[odd ^ 1, at, :] = handed[step - 1][slot]

    first = pl.ds(0, chunk)

    @pl.when(needed <= slots)
    def _():
        keys = keys_ref[first, :]
        values = values_ref[first, :]
        slot_keys[...] = keys
        values_t = values.T
        key_total, value_total = None, None
        for h in range(heads):
            query = query_ref[:, columns[h]]
            grad = grad_ref[:, columns[h]]
            scores = dot_t(keys, query) * scale + bias_ref[first, :]
            row_max = jnp.maximum(max_own[h], jnp.max(scores, axis=0, keepdims=True))
            shrink = jnp.exp2(max_own[h] - row_max)
            terms = jnp.exp2(scores - row_max)
            inverse = 1.0 / (total_own[h] * shrink + jnp.sum(terms, axis=0, keepdims=True))
            weighted = weighted_own[h] * shrink + dot(values_t, terms.astype(jnp.bfloat16))
            out = (weighted * inverse).astype(jnp.bfloat16)
            out_t_ref[h] = out
            delta = jnp.sum(
                grad_t_ref[h].astype(jnp.float32) * out.astype(jnp.float32), axis=0, keepdims=True
            )
            scale_out[h] = shrink * inverse
            delta_out[h] = delta
            probs = terms * inverse
            dscores = (probs * (dot_t(values, grad) - delta)).astype(jnp.bfloat16)
            dscores_ref[h] = dscores
            key_part = dot(dscores, query)
            value_part = dot(probs.astype(jnp.bfloat16), grad)
            key_total = key_part if h == 0 else key_total + key_part
            value_total = value_part if h == 0 else value_total + value_part
        key_sum[first, :] = key_total
        value_sum[first, :] = value_total

    @pl.when(needed > slots)
    def _():
        used = (needed + slots - 1) // slots
        own_first = pl.multiple_of(used * chunk, chunk)
        own_rows = pl.ds(own_first, rows)
        own_bias(tiles, bias_ref.at[own_rows, :], my_tiles, mask_ref)
        keys_ref[own_rows, :] = key_ref[...]
        values_ref[own_rows, :] = value_ref[...]

        def fetch(index, carry):
            copy = pltpu.make_async_copy(more_ref.at[index - 1], staged_ref, copy_sem)
            copy.start()
            copy.wait()
            first_row = pl.multiple_of(index * chunk, chunk)
            for slot in range(slots):
                for part in range(2):
                    held_ref[odd ^ part, tile_rows(first_row, slot), :] = staged_ref[part, slot]
                slot_bias(index * slots + slot, pl.multiple_of(first_row + slot * TILE, TILE))
            return carry

        lax.fori_loop(1, used, fetch, 0)
        key_sum[...] = jnp.zeros_like(key_sum)
        value_sum[...] = jnp.zeros_like(value_sum)
        blocks = used * slots + tiles

        for h in range(heads):
            query = query_ref[:, columns[h]]
            grad = grad_ref[:, columns[h]]

            def score(index, row_max):
                at = tile_rows(0, index)
                scores = dot_t(keys_ref[at, :], query) * scale + bias_ref[at, :]
                score_ref[at, :] = scores
                return jnp.maximum(row_max, jnp.max(scores, axis=0, keepdims=True))

            row_max = lax.fori_loop(0, blocks, score, jnp.full((1, rows), FAR_BELOW, jnp.float32))

            def forward(index, carry):
                total, weighted = carry
                at = tile_rows(0, index)
                terms = jnp.exp2(score_ref[at, :] - row_max)
                score_ref[at, :] = terms
                weighted = weighted + dot(values_ref[at, :].T, terms.astype(jnp.bfloat16))
                return total + jnp.sum(terms, axis=0, keepdims=True), weighted

            zeros = jnp.zeros((HD, rows), jnp.float32)
            start = (jnp.zeros((1, rows), jnp.float32), zeros)
            total, weighted = lax.fori_loop(0, blocks, forward, start)
            inverse = 1.0 / total
            out = (weighted * inverse).astype(jnp.bfloat16)
            attended_ref[:, columns[h]] = out.T
            delta = jnp.sum(
                grad_t_ref[h].astype(jnp.float32) * out.astype(jnp.float32), axis=0, keepdims=True
            )

            def backward(index, query_t):
                at = tile_rows(0, index)
                probs = score_ref[at, :] * inverse
                dprobs = dot_t(values_ref[at, :], grad)
                dscores = (probs * (dprobs - delta)).astype(jnp.bfloat16)
                key_sum[at, :] += dot(dscores, query)
                value_sum[at, :] += dot(probs.astype(jnp.bfloat16), grad)
                return query_t + dot(keys_ref[at, :].T, dscores)

            query_t = lax.fori_loop(0, blocks, backward, zeros)
            query_out[:, columns[h]] = (query_t * factor).T

        key_sum[own_rows, :] = key_sum[own_rows, :] * factor
        for source, target in (
            (attended_ref, attended_full),
            (query_out, query_full),
            (key_sum.at[own_rows, :], key_full),
            (value_sum.at[own_rows, :], value_full),
        ):
            copy = pltpu.make_async_copy(source, target, copy_sem)
            copy.start()
            copy.wait()

        def store(index, carry):
            for part in range(2):
                repack(staged_ref.at[part], part, pl.multiple_of(index * chunk, chunk))
            copy = pltpu.make_async_copy(staged_ref, more_out.at[index - 1], copy_sem)
            copy.start()
            copy.wait()
            return carry

        lax.fori_loop(1, used, store, 0)

    repack(keep_ref, 0, 0)
    repack(give_ref, 1, 0)


def rest_kernel(
    slots,
    heads,
    info_ref,
    query_ref,
    grad_ref,
    key_ref,
    terms_ref,
    dprobs_ref,
    scale_ref,
    delta_ref,
    out_t_ref,
    dscores_ref,
    slot_keys,
    attended_full,
    query_full,
    key_full,
    value_full,
    order_ref,
    attended_ref,
    query_out,
    key_out,
    value_out,
    copy_sem,
):
    del order_ref
    factor = HD**-0.5

    @pl.when(info_ref[0] <= slots)
    def _():
        keys_t = key_ref[...].T
        slot_keys_t = slot_keys[...].T
        key_total, value_total = None, None
        for h in range(heads):
            columns = pl.ds(h * HD, HD)
            query = query_ref[:, columns]
            grad = grad_ref[:, columns]
            attended_ref[:, columns] = out_t_ref[h].T
            probs = terms_ref[h] * scale_ref[h]
            dscores = (probs * (dprobs_ref[h] - delta_ref[h])).astype(jnp.bfloat16)
            query_t = dot(keys_t, dscores) + dot(slot_keys_t, dscores_ref[h])
            query_out[:, columns] = (query_t * factor).T
            key_part = dot(dscores, query)
            value_part = dot(probs.astype(jnp.bfloat16), grad)
            key_total = key_part if h == 0 else key_total + key_part
            value_total = value_part if h == 0 else value_total + value_part
        key_out[...] = key_total * factor
        value_out[...] = value_total

    @pl.when(info_ref[0] > slots)
    def _():
        for source, target in (
            (attended_full, attended_ref),
            (query_full, query_out),
            (key_full, key_out),
            (value_full, value_out),
        ):
            copy = pltpu.make_async_copy(source, target, copy_sem)
            copy.start()
            copy.wait()


def per_device(queries, key_rows, value_rows, out_grad, tile_ids, tile_mask):
    row_count = queries.shape[0]
    heads = queries.shape[1] // HD
    ranks = lax.axis_size("seq")
    chips = ranks // 2
    assert key_rows.shape[1] == HD and ranks > 1 and ranks & (ranks - 1) == 0
    tiles = row_count // TILE
    tile_total = tile_ids.shape[0]
    slots = tiles
    rounds = math.ceil(tile_total / slots)
    slot_shape = (slots, TILE, HD)
    buffer = (rounds - 1, 2) + slot_shape
    shape = jax.ShapeDtypeStruct
    bf16, f32 = jnp.bfloat16, jnp.float32

    def swap(values, step):
        return lax.ppermute(values, "seq", [(source, source ^ step) for source in range(ranks)])

    def across(values):
        return [swap(values, 2 * step) for step in range(1, chips)]

    def add(*values):
        total = values[0].astype(f32)
        for value in values[1:]:
            total = total + value.astype(f32)
        return total.astype(bf16)

    list_scratch = (
        pltpu.SMEM(tile_ids.shape, jnp.int32),
        pltpu.SMEM(tile_mask.shape, jnp.int32),
        pltpu.SemaphoreType.DMA,
        pltpu.SemaphoreType.DMA,
    )
    key_other, value_other = swap(key_rows, 1), swap(value_rows, 1)
    info, spare, spare_sums = call(
        functools.partial(shared_kernel, tile_total, tiles),
        [HBM_SPEC] * 2,
        (shape((2 * tile_total + 2,), jnp.int32), shape(buffer, bf16), shape(buffer, bf16)),
        (SMEM_SPEC, ANY_SPEC, ANY_SPEC),
        scratch=(pltpu.SMEM((tile_total,), jnp.int32),) + list_scratch,
        moved=4 * 1024 * 1024,
    )(tile_ids, tile_mask)
    used = (info[0] + slots - 1) // slots
    chip_rows = (key_rows, value_rows, key_other, value_other)

    def select(base, *lead):
        return call(
            functools.partial(select_kernel, tiles, slots, base),
            [SMEM_SPEC] * (1 + len(lead)) + [VMEM_SPEC] * 4,
            shape(slot_shape, bf16),
            VMEM_SPEC,
            moved=5 * row_count * HD * 2,
        )(info, *lead, *chip_rows)

    chosen = select(0)
    arrived = across(chosen)
    handed = [swap(values, 1) for values in arrived]

    def gather_more(index, buffered):
        chosen = select(None, index.reshape(1))
        total = add(chosen, *across(chosen))
        pair = jnp.stack([total, swap(total, 1)])
        return lax.dynamic_update_index_in_dim(buffered, pair, index - 1, 0)

    more = lax.fori_loop(1, used, gather_more, spare)

    all_rows = row_count + rounds * slots * TILE
    square = (heads, row_count, row_count)
    line = (heads, 1, row_count)
    head_t = (heads, HD, row_count)
    work = 2 * heads * row_count * row_count * HD
    terms, dprobs, max_own, total_own, weighted, grad_t = call(
        functools.partial(own_kernel, tiles, heads),
        [HBM_SPEC] * 2 + [VMEM_SPEC] * 4 + [ANY_SPEC],
        (
            shape(square, f32),
            shape(square, f32),
            shape(line, f32),
            shape(line, f32),
            shape(head_t, f32),
            shape(head_t, bf16),
        ),
        (VMEM_SPEC,) * 6,
        scratch=(pltpu.VMEM((row_count, row_count), f32),) + list_scratch,
        flops=3 * work,
        moved=4 * row_count * heads * HD,
    )(tile_ids, tile_mask, queries, out_grad, key_rows, value_rows, chosen)

    full = (
        shape(queries.shape, bf16),
        shape(queries.shape, f32),
        shape(key_rows.shape, f32),
        shape(value_rows.shape, f32),
    )
    keep, give, rescale, delta, out_t, dscores, slot_keys, more_terms, *full_values = call(
        functools.partial(gathered_kernel, chips, tiles, slots, heads),
        [SMEM_SPEC] * 3 + [VMEM_SPEC] * 10 + [ANY_SPEC] + [VMEM_SPEC] * (2 * chips - 2),
        (
            shape(slot_shape, bf16),
            shape(slot_shape, bf16),
            shape(line, f32),
            shape(line, f32),
            shape(head_t, bf16),
            shape((heads, slots * TILE, row_count), bf16),
            shape((slots * TILE, HD), bf16),
            shape(buffer, bf16),
        )
        + full,
        (VMEM_SPEC,) * 7 + (ANY_SPEC,) * 5,
        scratch=(
            pltpu.VMEM((all_rows, row_count), f32),
            pltpu.VMEM((2, all_rows, HD), bf16),
            pltpu.VMEM((2, all_rows, HD), f32),
            pltpu.VMEM((all_rows, row_count), f32),
            pltpu.VMEM((2,) + slot_shape, bf16),
            pltpu.VMEM(queries.shape, bf16),
            pltpu.VMEM(queries.shape, f32),
            pltpu.SemaphoreType.DMA,
        ),
        flops=5 * work,
        moved=4 * row_count * heads * HD,
    )(
        tile_ids,
        tile_mask,
        info,
        queries,
        out_grad,
        *chip_rows,
        max_own,
        total_own,
        weighted,
        grad_t,
        more,
        *arrived,
        *handed,
    )

    chip_sum = add(keep, swap(give, 1))
    attended, query_grad, key_own, value_own = call(
        functools.partial(rest_kernel, slots, heads),
        [SMEM_SPEC] + [VMEM_SPEC] * 10 + [ANY_SPEC] * 5,
        full,
        (VMEM_SPEC,) * 4,
        scratch=(pltpu.SemaphoreType.DMA,),
        flops=4 * work,
        moved=8 * row_count * heads * HD,
    )(
        info,
        queries,
        out_grad,
        key_rows,
        terms,
        dprobs,
        rescale,
        delta,
        out_t,
        dscores,
        slot_keys,
        *full_values,
        chip_sum,
    )
    sums = [chip_sum] + across(chip_sum)
    sums = sums + [swap(values, 1) for values in sums]

    def reduce_more(index, totals):
        terms = lax.dynamic_index_in_dim(more_terms, index - 1, 0, keepdims=False)
        part = add(terms[0], swap(terms[1], 1))
        total = add(part, *across(part))
        pair = jnp.stack([total, swap(total, 1)])
        return lax.dynamic_update_index_in_dim(totals, pair, index - 1, 0)

    extra = lax.fori_loop(1, used, reduce_more, spare_sums)
    key_grad, value_grad = call(
        functools.partial(final_kernel, tiles, slots, chips, tile_total),
        [SMEM_SPEC, ANY_SPEC] + [VMEM_SPEC] * (2 + 2 * chips),
        (shape(key_rows.shape, f32), shape(value_rows.shape, f32)),
        (VMEM_SPEC,) * 2,
        scratch=(
            pltpu.VMEM((2, row_count, HD), f32),
            pltpu.VMEM((TILE, HD), bf16),
            pltpu.SemaphoreType.DMA,
        ),
        moved=5 * row_count * HD * 4,
    )(info, extra, key_own, value_own, *sums)
    return attended, query_grad, key_grad, value_grad


def solution(mesh):
    return jax.shard_map(
        per_device,
        mesh=mesh,
        in_specs=(
            P(("batch", "seq"), "head"),
            P(("batch", "seq"), "head"),
            P(("batch", "seq"), "head"),
            P(("batch", "seq"), "head"),
            P("batch"),
            P("batch", None),
        ),
        out_specs=(P(("batch", "seq"), "head"),) * 4,
        check_vma=False,
    )
```

```python
import functools
import math

import jax
import jax.numpy as jnp
from jax import lax
from jax.experimental import pallas as pl
from jax.experimental.pallas import tpu as pltpu
from jax.sharding import PartitionSpec as P

HD = 128
TILE = 128
FAR_BELOW = -1e30
LOG2E = 1.4426950408889634
NT_DIMS = (((1,), (1,)), ((), ()))
VMEM_LIMIT = 32 * 1024 * 1024

SMEM_SPEC = pl.BlockSpec(memory_space=pltpu.SMEM)
VMEM_SPEC = pl.BlockSpec(memory_space=pltpu.VMEM)
ANY_SPEC = pl.BlockSpec(memory_space=pl.ANY)


def call(kernel, in_specs, out_shape, out_specs, scratch=(), flops=0, moved=0, aliases=None):
    return pl.pallas_call(
        kernel,
        in_specs=in_specs,
        out_shape=out_shape,
        out_specs=out_specs,
        scratch_shapes=list(scratch),
        input_output_aliases=aliases or {},
        compiler_params=pltpu.CompilerParams(vmem_limit_bytes=VMEM_LIMIT),
        cost_estimate=pl.CostEstimate(flops=flops, bytes_accessed=moved, transcendentals=0),
    )


def tile_rows(first_row, tile):
    return pl.ds(pl.multiple_of(first_row + tile * TILE, TILE), TILE)


def info_size(tile_total, tiles, slots):
    return 2 * tile_total + 2 + (slots + tiles) * tiles


def shared_kernel(tile_total, tiles, slots, table_ref, info_ref, spare_ref, spare_sums_ref, any_ref):
    del spare_ref, spare_sums_ref
    rank = lax.axis_index("seq")

    def ids(position):
        return table_ref[tile_total * tile_total + position]

    def mask(query_tile, key_tile):
        return table_ref[query_tile * tile_total + key_tile]

    for place in range(1, tile_total + 2):
        info_ref[place] = 0
    for tile in range(tile_total):
        users = mask(0, tile)
        for other in range(1, tile_total):
            users = users + mask(other, tile)
        any_ref[tile] = users
    count = jnp.int32(0)
    for position in range(tile_total):
        key_tile = ids(position)
        away = any_ref[key_tile]
        for local in range(tiles):
            away = away - mask(ids(position // tiles * tiles + local), key_tile)
        info_ref[1 + count] = position
        info_ref[tile_total + 2 + position] = jnp.where(away > 0, count, -1)
        count = count + jnp.where(away > 0, 1, 0)
    info_ref[0] = count
    my_tiles = [ids(rank * tiles + b) for b in range(tiles)]
    place = 2 * tile_total + 2
    for slot in range(slots):
        position = info_ref[1 + slot]
        usable = ((slot < count) & (position // tiles != rank)).astype(jnp.int32)
        for b in range(tiles):
            info_ref[place] = usable * mask(my_tiles[b], ids(position))
            place += 1
    for a in range(tiles):
        for b in range(tiles):
            info_ref[place] = mask(my_tiles[b], my_tiles[a])
            place += 1


def select_kernel(tiles, slots, base, info_ref, *refs):
    if base is None:
        base_ref, *refs = refs
        base = base_ref[0] * slots
    key_ref, value_ref, key_other, value_other, out_ref = refs
    rank = lax.axis_index("seq")
    odd = rank % 2
    out_ref[...] = jnp.zeros_like(out_ref)
    for slot in range(slots):
        position = info_ref[1 + base + slot]
        home = position // tiles
        rows = tile_rows(0, position % tiles)
        for kind, own, other in ((0, key_ref, key_other), (1, value_ref, value_other)):

            @pl.when((odd == kind) & (home == rank))
            def _():
                out_ref[slot] = own[rows, :]

            @pl.when((odd == kind) & (home == rank ^ 1))
            def _():
                out_ref[slot] = other[rows, :]


def final_kernel(tiles, slots, chips, tile_total, info_ref, extra_ref, key_ref, value_ref, *refs):
    sums, refs = refs[: 2 * chips], refs[2 * chips :]
    key_out, value_out, total_ref, staged_ref, copy_sem = refs
    rank = lax.axis_index("seq")
    odd = rank % 2
    total_ref[0] = key_ref[...]
    total_ref[1] = value_ref[...]
    for tile in range(tiles):
        slot = info_ref[tile_total + 2 + rank * tiles + tile]
        rows = tile_rows(0, tile)

        @pl.when((slot >= 0) & (slot < slots))
        def _():
            for part in range(2):
                terms = sums[part * chips : (part + 1) * chips]
                total = terms[0][slot].astype(jnp.float32)
                for source in terms[1:]:
                    total = total + source[slot].astype(jnp.float32)
                total_ref[odd ^ part, rows, :] += total

        @pl.when(slot >= slots)
        def _():
            for part in range(2):
                copy = pltpu.make_async_copy(
                    extra_ref.at[slot // slots - 1, part, slot % slots], staged_ref, copy_sem
                )
                copy.start()
                copy.wait()
                total_ref[odd ^ part, rows, :] += staged_ref[...].astype(jnp.float32)

    key_out[...] = total_ref[0]
    value_out[...] = total_ref[1]


def causal_bias():
    later = lax.broadcasted_iota(jnp.int32, (TILE, TILE), 1)
    return jnp.where(lax.broadcasted_iota(jnp.int32, (TILE, TILE), 0) <= later, 0.0, FAR_BELOW)


def block_bias(allowed):
    return jnp.full((TILE, TILE), jnp.where(allowed, 0.0, FAR_BELOW), jnp.float32)


def own_bias(tiles, bias_ref, allowed):
    for a in range(tiles):
        for b in range(tiles):
            bias = causal_bias() if a == b else block_bias(allowed(a, b) == 1)
            bias_ref[pl.ds(a * TILE, TILE), pl.ds(b * TILE, TILE)] = bias


def stacked(ref, heads):
    return jnp.concatenate([ref[:, h * HD : (h + 1) * HD] for h in range(heads)], axis=0)


def dot(one, other):
    return jnp.dot(one, other, preferred_element_type=jnp.float32)


def dot_t(one, other):
    return lax.dot_general(one, other, NT_DIMS, preferred_element_type=jnp.float32)


def own_scores(tiles, slots, heads, tile_total, info_ref, bias_ref, keys, query):
    place = 2 * tile_total + 2 + slots * tiles
    own_bias(tiles, bias_ref, lambda a, b: info_ref[place + a * tiles + b])
    bias = jnp.concatenate([bias_ref[...]] * heads, axis=1)
    return dot_t(keys, query) * (HD**-0.5 * LOG2E) + bias


def own_kernel(
    tiles,
    slots,
    heads,
    tile_total,
    info_ref,
    query_ref,
    grad_ref,
    key_ref,
    value_ref,
    order_ref,
    max_ref,
    total_ref,
    weighted_ref,
    grad_t_ref,
    bias_ref,
):
    del order_ref
    query = stacked(query_ref, heads)
    scores = own_scores(tiles, slots, heads, tile_total, info_ref, bias_ref, key_ref[...], query)
    row_max = jnp.max(scores, axis=0, keepdims=True)
    terms = jnp.exp2(scores - row_max)
    max_ref[...] = row_max
    total_ref[...] = jnp.sum(terms, axis=0, keepdims=True)
    weighted_ref[...] = dot(value_ref[...].T, terms.astype(jnp.bfloat16))
    grad_t_ref[...] = stacked(grad_ref, heads).T


def gathered_kernel(
    chips,
    tiles,
    slots,
    heads,
    tile_total,
    info_ref,
    table_any,
    query_ref,
    grad_ref,
    key_ref,
    value_ref,
    key_other,
    value_other,
    max_own,
    total_own,
    weighted_own,
    grad_t_ref,
    more_ref,
    *refs,
):
    arrived, handed, refs = refs[: chips - 1], refs[chips - 1 : 2 * chips - 2], refs[2 * chips - 2 :]
    keep_ref, give_ref, max_ref, inverse_ref, delta_ref, out_t_ref, dscores_ref, *refs = refs
    slot_keys, *refs = refs
    more_out, attended_full, query_full, key_full, value_full, *refs = refs
    bias_ref, held_ref, sum_ref, score_ref, staged_ref, *refs = refs
    attended_ref, query_out, table_ref, copy_sem = refs
    keys_ref, values_ref = held_ref.at[0], held_ref.at[1]
    key_sum, value_sum = sum_ref.at[0], sum_ref.at[1]
    rank = lax.axis_index("seq")
    odd = rank % 2
    rows = tiles * TILE
    chunk = slots * TILE
    factor = HD**-0.5
    scale = factor * LOG2E
    needed = info_ref[0]
    columns = [pl.ds(h * HD, HD) for h in range(heads)]

    def repack(target, part, first_row):
        kind = odd ^ part
        for slot in range(slots):
            total = sum_ref[kind, tile_rows(first_row, slot), :]
            target[slot] = (total * jnp.where(kind == 0, factor, 1.0)).astype(jnp.bfloat16)

    for slot in range(slots):
        for b in range(tiles):
            allowed = info_ref[2 * tile_total + 2 + slot * tiles + b] == 1
            bias_ref[pl.ds(slot * TILE, TILE), pl.ds(b * TILE, TILE)] = block_bias(allowed)
        position = info_ref[1 + slot]
        away = (position // (2 * tiles)) ^ (rank // 2)
        at = tile_rows(0, slot)

        @pl.when(away == 0)
        def _():
            source = tile_rows(0, position % tiles)
            keys_ref[at, :] = key_other[source, :]
            values_ref[at, :] = value_other[source, :]

        for step in range(1, chips):

            @pl.when(away == step)
            def _():
                held_ref[odd, at, :] = arrived[step - 1][slot]
                held_ref[odd ^ 1, at, :] = handed[step - 1][slot]

    first = pl.ds(0, chunk)

    @pl.when(needed <= slots)
    def _():
        keys = keys_ref[first, :]
        values = values_ref[first, :]
        slot_keys[...] = keys
        query = stacked(query_ref, heads)
        grad = stacked(grad_ref, heads)
        bias = jnp.concatenate([bias_ref[first, :]] * heads, axis=1)
        scores = dot_t(keys, query) * scale + bias
        dprobs = dot_t(values, grad)
        row_max = jnp.maximum(max_own[...], jnp.max(scores, axis=0, keepdims=True))
        shrink = jnp.exp2(max_own[...] - row_max)
        terms = jnp.exp2(scores - row_max)
        inverse = 1.0 / (total_own[...] * shrink + jnp.sum(terms, axis=0, keepdims=True))
        weighted = weighted_own[...] * shrink + dot(values.T, terms.astype(jnp.bfloat16))
        out = (weighted * inverse).astype(jnp.bfloat16)
        delta = jnp.sum(
            grad_t_ref[...].astype(jnp.float32) * out.astype(jnp.float32), axis=0, keepdims=True
        )
        probs = terms * inverse
        dscores = (probs * (dprobs - delta)).astype(jnp.bfloat16)
        value_sum[first, :] = dot(probs.astype(jnp.bfloat16), grad)
        key_sum[first, :] = dot(dscores, query)
        out_t_ref[...] = out
        max_ref[...] = row_max
        inverse_ref[...] = inverse
        delta_ref[...] = delta
        dscores_ref[...] = dscores

    @pl.when(needed > slots)
    def _():
        used = (needed + slots - 1) // slots
        own_first = pl.multiple_of(used * chunk, chunk)
        own_rows = pl.ds(own_first, rows)
        copy = pltpu.make_async_copy(table_any, table_ref, copy_sem)
        copy.start()
        copy.wait()

        def ids(position):
            return table_ref[tile_total * tile_total + position]

        def allowed(a, b):
            return table_ref[ids(rank * tiles + b) * tile_total + ids(rank * tiles + a)]

        own_bias(tiles, bias_ref.at[own_rows, :], allowed)
        keys_ref[own_rows, :] = key_ref[...]
        values_ref[own_rows, :] = value_ref[...]

        def fetch(index, carry):
            copy = pltpu.make_async_copy(more_ref.at[index - 1], staged_ref, copy_sem)
            copy.start()
            copy.wait()
            first_row = pl.multiple_of(index * chunk, chunk)
            for slot in range(slots):
                for part in range(2):
                    held_ref[odd ^ part, tile_rows(first_row, slot), :] = staged_ref[part, slot]
                listed = index * slots + slot
                position = info_ref[1 + listed]
                usable = (listed < needed) & (position // tiles != rank)
                for b in range(tiles):
                    seen = table_ref[ids(rank * tiles + b) * tile_total + ids(position)] == 1
                    bias_ref[tile_rows(first_row, slot), pl.ds(b * TILE, TILE)] = block_bias(
                        usable & seen
                    )
            return carry

        lax.fori_loop(1, used, fetch, 0)
        key_sum[...] = jnp.zeros_like(key_sum)
        value_sum[...] = jnp.zeros_like(value_sum)
        blocks = used * slots + tiles

        for h in range(heads):
            query = query_ref[:, columns[h]]
            grad = grad_ref[:, columns[h]]

            def score(index, row_max):
                at = tile_rows(0, index)
                scores = dot_t(keys_ref[at, :], query) * scale + bias_ref[at, :]
                score_ref[at, :] = scores
                return jnp.maximum(row_max, jnp.max(scores, axis=0, keepdims=True))

            row_max = lax.fori_loop(0, blocks, score, jnp.full((1, rows), FAR_BELOW, jnp.float32))

            def forward(index, carry):
                total, weighted = carry
                at = tile_rows(0, index)
                terms = jnp.exp2(score_ref[at, :] - row_max)
                score_ref[at, :] = terms
                weighted = weighted + dot(values_ref[at, :].T, terms.astype(jnp.bfloat16))
                return total + jnp.sum(terms, axis=0, keepdims=True), weighted

            zeros = jnp.zeros((HD, rows), jnp.float32)
            start = (jnp.zeros((1, rows), jnp.float32), zeros)
            total, weighted = lax.fori_loop(0, blocks, forward, start)
            inverse = 1.0 / total
            out = (weighted * inverse).astype(jnp.bfloat16)
            attended_ref[:, columns[h]] = out.T
            grad_t = grad_t_ref[:, pl.ds(h * rows, rows)].astype(jnp.float32)
            delta = jnp.sum(grad_t * out.astype(jnp.float32), axis=0, keepdims=True)

            def backward(index, query_t):
                at = tile_rows(0, index)
                probs = score_ref[at, :] * inverse
                dprobs = dot_t(values_ref[at, :], grad)
                dscores = (probs * (dprobs - delta)).astype(jnp.bfloat16)
                key_sum[at, :] += dot(dscores, query)
                value_sum[at, :] += dot(probs.astype(jnp.bfloat16), grad)
                return query_t + dot(keys_ref[at, :].T, dscores)

            query_t = lax.fori_loop(0, blocks, backward, zeros)
            query_out[:, columns[h]] = (query_t * factor).T

        key_sum[own_rows, :] = key_sum[own_rows, :] * factor
        for source, target in (
            (attended_ref, attended_full),
            (query_out, query_full),
            (key_sum.at[own_rows, :], key_full),
            (value_sum.at[own_rows, :], value_full),
        ):
            copy = pltpu.make_async_copy(source, target, copy_sem)
            copy.start()
            copy.wait()

        def store(index, carry):
            for part in range(2):
                repack(staged_ref.at[part], part, pl.multiple_of(index * chunk, chunk))
            copy = pltpu.make_async_copy(staged_ref, more_out.at[index - 1], copy_sem)
            copy.start()
            copy.wait()
            return carry

        lax.fori_loop(1, used, store, 0)

    repack(keep_ref, 0, 0)
    repack(give_ref, 1, 0)


def rest_kernel(
    tiles,
    slots,
    heads,
    tile_total,
    info_ref,
    query_ref,
    grad_ref,
    key_ref,
    value_ref,
    max_ref,
    inverse_ref,
    delta_ref,
    out_t_ref,
    dscores_ref,
    slot_keys,
    attended_full,
    query_full,
    key_full,
    value_full,
    order_ref,
    spare_ref,
    attended_ref,
    query_out,
    key_out,
    value_out,
    spare_out,
    bias_ref,
    copy_sem,
):
    del order_ref, spare_ref, spare_out
    factor = HD**-0.5
    rows = tiles * TILE

    @pl.when(info_ref[0] <= slots)
    def _():
        keys = key_ref[...]
        query = stacked(query_ref, heads)
        grad = stacked(grad_ref, heads)
        scores = own_scores(tiles, slots, heads, tile_total, info_ref, bias_ref, keys, query)
        probs = jnp.exp2(scores - max_ref[...]) * inverse_ref[...]
        dprobs = dot_t(value_ref[...], grad)
        dscores = (probs * (dprobs - delta_ref[...])).astype(jnp.bfloat16)
        value_out[...] = dot(probs.astype(jnp.bfloat16), grad)
        key_out[...] = dot(dscores, query) * factor
        query_t = (dot(keys.T, dscores) + dot(slot_keys[...].T, dscores_ref[...])) * factor
        for h in range(heads):
            columns = pl.ds(h * HD, HD)
            attended_ref[:, columns] = out_t_ref[:, pl.ds(h * rows, rows)].T
            query_out[:, columns] = query_t[:, h * rows : (h + 1) * rows].T

    @pl.when(info_ref[0] > slots)
    def _():
        for source, target in (
            (attended_full, attended_ref),
            (query_full, query_out),
            (key_full, key_out),
            (value_full, value_out),
        ):
            copy = pltpu.make_async_copy(source, target, copy_sem)
            copy.start()
            copy.wait()


def per_device(queries, key_rows, value_rows, out_grad, tile_ids, tile_mask):
    row_count = queries.shape[0]
    heads = queries.shape[1] // HD
    ranks = lax.axis_size("seq")
    chips = ranks // 2
    assert key_rows.shape[1] == HD and ranks > 1 and ranks & (ranks - 1) == 0
    tiles = row_count // TILE
    tile_total = tile_ids.shape[0]
    slots = tiles
    rounds = math.ceil(tile_total / slots)
    slot_shape = (slots, TILE, HD)
    buffer = (rounds - 1, 2) + slot_shape
    shape = jax.ShapeDtypeStruct
    bf16, f32 = jnp.bfloat16, jnp.float32

    def swap(values, step):
        return lax.ppermute(values, "seq", [(source, source ^ step) for source in range(ranks)])

    def across(values):
        return [swap(values, 2 * step) for step in range(1, chips)]

    def add(*values):
        total = values[0].astype(f32)
        for value in values[1:]:
            total = total + value.astype(f32)
        return total.astype(bf16)

    table = jnp.concatenate([tile_mask.reshape(-1), tile_ids])
    key_other, value_other = swap(key_rows, 1), swap(value_rows, 1)
    info, spare, spare_sums = call(
        functools.partial(shared_kernel, tile_total, tiles, slots),
        [SMEM_SPEC],
        (shape((info_size(tile_total, tiles, slots),), jnp.int32), shape(buffer, bf16), shape(buffer, bf16)),
        (SMEM_SPEC, ANY_SPEC, ANY_SPEC),
        scratch=(pltpu.SMEM((tile_total,), jnp.int32),),
        moved=4 * 1024 * 1024,
    )(table)
    used = (info[0] + slots - 1) // slots
    chip_rows = (key_rows, value_rows, key_other, value_other)

    def select(base, *lead):
        return call(
            functools.partial(select_kernel, tiles, slots, base),
            [SMEM_SPEC] * (1 + len(lead)) + [VMEM_SPEC] * 4,
            shape(slot_shape, bf16),
            VMEM_SPEC,
            moved=5 * row_count * HD * 2,
        )(info, *lead, *chip_rows)

    chosen = select(0)
    arrived = across(chosen)
    handed = [swap(values, 1) for values in arrived]

    def gather_more(index, buffered):
        chosen = select(None, index.reshape(1))
        total = add(chosen, *across(chosen))
        pair = jnp.stack([total, swap(total, 1)])
        return lax.dynamic_update_index_in_dim(buffered, pair, index - 1, 0)

    more = lax.fori_loop(1, used, gather_more, spare)

    all_rows = row_count + rounds * slots * TILE
    columns = heads * row_count
    line = shape((1, columns), f32)
    work = 2 * columns * row_count * HD
    max_own, total_own, weighted, grad_t = call(
        functools.partial(own_kernel, tiles, slots, heads, tile_total),
        [SMEM_SPEC] + [VMEM_SPEC] * 4 + [ANY_SPEC],
        (line, line, shape((HD, columns), f32), shape((HD, columns), bf16)),
        (VMEM_SPEC,) * 4,
        scratch=(pltpu.VMEM((row_count, row_count), f32),),
        flops=24 * work,
        moved=4 * row_count * heads * HD,
    )(info, queries, out_grad, key_rows, value_rows, more)

    full = (
        shape(queries.shape, bf16),
        shape(queries.shape, f32),
        shape(key_rows.shape, f32),
        shape(value_rows.shape, f32),
    )
    keep, give, row_max, inverse, delta, out_t, dscores, slot_keys, more_terms, *full_values = call(
        functools.partial(gathered_kernel, chips, tiles, slots, heads, tile_total),
        [SMEM_SPEC, ANY_SPEC] + [VMEM_SPEC] * 10 + [ANY_SPEC] + [VMEM_SPEC] * (2 * chips - 2),
        (
            shape(slot_shape, bf16),
            shape(slot_shape, bf16),
            line,
            line,
            line,
            shape((HD, columns), bf16),
            shape((slots * TILE, columns), bf16),
            shape((slots * TILE, HD), bf16),
            shape(buffer, bf16),
        )
        + full,
        (VMEM_SPEC,) * 8 + (ANY_SPEC,) * 5,
        scratch=(
            pltpu.VMEM((all_rows, row_count), f32),
            pltpu.VMEM((2, all_rows, HD), bf16),
            pltpu.VMEM((2, all_rows, HD), f32),
            pltpu.VMEM((all_rows, row_count), f32),
            pltpu.VMEM((2,) + slot_shape, bf16),
            pltpu.VMEM(queries.shape, bf16),
            pltpu.VMEM(queries.shape, f32),
            pltpu.SMEM(table.shape, jnp.int32),
            pltpu.SemaphoreType.DMA,
        ),
        flops=24 * work,
        moved=4 * row_count * heads * HD,
    )(
        info,
        table,
        queries,
        out_grad,
        *chip_rows,
        max_own,
        total_own,
        weighted,
        grad_t,
        more,
        *arrived,
        *handed,
    )

    chip_sum = add(keep, swap(give, 1))
    attended, query_grad, key_own, value_own, spare_sums = call(
        functools.partial(rest_kernel, tiles, slots, heads, tile_total),
        [SMEM_SPEC] + [VMEM_SPEC] * 10 + [ANY_SPEC] * 6,
        full + (shape(buffer, bf16),),
        (VMEM_SPEC,) * 4 + (ANY_SPEC,),
        scratch=(pltpu.VMEM((row_count, row_count), f32), pltpu.SemaphoreType.DMA),
        flops=32 * work,
        moved=8 * row_count * heads * HD,
        aliases={16: 4},
    )(
        info,
        queries,
        out_grad,
        key_rows,
        value_rows,
        row_max,
        inverse,
        delta,
        out_t,
        dscores,
        slot_keys,
        *full_values,
        chip_sum,
        spare_sums,
    )
    sums = [chip_sum] + across(chip_sum)
    sums = sums + [swap(values, 1) for values in sums]

    def reduce_more(index, totals):
        terms = lax.dynamic_index_in_dim(more_terms, index - 1, 0, keepdims=False)
        part = add(terms[0], swap(terms[1], 1))
        total = add(part, *across(part))
        pair = jnp.stack([total, swap(total, 1)])
        return lax.dynamic_update_index_in_dim(totals, pair, index - 1, 0)

    extra = lax.fori_loop(1, used, reduce_more, spare_sums)
    key_grad, value_grad = call(
        functools.partial(final_kernel, tiles, slots, chips, tile_total),
        [SMEM_SPEC, ANY_SPEC] + [VMEM_SPEC] * (2 + 2 * chips),
        (shape(key_rows.shape, f32), shape(value_rows.shape, f32)),
        (VMEM_SPEC,) * 2,
        scratch=(
            pltpu.VMEM((2, row_count, HD), f32),
            pltpu.VMEM((TILE, HD), bf16),
            pltpu.SemaphoreType.DMA,
        ),
        moved=5 * row_count * HD * 4,
    )(info, extra, key_own, value_own, *sums)
    return attended, query_grad, key_grad, value_grad


def solution(mesh):
    return jax.shard_map(
        per_device,
        mesh=mesh,
        in_specs=(
            P(("batch", "seq"), "head"),
            P(("batch", "seq"), "head"),
            P(("batch", "seq"), "head"),
            P(("batch", "seq"), "head"),
            P("batch"),
            P("batch", None),
        ),
        out_specs=(P(("batch", "seq"), "head"),) * 4,
        check_vma=False,
    )
```

```python
import functools
import math

import jax
import jax.numpy as jnp
from jax import lax
from jax.experimental import pallas as pl
from jax.experimental.pallas import tpu as pltpu
from jax.sharding import PartitionSpec as P

HD = 128
TILE = 128
FAR_BELOW = -1e30
LOG2E = 1.4426950408889634
NT_DIMS = (((1,), (1,)), ((), ()))
VMEM_LIMIT = 32 * 1024 * 1024

SMEM_SPEC = pl.BlockSpec(memory_space=pltpu.SMEM)
VMEM_SPEC = pl.BlockSpec(memory_space=pltpu.VMEM)
ANY_SPEC = pl.BlockSpec(memory_space=pl.ANY)


def call(kernel, in_specs, out_shape, out_specs, scratch=(), flops=0, moved=0, aliases=None):
    return pl.pallas_call(
        kernel,
        in_specs=in_specs,
        out_shape=out_shape,
        out_specs=out_specs,
        scratch_shapes=list(scratch),
        input_output_aliases=aliases or {},
        compiler_params=pltpu.CompilerParams(vmem_limit_bytes=VMEM_LIMIT),
        cost_estimate=pl.CostEstimate(flops=flops, bytes_accessed=moved, transcendentals=0),
    )


def tile_rows(first_row, tile):
    return pl.ds(pl.multiple_of(first_row + tile * TILE, TILE), TILE)


def info_size(tile_total, tiles, slots):
    return 2 * tile_total + 2 + (slots + tiles) * tiles


def list_kernel(tile_total, tiles, slots, table_ref, *refs):
    key_ref, value_ref, key_other, value_other, info_ref, out_ref, spare_ref, *refs = refs
    any_ref, own_ref, other_ref, own_sem, other_sem = refs
    del spare_ref
    rank = lax.axis_index("seq")

    def load(wait):
        for kind, own, other in ((0, key_ref, key_other), (1, value_ref, value_other)):

            @pl.when(rank % 2 == kind)
            def _():
                for copy in (
                    pltpu.make_async_copy(own, own_ref, own_sem),
                    pltpu.make_async_copy(other, other_ref, other_sem),
                ):
                    if wait:
                        copy.wait()
                    else:
                        copy.start()

    load(wait=False)

    def ids(position):
        return table_ref[tile_total, position]

    def mask(query_tile, key_tile):
        return table_ref[query_tile, key_tile]

    for place in range(1, tile_total + 2):
        info_ref[place] = 0
    for tile in range(tile_total):
        users = mask(0, tile)
        for other in range(1, tile_total):
            users = users + mask(other, tile)
        any_ref[tile] = users
    count = jnp.int32(0)
    for position in range(tile_total):
        key_tile = ids(position)
        away = any_ref[key_tile]
        for local in range(tiles):
            away = away - mask(ids(position // tiles * tiles + local), key_tile)
        info_ref[1 + count] = position
        info_ref[tile_total + 2 + position] = jnp.where(away > 0, count, -1)
        count = count + jnp.where(away > 0, 1, 0)
    info_ref[0] = count
    my_tiles = [ids(rank * tiles + b) for b in range(tiles)]
    place = 2 * tile_total + 2
    for slot in range(slots):
        position = info_ref[1 + slot]
        usable = ((slot < count) & (position // tiles != rank)).astype(jnp.int32)
        for b in range(tiles):
            info_ref[place] = usable * mask(my_tiles[b], ids(position))
            place += 1
    for a in range(tiles):
        for b in range(tiles):
            info_ref[place] = mask(my_tiles[b], my_tiles[a])
            place += 1
    load(wait=True)
    pick(tiles, slots, 0, info_ref, own_ref, other_ref, out_ref)


def pick(tiles, slots, base, info_ref, own_ref, other_ref, out_ref):
    rank = lax.axis_index("seq")
    for slot in range(slots):
        position = info_ref[1 + base + slot]
        home = position // tiles
        rows = tile_rows(0, position % tiles)
        out_ref[slot] = jnp.zeros_like(out_ref[slot])

        @pl.when(home == rank)
        def _():
            out_ref[slot] = own_ref[rows, :]

        @pl.when(home == rank ^ 1)
        def _():
            out_ref[slot] = other_ref[rows, :]


def select_kernel(tiles, slots, info_ref, round_ref, *refs):
    key_ref, value_ref, key_other, value_other, out_ref = refs
    rank = lax.axis_index("seq")
    for kind, own, other in ((0, key_ref, key_other), (1, value_ref, value_other)):

        @pl.when(rank % 2 == kind)
        def _():
            pick(tiles, slots, round_ref[0] * slots, info_ref, own, other, out_ref)


def final_kernel(tiles, slots, parts, tile_total, info_ref, round_ref, key_ref, value_ref, *refs):
    sums, (key_out, value_out) = refs[: 2 * parts], refs[2 * parts :]
    rank = lax.axis_index("seq")
    odd = rank % 2
    key_out[...] = key_ref[...]
    value_out[...] = value_ref[...]
    base = 0 if round_ref is None else round_ref[0] * slots
    for tile in range(tiles):
        slot = info_ref[tile_total + 2 + rank * tiles + tile] - base
        rows = tile_rows(0, tile)

        @pl.when((slot >= 0) & (slot < slots))
        def _():
            totals = []
            for part in range(2):
                total = sums[part * parts][slot].astype(jnp.float32)
                for source in sums[part * parts + 1 : (part + 1) * parts]:
                    total = total + source[slot].astype(jnp.float32)
                totals.append(total)
            for kind, out in ((0, key_out), (1, value_out)):
                out[rows, :] += jnp.where(odd == kind, totals[0], totals[1])


def causal_bias():
    later = lax.broadcasted_iota(jnp.int32, (TILE, TILE), 1)
    return jnp.where(lax.broadcasted_iota(jnp.int32, (TILE, TILE), 0) <= later, 0.0, FAR_BELOW)


def block_bias(allowed):
    return jnp.full((TILE, TILE), jnp.where(allowed, 0.0, FAR_BELOW), jnp.float32)


def own_bias(tiles, bias_ref, allowed):
    for a in range(tiles):
        for b in range(tiles):
            bias = causal_bias() if a == b else block_bias(allowed(a, b) == 1)
            bias_ref[pl.ds(a * TILE, TILE), pl.ds(b * TILE, TILE)] = bias


def stacked(ref, heads):
    return jnp.concatenate([ref[:, h * HD : (h + 1) * HD] for h in range(heads)], axis=0)


def dot(one, other):
    return jnp.dot(one, other, preferred_element_type=jnp.float32)


def dot_t(one, other):
    return lax.dot_general(one, other, NT_DIMS, preferred_element_type=jnp.float32)


def own_scores(tiles, slots, heads, tile_total, info_ref, bias_ref, keys, query):
    place = 2 * tile_total + 2 + slots * tiles
    own_bias(tiles, bias_ref, lambda a, b: info_ref[place + a * tiles + b])
    bias = jnp.concatenate([bias_ref[...]] * heads, axis=1)
    return dot_t(keys, query) * (HD**-0.5 * LOG2E) + bias


def own_kernel(
    tiles,
    slots,
    heads,
    tile_total,
    info_ref,
    query_ref,
    grad_ref,
    key_ref,
    value_ref,
    order_ref,
    max_ref,
    total_ref,
    weighted_ref,
    grad_t_ref,
    bias_ref,
):
    del order_ref
    query = stacked(query_ref, heads)
    scores = own_scores(tiles, slots, heads, tile_total, info_ref, bias_ref, key_ref[...], query)
    row_max = jnp.max(scores, axis=0, keepdims=True)
    terms = jnp.exp2(scores - row_max)
    max_ref[...] = row_max
    total_ref[...] = jnp.sum(terms, axis=0, keepdims=True)
    weighted_ref[...] = dot(value_ref[...].T, terms.astype(jnp.bfloat16))
    grad_t_ref[...] = stacked(grad_ref, heads).T


def gathered_kernel(
    chips,
    tiles,
    slots,
    heads,
    tile_total,
    info_ref,
    table_any,
    query_ref,
    grad_ref,
    key_ref,
    value_ref,
    key_other,
    value_other,
    max_own,
    total_own,
    weighted_own,
    grad_t_ref,
    more_ref,
    *refs,
):
    arrived, handed, refs = refs[: chips - 1], refs[chips - 1 : 2 * chips - 2], refs[2 * chips - 2 :]
    keep_ref, give_ref, max_ref, inverse_ref, delta_ref, out_t_ref, dscores_ref, *refs = refs
    slot_keys, *refs = refs
    more_out, attended_full, query_full, key_full, value_full, *refs = refs
    bias_ref, held_ref, sum_ref, score_ref, staged_ref, *refs = refs
    attended_ref, query_out, table_ref, copy_sem = refs
    keys_ref, values_ref = held_ref.at[0], held_ref.at[1]
    key_sum, value_sum = sum_ref.at[0], sum_ref.at[1]
    rank = lax.axis_index("seq")
    odd = rank % 2
    rows = tiles * TILE
    chunk = slots * TILE
    factor = HD**-0.5
    scale = factor * LOG2E
    needed = info_ref[0]
    columns = [pl.ds(h * HD, HD) for h in range(heads)]

    def repack(target, part, first_row):
        kind = odd ^ part
        for slot in range(slots):
            total = sum_ref[kind, tile_rows(first_row, slot), :]
            target[slot] = (total * jnp.where(kind == 0, factor, 1.0)).astype(jnp.bfloat16)

    for slot in range(slots):
        for b in range(tiles):
            allowed = info_ref[2 * tile_total + 2 + slot * tiles + b] == 1
            bias_ref[pl.ds(slot * TILE, TILE), pl.ds(b * TILE, TILE)] = block_bias(allowed)
        position = info_ref[1 + slot]
        away = (position // (2 * tiles)) ^ (rank // 2)
        at = tile_rows(0, slot)

        @pl.when(away == 0)
        def _():
            source = tile_rows(0, position % tiles)
            keys_ref[at, :] = key_other[source, :]
            values_ref[at, :] = value_other[source, :]

        for step in range(1, chips):

            @pl.when(away == step)
            def _():
                held_ref[odd, at, :] = arrived[step - 1][slot]
                held_ref[odd ^ 1, at, :] = handed[step - 1][slot]

    first = pl.ds(0, chunk)

    @pl.when(needed <= slots)
    def _():
        keys = keys_ref[first, :]
        values = values_ref[first, :]
        slot_keys[...] = keys
        query = stacked(query_ref, heads)
        grad = stacked(grad_ref, heads)
        bias = jnp.concatenate([bias_ref[first, :]] * heads, axis=1)
        scores = dot_t(keys, query) * scale + bias
        dprobs = dot_t(values, grad)
        row_max = jnp.maximum(max_own[...], jnp.max(scores, axis=0, keepdims=True))
        shrink = jnp.exp2(max_own[...] - row_max)
        terms = jnp.exp2(scores - row_max)
        inverse = 1.0 / (total_own[...] * shrink + jnp.sum(terms, axis=0, keepdims=True))
        weighted = weighted_own[...] * shrink + dot(values.T, terms.astype(jnp.bfloat16))
        out = (weighted * inverse).astype(jnp.bfloat16)
        delta = jnp.sum(
            grad_t_ref[...].astype(jnp.float32) * out.astype(jnp.float32), axis=0, keepdims=True
        )
        probs = terms * inverse
        dscores = (probs * (dprobs - delta)).astype(jnp.bfloat16)
        value_sum[first, :] = dot(probs.astype(jnp.bfloat16), grad)
        key_sum[first, :] = dot(dscores, query)
        out_t_ref[...] = out
        max_ref[...] = row_max
        inverse_ref[...] = inverse
        delta_ref[...] = delta
        dscores_ref[...] = dscores

    @pl.when(needed > slots)
    def _():
        used = (needed + slots - 1) // slots
        own_first = pl.multiple_of(used * chunk, chunk)
        own_rows = pl.ds(own_first, rows)
        copy = pltpu.make_async_copy(table_any, table_ref, copy_sem)
        copy.start()
        copy.wait()

        def ids(position):
            return table_ref[tile_total, position]

        def allowed(a, b):
            return table_ref[ids(rank * tiles + b), ids(rank * tiles + a)]

        own_bias(tiles, bias_ref.at[own_rows, :], allowed)
        keys_ref[own_rows, :] = key_ref[...]
        values_ref[own_rows, :] = value_ref[...]

        def fetch(index, carry):
            copy = pltpu.make_async_copy(more_ref.at[index - 1], staged_ref, copy_sem)
            copy.start()
            copy.wait()
            first_row = pl.multiple_of(index * chunk, chunk)
            for slot in range(slots):
                for part in range(2):
                    held_ref[odd ^ part, tile_rows(first_row, slot), :] = staged_ref[part, slot]
                listed = index * slots + slot
                position = info_ref[1 + listed]
                usable = (listed < needed) & (position // tiles != rank)
                for b in range(tiles):
                    seen = table_ref[ids(rank * tiles + b), ids(position)] == 1
                    bias_ref[tile_rows(first_row, slot), pl.ds(b * TILE, TILE)] = block_bias(
                        usable & seen
                    )
            return carry

        lax.fori_loop(1, used, fetch, 0)
        key_sum[...] = jnp.zeros_like(key_sum)
        value_sum[...] = jnp.zeros_like(value_sum)
        blocks = used * slots + tiles

        for h in range(heads):
            query = query_ref[:, columns[h]]
            grad = grad_ref[:, columns[h]]

            def score(index, row_max):
                at = tile_rows(0, index)
                scores = dot_t(keys_ref[at, :], query) * scale + bias_ref[at, :]
                score_ref[at, :] = scores
                return jnp.maximum(row_max, jnp.max(scores, axis=0, keepdims=True))

            row_max = lax.fori_loop(0, blocks, score, jnp.full((1, rows), FAR_BELOW, jnp.float32))

            def forward(index, carry):
                total, weighted = carry
                at = tile_rows(0, index)
                terms = jnp.exp2(score_ref[at, :] - row_max)
                score_ref[at, :] = terms
                weighted = weighted + dot(values_ref[at, :].T, terms.astype(jnp.bfloat16))
                return total + jnp.sum(terms, axis=0, keepdims=True), weighted

            zeros = jnp.zeros((HD, rows), jnp.float32)
            start = (jnp.zeros((1, rows), jnp.float32), zeros)
            total, weighted = lax.fori_loop(0, blocks, forward, start)
            inverse = 1.0 / total
            out = (weighted * inverse).astype(jnp.bfloat16)
            attended_ref[:, columns[h]] = out.T
            grad_t = grad_t_ref[:, pl.ds(h * rows, rows)].astype(jnp.float32)
            delta = jnp.sum(grad_t * out.astype(jnp.float32), axis=0, keepdims=True)

            def backward(index, query_t):
                at = tile_rows(0, index)
                probs = score_ref[at, :] * inverse
                dprobs = dot_t(values_ref[at, :], grad)
                dscores = (probs * (dprobs - delta)).astype(jnp.bfloat16)
                key_sum[at, :] += dot(dscores, query)
                value_sum[at, :] += dot(probs.astype(jnp.bfloat16), grad)
                return query_t + dot(keys_ref[at, :].T, dscores)

            query_t = lax.fori_loop(0, blocks, backward, zeros)
            query_out[:, columns[h]] = (query_t * factor).T

        key_sum[own_rows, :] = key_sum[own_rows, :] * factor
        for source, target in (
            (attended_ref, attended_full),
            (query_out, query_full),
            (key_sum.at[own_rows, :], key_full),
            (value_sum.at[own_rows, :], value_full),
        ):
            copy = pltpu.make_async_copy(source, target, copy_sem)
            copy.start()
            copy.wait()

        def store(index, carry):
            for part in range(2):
                repack(staged_ref.at[part], part, pl.multiple_of(index * chunk, chunk))
            copy = pltpu.make_async_copy(staged_ref, more_out.at[index - 1], copy_sem)
            copy.start()
            copy.wait()
            return carry

        lax.fori_loop(1, used, store, 0)

    repack(keep_ref, 0, 0)
    repack(give_ref, 1, 0)


def rest_kernel(
    tiles,
    slots,
    heads,
    tile_total,
    info_ref,
    query_ref,
    grad_ref,
    key_ref,
    value_ref,
    max_ref,
    inverse_ref,
    delta_ref,
    out_t_ref,
    dscores_ref,
    slot_keys,
    attended_full,
    query_full,
    key_full,
    value_full,
    order_ref,
    attended_ref,
    query_out,
    key_out,
    value_out,
    order_out,
    bias_ref,
    copy_sem,
):
    del order_ref, order_out
    factor = HD**-0.5
    rows = tiles * TILE

    @pl.when(info_ref[0] <= slots)
    def _():
        keys = key_ref[...]
        query = stacked(query_ref, heads)
        grad = stacked(grad_ref, heads)
        scores = own_scores(tiles, slots, heads, tile_total, info_ref, bias_ref, keys, query)
        probs = jnp.exp2(scores - max_ref[...]) * inverse_ref[...]
        dprobs = dot_t(value_ref[...], grad)
        dscores = (probs * (dprobs - delta_ref[...])).astype(jnp.bfloat16)
        value_out[...] = dot(probs.astype(jnp.bfloat16), grad)
        key_out[...] = dot(dscores, query) * factor
        query_t = (dot(keys.T, dscores) + dot(slot_keys[...].T, dscores_ref[...])) * factor
        for h in range(heads):
            columns = pl.ds(h * HD, HD)
            attended_ref[:, columns] = out_t_ref[:, pl.ds(h * rows, rows)].T
            query_out[:, columns] = query_t[:, h * rows : (h + 1) * rows].T

    @pl.when(info_ref[0] > slots)
    def _():
        for source, target in (
            (attended_full, attended_ref),
            (query_full, query_out),
            (key_full, key_out),
            (value_full, value_out),
        ):
            copy = pltpu.make_async_copy(source, target, copy_sem)
            copy.start()
            copy.wait()


def per_device(queries, key_rows, value_rows, out_grad, tile_ids, tile_mask):
    row_count = queries.shape[0]
    heads = queries.shape[1] // HD
    ranks = lax.axis_size("seq")
    chips = ranks // 2
    assert key_rows.shape[1] == HD and ranks > 1 and ranks & (ranks - 1) == 0
    tiles = row_count // TILE
    tile_total = tile_ids.shape[0]
    slots = tiles
    rounds = math.ceil(tile_total / slots)
    slot_shape = (slots, TILE, HD)
    buffer = (rounds - 1, 2) + slot_shape
    shape = jax.ShapeDtypeStruct
    bf16, f32 = jnp.bfloat16, jnp.float32

    def swap(values, step):
        return lax.ppermute(values, "seq", [(source, source ^ step) for source in range(ranks)])

    def across(values):
        return [swap(values, 2 * step) for step in range(1, chips)]

    def add(*values):
        total = values[0].astype(f32)
        for value in values[1:]:
            total = total + value.astype(f32)
        return total.astype(bf16)

    table = jnp.pad(tile_mask, ((0, 1), (0, 0)))
    table = table + jnp.pad(tile_ids[None], ((tile_total, 0), (0, 0)))
    key_other, value_other = swap(key_rows, 1), swap(value_rows, 1)
    chip_rows = (key_rows, value_rows, key_other, value_other)
    info, chosen, spare = call(
        functools.partial(list_kernel, tile_total, tiles, slots),
        [SMEM_SPEC] + [ANY_SPEC] * 4,
        (
            shape((info_size(tile_total, tiles, slots),), jnp.int32),
            shape(slot_shape, bf16),
            shape(buffer, bf16),
        ),
        (SMEM_SPEC, VMEM_SPEC, ANY_SPEC),
        scratch=(
            pltpu.SMEM((tile_total,), jnp.int32),
            pltpu.VMEM(key_rows.shape, bf16),
            pltpu.VMEM(key_rows.shape, bf16),
            pltpu.SemaphoreType.DMA,
            pltpu.SemaphoreType.DMA,
        ),
        moved=4 * 1024 * 1024,
    )(table, *chip_rows)
    used = (info[0] + slots - 1) // slots

    def select(index):
        return call(
            functools.partial(select_kernel, tiles, slots),
            [SMEM_SPEC] * 2 + [VMEM_SPEC] * 4,
            shape(slot_shape, bf16),
            VMEM_SPEC,
            moved=5 * row_count * HD * 2,
        )(info, index.reshape(1), *chip_rows)

    arrived = across(chosen)
    handed = [swap(values, 1) for values in arrived]

    def gather_more(index, buffered):
        chosen = select(index)
        total = add(chosen, *across(chosen))
        pair = jnp.stack([total, swap(total, 1)])
        return lax.dynamic_update_index_in_dim(buffered, pair, index - 1, 0)

    more = lax.fori_loop(1, used, gather_more, spare)

    all_rows = row_count + rounds * slots * TILE
    columns = heads * row_count
    line = shape((1, columns), f32)
    work = 2 * columns * row_count * HD
    max_own, total_own, weighted, grad_t = call(
        functools.partial(own_kernel, tiles, slots, heads, tile_total),
        [SMEM_SPEC] + [VMEM_SPEC] * 4 + [ANY_SPEC],
        (line, line, shape((HD, columns), f32), shape((HD, columns), bf16)),
        (VMEM_SPEC,) * 4,
        scratch=(pltpu.VMEM((row_count, row_count), f32),),
        flops=24 * work,
        moved=4 * row_count * heads * HD,
    )(info, queries, out_grad, key_rows, value_rows, more)

    full = (
        shape(queries.shape, bf16),
        shape(queries.shape, f32),
        shape(key_rows.shape, f32),
        shape(value_rows.shape, f32),
    )
    keep, give, row_max, inverse, delta, out_t, dscores, slot_keys, more_terms, *full_values = call(
        functools.partial(gathered_kernel, chips, tiles, slots, heads, tile_total),
        [SMEM_SPEC, ANY_SPEC] + [VMEM_SPEC] * 10 + [ANY_SPEC] + [VMEM_SPEC] * (2 * chips - 2),
        (
            shape(slot_shape, bf16),
            shape(slot_shape, bf16),
            line,
            line,
            line,
            shape((HD, columns), bf16),
            shape((slots * TILE, columns), bf16),
            shape((slots * TILE, HD), bf16),
            shape(buffer, bf16),
        )
        + full,
        (VMEM_SPEC,) * 8 + (ANY_SPEC,) * 5,
        scratch=(
            pltpu.VMEM((all_rows, row_count), f32),
            pltpu.VMEM((2, all_rows, HD), bf16),
            pltpu.VMEM((2, all_rows, HD), f32),
            pltpu.VMEM((all_rows, row_count), f32),
            pltpu.VMEM((2,) + slot_shape, bf16),
            pltpu.VMEM(queries.shape, bf16),
            pltpu.VMEM(queries.shape, f32),
            pltpu.SMEM(table.shape, jnp.int32),
            pltpu.SemaphoreType.DMA,
        ),
        flops=24 * work,
        moved=4 * row_count * heads * HD,
    )(
        info,
        table,
        queries,
        out_grad,
        *chip_rows,
        max_own,
        total_own,
        weighted,
        grad_t,
        more,
        *arrived,
        *handed,
    )

    chip_sum = add(keep, swap(give, 1))
    back = across(chip_sum)
    attended, query_grad, key_own, value_own, back[0] = call(
        functools.partial(rest_kernel, tiles, slots, heads, tile_total),
        [SMEM_SPEC] + [VMEM_SPEC] * 10 + [ANY_SPEC] * 5,
        full + (shape(slot_shape, bf16),),
        (VMEM_SPEC,) * 4 + (ANY_SPEC,),
        scratch=(pltpu.VMEM((row_count, row_count), f32), pltpu.SemaphoreType.DMA),
        flops=32 * work,
        moved=8 * row_count * heads * HD,
        aliases={15: 4},
    )(
        info,
        queries,
        out_grad,
        key_rows,
        value_rows,
        row_max,
        inverse,
        delta,
        out_t,
        dscores,
        slot_keys,
        *full_values,
        back[0],
    )
    sums = [chip_sum] + back
    sums = sums + [swap(values, 1) for values in sums]

    def close(sums, grads, *lead):
        kernel = functools.partial(final_kernel, tiles, slots, len(sums) // 2, tile_total)
        if not lead:
            kernel = lambda info_ref, *refs: final_kernel(
                tiles, slots, len(sums) // 2, tile_total, info_ref, None, *refs
            )
        return call(
            kernel,
            [SMEM_SPEC] * (1 + len(lead)) + [VMEM_SPEC] * (2 + len(sums)),
            (shape(key_rows.shape, f32), shape(value_rows.shape, f32)),
            (VMEM_SPEC,) * 2,
            moved=5 * row_count * HD * 4,
        )(info, *lead, *grads, *sums)

    def reduce_more(index, grads):
        terms = lax.dynamic_index_in_dim(more_terms, index - 1, 0, keepdims=False)
        part = add(terms[0], swap(terms[1], 1))
        total = add(part, *across(part))
        return tuple(close([total, swap(total, 1)], grads, index.reshape(1)))

    grads = tuple(close(sums, (key_own, value_own)))
    key_grad, value_grad = lax.fori_loop(1, used, reduce_more, grads)
    return attended, query_grad, key_grad, value_grad


def solution(mesh):
    return jax.shard_map(
        per_device,
        mesh=mesh,
        in_specs=(
            P(("batch", "seq"), "head"),
            P(("batch", "seq"), "head"),
            P(("batch", "seq"), "head"),
            P(("batch", "seq"), "head"),
            P("batch"),
            P("batch", None),
        ),
        out_specs=(P(("batch", "seq"), "head"),) * 4,
        check_vma=False,
    )
```

```python
import functools
import math

import jax
import jax.numpy as jnp
from jax import lax
from jax.experimental import pallas as pl
from jax.experimental.pallas import tpu as pltpu
from jax.sharding import PartitionSpec as P

HD = 128
TILE = 128
FAR_BELOW = -1e30
LOG2E = 1.4426950408889634
NT_DIMS = (((1,), (1,)), ((), ()))
VMEM_LIMIT = 32 * 1024 * 1024

SMEM_SPEC = pl.BlockSpec(memory_space=pltpu.SMEM)
VMEM_SPEC = pl.BlockSpec(memory_space=pltpu.VMEM)
ANY_SPEC = pl.BlockSpec(memory_space=pl.ANY)


def call(kernel, in_specs, out_shape, out_specs, scratch=(), flops=0, moved=0, aliases=None):
    return pl.pallas_call(
        kernel,
        in_specs=in_specs,
        out_shape=out_shape,
        out_specs=out_specs,
        scratch_shapes=list(scratch),
        input_output_aliases=aliases or {},
        compiler_params=pltpu.CompilerParams(vmem_limit_bytes=VMEM_LIMIT),
        cost_estimate=pl.CostEstimate(flops=flops, bytes_accessed=moved, transcendentals=0),
    )


def tile_rows(first_row, tile):
    return pl.ds(pl.multiple_of(first_row + tile * TILE, TILE), TILE)


def flag_place(tile_total):
    return 2 * tile_total + 2


def holder_place(tile_total, tiles, slots):
    return flag_place(tile_total) + (slots + tiles) * tiles


def holders(tile_total, tiles, slots, info_ref):
    place = holder_place(tile_total, tiles, slots)
    return info_ref[place] == 1, info_ref[place + 1], info_ref[place + 2]


def second_half(away, chips):
    return (away >= chips // 2) & (away != chips - 1)


def list_kernel(tile_total, tiles, slots, bits_ref, ids_ref, *refs):
    key_ref, value_ref, key_other, value_other, info_ref, one_ref, two_ref, *refs = refs
    held_ref, own_ref, other_ref, own_sem, other_sem = refs[-5:]
    rank = lax.axis_index("seq")

    def load(wait):
        for kind, own, other in ((0, key_ref, key_other), (1, value_ref, value_other)):

            @pl.when(rank % 2 == kind)
            def _():
                for copy in (
                    pltpu.make_async_copy(own, own_ref, own_sem),
                    pltpu.make_async_copy(other, other_ref, other_sem),
                ):
                    if wait:
                        copy.wait()
                    else:
                        copy.start()

    load(wait=False)
    for place in range(1, tile_total + 2):
        info_ref[place] = 0
    ids = [ids_ref[position] for position in range(tile_total)]
    rows = [bits_ref[tile] for tile in ids]
    wants = [
        functools.reduce(jnp.bitwise_or, rows[first : first + tiles])
        for first in range(0, tile_total, tiles)
    ]
    before, behind = [jnp.int32(0)], [jnp.int32(0)]
    for want in wants:
        before.append(before[-1] | want)
    for want in wants[::-1]:
        behind.append(behind[-1] | want)
    behind = behind[::-1]
    count = jnp.int32(0)
    for position in range(tile_total):
        home = position // tiles
        wanted = ((before[home] | behind[home + 1]) >> ids[position]) & 1
        info_ref[1 + count] = position
        info_ref[tile_total + 2 + position] = jnp.where(wanted == 1, count, -1)
        count = count + wanted
    info_ref[0] = count
    my_tiles = [ids_ref[rank * tiles + b] for b in range(tiles)]
    my_bits = [bits_ref[tile] for tile in my_tiles]
    place = flag_place(tile_total)
    for slot in range(slots):
        position = info_ref[1 + slot]
        usable = ((slot < count) & (position // tiles != rank)).astype(jnp.int32)
        for b in range(tiles):
            info_ref[place] = usable & (my_bits[b] >> ids_ref[position])
            place += 1
    for a in range(tiles):
        for b in range(tiles):
            info_ref[place] = (my_bits[b] >> my_tiles[a]) & 1
            place += 1
    first = jnp.where(count > 0, info_ref[1] // (2 * tiles), -1)
    second = jnp.where(count > 1, info_ref[2] // (2 * tiles), -1)
    both = (count > 1) & (first == second)
    info_ref[place] = both.astype(jnp.int32)
    info_ref[place + 1] = first
    info_ref[place + 2] = second
    load(wait=True)
    pick(tiles, slots, 0, info_ref, own_ref, other_ref, held_ref)
    mine = jnp.where((second == rank // 2) & jnp.logical_not(both), 1, 0)
    one_ref[...] = held_ref[mine]
    two_ref[...] = held_ref[jnp.where(both, 1, mine)]


def pick(tiles, slots, base, info_ref, own_ref, other_ref, out_ref):
    rank = lax.axis_index("seq")
    for slot in range(slots):
        position = info_ref[1 + base + slot]
        home = position // tiles
        rows = tile_rows(0, position % tiles)
        out_ref[slot] = jnp.zeros_like(out_ref[slot])

        @pl.when(home == rank)
        def _():
            out_ref[slot] = own_ref[rows, :]

        @pl.when(home == rank ^ 1)
        def _():
            out_ref[slot] = other_ref[rows, :]


def select_kernel(tiles, slots, info_ref, round_ref, *refs):
    key_ref, value_ref, key_other, value_other, out_ref = refs
    rank = lax.axis_index("seq")
    for kind, own, other in ((0, key_ref, key_other), (1, value_ref, value_other)):

        @pl.when(rank % 2 == kind)
        def _():
            pick(tiles, slots, round_ref[0] * slots, info_ref, own, other, out_ref)


def close_kernel(tiles, slots, chips, tile_total, info_ref, key_ref, value_ref, *refs):
    sums, (key_out, value_out) = refs[:-2], refs[-2:]
    rank = lax.axis_index("seq")
    odd = rank % 2
    both, _, _ = holders(tile_total, tiles, slots, info_ref)
    key_out[...] = key_ref[...]
    value_out[...] = value_ref[...]
    for tile in range(tiles):
        slot = info_ref[tile_total + 2 + rank * tiles + tile]
        rows = tile_rows(0, tile)

        @pl.when((slot >= 0) & (slot < slots))
        def _():
            totals = []
            for part in range(2):
                own, *terms, extra = sums[part * (chips + 1) : (part + 1) * (chips + 1)]
                total = own[slot].astype(jnp.float32)
                for step, source in enumerate(terms, 1):
                    other = 1 if second_half(step, chips) else 0
                    use = jnp.logical_not(both) | (slot == other)
                    total = total + jnp.where(use, source[...].astype(jnp.float32), 0.0)
                use = both & (slot == 1)
                totals.append(total + jnp.where(use, extra[...].astype(jnp.float32), 0.0))
            for kind, out in ((0, key_out), (1, value_out)):
                out[rows, :] += jnp.where(odd == kind, totals[0], totals[1])


def later_kernel(tiles, slots, tile_total, info_ref, round_ref, key_ref, value_ref, *refs):
    own_sums, other_sums, key_out, value_out = refs
    rank = lax.axis_index("seq")
    odd = rank % 2
    key_out[...] = key_ref[...]
    value_out[...] = value_ref[...]
    for tile in range(tiles):
        slot = info_ref[tile_total + 2 + rank * tiles + tile] - round_ref[0] * slots
        rows = tile_rows(0, tile)

        @pl.when((slot >= 0) & (slot < slots))
        def _():
            own = own_sums[slot].astype(jnp.float32)
            other = other_sums[slot].astype(jnp.float32)
            for kind, out in ((0, key_out), (1, value_out)):
                out[rows, :] += jnp.where(odd == kind, own, other)


def causal_bias():
    later = lax.broadcasted_iota(jnp.int32, (TILE, TILE), 1)
    return jnp.where(lax.broadcasted_iota(jnp.int32, (TILE, TILE), 0) <= later, 0.0, FAR_BELOW)


def block_bias(allowed):
    return jnp.full((TILE, TILE), jnp.where(allowed, 0.0, FAR_BELOW), jnp.float32)


def own_bias(tiles, bias_ref, allowed):
    for a in range(tiles):
        for b in range(tiles):
            bias = causal_bias() if a == b else block_bias(allowed(a, b) == 1)
            bias_ref[pl.ds(a * TILE, TILE), pl.ds(b * TILE, TILE)] = bias


def stacked(ref, heads):
    return jnp.concatenate([ref[:, h * HD : (h + 1) * HD] for h in range(heads)], axis=0)


def dot(one, other):
    return jnp.dot(one, other, preferred_element_type=jnp.float32)


def dot_t(one, other):
    return lax.dot_general(one, other, NT_DIMS, preferred_element_type=jnp.float32)


def own_scores(tiles, slots, heads, tile_total, info_ref, bias_ref, keys, query):
    place = flag_place(tile_total) + slots * tiles
    own_bias(tiles, bias_ref, lambda a, b: info_ref[place + a * tiles + b])
    bias = jnp.concatenate([bias_ref[...]] * heads, axis=1)
    return dot_t(keys, query) * (HD**-0.5 * LOG2E) + bias


def own_kernel(
    tiles,
    slots,
    heads,
    tile_total,
    info_ref,
    query_ref,
    grad_ref,
    key_ref,
    value_ref,
    order_ref,
    max_ref,
    total_ref,
    weighted_ref,
    grad_t_ref,
    bias_ref,
):
    del order_ref
    query = stacked(query_ref, heads)
    scores = own_scores(tiles, slots, heads, tile_total, info_ref, bias_ref, key_ref[...], query)
    row_max = jnp.max(scores, axis=0, keepdims=True)
    terms = jnp.exp2(scores - row_max)
    max_ref[...] = row_max
    total_ref[...] = jnp.sum(terms, axis=0, keepdims=True)
    weighted_ref[...] = dot(value_ref[...].T, terms.astype(jnp.bfloat16))
    grad_t_ref[...] = stacked(grad_ref, heads).T


def gathered_kernel(
    chips,
    tiles,
    slots,
    heads,
    tile_total,
    info_ref,
    bits_any,
    ids_any,
    query_ref,
    grad_ref,
    key_ref,
    value_ref,
    key_other,
    value_other,
    max_own,
    total_own,
    weighted_own,
    grad_t_ref,
    more_ref,
    *refs,
):
    arrived, handed, refs = refs[:chips], refs[chips : 2 * chips], refs[2 * chips :]
    keep_ref, give_ref, max_ref, inverse_ref, delta_ref, out_t_ref, dscores_ref, *refs = refs
    slot_keys, *refs = refs
    more_out, full_ref, spare_own, spare_other, *refs = refs
    del spare_own, spare_other
    bias_ref, held_ref, sum_ref, score_ref, staged_ref, *refs = refs
    attended_ref, query_out, bits_ref, ids_ref, copy_sem = refs
    keys_ref, values_ref = held_ref.at[0], held_ref.at[1]
    key_sum, value_sum = sum_ref.at[0], sum_ref.at[1]
    rank = lax.axis_index("seq")
    odd = rank % 2
    chip = rank // 2
    both, first_chip, second_chip = holders(tile_total, tiles, slots, info_ref)
    rows = tiles * TILE
    chunk = slots * TILE
    factor = HD**-0.5
    scale = factor * LOG2E
    needed = info_ref[0]
    columns = [pl.ds(h * HD, HD) for h in range(heads)]

    def repack(target, part, first_row):
        kind = odd ^ part
        for slot in range(slots):
            total = sum_ref[kind, tile_rows(first_row, slot), :]
            target[slot] = (total * jnp.where(kind == 0, factor, 1.0)).astype(jnp.bfloat16)

    def route(target, part):
        kind = odd ^ part
        for index in range(chips + 1):
            if index < chips - 1:
                other = second_half(index + 1, chips)
                slot = jnp.where(both, int(other), (chip ^ (index + 1) == second_chip).astype(jnp.int32))
            else:
                slot = index - (chips - 1)
            total = sum_ref[kind, tile_rows(0, slot), :]
            target[index] = (total * jnp.where(kind == 0, factor, 1.0)).astype(jnp.bfloat16)

    for slot in range(slots):
        for b in range(tiles):
            allowed = info_ref[flag_place(tile_total) + slot * tiles + b] == 1
            bias_ref[pl.ds(slot * TILE, TILE), pl.ds(b * TILE, TILE)] = block_bias(allowed)
        position = info_ref[1 + slot]
        away = jnp.where(slot < needed, (second_chip if slot else first_chip) ^ chip, 0)
        late = both & (second_half(away, chips) != (slot == 1))
        source_index = jnp.where(late, chips, away)
        at = tile_rows(0, slot)

        @pl.when(away == 0)
        def _():
            source = tile_rows(0, position % tiles)
            keys_ref[at, :] = key_other[source, :]
            values_ref[at, :] = value_other[source, :]

        for step in range(1, chips + 1):

            @pl.when((away != 0) & (source_index == step))
            def _():
                held_ref[odd, at, :] = arrived[step - 1][...]
                held_ref[odd ^ 1, at, :] = handed[step - 1][...]

    first = pl.ds(0, chunk)

    @pl.when(needed <= slots)
    def _():
        keys = keys_ref[first, :]
        values = values_ref[first, :]
        slot_keys[...] = keys
        query = stacked(query_ref, heads)
        grad = stacked(grad_ref, heads)
        bias = jnp.concatenate([bias_ref[first, :]] * heads, axis=1)
        scores = dot_t(keys, query) * scale + bias
        dprobs = dot_t(values, grad)
        row_max = jnp.maximum(max_own[...], jnp.max(scores, axis=0, keepdims=True))
        shrink = jnp.exp2(max_own[...] - row_max)
        terms = jnp.exp2(scores - row_max)
        inverse = 1.0 / (total_own[...] * shrink + jnp.sum(terms, axis=0, keepdims=True))
        weighted = weighted_own[...] * shrink + dot(values.T, terms.astype(jnp.bfloat16))
        out = (weighted * inverse).astype(jnp.bfloat16)
        delta = jnp.sum(
            grad_t_ref[...].astype(jnp.float32) * out.astype(jnp.float32), axis=0, keepdims=True
        )
        probs = terms * inverse
        dscores = (probs * (dprobs - delta)).astype(jnp.bfloat16)
        value_sum[first, :] = dot(probs.astype(jnp.bfloat16), grad)
        key_sum[first, :] = dot(dscores, query)
        out_t_ref[...] = out
        max_ref[...] = row_max
        inverse_ref[...] = inverse
        delta_ref[...] = delta
        dscores_ref[...] = dscores

    @pl.when(needed > slots)
    def _():
        used = (needed + slots - 1) // slots
        own_first = pl.multiple_of(used * chunk, chunk)
        own_rows = pl.ds(own_first, rows)
        for source, target in ((bits_any, bits_ref), (ids_any, ids_ref)):
            copy = pltpu.make_async_copy(source, target, copy_sem)
            copy.start()
            copy.wait()

        def seen(query_position, key_position):
            return (bits_ref[ids_ref[query_position]] >> ids_ref[key_position]) & 1

        def allowed(a, b):
            return seen(rank * tiles + b, rank * tiles + a)

        own_bias(tiles, bias_ref.at[own_rows, :], allowed)
        keys_ref[own_rows, :] = key_ref[...]
        values_ref[own_rows, :] = value_ref[...]

        def fetch(index, carry):
            copy = pltpu.make_async_copy(more_ref.at[index - 1], staged_ref, copy_sem)
            copy.start()
            copy.wait()
            first_row = pl.multiple_of(index * chunk, chunk)
            for slot in range(slots):
                for part in range(2):
                    held_ref[odd ^ part, tile_rows(first_row, slot), :] = staged_ref[part, slot]
                listed = index * slots + slot
                position = info_ref[1 + listed]
                usable = (listed < needed) & (position // tiles != rank)
                for b in range(tiles):
                    bias_ref[tile_rows(first_row, slot), pl.ds(b * TILE, TILE)] = block_bias(
                        usable & (seen(rank * tiles + b, position) == 1)
                    )
            return carry

        lax.fori_loop(1, used, fetch, 0)
        key_sum[...] = jnp.zeros_like(key_sum)
        value_sum[...] = jnp.zeros_like(value_sum)
        blocks = used * slots + tiles

        for h in range(heads):
            query = query_ref[:, columns[h]]
            grad = grad_ref[:, columns[h]]

            def score(index, row_max):
                at = tile_rows(0, index)
                scores = dot_t(keys_ref[at, :], query) * scale + bias_ref[at, :]
                score_ref[at, :] = scores
                return jnp.maximum(row_max, jnp.max(scores, axis=0, keepdims=True))

            row_max = lax.fori_loop(0, blocks, score, jnp.full((1, rows), FAR_BELOW, jnp.float32))

            def forward(index, carry):
                total, weighted = carry
                at = tile_rows(0, index)
                terms = jnp.exp2(score_ref[at, :] - row_max)
                score_ref[at, :] = terms
                weighted = weighted + dot(values_ref[at, :].T, terms.astype(jnp.bfloat16))
                return total + jnp.sum(terms, axis=0, keepdims=True), weighted

            zeros = jnp.zeros((HD, rows), jnp.float32)
            start = (jnp.zeros((1, rows), jnp.float32), zeros)
            total, weighted = lax.fori_loop(0, blocks, forward, start)
            inverse = 1.0 / total
            out = (weighted * inverse).astype(jnp.bfloat16)
            attended_ref[:, columns[h]] = out.T.astype(jnp.float32)
            grad_t = grad_t_ref[:, pl.ds(h * rows, rows)].astype(jnp.float32)
            delta = jnp.sum(grad_t * out.astype(jnp.float32), axis=0, keepdims=True)

            def backward(index, query_t):
                at = tile_rows(0, index)
                probs = score_ref[at, :] * inverse
                dprobs = dot_t(values_ref[at, :], grad)
                dscores = (probs * (dprobs - delta)).astype(jnp.bfloat16)
                key_sum[at, :] += dot(dscores, query)
                value_sum[at, :] += dot(probs.astype(jnp.bfloat16), grad)
                return query_t + dot(keys_ref[at, :].T, dscores)

            query_t = lax.fori_loop(0, blocks, backward, zeros)
            query_out[:, columns[h]] = (query_t * factor).T

        key_sum[own_rows, :] = key_sum[own_rows, :] * factor
        for source, target in (
            (attended_ref, full_ref.at[0]),
            (query_out, full_ref.at[1]),
            (key_sum.at[own_rows, :], full_ref.at[2, :, columns[0]]),
            (value_sum.at[own_rows, :], full_ref.at[2, :, columns[1]]),
        ):
            copy = pltpu.make_async_copy(source, target, copy_sem)
            copy.start()
            copy.wait()

        def store(index, carry):
            for part in range(2):
                repack(staged_ref.at[part], part, pl.multiple_of(index * chunk, chunk))
            copy = pltpu.make_async_copy(staged_ref, more_out.at[index - 1], copy_sem)
            copy.start()
            copy.wait()
            return carry

        lax.fori_loop(1, used, store, 0)

    route(keep_ref, 0)
    route(give_ref, 1)


def rest_kernel(
    tiles,
    slots,
    heads,
    tile_total,
    info_ref,
    query_ref,
    grad_ref,
    key_ref,
    value_ref,
    max_ref,
    inverse_ref,
    delta_ref,
    out_t_ref,
    dscores_ref,
    slot_keys,
    full_ref,
    order_ref,
    attended_ref,
    query_out,
    key_out,
    value_out,
    order_out,
    bias_ref,
    staged_ref,
    copy_sem,
):
    del order_ref, order_out
    factor = HD**-0.5
    rows = tiles * TILE

    @pl.when(info_ref[0] <= slots)
    def _():
        keys = key_ref[...]
        query = stacked(query_ref, heads)
        grad = stacked(grad_ref, heads)
        scores = own_scores(tiles, slots, heads, tile_total, info_ref, bias_ref, keys, query)
        probs = jnp.exp2(scores - max_ref[...]) * inverse_ref[...]
        dprobs = dot_t(value_ref[...], grad)
        dscores = (probs * (dprobs - delta_ref[...])).astype(jnp.bfloat16)
        value_out[...] = dot(probs.astype(jnp.bfloat16), grad)
        key_out[...] = dot(dscores, query) * factor
        query_t = (dot(keys.T, dscores) + dot(slot_keys[...].T, dscores_ref[...])) * factor
        for h in range(heads):
            columns = pl.ds(h * HD, HD)
            attended_ref[:, columns] = out_t_ref[:, pl.ds(h * rows, rows)].T
            query_out[:, columns] = query_t[:, h * rows : (h + 1) * rows].T

    @pl.when(info_ref[0] > slots)
    def _():
        for source, target in (
            (full_ref.at[0], staged_ref),
            (full_ref.at[1], query_out),
            (full_ref.at[2, :, pl.ds(0, HD)], key_out),
            (full_ref.at[2, :, pl.ds(HD, HD)], value_out),
        ):
            copy = pltpu.make_async_copy(source, target, copy_sem)
            copy.start()
            copy.wait()
        attended_ref[...] = staged_ref[...].astype(jnp.bfloat16)


def per_device(queries, key_rows, value_rows, out_grad, tile_ids, tile_mask):
    row_count = queries.shape[0]
    heads = queries.shape[1] // HD
    ranks = lax.axis_size("seq")
    chips = ranks // 2
    assert key_rows.shape[1] == HD and ranks > 1 and ranks & (ranks - 1) == 0
    tiles = row_count // TILE
    tile_total = tile_ids.shape[0]
    slots = 2
    assert tile_total <= 32 and heads > 1
    rounds = math.ceil(tile_total / slots)
    slot_shape = (slots, TILE, HD)
    buffer = (max(rounds, 32), 2) + slot_shape
    full_shape = (max(8, 2 * heads), row_count, heads * HD)
    shape = jax.ShapeDtypeStruct
    bf16, f32 = jnp.bfloat16, jnp.float32

    def swap(values, step):
        return lax.ppermute(values, "seq", [(source, source ^ step) for source in range(ranks)])

    def across(values):
        return [swap(value, 2 * step) for step, value in enumerate(values, 1)]

    def add(*values):
        total = values[0].astype(f32)
        for value in values[1:]:
            total = total + value.astype(f32)
        return total.astype(bf16)

    tile_shape = (TILE, HD)
    bits = jnp.where(tile_mask == 1, 1 << jnp.arange(tile_total, dtype=jnp.int32), 0)
    bits = jnp.sum(bits, axis=1, dtype=jnp.int32)
    key_other, value_other = swap(key_rows, 1), swap(value_rows, 1)
    chip_rows = (key_rows, value_rows, key_other, value_other)
    holder = holder_place(tile_total, tiles, slots)
    info, one, two, spare, spare_own, spare_other = call(
        functools.partial(list_kernel, tile_total, tiles, slots),
        [SMEM_SPEC] * 2 + [ANY_SPEC] * 4,
        (
            shape((holder + 3,), jnp.int32),
            shape(tile_shape, bf16),
            shape(tile_shape, bf16),
            shape(buffer, bf16),
            shape(tile_shape, bf16),
            shape(tile_shape, bf16),
        ),
        (SMEM_SPEC,) + (VMEM_SPEC,) * 2 + (ANY_SPEC,) * 3,
        scratch=(
            pltpu.VMEM(slot_shape, bf16),
            pltpu.VMEM(key_rows.shape, bf16),
            pltpu.VMEM(key_rows.shape, bf16),
            pltpu.SemaphoreType.DMA,
            pltpu.SemaphoreType.DMA,
        ),
        moved=4 * 1024 * 1024,
    )(bits, tile_ids, *chip_rows)
    once = info[holder]
    used = (info[0] + slots - 1) // slots

    def select(index):
        return call(
            functools.partial(select_kernel, tiles, slots),
            [SMEM_SPEC] * 2 + [VMEM_SPEC] * 4,
            shape(slot_shape, bf16),
            VMEM_SPEC,
            moved=5 * row_count * HD * 2,
        )(info, index.reshape(1), *chip_rows)

    def distance():
        return (lax.axis_index("seq") // 2) ^ info[holder + 1]

    arrived = across([two if second_half(step, chips) else one for step in range(1, chips)])
    handed = [swap(value, 1) for value in arrived]

    def trade(index, spares):
        sent = two
        for step, value in enumerate(arrived, 1):
            sent = jnp.where(distance() == step, value, sent)
        late = swap(sent, 2 * (chips - 1))
        return late, swap(late, 1)

    late_own, late_other = lax.fori_loop(0, once, trade, (spare_own, spare_other))

    def gather_more(index, buffered):
        chosen = select(index)
        total = add(chosen, *across([chosen] * (chips - 1)))
        pair = jnp.stack([total, swap(total, 1)])
        return lax.dynamic_update_index_in_dim(buffered, pair, index - 1, 0)

    more = lax.fori_loop(1, used, gather_more, spare)

    all_rows = row_count + rounds * slots * TILE
    columns = heads * row_count
    line = shape((1, columns), f32)
    work = 2 * columns * row_count * HD
    max_own, total_own, weighted, grad_t = call(
        functools.partial(own_kernel, tiles, slots, heads, tile_total),
        [SMEM_SPEC] + [VMEM_SPEC] * 4 + [ANY_SPEC],
        (line, line, shape((HD, columns), f32), shape((HD, columns), bf16)),
        (VMEM_SPEC,) * 4,
        scratch=(pltpu.VMEM((row_count, row_count), f32),),
        flops=24 * work,
        moved=4 * row_count * heads * HD,
    )(info, queries, out_grad, key_rows, value_rows, more)

    keep, give, row_max, inverse, delta, out_t, dscores, slot_keys, more_terms, *spares = call(
        functools.partial(gathered_kernel, chips, tiles, slots, heads, tile_total),
        [SMEM_SPEC] + [ANY_SPEC] * 2 + [VMEM_SPEC] * 10 + [ANY_SPEC] + [VMEM_SPEC] * (2 * chips),
        (
            shape((chips + 1,) + tile_shape, bf16),
            shape((chips + 1,) + tile_shape, bf16),
            line,
            line,
            line,
            shape((HD, columns), bf16),
            shape((slots * TILE, columns), bf16),
            shape((slots * TILE, HD), bf16),
            shape(buffer, bf16),
            shape(full_shape, f32),
            shape(tile_shape, bf16),
            shape(tile_shape, bf16),
        ),
        (VMEM_SPEC,) * 8 + (ANY_SPEC,) * 4,
        scratch=(
            pltpu.VMEM((all_rows, row_count), f32),
            pltpu.VMEM((2, all_rows, HD), bf16),
            pltpu.VMEM((2, all_rows, HD), f32),
            pltpu.VMEM((all_rows, row_count), f32),
            pltpu.VMEM((2,) + slot_shape, bf16),
            pltpu.VMEM(queries.shape, f32),
            pltpu.VMEM(queries.shape, f32),
            pltpu.SMEM(bits.shape, jnp.int32),
            pltpu.SMEM(tile_ids.shape, jnp.int32),
            pltpu.SemaphoreType.DMA,
        ),
        flops=24 * work,
        moved=4 * row_count * heads * HD,
    )(
        info,
        bits,
        tile_ids,
        queries,
        out_grad,
        *chip_rows,
        max_own,
        total_own,
        weighted,
        grad_t,
        more,
        *arrived,
        late_own,
        *handed,
        late_other,
    )

    chip_sum = add(keep, swap(give, 1))
    pair = chip_sum[chips - 1 :]

    def trade_back(index, carry):
        away = distance()
        sent = jnp.where(second_half(away, chips), pair[0], pair[1])
        late = swap(sent, 2 * (chips - 1))
        sends = [add(value, late) for value in carry[: chips - 2]]
        return *sends, carry[chips - 2], late, swap(late, 1)

    *sends, late_own, late_other = lax.fori_loop(
        0,
        once,
        trade_back,
        (*[chip_sum[step] for step in range(chips - 1)], *spares[1:]),
    )
    back = across(sends)
    attended, query_grad, key_own, value_own, back[0] = call(
        functools.partial(rest_kernel, tiles, slots, heads, tile_total),
        [SMEM_SPEC] + [VMEM_SPEC] * 10 + [ANY_SPEC] * 2,
        (
            shape(queries.shape, bf16),
            shape(queries.shape, f32),
            shape(key_rows.shape, f32),
            shape(value_rows.shape, f32),
            shape(tile_shape, bf16),
        ),
        (VMEM_SPEC,) * 4 + (ANY_SPEC,),
        scratch=(
            pltpu.VMEM((row_count, row_count), f32),
            pltpu.VMEM(queries.shape, f32),
            pltpu.SemaphoreType.DMA,
        ),
        flops=32 * work,
        moved=8 * row_count * heads * HD,
        aliases={12: 4},
    )(
        info,
        queries,
        out_grad,
        key_rows,
        value_rows,
        row_max,
        inverse,
        delta,
        out_t,
        dscores,
        slot_keys,
        spares[0],
        back[0],
    )
    sums = [pair, *back, late_own]
    sums += [swap(values, 1) for values in (pair, *back)] + [late_other]

    def close(kernel, lead, grads, sums):
        return call(
            kernel,
            [SMEM_SPEC] * len(lead) + [VMEM_SPEC] * (2 + len(sums)),
            (shape(key_rows.shape, f32), shape(value_rows.shape, f32)),
            (VMEM_SPEC,) * 2,
            moved=5 * row_count * HD * 4,
        )(*lead, *grads, *sums)

    def reduce_more(index, grads):
        terms = lax.dynamic_index_in_dim(more_terms, index - 1, 0, keepdims=False)
        part = add(terms[0], swap(terms[1], 1))
        total = add(part, *across([part] * (chips - 1)))
        kernel = functools.partial(later_kernel, tiles, slots, tile_total)
        return tuple(close(kernel, (info, index.reshape(1)), grads, (total, swap(total, 1))))

    kernel = functools.partial(close_kernel, tiles, slots, chips, tile_total)
    grads = tuple(close(kernel, (info,), (key_own, value_own), sums))
    key_grad, value_grad = lax.fori_loop(1, used, reduce_more, grads)
    return attended, query_grad, key_grad, value_grad


def solution(mesh):
    return jax.shard_map(
        per_device,
        mesh=mesh,
        in_specs=(
            P(("batch", "seq"), "head"),
            P(("batch", "seq"), "head"),
            P(("batch", "seq"), "head"),
            P(("batch", "seq"), "head"),
            P("batch"),
            P("batch", None),
        ),
        out_specs=(P(("batch", "seq"), "head"),) * 4,
        check_vma=False,
    )
```

```python
import functools
import math

import jax
import jax.numpy as jnp
from jax import lax
from jax.experimental import pallas as pl
from jax.experimental.pallas import tpu as pltpu
from jax.sharding import PartitionSpec as P

HD = 128
TILE = 128
FAR_BELOW = -1e30
LOG2E = 1.4426950408889634
NT_DIMS = (((1,), (1,)), ((), ()))
VMEM_LIMIT = 32 * 1024 * 1024

SMEM_SPEC = pl.BlockSpec(memory_space=pltpu.SMEM)
VMEM_SPEC = pl.BlockSpec(memory_space=pltpu.VMEM)
ANY_SPEC = pl.BlockSpec(memory_space=pl.ANY)


def call(kernel, in_specs, out_shape, out_specs, scratch=(), flops=0, moved=0, aliases=None):
    return pl.pallas_call(
        kernel,
        in_specs=in_specs,
        out_shape=out_shape,
        out_specs=out_specs,
        scratch_shapes=list(scratch),
        input_output_aliases=aliases or {},
        compiler_params=pltpu.CompilerParams(vmem_limit_bytes=VMEM_LIMIT),
        cost_estimate=pl.CostEstimate(flops=flops, bytes_accessed=moved, transcendentals=0),
    )


def tile_rows(first_row, tile):
    return pl.ds(pl.multiple_of(first_row + tile * TILE, TILE), TILE)


def info_size(tile_total, tiles, slots):
    return 2 * tile_total + 2 + (slots + tiles) * tiles


def list_kernel(tile_total, tiles, slots, table_ref, *refs):
    key_ref, value_ref, key_other, value_other, info_ref, out_ref, spare_ref, *refs = refs
    any_ref, own_ref, other_ref, own_sem, other_sem = refs
    del spare_ref
    rank = lax.axis_index("seq")

    def load(wait):
        for kind, own, other in ((0, key_ref, key_other), (1, value_ref, value_other)):

            @pl.when(rank % 2 == kind)
            def _():
                for copy in (
                    pltpu.make_async_copy(own, own_ref, own_sem),
                    pltpu.make_async_copy(other, other_ref, other_sem),
                ):
                    if wait:
                        copy.wait()
                    else:
                        copy.start()

    load(wait=False)

    def ids(position):
        return table_ref[tile_total, position]

    def mask(query_tile, key_tile):
        return table_ref[query_tile, key_tile]

    for place in range(1, tile_total + 2):
        info_ref[place] = 0
    for tile in range(tile_total):
        users = mask(0, tile)
        for other in range(1, tile_total):
            users = users + mask(other, tile)
        any_ref[tile] = users
    count = jnp.int32(0)
    for position in range(tile_total):
        key_tile = ids(position)
        away = any_ref[key_tile]
        for local in range(tiles):
            away = away - mask(ids(position // tiles * tiles + local), key_tile)
        info_ref[1 + count] = position
        info_ref[tile_total + 2 + position] = jnp.where(away > 0, count, -1)
        count = count + jnp.where(away > 0, 1, 0)
    info_ref[0] = count
    my_tiles = [ids(rank * tiles + b) for b in range(tiles)]
    place = 2 * tile_total + 2
    for slot in range(slots):
        position = info_ref[1 + slot]
        usable = ((slot < count) & (position // tiles != rank)).astype(jnp.int32)
        for b in range(tiles):
            info_ref[place] = usable * mask(my_tiles[b], ids(position))
            place += 1
    for a in range(tiles):
        for b in range(tiles):
            info_ref[place] = mask(my_tiles[b], my_tiles[a])
            place += 1
    load(wait=True)
    pick(tiles, slots, 0, info_ref, own_ref, other_ref, out_ref)


def pick(tiles, slots, base, info_ref, own_ref, other_ref, out_ref):
    rank = lax.axis_index("seq")
    for slot in range(slots):
        position = info_ref[1 + base + slot]
        home = position // tiles
        rows = tile_rows(0, position % tiles)
        out_ref[slot] = jnp.zeros_like(out_ref[slot])

        @pl.when(home == rank)
        def _():
            out_ref[slot] = own_ref[rows, :]

        @pl.when(home == rank ^ 1)
        def _():
            out_ref[slot] = other_ref[rows, :]


def select_kernel(tiles, slots, info_ref, round_ref, *refs):
    key_ref, value_ref, key_other, value_other, out_ref = refs
    rank = lax.axis_index("seq")
    for kind, own, other in ((0, key_ref, key_other), (1, value_ref, value_other)):

        @pl.when(rank % 2 == kind)
        def _():
            pick(tiles, slots, round_ref[0] * slots, info_ref, own, other, out_ref)


def final_kernel(tiles, slots, parts, tile_total, info_ref, round_ref, key_ref, value_ref, *refs):
    sums, (key_out, value_out) = refs[: 2 * parts], refs[2 * parts :]
    rank = lax.axis_index("seq")
    odd = rank % 2
    key_out[...] = key_ref[...]
    value_out[...] = value_ref[...]
    base = 0 if round_ref is None else round_ref[0] * slots
    for tile in range(tiles):
        slot = info_ref[tile_total + 2 + rank * tiles + tile] - base
        rows = tile_rows(0, tile)

        @pl.when((slot >= 0) & (slot < slots))
        def _():
            totals = []
            for part in range(2):
                total = sums[part * parts][slot].astype(jnp.float32)
                for source in sums[part * parts + 1 : (part + 1) * parts]:
                    total = total + source[slot].astype(jnp.float32)
                totals.append(total)
            for kind, out in ((0, key_out), (1, value_out)):
                out[rows, :] += jnp.where(odd == kind, totals[0], totals[1])


def causal_bias():
    later = lax.broadcasted_iota(jnp.int32, (TILE, TILE), 1)
    return jnp.where(lax.broadcasted_iota(jnp.int32, (TILE, TILE), 0) <= later, 0.0, FAR_BELOW)


def block_bias(allowed):
    return jnp.full((TILE, TILE), jnp.where(allowed, 0.0, FAR_BELOW), jnp.float32)


def own_bias(tiles, bias_ref, allowed):
    for a in range(tiles):
        for b in range(tiles):
            bias = causal_bias() if a == b else block_bias(allowed(a, b) == 1)
            bias_ref[pl.ds(a * TILE, TILE), pl.ds(b * TILE, TILE)] = bias


def stacked(ref, heads):
    return jnp.concatenate([ref[:, h * HD : (h + 1) * HD] for h in range(heads)], axis=0)


def dot(one, other):
    return jnp.dot(one, other, preferred_element_type=jnp.float32)


def dot_t(one, other):
    return lax.dot_general(one, other, NT_DIMS, preferred_element_type=jnp.float32)


def own_scores(tiles, slots, heads, tile_total, info_ref, bias_ref, keys, query):
    place = 2 * tile_total + 2 + slots * tiles
    own_bias(tiles, bias_ref, lambda a, b: info_ref[place + a * tiles + b])
    bias = jnp.concatenate([bias_ref[...]] * heads, axis=1)
    return dot_t(keys, query) * (HD**-0.5 * LOG2E) + bias


def own_kernel(
    tiles,
    slots,
    heads,
    tile_total,
    info_ref,
    query_ref,
    grad_ref,
    key_ref,
    value_ref,
    order_ref,
    max_ref,
    total_ref,
    weighted_ref,
    grad_t_ref,
    bias_ref,
):
    del order_ref
    query = stacked(query_ref, heads)
    scores = own_scores(tiles, slots, heads, tile_total, info_ref, bias_ref, key_ref[...], query)
    row_max = jnp.max(scores, axis=0, keepdims=True)
    terms = jnp.exp2(scores - row_max)
    max_ref[...] = row_max
    total_ref[...] = jnp.sum(terms, axis=0, keepdims=True)
    weighted_ref[...] = dot(value_ref[...].T, terms.astype(jnp.bfloat16))
    grad_t_ref[...] = stacked(grad_ref, heads).T


def gathered_kernel(
    chips,
    tiles,
    slots,
    heads,
    tile_total,
    info_ref,
    table_any,
    query_ref,
    grad_ref,
    key_ref,
    value_ref,
    key_other,
    value_other,
    max_own,
    total_own,
    weighted_own,
    grad_t_ref,
    more_ref,
    *refs,
):
    arrived, handed, refs = refs[: chips - 1], refs[chips - 1 : 2 * chips - 2], refs[2 * chips - 2 :]
    keep_ref, give_ref, max_ref, inverse_ref, delta_ref, out_t_ref, dscores_ref, *refs = refs
    slot_keys, *refs = refs
    more_out, attended_full, query_full, key_full, value_full, *refs = refs
    bias_ref, held_ref, sum_ref, score_ref, staged_ref, *refs = refs
    attended_ref, query_out, table_ref, copy_sem = refs
    keys_ref, values_ref = held_ref.at[0], held_ref.at[1]
    key_sum, value_sum = sum_ref.at[0], sum_ref.at[1]
    rank = lax.axis_index("seq")
    odd = rank % 2
    rows = tiles * TILE
    chunk = slots * TILE
    factor = HD**-0.5
    scale = factor * LOG2E
    needed = info_ref[0]
    columns = [pl.ds(h * HD, HD) for h in range(heads)]

    def repack(target, part, first_row):
        kind = odd ^ part
        for slot in range(slots):
            total = sum_ref[kind, tile_rows(first_row, slot), :]
            target[slot] = (total * jnp.where(kind == 0, factor, 1.0)).astype(jnp.bfloat16)

    for slot in range(slots):
        for b in range(tiles):
            allowed = info_ref[2 * tile_total + 2 + slot * tiles + b] == 1
            bias_ref[pl.ds(slot * TILE, TILE), pl.ds(b * TILE, TILE)] = block_bias(allowed)
        position = info_ref[1 + slot]
        away = (position // (2 * tiles)) ^ (rank // 2)
        at = tile_rows(0, slot)

        @pl.when(away == 0)
        def _():
            source = tile_rows(0, position % tiles)
            keys_ref[at, :] = key_other[source, :]
            values_ref[at, :] = value_other[source, :]

        for step in range(1, chips):

            @pl.when(away == step)
            def _():
                held_ref[odd, at, :] = arrived[step - 1][slot]
                held_ref[odd ^ 1, at, :] = handed[step - 1][slot]

    first = pl.ds(0, chunk)

    @pl.when(needed <= slots)
    def _():
        keys = keys_ref[first, :]
        values = values_ref[first, :]
        slot_keys[...] = keys
        query = stacked(query_ref, heads)
        grad = stacked(grad_ref, heads)
        bias = jnp.concatenate([bias_ref[first, :]] * heads, axis=1)
        scores = dot_t(keys, query) * scale + bias
        dprobs = dot_t(values, grad)
        row_max = jnp.maximum(max_own[...], jnp.max(scores, axis=0, keepdims=True))
        shrink = jnp.exp2(max_own[...] - row_max)
        terms = jnp.exp2(scores - row_max)
        inverse = 1.0 / (total_own[...] * shrink + jnp.sum(terms, axis=0, keepdims=True))
        weighted = weighted_own[...] * shrink + dot(values.T, terms.astype(jnp.bfloat16))
        out = (weighted * inverse).astype(jnp.bfloat16)
        delta = jnp.sum(
            grad_t_ref[...].astype(jnp.float32) * out.astype(jnp.float32), axis=0, keepdims=True
        )
        probs = terms * inverse
        dscores = (probs * (dprobs - delta)).astype(jnp.bfloat16)
        value_sum[first, :] = dot(probs.astype(jnp.bfloat16), grad)
        key_sum[first, :] = dot(dscores, query)
        out_t_ref[...] = out
        max_ref[...] = row_max
        inverse_ref[...] = inverse
        delta_ref[...] = delta
        dscores_ref[...] = dscores

    @pl.when(needed > slots)
    def _():
        used = (needed + slots - 1) // slots
        own_first = pl.multiple_of(used * chunk, chunk)
        own_rows = pl.ds(own_first, rows)
        copy = pltpu.make_async_copy(table_any, table_ref, copy_sem)
        copy.start()
        copy.wait()

        def ids(position):
            return table_ref[tile_total, position]

        def allowed(a, b):
            return table_ref[ids(rank * tiles + b), ids(rank * tiles + a)]

        own_bias(tiles, bias_ref.at[own_rows, :], allowed)
        keys_ref[own_rows, :] = key_ref[...]
        values_ref[own_rows, :] = value_ref[...]

        def fetch(index, carry):
            copy = pltpu.make_async_copy(more_ref.at[index - 1], staged_ref, copy_sem)
            copy.start()
            copy.wait()
            first_row = pl.multiple_of(index * chunk, chunk)
            for slot in range(slots):
                for part in range(2):
                    held_ref[odd ^ part, tile_rows(first_row, slot), :] = staged_ref[part, slot]
                listed = index * slots + slot
                position = info_ref[1 + listed]
                usable = (listed < needed) & (position // tiles != rank)
                for b in range(tiles):
                    seen = table_ref[ids(rank * tiles + b), ids(position)] == 1
                    bias_ref[tile_rows(first_row, slot), pl.ds(b * TILE, TILE)] = block_bias(
                        usable & seen
                    )
            return carry

        lax.fori_loop(1, used, fetch, 0)
        key_sum[...] = jnp.zeros_like(key_sum)
        value_sum[...] = jnp.zeros_like(value_sum)
        blocks = used * slots + tiles

        for h in range(heads):
            query = query_ref[:, columns[h]]
            grad = grad_ref[:, columns[h]]

            def score(index, row_max):
                at = tile_rows(0, index)
                scores = dot_t(keys_ref[at, :], query) * scale + bias_ref[at, :]
                score_ref[at, :] = scores
                return jnp.maximum(row_max, jnp.max(scores, axis=0, keepdims=True))

            row_max = lax.fori_loop(0, blocks, score, jnp.full((1, rows), FAR_BELOW, jnp.float32))

            def forward(index, carry):
                total, weighted = carry
                at = tile_rows(0, index)
                terms = jnp.exp2(score_ref[at, :] - row_max)
                score_ref[at, :] = terms
                weighted = weighted + dot(values_ref[at, :].T, terms.astype(jnp.bfloat16))
                return total + jnp.sum(terms, axis=0, keepdims=True), weighted

            zeros = jnp.zeros((HD, rows), jnp.float32)
            start = (jnp.zeros((1, rows), jnp.float32), zeros)
            total, weighted = lax.fori_loop(0, blocks, forward, start)
            inverse = 1.0 / total
            out = (weighted * inverse).astype(jnp.bfloat16)
            attended_ref[:, columns[h]] = out.T
            grad_t = grad_t_ref[:, pl.ds(h * rows, rows)].astype(jnp.float32)
            delta = jnp.sum(grad_t * out.astype(jnp.float32), axis=0, keepdims=True)

            def backward(index, query_t):
                at = tile_rows(0, index)
                probs = score_ref[at, :] * inverse
                dprobs = dot_t(values_ref[at, :], grad)
                dscores = (probs * (dprobs - delta)).astype(jnp.bfloat16)
                key_sum[at, :] += dot(dscores, query)
                value_sum[at, :] += dot(probs.astype(jnp.bfloat16), grad)
                return query_t + dot(keys_ref[at, :].T, dscores)

            query_t = lax.fori_loop(0, blocks, backward, zeros)
            query_out[:, columns[h]] = (query_t * factor).T

        key_sum[own_rows, :] = key_sum[own_rows, :] * factor
        for source, target in (
            (attended_ref, attended_full),
            (query_out, query_full),
            (key_sum.at[own_rows, :], key_full),
            (value_sum.at[own_rows, :], value_full),
        ):
            copy = pltpu.make_async_copy(source, target, copy_sem)
            copy.start()
            copy.wait()

        def store(index, carry):
            for part in range(2):
                repack(staged_ref.at[part], part, pl.multiple_of(index * chunk, chunk))
            copy = pltpu.make_async_copy(staged_ref, more_out.at[index - 1], copy_sem)
            copy.start()
            copy.wait()
            return carry

        lax.fori_loop(1, used, store, 0)

    repack(keep_ref, 0, 0)
    repack(give_ref, 1, 0)


def rest_kernel(
    tiles,
    slots,
    heads,
    tile_total,
    info_ref,
    query_ref,
    grad_ref,
    key_ref,
    value_ref,
    max_ref,
    inverse_ref,
    delta_ref,
    out_t_ref,
    dscores_ref,
    slot_keys,
    attended_full,
    query_full,
    key_full,
    value_full,
    order_ref,
    attended_ref,
    query_out,
    key_out,
    value_out,
    order_out,
    bias_ref,
    copy_sem,
):
    del order_ref, order_out
    factor = HD**-0.5
    rows = tiles * TILE

    @pl.when(info_ref[0] <= slots)
    def _():
        keys = key_ref[...]
        query = stacked(query_ref, heads)
        grad = stacked(grad_ref, heads)
        scores = own_scores(tiles, slots, heads, tile_total, info_ref, bias_ref, keys, query)
        probs = jnp.exp2(scores - max_ref[...]) * inverse_ref[...]
        dprobs = dot_t(value_ref[...], grad)
        dscores = (probs * (dprobs - delta_ref[...])).astype(jnp.bfloat16)
        value_out[...] = dot(probs.astype(jnp.bfloat16), grad)
        key_out[...] = dot(dscores, query) * factor
        query_t = (dot(keys.T, dscores) + dot(slot_keys[...].T, dscores_ref[...])) * factor
        for h in range(heads):
            columns = pl.ds(h * HD, HD)
            attended_ref[:, columns] = out_t_ref[:, pl.ds(h * rows, rows)].T
            query_out[:, columns] = query_t[:, h * rows : (h + 1) * rows].T

    @pl.when(info_ref[0] > slots)
    def _():
        for source, target in (
            (attended_full, attended_ref),
            (query_full, query_out),
            (key_full, key_out),
            (value_full, value_out),
        ):
            copy = pltpu.make_async_copy(source, target, copy_sem)
            copy.start()
            copy.wait()


def per_device(queries, key_rows, value_rows, out_grad, tile_ids, tile_mask):
    row_count = queries.shape[0]
    heads = queries.shape[1] // HD
    ranks = lax.axis_size("seq")
    chips = ranks // 2
    assert key_rows.shape[1] == HD and ranks > 1 and ranks & (ranks - 1) == 0
    tiles = row_count // TILE
    tile_total = tile_ids.shape[0]
    slots = tiles
    rounds = math.ceil(tile_total / slots)
    slot_shape = (slots, TILE, HD)
    buffer = (rounds - 1, 2) + slot_shape
    shape = jax.ShapeDtypeStruct
    bf16, f32 = jnp.bfloat16, jnp.float32

    def swap(values, step):
        return lax.ppermute(values, "seq", [(source, source ^ step) for source in range(ranks)])

    def across(values, order):
        got = {step: swap(values, 2 * step) for step in order}
        return [got[step] for step in range(1, chips)]

    far_first = [*range(2, chips), 1] if chips > 1 else []
    near_second = far_first[:1] + [1] * (chips > 2) + far_first[1:-1]

    def add(*values):
        total = values[0].astype(f32)
        for value in values[1:]:
            total = total + value.astype(f32)
        return total.astype(bf16)

    table = jnp.pad(tile_mask, ((0, 1), (0, 0)))
    table = table + jnp.pad(tile_ids[None], ((tile_total, 0), (0, 0)))
    key_other, value_other = swap(key_rows, 1), swap(value_rows, 1)
    chip_rows = (key_rows, value_rows, key_other, value_other)
    info, chosen, spare = call(
        functools.partial(list_kernel, tile_total, tiles, slots),
        [SMEM_SPEC] + [ANY_SPEC] * 4,
        (
            shape((info_size(tile_total, tiles, slots),), jnp.int32),
            shape(slot_shape, bf16),
            shape(buffer, bf16),
        ),
        (SMEM_SPEC, VMEM_SPEC, ANY_SPEC),
        scratch=(
            pltpu.SMEM((tile_total,), jnp.int32),
            pltpu.VMEM(key_rows.shape, bf16),
            pltpu.VMEM(key_rows.shape, bf16),
            pltpu.SemaphoreType.DMA,
            pltpu.SemaphoreType.DMA,
        ),
        moved=4 * 1024 * 1024,
    )(table, *chip_rows)
    used = (info[0] + slots - 1) // slots

    def select(index):
        return call(
            functools.partial(select_kernel, tiles, slots),
            [SMEM_SPEC] * 2 + [VMEM_SPEC] * 4,
            shape(slot_shape, bf16),
            VMEM_SPEC,
            moved=5 * row_count * HD * 2,
        )(info, index.reshape(1), *chip_rows)

    arrived = across(chosen, far_first)
    handed = [swap(values, 1) for values in arrived]

    def gather_more(index, buffered):
        chosen = select(index)
        total = add(chosen, *across(chosen, far_first))
        pair = jnp.stack([total, swap(total, 1)])
        return lax.dynamic_update_index_in_dim(buffered, pair, index - 1, 0)

    more = lax.fori_loop(1, used, gather_more, spare)

    all_rows = row_count + rounds * slots * TILE
    columns = heads * row_count
    line = shape((1, columns), f32)
    work = 2 * columns * row_count * HD
    max_own, total_own, weighted, grad_t = call(
        functools.partial(own_kernel, tiles, slots, heads, tile_total),
        [SMEM_SPEC] + [VMEM_SPEC] * 4 + [ANY_SPEC],
        (line, line, shape((HD, columns), f32), shape((HD, columns), bf16)),
        (VMEM_SPEC,) * 4,
        scratch=(pltpu.VMEM((row_count, row_count), f32),),
        flops=24 * work,
        moved=4 * row_count * heads * HD,
    )(info, queries, out_grad, key_rows, value_rows, more)

    full = (
        shape(queries.shape, bf16),
        shape(queries.shape, f32),
        shape(key_rows.shape, f32),
        shape(value_rows.shape, f32),
    )
    keep, give, row_max, inverse, delta, out_t, dscores, slot_keys, more_terms, *full_values = call(
        functools.partial(gathered_kernel, chips, tiles, slots, heads, tile_total),
        [SMEM_SPEC, ANY_SPEC] + [VMEM_SPEC] * 10 + [ANY_SPEC] + [VMEM_SPEC] * (2 * chips - 2),
        (
            shape(slot_shape, bf16),
            shape(slot_shape, bf16),
            line,
            line,
            line,
            shape((HD, columns), bf16),
            shape((slots * TILE, columns), bf16),
            shape((slots * TILE, HD), bf16),
            shape(buffer, bf16),
        )
        + full,
        (VMEM_SPEC,) * 8 + (ANY_SPEC,) * 5,
        scratch=(
            pltpu.VMEM((all_rows, row_count), f32),
            pltpu.VMEM((2, all_rows, HD), bf16),
            pltpu.VMEM((2, all_rows, HD), f32),
            pltpu.VMEM((all_rows, row_count), f32),
            pltpu.VMEM((2,) + slot_shape, bf16),
            pltpu.VMEM(queries.shape, bf16),
            pltpu.VMEM(queries.shape, f32),
            pltpu.SMEM(table.shape, jnp.int32),
            pltpu.SemaphoreType.DMA,
        ),
        flops=24 * work,
        moved=4 * row_count * heads * HD,
    )(
        info,
        table,
        queries,
        out_grad,
        *chip_rows,
        max_own,
        total_own,
        weighted,
        grad_t,
        more,
        *arrived,
        *handed,
    )

    chip_sum = add(keep, swap(give, 1))
    back = across(chip_sum, near_second)
    attended, query_grad, key_own, value_own, back[0] = call(
        functools.partial(rest_kernel, tiles, slots, heads, tile_total),
        [SMEM_SPEC] + [VMEM_SPEC] * 10 + [ANY_SPEC] * 5,
        full + (shape(slot_shape, bf16),),
        (VMEM_SPEC,) * 4 + (ANY_SPEC,),
        scratch=(pltpu.VMEM((row_count, row_count), f32), pltpu.SemaphoreType.DMA),
        flops=32 * work,
        moved=8 * row_count * heads * HD,
        aliases={15: 4},
    )(
        info,
        queries,
        out_grad,
        key_rows,
        value_rows,
        row_max,
        inverse,
        delta,
        out_t,
        dscores,
        slot_keys,
        *full_values,
        back[0],
    )
    sums = [chip_sum] + back
    sums = sums + [swap(values, 1) for values in sums]

    def close(sums, grads, *lead):
        kernel = functools.partial(final_kernel, tiles, slots, len(sums) // 2, tile_total)
        if not lead:
            kernel = lambda info_ref, *refs: final_kernel(
                tiles, slots, len(sums) // 2, tile_total, info_ref, None, *refs
            )
        return call(
            kernel,
            [SMEM_SPEC] * (1 + len(lead)) + [VMEM_SPEC] * (2 + len(sums)),
            (shape(key_rows.shape, f32), shape(value_rows.shape, f32)),
            (VMEM_SPEC,) * 2,
            moved=5 * row_count * HD * 4,
        )(info, *lead, *grads, *sums)

    def reduce_more(index, grads):
        terms = lax.dynamic_index_in_dim(more_terms, index - 1, 0, keepdims=False)
        part = add(terms[0], swap(terms[1], 1))
        total = add(part, *across(part, far_first))
        return tuple(close([total, swap(total, 1)], grads, index.reshape(1)))

    grads = tuple(close(sums, (key_own, value_own)))
    key_grad, value_grad = lax.fori_loop(1, used, reduce_more, grads)
    return attended, query_grad, key_grad, value_grad


def solution(mesh):
    return jax.shard_map(
        per_device,
        mesh=mesh,
        in_specs=(
            P(("batch", "seq"), "head"),
            P(("batch", "seq"), "head"),
            P(("batch", "seq"), "head"),
            P(("batch", "seq"), "head"),
            P("batch"),
            P("batch", None),
        ),
        out_specs=(P(("batch", "seq"), "head"),) * 4,
        check_vma=False,
    )
```

```python
import functools
import math

import jax
import jax.numpy as jnp
from jax import lax
from jax.experimental import pallas as pl
from jax.experimental.pallas import tpu as pltpu
from jax.sharding import PartitionSpec as P

HD = 128
TILE = 128
FAR_BELOW = -1e30
LOG2E = 1.4426950408889634
NT_DIMS = (((1,), (1,)), ((), ()))
VMEM_LIMIT = 32 * 1024 * 1024

SMEM_SPEC = pl.BlockSpec(memory_space=pltpu.SMEM)
VMEM_SPEC = pl.BlockSpec(memory_space=pltpu.VMEM)
ANY_SPEC = pl.BlockSpec(memory_space=pl.ANY)


def call(kernel, in_specs, out_shape, out_specs, scratch=(), flops=0, moved=0, aliases=None):
    return pl.pallas_call(
        kernel,
        in_specs=in_specs,
        out_shape=out_shape,
        out_specs=out_specs,
        scratch_shapes=list(scratch),
        input_output_aliases=aliases or {},
        compiler_params=pltpu.CompilerParams(vmem_limit_bytes=VMEM_LIMIT),
        cost_estimate=pl.CostEstimate(flops=flops, bytes_accessed=moved, transcendentals=0),
    )


def far_first(chips):
    return [*range(2, chips), 1][: chips - 1]


def tile_rows(first_row, tile):
    return pl.ds(pl.multiple_of(first_row + tile * TILE, TILE), TILE)


def info_size(tile_total, tiles, slots):
    return 2 * tile_total + 2 + (slots + tiles) * tiles


def list_kernel(tile_total, tiles, slots, table_ref, *refs):
    key_ref, value_ref, key_other, value_other, info_ref, out_ref, spare_ref, *refs = refs
    any_ref, own_ref, other_ref, own_sem, other_sem = refs
    del spare_ref
    rank = lax.axis_index("seq")

    def load(wait):
        for kind, own, other in ((0, key_ref, key_other), (1, value_ref, value_other)):

            @pl.when(rank % 2 == kind)
            def _():
                for copy in (
                    pltpu.make_async_copy(own, own_ref, own_sem),
                    pltpu.make_async_copy(other, other_ref, other_sem),
                ):
                    if wait:
                        copy.wait()
                    else:
                        copy.start()

    load(wait=False)

    def ids(position):
        return table_ref[tile_total, position]

    def mask(query_tile, key_tile):
        return table_ref[query_tile, key_tile]

    for place in range(1, tile_total + 2):
        info_ref[place] = 0
    for tile in range(tile_total):
        users = mask(0, tile)
        for other in range(1, tile_total):
            users = users + mask(other, tile)
        any_ref[tile] = users
    count = jnp.int32(0)
    for position in range(tile_total):
        key_tile = ids(position)
        away = any_ref[key_tile]
        for local in range(tiles):
            away = away - mask(ids(position // tiles * tiles + local), key_tile)
        info_ref[1 + count] = position
        info_ref[tile_total + 2 + position] = jnp.where(away > 0, count, -1)
        count = count + jnp.where(away > 0, 1, 0)
    info_ref[0] = count
    my_tiles = [ids(rank * tiles + b) for b in range(tiles)]
    place = 2 * tile_total + 2
    for slot in range(slots):
        position = info_ref[1 + slot]
        usable = ((slot < count) & (position // tiles != rank)).astype(jnp.int32)
        for b in range(tiles):
            info_ref[place] = usable * mask(my_tiles[b], ids(position))
            place += 1
    for a in range(tiles):
        for b in range(tiles):
            info_ref[place] = mask(my_tiles[b], my_tiles[a])
            place += 1
    load(wait=True)
    pick(tiles, slots, 0, info_ref, own_ref, other_ref, out_ref)


def pick(tiles, slots, base, info_ref, own_ref, other_ref, out_ref):
    rank = lax.axis_index("seq")
    for slot in range(slots):
        position = info_ref[1 + base + slot]
        home = position // tiles
        rows = tile_rows(0, position % tiles)
        out_ref[slot] = jnp.zeros_like(out_ref[slot])

        @pl.when(home == rank)
        def _():
            out_ref[slot] = own_ref[rows, :]

        @pl.when(home == rank ^ 1)
        def _():
            out_ref[slot] = other_ref[rows, :]


def select_kernel(tiles, slots, info_ref, round_ref, *refs):
    key_ref, value_ref, key_other, value_other, out_ref = refs
    rank = lax.axis_index("seq")
    for kind, own, other in ((0, key_ref, key_other), (1, value_ref, value_other)):

        @pl.when(rank % 2 == kind)
        def _():
            pick(tiles, slots, round_ref[0] * slots, info_ref, own, other, out_ref)


def final_kernel(tiles, slots, parts, tile_total, info_ref, round_ref, key_ref, value_ref, *refs):
    sums, (key_out, value_out) = refs[: 2 * parts], refs[2 * parts :]
    rank = lax.axis_index("seq")
    odd = rank % 2
    key_out[...] = key_ref[...]
    value_out[...] = value_ref[...]
    base = 0 if round_ref is None else round_ref[0] * slots
    for tile in range(tiles):
        slot = info_ref[tile_total + 2 + rank * tiles + tile] - base
        rows = tile_rows(0, tile)

        @pl.when((slot >= 0) & (slot < slots))
        def _():
            totals = []
            for part in range(2):
                total = sums[part * parts][slot].astype(jnp.float32)
                for source in sums[part * parts + 1 : (part + 1) * parts]:
                    total = total + source[slot].astype(jnp.float32)
                totals.append(total)
            for kind, out in ((0, key_out), (1, value_out)):
                out[rows, :] += jnp.where(odd == kind, totals[0], totals[1])


def causal_bias():
    later = lax.broadcasted_iota(jnp.int32, (TILE, TILE), 1)
    return jnp.where(lax.broadcasted_iota(jnp.int32, (TILE, TILE), 0) <= later, 0.0, FAR_BELOW)


def block_bias(allowed):
    return jnp.full((TILE, TILE), jnp.where(allowed, 0.0, FAR_BELOW), jnp.float32)


def own_bias(tiles, bias_ref, allowed):
    for a in range(tiles):
        for b in range(tiles):
            bias = causal_bias() if a == b else block_bias(allowed(a, b) == 1)
            bias_ref[pl.ds(a * TILE, TILE), pl.ds(b * TILE, TILE)] = bias


def stacked(ref, heads):
    return jnp.concatenate([ref[:, h * HD : (h + 1) * HD] for h in range(heads)], axis=0)


def dot(one, other):
    return jnp.dot(one, other, preferred_element_type=jnp.float32)


def dot_t(one, other):
    return lax.dot_general(one, other, NT_DIMS, preferred_element_type=jnp.float32)


def own_scores(tiles, slots, heads, tile_total, info_ref, bias_ref, keys, query):
    place = 2 * tile_total + 2 + slots * tiles
    own_bias(tiles, bias_ref, lambda a, b: info_ref[place + a * tiles + b])
    bias = jnp.concatenate([bias_ref[...]] * heads, axis=1)
    return dot_t(keys, query) * (HD**-0.5 * LOG2E) + bias


def own_kernel(
    tiles,
    slots,
    heads,
    tile_total,
    info_ref,
    query_ref,
    grad_ref,
    key_ref,
    value_ref,
    order_ref,
    max_ref,
    total_ref,
    weighted_ref,
    grad_t_ref,
    bias_ref,
):
    del order_ref
    query = stacked(query_ref, heads)
    scores = own_scores(tiles, slots, heads, tile_total, info_ref, bias_ref, key_ref[...], query)
    row_max = jnp.max(scores, axis=0, keepdims=True)
    terms = jnp.exp2(scores - row_max)
    max_ref[...] = row_max
    total_ref[...] = jnp.sum(terms, axis=0, keepdims=True)
    weighted_ref[...] = dot(value_ref[...].T, terms.astype(jnp.bfloat16))
    grad_t_ref[...] = stacked(grad_ref, heads).T


def gathered_kernel(
    chips,
    tiles,
    slots,
    heads,
    tile_total,
    info_ref,
    table_any,
    query_ref,
    grad_ref,
    key_ref,
    value_ref,
    key_other,
    value_other,
    max_own,
    total_own,
    weighted_own,
    grad_t_ref,
    more_ref,
    *refs,
):
    arrived, handed, refs = refs[: chips - 1], refs[chips - 1 : 2 * chips - 2], refs[2 * chips - 2 :]
    keep_ref, give_ref, max_ref, inverse_ref, delta_ref, out_t_ref, dscores_ref, *refs = refs
    slot_keys, *refs = refs
    more_out, attended_full, query_full, key_full, value_full, *refs = refs
    bias_ref, held_ref, sum_ref, score_ref, staged_ref, *refs = refs
    attended_ref, query_out, table_ref, copy_sem = refs
    keys_ref, values_ref = held_ref.at[0], held_ref.at[1]
    key_sum, value_sum = sum_ref.at[0], sum_ref.at[1]
    rank = lax.axis_index("seq")
    odd = rank % 2
    rows = tiles * TILE
    chunk = slots * TILE
    factor = HD**-0.5
    scale = factor * LOG2E
    needed = info_ref[0]
    columns = [pl.ds(h * HD, HD) for h in range(heads)]

    def repack(target, part, first_row):
        kind = odd ^ part
        for slot in range(slots):
            total = sum_ref[kind, tile_rows(first_row, slot), :]
            target[slot] = (total * jnp.where(kind == 0, factor, 1.0)).astype(jnp.bfloat16)

    for slot in range(slots):
        for b in range(tiles):
            allowed = info_ref[2 * tile_total + 2 + slot * tiles + b] == 1
            bias_ref[pl.ds(slot * TILE, TILE), pl.ds(b * TILE, TILE)] = block_bias(allowed)
        position = info_ref[1 + slot]
        away = (position // (2 * tiles)) ^ (rank // 2)
        at = tile_rows(0, slot)

        @pl.when(away == 0)
        def _():
            source = tile_rows(0, position % tiles)
            keys_ref[at, :] = key_other[source, :]
            values_ref[at, :] = value_other[source, :]

        for index, step in enumerate(far_first(chips)):

            @pl.when(away == step)
            def _():
                held_ref[odd, at, :] = arrived[index][slot]
                held_ref[odd ^ 1, at, :] = handed[index][slot]

    first = pl.ds(0, chunk)

    @pl.when(needed <= slots)
    def _():
        keys = keys_ref[first, :]
        values = values_ref[first, :]
        slot_keys[...] = keys
        query = stacked(query_ref, heads)
        grad = stacked(grad_ref, heads)
        bias = jnp.concatenate([bias_ref[first, :]] * heads, axis=1)
        scores = dot_t(keys, query) * scale + bias
        dprobs = dot_t(values, grad)
        row_max = jnp.maximum(max_own[...], jnp.max(scores, axis=0, keepdims=True))
        shrink = jnp.exp2(max_own[...] - row_max)
        terms = jnp.exp2(scores - row_max)
        inverse = 1.0 / (total_own[...] * shrink + jnp.sum(terms, axis=0, keepdims=True))
        weighted = weighted_own[...] * shrink + dot(values.T, terms.astype(jnp.bfloat16))
        out = (weighted * inverse).astype(jnp.bfloat16)
        delta = jnp.sum(
            grad_t_ref[...].astype(jnp.float32) * out.astype(jnp.float32), axis=0, keepdims=True
        )
        probs = terms * inverse
        dscores = (probs * (dprobs - delta)).astype(jnp.bfloat16)
        value_sum[first, :] = dot(probs.astype(jnp.bfloat16), grad)
        key_sum[first, :] = dot(dscores, query)
        out_t_ref[...] = out
        max_ref[...] = row_max
        inverse_ref[...] = inverse
        delta_ref[...] = delta
        dscores_ref[...] = dscores

    @pl.when(needed > slots)
    def _():
        used = (needed + slots - 1) // slots
        own_first = pl.multiple_of(used * chunk, chunk)
        own_rows = pl.ds(own_first, rows)
        copy = pltpu.make_async_copy(table_any, table_ref, copy_sem)
        copy.start()
        copy.wait()

        def ids(position):
            return table_ref[tile_total, position]

        def allowed(a, b):
            return table_ref[ids(rank * tiles + b), ids(rank * tiles + a)]

        own_bias(tiles, bias_ref.at[own_rows, :], allowed)
        keys_ref[own_rows, :] = key_ref[...]
        values_ref[own_rows, :] = value_ref[...]

        def fetch(index, carry):
            copy = pltpu.make_async_copy(more_ref.at[index - 1], staged_ref, copy_sem)
            copy.start()
            copy.wait()
            first_row = pl.multiple_of(index * chunk, chunk)
            for slot in range(slots):
                for part in range(2):
                    held_ref[odd ^ part, tile_rows(first_row, slot), :] = staged_ref[part, slot]
                listed = index * slots + slot
                position = info_ref[1 + listed]
                usable = (listed < needed) & (position // tiles != rank)
                for b in range(tiles):
                    seen = table_ref[ids(rank * tiles + b), ids(position)] == 1
                    bias_ref[tile_rows(first_row, slot), pl.ds(b * TILE, TILE)] = block_bias(
                        usable & seen
                    )
            return carry

        lax.fori_loop(1, used, fetch, 0)
        key_sum[...] = jnp.zeros_like(key_sum)
        value_sum[...] = jnp.zeros_like(value_sum)
        blocks = used * slots + tiles

        for h in range(heads):
            query = query_ref[:, columns[h]]
            grad = grad_ref[:, columns[h]]

            def score(index, row_max):
                at = tile_rows(0, index)
                scores = dot_t(keys_ref[at, :], query) * scale + bias_ref[at, :]
                score_ref[at, :] = scores
                return jnp.maximum(row_max, jnp.max(scores, axis=0, keepdims=True))

            row_max = lax.fori_loop(0, blocks, score, jnp.full((1, rows), FAR_BELOW, jnp.float32))

            def forward(index, carry):
                total, weighted = carry
                at = tile_rows(0, index)
                terms = jnp.exp2(score_ref[at, :] - row_max)
                score_ref[at, :] = terms
                weighted = weighted + dot(values_ref[at, :].T, terms.astype(jnp.bfloat16))
                return total + jnp.sum(terms, axis=0, keepdims=True), weighted

            zeros = jnp.zeros((HD, rows), jnp.float32)
            start = (jnp.zeros((1, rows), jnp.float32), zeros)
            total, weighted = lax.fori_loop(0, blocks, forward, start)
            inverse = 1.0 / total
            out = (weighted * inverse).astype(jnp.bfloat16)
            attended_ref[:, columns[h]] = out.T
            grad_t = grad_t_ref[:, pl.ds(h * rows, rows)].astype(jnp.float32)
            delta = jnp.sum(grad_t * out.astype(jnp.float32), axis=0, keepdims=True)

            def backward(index, query_t):
                at = tile_rows(0, index)
                probs = score_ref[at, :] * inverse
                dprobs = dot_t(values_ref[at, :], grad)
                dscores = (probs * (dprobs - delta)).astype(jnp.bfloat16)
                key_sum[at, :] += dot(dscores, query)
                value_sum[at, :] += dot(probs.astype(jnp.bfloat16), grad)
                return query_t + dot(keys_ref[at, :].T, dscores)

            query_t = lax.fori_loop(0, blocks, backward, zeros)
            query_out[:, columns[h]] = (query_t * factor).T

        key_sum[own_rows, :] = key_sum[own_rows, :] * factor
        for source, target in (
            (attended_ref, attended_full),
            (query_out, query_full),
            (key_sum.at[own_rows, :], key_full),
            (value_sum.at[own_rows, :], value_full),
        ):
            copy = pltpu.make_async_copy(source, target, copy_sem)
            copy.start()
            copy.wait()

        def store(index, carry):
            for part in range(2):
                repack(staged_ref.at[part], part, pl.multiple_of(index * chunk, chunk))
            copy = pltpu.make_async_copy(staged_ref, more_out.at[index - 1], copy_sem)
            copy.start()
            copy.wait()
            return carry

        lax.fori_loop(1, used, store, 0)

    repack(keep_ref, 0, 0)
    repack(give_ref, 1, 0)


def rest_kernel(
    tiles,
    slots,
    heads,
    tile_total,
    info_ref,
    query_ref,
    grad_ref,
    key_ref,
    value_ref,
    max_ref,
    inverse_ref,
    delta_ref,
    out_t_ref,
    dscores_ref,
    slot_keys,
    attended_full,
    query_full,
    key_full,
    value_full,
    order_ref,
    attended_ref,
    query_out,
    key_out,
    value_out,
    order_out,
    bias_ref,
    copy_sem,
):
    del order_ref, order_out
    factor = HD**-0.5
    rows = tiles * TILE

    @pl.when(info_ref[0] <= slots)
    def _():
        keys = key_ref[...]
        query = stacked(query_ref, heads)
        grad = stacked(grad_ref, heads)
        scores = own_scores(tiles, slots, heads, tile_total, info_ref, bias_ref, keys, query)
        probs = jnp.exp2(scores - max_ref[...]) * inverse_ref[...]
        dprobs = dot_t(value_ref[...], grad)
        dscores = (probs * (dprobs - delta_ref[...])).astype(jnp.bfloat16)
        value_out[...] = dot(probs.astype(jnp.bfloat16), grad)
        key_out[...] = dot(dscores, query) * factor
        query_t = (dot(keys.T, dscores) + dot(slot_keys[...].T, dscores_ref[...])) * factor
        for h in range(heads):
            columns = pl.ds(h * HD, HD)
            attended_ref[:, columns] = out_t_ref[:, pl.ds(h * rows, rows)].T
            query_out[:, columns] = query_t[:, h * rows : (h + 1) * rows].T

    @pl.when(info_ref[0] > slots)
    def _():
        for source, target in (
            (attended_full, attended_ref),
            (query_full, query_out),
            (key_full, key_out),
            (value_full, value_out),
        ):
            copy = pltpu.make_async_copy(source, target, copy_sem)
            copy.start()
            copy.wait()


def per_device(queries, key_rows, value_rows, out_grad, tile_ids, tile_mask):
    row_count = queries.shape[0]
    heads = queries.shape[1] // HD
    ranks = lax.axis_size("seq")
    chips = ranks // 2
    assert key_rows.shape[1] == HD and ranks > 1 and ranks & (ranks - 1) == 0
    tiles = row_count // TILE
    tile_total = tile_ids.shape[0]
    slots = tiles
    rounds = math.ceil(tile_total / slots)
    slot_shape = (slots, TILE, HD)
    buffer = (rounds - 1, 2) + slot_shape
    shape = jax.ShapeDtypeStruct
    bf16, f32 = jnp.bfloat16, jnp.float32

    def swap(values, step):
        return lax.ppermute(values, "seq", [(source, source ^ step) for source in range(ranks)])

    def across(values):
        return [swap(values, 2 * step) for step in far_first(chips)]

    def add(*values):
        total = values[0].astype(f32)
        for value in values[1:]:
            total = total + value.astype(f32)
        return total.astype(bf16)

    table = jnp.pad(tile_mask, ((0, 1), (0, 0)))
    table = table + jnp.pad(tile_ids[None], ((tile_total, 0), (0, 0)))
    key_other, value_other = swap(key_rows, 1), swap(value_rows, 1)
    chip_rows = (key_rows, value_rows, key_other, value_other)
    info, chosen, spare = call(
        functools.partial(list_kernel, tile_total, tiles, slots),
        [SMEM_SPEC] + [ANY_SPEC] * 4,
        (
            shape((info_size(tile_total, tiles, slots),), jnp.int32),
            shape(slot_shape, bf16),
            shape(buffer, bf16),
        ),
        (SMEM_SPEC, VMEM_SPEC, ANY_SPEC),
        scratch=(
            pltpu.SMEM((tile_total,), jnp.int32),
            pltpu.VMEM(key_rows.shape, bf16),
            pltpu.VMEM(key_rows.shape, bf16),
            pltpu.SemaphoreType.DMA,
            pltpu.SemaphoreType.DMA,
        ),
        moved=4 * 1024 * 1024,
    )(table, *chip_rows)
    used = (info[0] + slots - 1) // slots

    def select(index):
        return call(
            functools.partial(select_kernel, tiles, slots),
            [SMEM_SPEC] * 2 + [VMEM_SPEC] * 4,
            shape(slot_shape, bf16),
            VMEM_SPEC,
            moved=5 * row_count * HD * 2,
        )(info, index.reshape(1), *chip_rows)

    arrived = across(chosen)
    handed = [swap(values, 1) for values in arrived]

    def gather_more(index, buffered):
        chosen = select(index)
        total = add(chosen, *across(chosen))
        pair = jnp.stack([total, swap(total, 1)])
        return lax.dynamic_update_index_in_dim(buffered, pair, index - 1, 0)

    more = lax.fori_loop(1, used, gather_more, spare)

    all_rows = row_count + rounds * slots * TILE
    columns = heads * row_count
    line = shape((1, columns), f32)
    work = 2 * columns * row_count * HD
    max_own, total_own, weighted, grad_t = call(
        functools.partial(own_kernel, tiles, slots, heads, tile_total),
        [SMEM_SPEC] + [VMEM_SPEC] * 4 + [ANY_SPEC],
        (line, line, shape((HD, columns), f32), shape((HD, columns), bf16)),
        (VMEM_SPEC,) * 4,
        scratch=(pltpu.VMEM((row_count, row_count), f32),),
        flops=24 * work,
        moved=4 * row_count * heads * HD,
    )(info, queries, out_grad, key_rows, value_rows, more)

    full = (
        shape(queries.shape, bf16),
        shape(queries.shape, f32),
        shape(key_rows.shape, f32),
        shape(value_rows.shape, f32),
    )
    keep, give, row_max, inverse, delta, out_t, dscores, slot_keys, more_terms, *full_values = call(
        functools.partial(gathered_kernel, chips, tiles, slots, heads, tile_total),
        [SMEM_SPEC, ANY_SPEC] + [VMEM_SPEC] * 10 + [ANY_SPEC] + [VMEM_SPEC] * (2 * chips - 2),
        (
            shape(slot_shape, bf16),
            shape(slot_shape, bf16),
            line,
            line,
            line,
            shape((HD, columns), bf16),
            shape((slots * TILE, columns), bf16),
            shape((slots * TILE, HD), bf16),
            shape(buffer, bf16),
        )
        + full,
        (VMEM_SPEC,) * 8 + (ANY_SPEC,) * 5,
        scratch=(
            pltpu.VMEM((all_rows, row_count), f32),
            pltpu.VMEM((2, all_rows, HD), bf16),
            pltpu.VMEM((2, all_rows, HD), f32),
            pltpu.VMEM((all_rows, row_count), f32),
            pltpu.VMEM((2,) + slot_shape, bf16),
            pltpu.VMEM(queries.shape, bf16),
            pltpu.VMEM(queries.shape, f32),
            pltpu.SMEM(table.shape, jnp.int32),
            pltpu.SemaphoreType.DMA,
        ),
        flops=24 * work,
        moved=4 * row_count * heads * HD,
    )(
        info,
        table,
        queries,
        out_grad,
        *chip_rows,
        max_own,
        total_own,
        weighted,
        grad_t,
        more,
        *arrived,
        *handed,
    )

    chip_sum = add(keep, swap(give, 1))
    back = across(chip_sum)
    attended, query_grad, key_own, value_own, back[0] = call(
        functools.partial(rest_kernel, tiles, slots, heads, tile_total),
        [SMEM_SPEC] + [VMEM_SPEC] * 10 + [ANY_SPEC] * 5,
        full + (shape(slot_shape, bf16),),
        (VMEM_SPEC,) * 4 + (ANY_SPEC,),
        scratch=(pltpu.VMEM((row_count, row_count), f32), pltpu.SemaphoreType.DMA),
        flops=32 * work,
        moved=8 * row_count * heads * HD,
        aliases={15: 4},
    )(
        info,
        queries,
        out_grad,
        key_rows,
        value_rows,
        row_max,
        inverse,
        delta,
        out_t,
        dscores,
        slot_keys,
        *full_values,
        back[0],
    )
    sums = back + [chip_sum]
    sums = sums + [swap(values, 1) for values in sums]

    def close(sums, grads, *lead):
        kernel = functools.partial(final_kernel, tiles, slots, len(sums) // 2, tile_total)
        if not lead:
            kernel = lambda info_ref, *refs: final_kernel(
                tiles, slots, len(sums) // 2, tile_total, info_ref, None, *refs
            )
        return call(
            kernel,
            [SMEM_SPEC] * (1 + len(lead)) + [VMEM_SPEC] * (2 + len(sums)),
            (shape(key_rows.shape, f32), shape(value_rows.shape, f32)),
            (VMEM_SPEC,) * 2,
            moved=5 * row_count * HD * 4,
        )(info, *lead, *grads, *sums)

    def reduce_more(index, grads):
        terms = lax.dynamic_index_in_dim(more_terms, index - 1, 0, keepdims=False)
        part = add(terms[0], swap(terms[1], 1))
        total = add(part, *across(part))
        return tuple(close([total, swap(total, 1)], grads, index.reshape(1)))

    grads = tuple(close(sums, (key_own, value_own)))
    key_grad, value_grad = lax.fori_loop(1, used, reduce_more, grads)
    return attended, query_grad, key_grad, value_grad


def solution(mesh):
    return jax.shard_map(
        per_device,
        mesh=mesh,
        in_specs=(
            P(("batch", "seq"), "head"),
            P(("batch", "seq"), "head"),
            P(("batch", "seq"), "head"),
            P(("batch", "seq"), "head"),
            P("batch"),
            P("batch", None),
        ),
        out_specs=(P(("batch", "seq"), "head"),) * 4,
        check_vma=False,
    )
```

```python
import functools
import math

import jax
import jax.numpy as jnp
from jax import lax
from jax.experimental import pallas as pl
from jax.experimental.pallas import tpu as pltpu
from jax.sharding import PartitionSpec as P

HD = 128
TILE = 128
FAR_BELOW = -1e30
LOG2E = 1.4426950408889634
NT_DIMS = (((1,), (1,)), ((), ()))
VMEM_LIMIT = 32 * 1024 * 1024

SMEM_SPEC = pl.BlockSpec(memory_space=pltpu.SMEM)
VMEM_SPEC = pl.BlockSpec(memory_space=pltpu.VMEM)
ANY_SPEC = pl.BlockSpec(memory_space=pl.ANY)


def call(kernel, in_specs, out_shape, out_specs, scratch=(), flops=0, moved=0, aliases=None):
    return pl.pallas_call(
        kernel,
        in_specs=in_specs,
        out_shape=out_shape,
        out_specs=out_specs,
        scratch_shapes=list(scratch),
        input_output_aliases=aliases or {},
        compiler_params=pltpu.CompilerParams(vmem_limit_bytes=VMEM_LIMIT),
        cost_estimate=pl.CostEstimate(flops=flops, bytes_accessed=moved, transcendentals=0),
    )


def tile_rows(first_row, tile):
    return pl.ds(pl.multiple_of(first_row + tile * TILE, TILE), TILE)


def info_size(tile_total, tiles, slots):
    return 2 * tile_total + 2 + (slots + tiles) * tiles


def pairs_of(chips):
    return [(step, step + 1) for step in range(1, chips - 1, 2)]


def list_kernel(tile_total, tiles, slots, table_ref, *refs):
    sources, (info_ref, full_ref, half_ref, spare_ref, *refs) = refs[:4], refs[4:]
    any_ref, loaded, sems = refs[0], refs[1:5], refs[5:]
    del spare_ref
    rank = lax.axis_index("seq")
    copies = [
        pltpu.make_async_copy(source, target, sem)
        for source, target, sem in zip(sources, loaded, sems)
    ]
    for copy in copies:
        copy.start()

    def ids(position):
        return table_ref[tile_total, position]

    def mask(query_tile, key_tile):
        return table_ref[query_tile, key_tile]

    for place in range(1, tile_total + 2):
        info_ref[place] = 0
    for tile in range(tile_total):
        users = mask(0, tile)
        for other in range(1, tile_total):
            users = users + mask(other, tile)
        any_ref[tile] = users
    count = jnp.int32(0)
    for position in range(tile_total):
        key_tile = ids(position)
        away = any_ref[key_tile]
        for local in range(tiles):
            away = away - mask(ids(position // tiles * tiles + local), key_tile)
        info_ref[1 + count] = position
        info_ref[tile_total + 2 + position] = jnp.where(away > 0, count, -1)
        count = count + jnp.where(away > 0, 1, 0)
    info_ref[0] = count
    my_tiles = [ids(rank * tiles + b) for b in range(tiles)]
    place = 2 * tile_total + 2
    for slot in range(slots):
        position = info_ref[1 + slot]
        usable = ((slot < count) & (position // tiles != rank)).astype(jnp.int32)
        for b in range(tiles):
            info_ref[place] = usable * mask(my_tiles[b], ids(position))
            place += 1
    for a in range(tiles):
        for b in range(tiles):
            info_ref[place] = mask(my_tiles[b], my_tiles[a])
            place += 1
    for copy in copies:
        copy.wait()
    odd = rank % 2
    for kind in range(2):
        part = odd ^ kind
        target = full_ref.at[pl.ds(part * slots, slots)]
        pick(tiles, slots, 0, info_ref, loaded[kind], loaded[2 + kind], target)
    half_ref[...] = full_ref[:slots]


def pick(tiles, slots, base, info_ref, own_ref, other_ref, out_ref):
    rank = lax.axis_index("seq")
    for slot in range(slots):
        position = info_ref[1 + base + slot]
        home = position // tiles
        rows = tile_rows(0, position % tiles)
        out_ref[slot] = jnp.zeros_like(out_ref[slot])

        @pl.when(home == rank)
        def _():
            out_ref[slot] = own_ref[rows, :]

        @pl.when(home == rank ^ 1)
        def _():
            out_ref[slot] = other_ref[rows, :]


def select_kernel(tiles, slots, info_ref, round_ref, *refs):
    key_ref, value_ref, key_other, value_other, out_ref = refs
    rank = lax.axis_index("seq")
    for kind, own, other in ((0, key_ref, key_other), (1, value_ref, value_other)):

        @pl.when(rank % 2 == kind)
        def _():
            pick(tiles, slots, round_ref[0] * slots, info_ref, own, other, out_ref)


def add_sums(tiles, slots, tile_total, base, info_ref, grads, outs, sums_of):
    rank = lax.axis_index("seq")
    odd = rank % 2
    for grad, out in zip(grads, outs):
        out[...] = grad[...]
    for tile in range(tiles):
        slot = info_ref[tile_total + 2 + rank * tiles + tile] - base
        rows = tile_rows(0, tile)

        @pl.when((slot >= 0) & (slot < slots))
        def _():
            totals = []
            for part in range(2):
                total = None
                for source in sums_of(part, slot):
                    source = source.astype(jnp.float32)
                    total = source if total is None else total + source
                totals.append(total)
            for kind, out in enumerate(outs):
                out[rows, :] += jnp.where(odd == kind, totals[0], totals[1])


def close_kernel(tiles, slots, chips, tile_total, info_ref, *refs):
    grads, (chip_ref, *sums), outs = refs[:2], refs[2:-2], refs[-2:]
    half = len(sums) // 2
    arrived, handed = sums[:half], sums[half:]

    def sums_of(part, slot):
        yield chip_ref[part * slots + slot]
        for own, other in zip(arrived[:-1], handed[:-1]):
            yield own[part * slots + slot]
            yield other[(1 - part) * slots + slot]
        yield (handed if part else arrived)[-1][slot]

    add_sums(tiles, slots, tile_total, 0, info_ref, grads, outs, sums_of)


def later_kernel(tiles, slots, tile_total, info_ref, round_ref, *refs):
    grads, sums, outs = refs[:2], refs[2:-2], refs[-2:]

    def sums_of(part, slot):
        yield sums[part][slot]

    base = round_ref[0] * slots
    add_sums(tiles, slots, tile_total, base, info_ref, grads, outs, sums_of)


def causal_bias():
    later = lax.broadcasted_iota(jnp.int32, (TILE, TILE), 1)
    return jnp.where(lax.broadcasted_iota(jnp.int32, (TILE, TILE), 0) <= later, 0.0, FAR_BELOW)


def block_bias(allowed):
    return jnp.full((TILE, TILE), jnp.where(allowed, 0.0, FAR_BELOW), jnp.float32)


def own_bias(tiles, bias_ref, allowed):
    for a in range(tiles):
        for b in range(tiles):
            bias = causal_bias() if a == b else block_bias(allowed(a, b) == 1)
            bias_ref[pl.ds(a * TILE, TILE), pl.ds(b * TILE, TILE)] = bias


def stacked(ref, heads):
    return jnp.concatenate([ref[:, h * HD : (h + 1) * HD] for h in range(heads)], axis=0)


def dot(one, other):
    return jnp.dot(one, other, preferred_element_type=jnp.float32)


def dot_t(one, other):
    return lax.dot_general(one, other, NT_DIMS, preferred_element_type=jnp.float32)


def own_scores(tiles, slots, heads, tile_total, info_ref, bias_ref, keys, query):
    place = 2 * tile_total + 2 + slots * tiles
    own_bias(tiles, bias_ref, lambda a, b: info_ref[place + a * tiles + b])
    bias = jnp.concatenate([bias_ref[...]] * heads, axis=1)
    return dot_t(keys, query) * (HD**-0.5 * LOG2E) + bias


def own_kernel(
    tiles,
    slots,
    heads,
    tile_total,
    info_ref,
    query_ref,
    grad_ref,
    key_ref,
    value_ref,
    order_ref,
    max_ref,
    total_ref,
    weighted_ref,
    grad_t_ref,
    bias_ref,
):
    del order_ref
    query = stacked(query_ref, heads)
    scores = own_scores(tiles, slots, heads, tile_total, info_ref, bias_ref, key_ref[...], query)
    row_max = jnp.max(scores, axis=0, keepdims=True)
    terms = jnp.exp2(scores - row_max)
    max_ref[...] = row_max
    total_ref[...] = jnp.sum(terms, axis=0, keepdims=True)
    weighted_ref[...] = dot(value_ref[...].T, terms.astype(jnp.bfloat16))
    grad_t_ref[...] = stacked(grad_ref, heads).T


def gathered_kernel(
    chips,
    tiles,
    slots,
    heads,
    tile_total,
    info_ref,
    table_any,
    query_ref,
    grad_ref,
    key_ref,
    value_ref,
    key_other,
    value_other,
    max_own,
    total_own,
    weighted_own,
    grad_t_ref,
    more_ref,
    *refs,
):
    count = len(pairs_of(chips)) + 1
    arrived, handed, refs = refs[:count], refs[count : 2 * count], refs[2 * count :]
    parts_ref, max_ref, inverse_ref, delta_ref, out_t_ref, dscores_ref, *refs = refs
    slot_keys, *refs = refs
    more_out, attended_full, query_full, key_full, value_full, *refs = refs
    bias_ref, held_ref, sum_ref, score_ref, staged_ref, *refs = refs
    attended_ref, query_out, table_ref, copy_sem = refs
    keys_ref, values_ref = held_ref.at[0], held_ref.at[1]
    key_sum, value_sum = sum_ref.at[0], sum_ref.at[1]
    rank = lax.axis_index("seq")
    odd = rank % 2
    rows = tiles * TILE
    chunk = slots * TILE
    factor = HD**-0.5
    scale = factor * LOG2E
    needed = info_ref[0]
    columns = [pl.ds(h * HD, HD) for h in range(heads)]

    def repack(target, part, first_row):
        kind = odd ^ part
        for slot in range(slots):
            total = sum_ref[kind, tile_rows(first_row, slot), :]
            target[slot] = (total * jnp.where(kind == 0, factor, 1.0)).astype(jnp.bfloat16)

    for slot in range(slots):
        for b in range(tiles):
            allowed = info_ref[2 * tile_total + 2 + slot * tiles + b] == 1
            bias_ref[pl.ds(slot * TILE, TILE), pl.ds(b * TILE, TILE)] = block_bias(allowed)
        position = info_ref[1 + slot]
        away = (position // (2 * tiles)) ^ (rank // 2)
        at = tile_rows(0, slot)

        @pl.when(away == 0)
        def _():
            source = tile_rows(0, position % tiles)
            keys_ref[at, :] = key_other[source, :]
            values_ref[at, :] = value_other[source, :]

        @pl.when(away == chips - 1)
        def _():
            held_ref[odd, at, :] = arrived[-1][slot]
            held_ref[odd ^ 1, at, :] = handed[-1][slot]

        for index, pair in enumerate(pairs_of(chips)):
            for core, step in enumerate(pair):

                @pl.when((away == step) & (odd == core))
                def _():
                    held_ref[odd, at, :] = arrived[index][slot]
                    held_ref[odd ^ 1, at, :] = arrived[index][slots + slot]

                @pl.when((away == step) & (odd != core))
                def _():
                    held_ref[odd ^ 1, at, :] = handed[index][slot]
                    held_ref[odd, at, :] = handed[index][slots + slot]

    first = pl.ds(0, chunk)

    @pl.when(needed <= slots)
    def _():
        keys = keys_ref[first, :]
        values = values_ref[first, :]
        slot_keys[...] = keys
        query = stacked(query_ref, heads)
        grad = stacked(grad_ref, heads)
        bias = jnp.concatenate([bias_ref[first, :]] * heads, axis=1)
        scores = dot_t(keys, query) * scale + bias
        dprobs = dot_t(values, grad)
        row_max = jnp.maximum(max_own[...], jnp.max(scores, axis=0, keepdims=True))
        shrink = jnp.exp2(max_own[...] - row_max)
        terms = jnp.exp2(scores - row_max)
        inverse = 1.0 / (total_own[...] * shrink + jnp.sum(terms, axis=0, keepdims=True))
        weighted = weighted_own[...] * shrink + dot(values.T, terms.astype(jnp.bfloat16))
        out = (weighted * inverse).astype(jnp.bfloat16)
        delta = jnp.sum(
            grad_t_ref[...].astype(jnp.float32) * out.astype(jnp.float32), axis=0, keepdims=True
        )
        probs = terms * inverse
        dscores = (probs * (dprobs - delta)).astype(jnp.bfloat16)
        value_sum[first, :] = dot(probs.astype(jnp.bfloat16), grad)
        key_sum[first, :] = dot(dscores, query)
        out_t_ref[...] = out
        max_ref[...] = row_max
        inverse_ref[...] = inverse
        delta_ref[...] = delta
        dscores_ref[...] = dscores

    @pl.when(needed > slots)
    def _():
        used = (needed + slots - 1) // slots
        own_first = pl.multiple_of(used * chunk, chunk)
        own_rows = pl.ds(own_first, rows)
        copy = pltpu.make_async_copy(table_any, table_ref, copy_sem)
        copy.start()
        copy.wait()

        def ids(position):
            return table_ref[tile_total, position]

        def allowed(a, b):
            return table_ref[ids(rank * tiles + b), ids(rank * tiles + a)]

        own_bias(tiles, bias_ref.at[own_rows, :], allowed)
        keys_ref[own_rows, :] = key_ref[...]
        values_ref[own_rows, :] = value_ref[...]

        def fetch(index, carry):
            copy = pltpu.make_async_copy(more_ref.at[index - 1], staged_ref, copy_sem)
            copy.start()
            copy.wait()
            first_row = pl.multiple_of(index * chunk, chunk)
            for slot in range(slots):
                for part in range(2):
                    held_ref[odd ^ part, tile_rows(first_row, slot), :] = staged_ref[part, slot]
                listed = index * slots + slot
                position = info_ref[1 + listed]
                usable = (listed < needed) & (position // tiles != rank)
                for b in range(tiles):
                    seen = table_ref[ids(rank * tiles + b), ids(position)] == 1
                    bias_ref[tile_rows(first_row, slot), pl.ds(b * TILE, TILE)] = block_bias(
                        usable & seen
                    )
            return carry

        lax.fori_loop(1, used, fetch, 0)
        key_sum[...] = jnp.zeros_like(key_sum)
        value_sum[...] = jnp.zeros_like(value_sum)
        blocks = used * slots + tiles

        for h in range(heads):
            query = query_ref[:, columns[h]]
            grad = grad_ref[:, columns[h]]

            def score(index, row_max):
                at = tile_rows(0, index)
                scores = dot_t(keys_ref[at, :], query) * scale + bias_ref[at, :]
                score_ref[at, :] = scores
                return jnp.maximum(row_max, jnp.max(scores, axis=0, keepdims=True))

            row_max = lax.fori_loop(0, blocks, score, jnp.full((1, rows), FAR_BELOW, jnp.float32))

            def forward(index, carry):
                total, weighted = carry
                at = tile_rows(0, index)
                terms = jnp.exp2(score_ref[at, :] - row_max)
                score_ref[at, :] = terms
                weighted = weighted + dot(values_ref[at, :].T, terms.astype(jnp.bfloat16))
                return total + jnp.sum(terms, axis=0, keepdims=True), weighted

            zeros = jnp.zeros((HD, rows), jnp.float32)
            start = (jnp.zeros((1, rows), jnp.float32), zeros)
            total, weighted = lax.fori_loop(0, blocks, forward, start)
            inverse = 1.0 / total
            out = (weighted * inverse).astype(jnp.bfloat16)
            attended_ref[:, columns[h]] = out.T
            grad_t = grad_t_ref[:, pl.ds(h * rows, rows)].astype(jnp.float32)
            delta = jnp.sum(grad_t * out.astype(jnp.float32), axis=0, keepdims=True)

            def backward(index, query_t):
                at = tile_rows(0, index)
                probs = score_ref[at, :] * inverse
                dprobs = dot_t(values_ref[at, :], grad)
                dscores = (probs * (dprobs - delta)).astype(jnp.bfloat16)
                key_sum[at, :] += dot(dscores, query)
                value_sum[at, :] += dot(probs.astype(jnp.bfloat16), grad)
                return query_t + dot(keys_ref[at, :].T, dscores)

            query_t = lax.fori_loop(0, blocks, backward, zeros)
            query_out[:, columns[h]] = (query_t * factor).T

        key_sum[own_rows, :] = key_sum[own_rows, :] * factor
        for source, target in (
            (attended_ref, attended_full),
            (query_out, query_full),
            (key_sum.at[own_rows, :], key_full),
            (value_sum.at[own_rows, :], value_full),
        ):
            copy = pltpu.make_async_copy(source, target, copy_sem)
            copy.start()
            copy.wait()

        def store(index, carry):
            for part in range(2):
                repack(staged_ref.at[part], part, pl.multiple_of(index * chunk, chunk))
            copy = pltpu.make_async_copy(staged_ref, more_out.at[index - 1], copy_sem)
            copy.start()
            copy.wait()
            return carry

        lax.fori_loop(1, used, store, 0)

    for part in range(2):
        repack(parts_ref.at[pl.ds(part * slots, slots)], part, 0)


def rest_kernel(
    tiles,
    slots,
    heads,
    tile_total,
    info_ref,
    query_ref,
    grad_ref,
    key_ref,
    value_ref,
    max_ref,
    inverse_ref,
    delta_ref,
    out_t_ref,
    dscores_ref,
    slot_keys,
    attended_full,
    query_full,
    key_full,
    value_full,
    order_ref,
    attended_ref,
    query_out,
    key_out,
    value_out,
    order_out,
    bias_ref,
    copy_sem,
):
    del order_ref, order_out
    factor = HD**-0.5
    rows = tiles * TILE

    @pl.when(info_ref[0] <= slots)
    def _():
        keys = key_ref[...]
        query = stacked(query_ref, heads)
        grad = stacked(grad_ref, heads)
        scores = own_scores(tiles, slots, heads, tile_total, info_ref, bias_ref, keys, query)
        probs = jnp.exp2(scores - max_ref[...]) * inverse_ref[...]
        dprobs = dot_t(value_ref[...], grad)
        dscores = (probs * (dprobs - delta_ref[...])).astype(jnp.bfloat16)
        value_out[...] = dot(probs.astype(jnp.bfloat16), grad)
        key_out[...] = dot(dscores, query) * factor
        query_t = (dot(keys.T, dscores) + dot(slot_keys[...].T, dscores_ref[...])) * factor
        for h in range(heads):
            columns = pl.ds(h * HD, HD)
            attended_ref[:, columns] = out_t_ref[:, pl.ds(h * rows, rows)].T
            query_out[:, columns] = query_t[:, h * rows : (h + 1) * rows].T

    @pl.when(info_ref[0] > slots)
    def _():
        for source, target in (
            (attended_full, attended_ref),
            (query_full, query_out),
            (key_full, key_out),
            (value_full, value_out),
        ):
            copy = pltpu.make_async_copy(source, target, copy_sem)
            copy.start()
            copy.wait()


def per_device(queries, key_rows, value_rows, out_grad, tile_ids, tile_mask):
    row_count = queries.shape[0]
    heads = queries.shape[1] // HD
    ranks = lax.axis_size("seq")
    chips = ranks // 2
    assert key_rows.shape[1] == HD and ranks > 1 and ranks & (ranks - 1) == 0
    tiles = row_count // TILE
    tile_total = tile_ids.shape[0]
    slots = tiles
    rounds = math.ceil(tile_total / slots)
    slot_shape = (slots, TILE, HD)
    buffer = (rounds - 1, 2) + slot_shape
    shape = jax.ShapeDtypeStruct
    bf16, f32 = jnp.bfloat16, jnp.float32

    def swap(values, step):
        return lax.ppermute(values, "seq", [(source, source ^ step) for source in range(ranks)])

    def across(values):
        return [swap(values, 2 * step) for step in range(1, chips)]

    def trade(full, half):
        got = []
        for pair in pairs_of(chips):
            routes = [(source, source ^ 2 * pair[source % 2]) for source in range(ranks)]
            got.append(lax.ppermute(full, "seq", routes))
        return got + [swap(half, 2 * (chips - 1))]

    def add(*values):
        total = values[0].astype(f32)
        for value in values[1:]:
            total = total + value.astype(f32)
        return total.astype(bf16)

    table = jnp.pad(tile_mask, ((0, 1), (0, 0)))
    table = table + jnp.pad(tile_ids[None], ((tile_total, 0), (0, 0)))
    key_other, value_other = swap(key_rows, 1), swap(value_rows, 1)
    chip_rows = (key_rows, value_rows, key_other, value_other)
    info, chosen, chosen_half, spare = call(
        functools.partial(list_kernel, tile_total, tiles, slots),
        [SMEM_SPEC] + [ANY_SPEC] * 4,
        (
            shape((info_size(tile_total, tiles, slots),), jnp.int32),
            shape((2 * slots, TILE, HD), bf16),
            shape(slot_shape, bf16),
            shape(buffer, bf16),
        ),
        (SMEM_SPEC, VMEM_SPEC, VMEM_SPEC, ANY_SPEC),
        scratch=(
            pltpu.SMEM((tile_total,), jnp.int32),
            *[pltpu.VMEM(key_rows.shape, bf16)] * 4,
            *[pltpu.SemaphoreType.DMA] * 4,
        ),
        moved=4 * 1024 * 1024,
    )(table, *chip_rows)
    used = (info[0] + slots - 1) // slots

    def select(index):
        return call(
            functools.partial(select_kernel, tiles, slots),
            [SMEM_SPEC] * 2 + [VMEM_SPEC] * 4,
            shape(slot_shape, bf16),
            VMEM_SPEC,
            moved=5 * row_count * HD * 2,
        )(info, index.reshape(1), *chip_rows)

    arrived = trade(chosen, chosen_half)
    handed = [swap(values, 1) for values in arrived]

    def gather_more(index, buffered):
        chosen = select(index)
        total = add(chosen, *across(chosen))
        pair = jnp.stack([total, swap(total, 1)])
        return lax.dynamic_update_index_in_dim(buffered, pair, index - 1, 0)

    more = lax.fori_loop(1, used, gather_more, spare)

    all_rows = row_count + rounds * slots * TILE
    columns = heads * row_count
    line = shape((1, columns), f32)
    work = 2 * columns * row_count * HD
    max_own, total_own, weighted, grad_t = call(
        functools.partial(own_kernel, tiles, slots, heads, tile_total),
        [SMEM_SPEC] + [VMEM_SPEC] * 4 + [ANY_SPEC],
        (line, line, shape((HD, columns), f32), shape((HD, columns), bf16)),
        (VMEM_SPEC,) * 4,
        scratch=(pltpu.VMEM((row_count, row_count), f32),),
        flops=24 * work,
        moved=4 * row_count * heads * HD,
    )(info, queries, out_grad, key_rows, value_rows, more)

    full = (
        shape(queries.shape, bf16),
        shape(queries.shape, f32),
        shape(key_rows.shape, f32),
        shape(value_rows.shape, f32),
    )
    parts, row_max, inverse, delta, out_t, dscores, slot_keys, more_terms, *full_values = call(
        functools.partial(gathered_kernel, chips, tiles, slots, heads, tile_total),
        [SMEM_SPEC, ANY_SPEC] + [VMEM_SPEC] * 10 + [ANY_SPEC] + [VMEM_SPEC] * (2 * len(arrived)),
        (
            shape((2 * slots, TILE, HD), bf16),
            line,
            line,
            line,
            shape((HD, columns), bf16),
            shape((slots * TILE, columns), bf16),
            shape((slots * TILE, HD), bf16),
            shape(buffer, bf16),
        )
        + full,
        (VMEM_SPEC,) * 7 + (ANY_SPEC,) * 5,
        scratch=(
            pltpu.VMEM((all_rows, row_count), f32),
            pltpu.VMEM((2, all_rows, HD), bf16),
            pltpu.VMEM((2, all_rows, HD), f32),
            pltpu.VMEM((all_rows, row_count), f32),
            pltpu.VMEM((2,) + slot_shape, bf16),
            pltpu.VMEM(queries.shape, bf16),
            pltpu.VMEM(queries.shape, f32),
            pltpu.SMEM(table.shape, jnp.int32),
            pltpu.SemaphoreType.DMA,
        ),
        flops=24 * work,
        moved=4 * row_count * heads * HD,
    )(
        info,
        table,
        queries,
        out_grad,
        *chip_rows,
        max_own,
        total_own,
        weighted,
        grad_t,
        more,
        *arrived,
        *handed,
    )

    partner = swap(parts, 1)
    half_sum = add(parts[:slots], partner[slots:])
    chip_sum = jnp.concatenate([half_sum, add(parts[slots:], partner[:slots])])
    back = trade(chip_sum, half_sum)
    attended, query_grad, key_own, value_own, back[0] = call(
        functools.partial(rest_kernel, tiles, slots, heads, tile_total),
        [SMEM_SPEC] + [VMEM_SPEC] * 10 + [ANY_SPEC] * 5,
        full + (shape(back[0].shape, bf16),),
        (VMEM_SPEC,) * 4 + (ANY_SPEC,),
        scratch=(pltpu.VMEM((row_count, row_count), f32), pltpu.SemaphoreType.DMA),
        flops=32 * work,
        moved=8 * row_count * heads * HD,
        aliases={15: 4},
    )(
        info,
        queries,
        out_grad,
        key_rows,
        value_rows,
        row_max,
        inverse,
        delta,
        out_t,
        dscores,
        slot_keys,
        *full_values,
        back[0],
    )
    sums = [chip_sum] + back + [swap(values, 1) for values in back]

    def close(kernel, lead, grads, sums):
        return call(
            kernel,
            [SMEM_SPEC] * len(lead) + [VMEM_SPEC] * (2 + len(sums)),
            (shape(key_rows.shape, f32), shape(value_rows.shape, f32)),
            (VMEM_SPEC,) * 2,
            moved=5 * row_count * HD * 4,
        )(*lead, *grads, *sums)

    def reduce_more(index, grads):
        terms = lax.dynamic_index_in_dim(more_terms, index - 1, 0, keepdims=False)
        part = add(terms[0], swap(terms[1], 1))
        total = add(part, *across(part))
        kernel = functools.partial(later_kernel, tiles, slots, tile_total)
        return tuple(close(kernel, (info, index.reshape(1)), grads, (total, swap(total, 1))))

    kernel = functools.partial(close_kernel, tiles, slots, chips, tile_total)
    grads = tuple(close(kernel, (info,), (key_own, value_own), sums))
    key_grad, value_grad = lax.fori_loop(1, used, reduce_more, grads)
    return attended, query_grad, key_grad, value_grad


def solution(mesh):
    return jax.shard_map(
        per_device,
        mesh=mesh,
        in_specs=(
            P(("batch", "seq"), "head"),
            P(("batch", "seq"), "head"),
            P(("batch", "seq"), "head"),
            P(("batch", "seq"), "head"),
            P("batch"),
            P("batch", None),
        ),
        out_specs=(P(("batch", "seq"), "head"),) * 4,
        check_vma=False,
    )
```

```python
import functools
import math

import jax
import jax.numpy as jnp
from jax import lax
from jax.experimental import pallas as pl
from jax.experimental.pallas import tpu as pltpu
from jax.sharding import PartitionSpec as P

HD = 128
TILE = 128
FAR_BELOW = -1e30
LOG2E = 1.4426950408889634
NT_DIMS = (((1,), (1,)), ((), ()))
VMEM_LIMIT = 32 * 1024 * 1024

SMEM_SPEC = pl.BlockSpec(memory_space=pltpu.SMEM)
VMEM_SPEC = pl.BlockSpec(memory_space=pltpu.VMEM)
ANY_SPEC = pl.BlockSpec(memory_space=pl.ANY)


def call(kernel, in_specs, out_shape, out_specs, scratch=(), flops=0, moved=0, aliases=None):
    return pl.pallas_call(
        kernel,
        in_specs=in_specs,
        out_shape=out_shape,
        out_specs=out_specs,
        scratch_shapes=list(scratch),
        input_output_aliases=aliases or {},
        compiler_params=pltpu.CompilerParams(vmem_limit_bytes=VMEM_LIMIT),
        cost_estimate=pl.CostEstimate(flops=flops, bytes_accessed=moved, transcendentals=0),
    )


def tile_rows(first_row, tile):
    return pl.ds(pl.multiple_of(first_row + tile * TILE, TILE), TILE)


def info_size(tile_total, tiles, slots):
    return 2 * tile_total + 2 + (slots + tiles) * tiles


def pairs_of(chips):
    return [(step, step + 1) for step in range(1, chips - 1, 2)]


def list_kernel(tile_total, tiles, slots, table_ref, *refs):
    sources, (info_ref, full_ref, half_ref, spare_ref, *refs) = refs[:4], refs[4:]
    any_ref, loaded, sems = refs[0], refs[1:5], refs[5:]
    del spare_ref
    rank = lax.axis_index("seq")
    copies = [
        pltpu.make_async_copy(source, target, sem)
        for source, target, sem in zip(sources, loaded, sems)
    ]
    for copy in copies:
        copy.start()

    def ids(position):
        return table_ref[tile_total, position]

    def mask(query_tile, key_tile):
        return table_ref[query_tile, key_tile]

    for place in range(1, tile_total + 2):
        info_ref[place] = 0
    for tile in range(tile_total):
        users = mask(0, tile)
        for other in range(1, tile_total):
            users = users + mask(other, tile)
        any_ref[tile] = users
    count = jnp.int32(0)
    for position in range(tile_total):
        key_tile = ids(position)
        away = any_ref[key_tile]
        for local in range(tiles):
            away = away - mask(ids(position // tiles * tiles + local), key_tile)
        info_ref[1 + count] = position
        info_ref[tile_total + 2 + position] = jnp.where(away > 0, count, -1)
        count = count + jnp.where(away > 0, 1, 0)
    info_ref[0] = count
    my_tiles = [ids(rank * tiles + b) for b in range(tiles)]
    place = 2 * tile_total + 2
    for slot in range(slots):
        position = info_ref[1 + slot]
        usable = ((slot < count) & (position // tiles != rank)).astype(jnp.int32)
        for b in range(tiles):
            info_ref[place] = usable * mask(my_tiles[b], ids(position))
            place += 1
    for a in range(tiles):
        for b in range(tiles):
            info_ref[place] = mask(my_tiles[b], my_tiles[a])
            place += 1
    for copy in copies:
        copy.wait()
    odd = rank % 2
    for kind in range(2):
        part = odd ^ kind
        target = full_ref.at[pl.ds(part * slots, slots)]
        pick(tiles, slots, 0, info_ref, loaded[kind], loaded[2 + kind], target)
    half_ref[...] = full_ref[:slots]


def pick(tiles, slots, base, info_ref, own_ref, other_ref, out_ref):
    rank = lax.axis_index("seq")
    for slot in range(slots):
        position = info_ref[1 + base + slot]
        home = position // tiles
        rows = tile_rows(0, position % tiles)
        out_ref[slot] = jnp.zeros_like(out_ref[slot])

        @pl.when(home == rank)
        def _():
            out_ref[slot] = own_ref[rows, :]

        @pl.when(home == rank ^ 1)
        def _():
            out_ref[slot] = other_ref[rows, :]


def select_kernel(tiles, slots, info_ref, round_ref, *refs):
    key_ref, value_ref, key_other, value_other, out_ref = refs
    rank = lax.axis_index("seq")
    for kind, own, other in ((0, key_ref, key_other), (1, value_ref, value_other)):

        @pl.when(rank % 2 == kind)
        def _():
            pick(tiles, slots, round_ref[0] * slots, info_ref, own, other, out_ref)


def add_sums(tiles, slots, tile_total, base, info_ref, grads, outs, sums_of):
    rank = lax.axis_index("seq")
    odd = rank % 2
    for grad, out in zip(grads, outs):
        out[...] = grad[...]
    for tile in range(tiles):
        slot = info_ref[tile_total + 2 + rank * tiles + tile] - base
        rows = tile_rows(0, tile)

        @pl.when((slot >= 0) & (slot < slots))
        def _():
            totals = []
            for part in range(2):
                total = None
                for source in sums_of(part, slot):
                    source = source.astype(jnp.float32)
                    total = source if total is None else total + source
                totals.append(total)
            for kind, out in enumerate(outs):
                out[rows, :] += jnp.where(odd == kind, totals[0], totals[1])


def close_kernel(tiles, slots, chips, tile_total, info_ref, *refs):
    grads, (chip_ref, *sums), outs = refs[:2], refs[2:-2], refs[-2:]
    half = len(sums) // 2
    arrived, handed = sums[:half], sums[half:]

    def sums_of(part, slot):
        yield chip_ref[part * slots + slot]
        for own, other in zip(arrived[:-1], handed[:-1]):
            yield own[part * slots + slot]
            yield other[(1 - part) * slots + slot]
        yield (handed if part else arrived)[-1][slot]

    add_sums(tiles, slots, tile_total, 0, info_ref, grads, outs, sums_of)


def later_kernel(tiles, slots, tile_total, info_ref, round_ref, *refs):
    grads, sums, outs = refs[:2], refs[2:-2], refs[-2:]

    def sums_of(part, slot):
        yield sums[part][slot]

    base = round_ref[0] * slots
    add_sums(tiles, slots, tile_total, base, info_ref, grads, outs, sums_of)


def causal_bias():
    later = lax.broadcasted_iota(jnp.int32, (TILE, TILE), 1)
    return jnp.where(lax.broadcasted_iota(jnp.int32, (TILE, TILE), 0) <= later, 0.0, FAR_BELOW)


def block_bias(allowed):
    return jnp.full((TILE, TILE), jnp.where(allowed, 0.0, FAR_BELOW), jnp.float32)


def own_bias(tiles, bias_ref, allowed):
    for a in range(tiles):
        for b in range(tiles):
            bias = causal_bias() if a == b else block_bias(allowed(a, b) == 1)
            bias_ref[pl.ds(a * TILE, TILE), pl.ds(b * TILE, TILE)] = bias


def stacked(ref, heads):
    return jnp.concatenate([ref[:, h * HD : (h + 1) * HD] for h in range(heads)], axis=0)


def dot(one, other):
    return jnp.dot(one, other, preferred_element_type=jnp.float32)


def dot_t(one, other):
    return lax.dot_general(one, other, NT_DIMS, preferred_element_type=jnp.float32)


def own_scores(tiles, slots, heads, tile_total, info_ref, bias_ref, keys, query):
    place = 2 * tile_total + 2 + slots * tiles
    own_bias(tiles, bias_ref, lambda a, b: info_ref[place + a * tiles + b])
    bias = jnp.concatenate([bias_ref[...]] * heads, axis=1)
    return dot_t(keys, query) * (HD**-0.5 * LOG2E) + bias


def own_kernel(
    tiles,
    slots,
    heads,
    tile_total,
    info_ref,
    query_ref,
    grad_ref,
    key_ref,
    value_ref,
    max_ref,
    total_ref,
    weighted_ref,
    grad_t_ref,
    bias_ref,
):
    query = stacked(query_ref, heads)
    scores = own_scores(tiles, slots, heads, tile_total, info_ref, bias_ref, key_ref[...], query)
    row_max = jnp.max(scores, axis=0, keepdims=True)
    terms = jnp.exp2(scores - row_max)
    max_ref[...] = row_max
    total_ref[...] = jnp.sum(terms, axis=0, keepdims=True)
    weighted_ref[...] = dot(value_ref[...].T, terms.astype(jnp.bfloat16))
    grad_t_ref[...] = stacked(grad_ref, heads).T


def gathered_kernel(
    chips,
    tiles,
    slots,
    heads,
    tile_total,
    info_ref,
    table_any,
    query_ref,
    grad_ref,
    key_ref,
    value_ref,
    key_other,
    value_other,
    max_own,
    total_own,
    weighted_own,
    grad_t_ref,
    more_ref,
    *refs,
):
    count = len(pairs_of(chips)) + 1
    arrived, handed, refs = refs[:count], refs[count : 2 * count], refs[2 * count :]
    parts_ref, max_ref, inverse_ref, delta_ref, out_t_ref, dscores_ref, *refs = refs
    slot_keys, *refs = refs
    more_out, attended_full, query_full, key_full, value_full, *refs = refs
    bias_ref, held_ref, sum_ref, score_ref, staged_ref, *refs = refs
    attended_ref, query_out, table_ref, copy_sem = refs
    keys_ref, values_ref = held_ref.at[0], held_ref.at[1]
    key_sum, value_sum = sum_ref.at[0], sum_ref.at[1]
    rank = lax.axis_index("seq")
    odd = rank % 2
    rows = tiles * TILE
    chunk = slots * TILE
    factor = HD**-0.5
    scale = factor * LOG2E
    needed = info_ref[0]
    columns = [pl.ds(h * HD, HD) for h in range(heads)]

    def repack(target, part, first_row):
        kind = odd ^ part
        for slot in range(slots):
            total = sum_ref[kind, tile_rows(first_row, slot), :]
            target[slot] = (total * jnp.where(kind == 0, factor, 1.0)).astype(jnp.bfloat16)

    for slot in range(slots):
        for b in range(tiles):
            allowed = info_ref[2 * tile_total + 2 + slot * tiles + b] == 1
            bias_ref[pl.ds(slot * TILE, TILE), pl.ds(b * TILE, TILE)] = block_bias(allowed)
        position = info_ref[1 + slot]
        away = (position // (2 * tiles)) ^ (rank // 2)
        at = tile_rows(0, slot)

        @pl.when(away == 0)
        def _():
            source = tile_rows(0, position % tiles)
            keys_ref[at, :] = key_other[source, :]
            values_ref[at, :] = value_other[source, :]

        @pl.when(away == chips - 1)
        def _():
            held_ref[odd, at, :] = arrived[-1][slot]
            held_ref[odd ^ 1, at, :] = handed[-1][slot]

        for index, pair in enumerate(pairs_of(chips)):
            for core, step in enumerate(pair):

                @pl.when((away == step) & (odd == core))
                def _():
                    held_ref[odd, at, :] = arrived[index][slot]
                    held_ref[odd ^ 1, at, :] = arrived[index][slots + slot]

                @pl.when((away == step) & (odd != core))
                def _():
                    held_ref[odd ^ 1, at, :] = handed[index][slot]
                    held_ref[odd, at, :] = handed[index][slots + slot]

    first = pl.ds(0, chunk)

    @pl.when(needed <= slots)
    def _():
        keys = keys_ref[first, :]
        values = values_ref[first, :]
        slot_keys[...] = keys
        query = stacked(query_ref, heads)
        grad = stacked(grad_ref, heads)
        bias = jnp.concatenate([bias_ref[first, :]] * heads, axis=1)
        scores = dot_t(keys, query) * scale + bias
        dprobs = dot_t(values, grad)
        row_max = jnp.maximum(max_own[...], jnp.max(scores, axis=0, keepdims=True))
        shrink = jnp.exp2(max_own[...] - row_max)
        terms = jnp.exp2(scores - row_max)
        inverse = 1.0 / (total_own[...] * shrink + jnp.sum(terms, axis=0, keepdims=True))
        weighted = weighted_own[...] * shrink + dot(values.T, terms.astype(jnp.bfloat16))
        out = (weighted * inverse).astype(jnp.bfloat16)
        delta = jnp.sum(
            grad_t_ref[...].astype(jnp.float32) * out.astype(jnp.float32), axis=0, keepdims=True
        )
        probs = terms * inverse
        dscores = (probs * (dprobs - delta)).astype(jnp.bfloat16)
        value_sum[first, :] = dot(probs.astype(jnp.bfloat16), grad)
        key_sum[first, :] = dot(dscores, query)
        out_t_ref[...] = out
        max_ref[...] = row_max
        inverse_ref[...] = inverse
        delta_ref[...] = delta
        dscores_ref[...] = dscores

    @pl.when(needed > slots)
    def _():
        used = (needed + slots - 1) // slots
        own_first = pl.multiple_of(used * chunk, chunk)
        own_rows = pl.ds(own_first, rows)
        copy = pltpu.make_async_copy(table_any, table_ref, copy_sem)
        copy.start()
        copy.wait()

        def ids(position):
            return table_ref[tile_total, position]

        def allowed(a, b):
            return table_ref[ids(rank * tiles + b), ids(rank * tiles + a)]

        own_bias(tiles, bias_ref.at[own_rows, :], allowed)
        keys_ref[own_rows, :] = key_ref[...]
        values_ref[own_rows, :] = value_ref[...]

        def fetch(index, carry):
            copy = pltpu.make_async_copy(more_ref.at[index - 1], staged_ref, copy_sem)
            copy.start()
            copy.wait()
            first_row = pl.multiple_of(index * chunk, chunk)
            for slot in range(slots):
                for part in range(2):
                    held_ref[odd ^ part, tile_rows(first_row, slot), :] = staged_ref[part, slot]
                listed = index * slots + slot
                position = info_ref[1 + listed]
                usable = (listed < needed) & (position // tiles != rank)
                for b in range(tiles):
                    seen = table_ref[ids(rank * tiles + b), ids(position)] == 1
                    bias_ref[tile_rows(first_row, slot), pl.ds(b * TILE, TILE)] = block_bias(
                        usable & seen
                    )
            return carry

        lax.fori_loop(1, used, fetch, 0)
        key_sum[...] = jnp.zeros_like(key_sum)
        value_sum[...] = jnp.zeros_like(value_sum)
        blocks = used * slots + tiles

        for h in range(heads):
            query = query_ref[:, columns[h]]
            grad = grad_ref[:, columns[h]]

            def score(index, row_max):
                at = tile_rows(0, index)
                scores = dot_t(keys_ref[at, :], query) * scale + bias_ref[at, :]
                score_ref[at, :] = scores
                return jnp.maximum(row_max, jnp.max(scores, axis=0, keepdims=True))

            row_max = lax.fori_loop(0, blocks, score, jnp.full((1, rows), FAR_BELOW, jnp.float32))

            def forward(index, carry):
                total, weighted = carry
                at = tile_rows(0, index)
                terms = jnp.exp2(score_ref[at, :] - row_max)
                score_ref[at, :] = terms
                weighted = weighted + dot(values_ref[at, :].T, terms.astype(jnp.bfloat16))
                return total + jnp.sum(terms, axis=0, keepdims=True), weighted

            zeros = jnp.zeros((HD, rows), jnp.float32)
            start = (jnp.zeros((1, rows), jnp.float32), zeros)
            total, weighted = lax.fori_loop(0, blocks, forward, start)
            inverse = 1.0 / total
            out = (weighted * inverse).astype(jnp.bfloat16)
            attended_ref[:, columns[h]] = out.T
            grad_t = grad_t_ref[:, pl.ds(h * rows, rows)].astype(jnp.float32)
            delta = jnp.sum(grad_t * out.astype(jnp.float32), axis=0, keepdims=True)

            def backward(index, query_t):
                at = tile_rows(0, index)
                probs = score_ref[at, :] * inverse
                dprobs = dot_t(values_ref[at, :], grad)
                dscores = (probs * (dprobs - delta)).astype(jnp.bfloat16)
                key_sum[at, :] += dot(dscores, query)
                value_sum[at, :] += dot(probs.astype(jnp.bfloat16), grad)
                return query_t + dot(keys_ref[at, :].T, dscores)

            query_t = lax.fori_loop(0, blocks, backward, zeros)
            query_out[:, columns[h]] = (query_t * factor).T

        key_sum[own_rows, :] = key_sum[own_rows, :] * factor
        for source, target in (
            (attended_ref, attended_full),
            (query_out, query_full),
            (key_sum.at[own_rows, :], key_full),
            (value_sum.at[own_rows, :], value_full),
        ):
            copy = pltpu.make_async_copy(source, target, copy_sem)
            copy.start()
            copy.wait()

        def store(index, carry):
            for part in range(2):
                repack(staged_ref.at[part], part, pl.multiple_of(index * chunk, chunk))
            copy = pltpu.make_async_copy(staged_ref, more_out.at[index - 1], copy_sem)
            copy.start()
            copy.wait()
            return carry

        lax.fori_loop(1, used, store, 0)

    for part in range(2):
        repack(parts_ref.at[pl.ds(part * slots, slots)], part, 0)


def rest_kernel(
    tiles,
    slots,
    heads,
    tile_total,
    info_ref,
    query_ref,
    grad_ref,
    key_ref,
    value_ref,
    max_ref,
    inverse_ref,
    delta_ref,
    out_t_ref,
    dscores_ref,
    slot_keys,
    attended_full,
    query_full,
    key_full,
    value_full,
    order_ref,
    attended_ref,
    query_out,
    key_out,
    value_out,
    order_out,
    bias_ref,
    copy_sem,
):
    del order_ref, order_out
    factor = HD**-0.5
    rows = tiles * TILE

    @pl.when(info_ref[0] <= slots)
    def _():
        keys = key_ref[...]
        query = stacked(query_ref, heads)
        grad = stacked(grad_ref, heads)
        scores = own_scores(tiles, slots, heads, tile_total, info_ref, bias_ref, keys, query)
        probs = jnp.exp2(scores - max_ref[...]) * inverse_ref[...]
        dprobs = dot_t(value_ref[...], grad)
        dscores = (probs * (dprobs - delta_ref[...])).astype(jnp.bfloat16)
        value_out[...] = dot(probs.astype(jnp.bfloat16), grad)
        key_out[...] = dot(dscores, query) * factor
        query_t = (dot(keys.T, dscores) + dot(slot_keys[...].T, dscores_ref[...])) * factor
        for h in range(heads):
            columns = pl.ds(h * HD, HD)
            attended_ref[:, columns] = out_t_ref[:, pl.ds(h * rows, rows)].T
            query_out[:, columns] = query_t[:, h * rows : (h + 1) * rows].T

    @pl.when(info_ref[0] > slots)
    def _():
        for source, target in (
            (attended_full, attended_ref),
            (query_full, query_out),
            (key_full, key_out),
            (value_full, value_out),
        ):
            copy = pltpu.make_async_copy(source, target, copy_sem)
            copy.start()
            copy.wait()


def per_device(queries, key_rows, value_rows, out_grad, tile_ids, tile_mask):
    row_count = queries.shape[0]
    heads = queries.shape[1] // HD
    ranks = lax.axis_size("seq")
    chips = ranks // 2
    assert key_rows.shape[1] == HD and ranks > 1 and ranks & (ranks - 1) == 0
    tiles = row_count // TILE
    tile_total = tile_ids.shape[0]
    slots = tiles
    rounds = math.ceil(tile_total / slots)
    slot_shape = (slots, TILE, HD)
    buffer = (rounds - 1, 2) + slot_shape
    shape = jax.ShapeDtypeStruct
    bf16, f32 = jnp.bfloat16, jnp.float32

    def swap(values, step):
        return lax.ppermute(values, "seq", [(source, source ^ step) for source in range(ranks)])

    def across(values):
        return [swap(values, 2 * step) for step in range(1, chips)]

    def trade(full, half):
        got = []
        for pair in pairs_of(chips):
            routes = [(source, source ^ 2 * pair[source % 2]) for source in range(ranks)]
            got.append(lax.ppermute(full, "seq", routes))
        return got + [swap(half, 2 * (chips - 1))]

    def add(*values):
        total = values[0].astype(f32)
        for value in values[1:]:
            total = total + value.astype(f32)
        return total.astype(bf16)

    table = jnp.pad(tile_mask, ((0, 1), (0, 0)))
    table = table + jnp.pad(tile_ids[None], ((tile_total, 0), (0, 0)))
    key_other, value_other = swap(key_rows, 1), swap(value_rows, 1)
    chip_rows = (key_rows, value_rows, key_other, value_other)
    info, chosen, chosen_half, spare = call(
        functools.partial(list_kernel, tile_total, tiles, slots),
        [SMEM_SPEC] + [ANY_SPEC] * 4,
        (
            shape((info_size(tile_total, tiles, slots),), jnp.int32),
            shape((2 * slots, TILE, HD), bf16),
            shape(slot_shape, bf16),
            shape(buffer, bf16),
        ),
        (SMEM_SPEC, VMEM_SPEC, VMEM_SPEC, ANY_SPEC),
        scratch=(
            pltpu.SMEM((tile_total,), jnp.int32),
            *[pltpu.VMEM(key_rows.shape, bf16)] * 4,
            *[pltpu.SemaphoreType.DMA] * 4,
        ),
        moved=4 * 1024 * 1024,
    )(table, *chip_rows)
    used = (info[0] + slots - 1) // slots

    def select(index):
        return call(
            functools.partial(select_kernel, tiles, slots),
            [SMEM_SPEC] * 2 + [VMEM_SPEC] * 4,
            shape(slot_shape, bf16),
            VMEM_SPEC,
            moved=5 * row_count * HD * 2,
        )(info, index.reshape(1), *chip_rows)

    arrived = trade(chosen, chosen_half)
    handed = [swap(values, 1) for values in arrived]

    def gather_more(index, buffered):
        chosen = select(index)
        total = add(chosen, *across(chosen))
        pair = jnp.stack([total, swap(total, 1)])
        return lax.dynamic_update_index_in_dim(buffered, pair, index - 1, 0)

    more = lax.fori_loop(1, used, gather_more, spare)

    all_rows = row_count + rounds * slots * TILE
    columns = heads * row_count
    line = shape((1, columns), f32)
    work = 2 * columns * row_count * HD
    max_own, total_own, weighted, grad_t = call(
        functools.partial(own_kernel, tiles, slots, heads, tile_total),
        [SMEM_SPEC] + [VMEM_SPEC] * 4,
        (line, line, shape((HD, columns), f32), shape((HD, columns), bf16)),
        (VMEM_SPEC,) * 4,
        scratch=(pltpu.VMEM((row_count, row_count), f32),),
        flops=24 * work,
        moved=4 * row_count * heads * HD,
    )(info, queries, out_grad, key_rows, value_rows)

    full = (
        shape(queries.shape, bf16),
        shape(queries.shape, f32),
        shape(key_rows.shape, f32),
        shape(value_rows.shape, f32),
    )
    parts, row_max, inverse, delta, out_t, dscores, slot_keys, more_terms, *full_values = call(
        functools.partial(gathered_kernel, chips, tiles, slots, heads, tile_total),
        [SMEM_SPEC, ANY_SPEC] + [VMEM_SPEC] * 10 + [ANY_SPEC] + [VMEM_SPEC] * (2 * len(arrived)),
        (
            shape((2 * slots, TILE, HD), bf16),
            line,
            line,
            line,
            shape((HD, columns), bf16),
            shape((slots * TILE, columns), bf16),
            shape((slots * TILE, HD), bf16),
            shape(buffer, bf16),
        )
        + full,
        (VMEM_SPEC,) * 7 + (ANY_SPEC,) * 5,
        scratch=(
            pltpu.VMEM((all_rows, row_count), f32),
            pltpu.VMEM((2, all_rows, HD), bf16),
            pltpu.VMEM((2, all_rows, HD), f32),
            pltpu.VMEM((all_rows, row_count), f32),
            pltpu.VMEM((2,) + slot_shape, bf16),
            pltpu.VMEM(queries.shape, bf16),
            pltpu.VMEM(queries.shape, f32),
            pltpu.SMEM(table.shape, jnp.int32),
            pltpu.SemaphoreType.DMA,
        ),
        flops=24 * work,
        moved=4 * row_count * heads * HD,
    )(
        info,
        table,
        queries,
        out_grad,
        *chip_rows,
        max_own,
        total_own,
        weighted,
        grad_t,
        more,
        *arrived,
        *handed,
    )

    partner = swap(parts, 1)
    half_sum = add(parts[:slots], partner[slots:])
    chip_sum = jnp.concatenate([half_sum, add(parts[slots:], partner[:slots])])
    attended, query_grad, key_own, value_own, half_sum = call(
        functools.partial(rest_kernel, tiles, slots, heads, tile_total),
        [SMEM_SPEC] + [VMEM_SPEC] * 10 + [ANY_SPEC] * 5,
        full + (shape(slot_shape, bf16),),
        (VMEM_SPEC,) * 4 + (ANY_SPEC,),
        scratch=(pltpu.VMEM((row_count, row_count), f32), pltpu.SemaphoreType.DMA),
        flops=32 * work,
        moved=8 * row_count * heads * HD,
        aliases={15: 4},
    )(
        info,
        queries,
        out_grad,
        key_rows,
        value_rows,
        row_max,
        inverse,
        delta,
        out_t,
        dscores,
        slot_keys,
        *full_values,
        half_sum,
    )
    back = trade(chip_sum, half_sum)
    sums = [chip_sum] + back + [swap(values, 1) for values in back]

    def close(kernel, lead, grads, sums):
        return call(
            kernel,
            [SMEM_SPEC] * len(lead) + [VMEM_SPEC] * (2 + len(sums)),
            (shape(key_rows.shape, f32), shape(value_rows.shape, f32)),
            (VMEM_SPEC,) * 2,
            moved=5 * row_count * HD * 4,
        )(*lead, *grads, *sums)

    def reduce_more(index, grads):
        terms = lax.dynamic_index_in_dim(more_terms, index - 1, 0, keepdims=False)
        part = add(terms[0], swap(terms[1], 1))
        total = add(part, *across(part))
        kernel = functools.partial(later_kernel, tiles, slots, tile_total)
        return tuple(close(kernel, (info, index.reshape(1)), grads, (total, swap(total, 1))))

    kernel = functools.partial(close_kernel, tiles, slots, chips, tile_total)
    grads = tuple(close(kernel, (info,), (key_own, value_own), sums))
    key_grad, value_grad = lax.fori_loop(1, used, reduce_more, grads)
    return attended, query_grad, key_grad, value_grad


def solution(mesh):
    return jax.shard_map(
        per_device,
        mesh=mesh,
        in_specs=(
            P(("batch", "seq"), "head"),
            P(("batch", "seq"), "head"),
            P(("batch", "seq"), "head"),
            P(("batch", "seq"), "head"),
            P("batch"),
            P("batch", None),
        ),
        out_specs=(P(("batch", "seq"), "head"),) * 4,
        check_vma=False,
    )
```

```python
import functools
import math

import jax
import jax.numpy as jnp
from jax import lax
from jax.experimental import pallas as pl
from jax.experimental.pallas import tpu as pltpu
from jax.sharding import PartitionSpec as P

HD = 128
TILE = 128
FAR_BELOW = -1e30
LOG2E = 1.4426950408889634
NT_DIMS = (((1,), (1,)), ((), ()))
VMEM_LIMIT = 32 * 1024 * 1024

SMEM_SPEC = pl.BlockSpec(memory_space=pltpu.SMEM)
VMEM_SPEC = pl.BlockSpec(memory_space=pltpu.VMEM)
ANY_SPEC = pl.BlockSpec(memory_space=pl.ANY)


def call(kernel, in_specs, out_shape, out_specs, scratch=(), flops=0, moved=0, aliases=None):
    return pl.pallas_call(
        kernel,
        in_specs=in_specs,
        out_shape=out_shape,
        out_specs=out_specs,
        scratch_shapes=list(scratch),
        input_output_aliases=aliases or {},
        compiler_params=pltpu.CompilerParams(vmem_limit_bytes=VMEM_LIMIT),
        cost_estimate=pl.CostEstimate(flops=flops, bytes_accessed=moved, transcendentals=0),
    )


def tile_rows(first_row, tile):
    return pl.ds(pl.multiple_of(first_row + tile * TILE, TILE), TILE)


def info_size(tile_total, tiles, slots):
    return 2 * tile_total + 2 + (slots + tiles) * tiles


def pairs_of(chips):
    return [(step, step + 1) for step in range(1, chips - 1, 2)]


def list_kernel(tile_total, tiles, slots, table_ref, *refs):
    sources, (info_ref, full_ref, half_ref, spare_ref, *refs) = refs[:4], refs[4:]
    any_ref, loaded, sems = refs[0], refs[1:5], refs[5:]
    del spare_ref
    rank = lax.axis_index("seq")
    copies = [
        pltpu.make_async_copy(source, target, sem)
        for source, target, sem in zip(sources, loaded, sems)
    ]
    for copy in copies:
        copy.start()

    def ids(position):
        return table_ref[tile_total, position]

    def mask(query_tile, key_tile):
        return table_ref[query_tile, key_tile]

    for place in range(1, tile_total + 2):
        info_ref[place] = 0
    for tile in range(tile_total):
        users = mask(0, tile)
        for other in range(1, tile_total):
            users = users + mask(other, tile)
        any_ref[tile] = users
    count = jnp.int32(0)
    for position in range(tile_total):
        key_tile = ids(position)
        away = any_ref[key_tile]
        for local in range(tiles):
            away = away - mask(ids(position // tiles * tiles + local), key_tile)
        info_ref[1 + count] = position
        info_ref[tile_total + 2 + position] = jnp.where(away > 0, count, -1)
        count = count + jnp.where(away > 0, 1, 0)
    info_ref[0] = count
    my_tiles = [ids(rank * tiles + b) for b in range(tiles)]
    place = 2 * tile_total + 2
    for slot in range(slots):
        position = info_ref[1 + slot]
        usable = ((slot < count) & (position // tiles != rank)).astype(jnp.int32)
        for b in range(tiles):
            info_ref[place] = usable * mask(my_tiles[b], ids(position))
            place += 1
    for a in range(tiles):
        for b in range(tiles):
            info_ref[place] = mask(my_tiles[b], my_tiles[a])
            place += 1
    for copy in copies:
        copy.wait()
    odd = rank % 2
    for kind in range(2):
        part = odd ^ kind
        target = full_ref.at[pl.ds(part * slots, slots)]
        pick(tiles, slots, 0, info_ref, loaded[kind], loaded[2 + kind], target)
    half_ref[...] = full_ref[:slots]


def pick(tiles, slots, base, info_ref, own_ref, other_ref, out_ref):
    rank = lax.axis_index("seq")
    for slot in range(slots):
        position = info_ref[1 + base + slot]
        home = position // tiles
        rows = tile_rows(0, position % tiles)
        out_ref[slot] = jnp.zeros_like(out_ref[slot])

        @pl.when(home == rank)
        def _():
            out_ref[slot] = own_ref[rows, :]

        @pl.when(home == rank ^ 1)
        def _():
            out_ref[slot] = other_ref[rows, :]


def select_kernel(tiles, slots, info_ref, round_ref, *refs):
    key_ref, value_ref, key_other, value_other, out_ref = refs
    rank = lax.axis_index("seq")
    for kind, own, other in ((0, key_ref, key_other), (1, value_ref, value_other)):

        @pl.when(rank % 2 == kind)
        def _():
            pick(tiles, slots, round_ref[0] * slots, info_ref, own, other, out_ref)


def add_sums(tiles, slots, tile_total, base, info_ref, grads, outs, sums_of):
    rank = lax.axis_index("seq")
    odd = rank % 2
    for grad, out in zip(grads, outs):
        out[...] = grad[...]
    for tile in range(tiles):
        slot = info_ref[tile_total + 2 + rank * tiles + tile] - base
        rows = tile_rows(0, tile)

        @pl.when((slot >= 0) & (slot < slots))
        def _():
            totals = []
            for part in range(2):
                total = None
                for source in sums_of(part, slot):
                    source = source.astype(jnp.float32)
                    total = source if total is None else total + source
                totals.append(total)
            for kind, out in enumerate(outs):
                out[rows, :] += jnp.where(odd == kind, totals[0], totals[1])


def close_kernel(tiles, slots, chips, tile_total, info_ref, *refs):
    grads, (chip_ref, *sums), outs = refs[:2], refs[2:-2], refs[-2:]
    half = len(sums) // 2
    arrived, handed = sums[:half], sums[half:]

    def sums_of(part, slot):
        yield chip_ref[part * slots + slot]
        for own, other in zip(arrived[:-1], handed[:-1]):
            yield own[part * slots + slot]
            yield other[(1 - part) * slots + slot]
        yield (handed if part else arrived)[-1][slot]

    add_sums(tiles, slots, tile_total, 0, info_ref, grads, outs, sums_of)


def later_kernel(tiles, slots, tile_total, info_ref, round_ref, *refs):
    grads, sums, outs = refs[:2], refs[2:-2], refs[-2:]

    def sums_of(part, slot):
        yield sums[part][slot]

    base = round_ref[0] * slots
    add_sums(tiles, slots, tile_total, base, info_ref, grads, outs, sums_of)


def causal_bias():
    later = lax.broadcasted_iota(jnp.int32, (TILE, TILE), 1)
    return jnp.where(lax.broadcasted_iota(jnp.int32, (TILE, TILE), 0) <= later, 0.0, FAR_BELOW)


def block_bias(allowed):
    return jnp.full((TILE, TILE), jnp.where(allowed, 0.0, FAR_BELOW), jnp.float32)


def own_bias(tiles, bias_ref, allowed):
    for a in range(tiles):
        for b in range(tiles):
            bias = causal_bias() if a == b else block_bias(allowed(a, b) == 1)
            bias_ref[pl.ds(a * TILE, TILE), pl.ds(b * TILE, TILE)] = bias


def stacked(ref, heads):
    return jnp.concatenate([ref[:, h * HD : (h + 1) * HD] for h in range(heads)], axis=0)


def dot(one, other):
    return jnp.dot(one, other, preferred_element_type=jnp.float32)


def dot_t(one, other):
    return lax.dot_general(one, other, NT_DIMS, preferred_element_type=jnp.float32)


def own_scores(tiles, slots, heads, tile_total, info_ref, bias_ref, keys, query):
    place = 2 * tile_total + 2 + slots * tiles
    own_bias(tiles, bias_ref, lambda a, b: info_ref[place + a * tiles + b])
    bias = jnp.concatenate([bias_ref[...]] * heads, axis=1)
    return dot_t(keys, query) * (HD**-0.5 * LOG2E) + bias


def own_kernel(
    tiles,
    slots,
    heads,
    tile_total,
    info_ref,
    query_ref,
    grad_ref,
    key_ref,
    value_ref,
    max_ref,
    total_ref,
    weighted_ref,
    grad_t_ref,
    bias_ref,
):
    query = stacked(query_ref, heads)
    scores = own_scores(tiles, slots, heads, tile_total, info_ref, bias_ref, key_ref[...], query)
    row_max = jnp.max(scores, axis=0, keepdims=True)
    terms = jnp.exp2(scores - row_max)
    max_ref[...] = row_max
    total_ref[...] = jnp.sum(terms, axis=0, keepdims=True)
    weighted_ref[...] = dot(value_ref[...].T, terms.astype(jnp.bfloat16))
    grad_t_ref[...] = stacked(grad_ref, heads).T


def gathered_kernel(
    chips,
    tiles,
    slots,
    heads,
    tile_total,
    info_ref,
    table_any,
    query_ref,
    grad_ref,
    key_ref,
    value_ref,
    key_other,
    value_other,
    max_own,
    total_own,
    weighted_own,
    grad_t_ref,
    more_ref,
    *refs,
):
    count = len(pairs_of(chips)) + 1
    arrived, handed, refs = refs[:count], refs[count : 2 * count], refs[2 * count :]
    parts_ref, max_ref, inverse_ref, delta_ref, out_t_ref, dscores_ref, *refs = refs
    slot_keys, *refs = refs
    more_out, attended_full, query_full, key_full, value_full, *refs = refs
    bias_ref, held_ref, sum_ref, score_ref, staged_ref, *refs = refs
    attended_ref, query_out, table_ref, copy_sem = refs
    keys_ref, values_ref = held_ref.at[0], held_ref.at[1]
    key_sum, value_sum = sum_ref.at[0], sum_ref.at[1]
    rank = lax.axis_index("seq")
    odd = rank % 2
    rows = tiles * TILE
    chunk = slots * TILE
    factor = HD**-0.5
    scale = factor * LOG2E
    needed = info_ref[0]
    columns = [pl.ds(h * HD, HD) for h in range(heads)]

    def repack(target, part, first_row):
        kind = odd ^ part
        for slot in range(slots):
            total = sum_ref[kind, tile_rows(first_row, slot), :]
            target[slot] = (total * jnp.where(kind == 0, factor, 1.0)).astype(jnp.bfloat16)

    for slot in range(slots):
        for b in range(tiles):
            allowed = info_ref[2 * tile_total + 2 + slot * tiles + b] == 1
            bias_ref[pl.ds(slot * TILE, TILE), pl.ds(b * TILE, TILE)] = block_bias(allowed)
        position = info_ref[1 + slot]
        away = (position // (2 * tiles)) ^ (rank // 2)
        at = tile_rows(0, slot)

        @pl.when(away == 0)
        def _():
            source = tile_rows(0, position % tiles)
            keys_ref[at, :] = key_other[source, :]
            values_ref[at, :] = value_other[source, :]

        @pl.when(away == chips - 1)
        def _():
            held_ref[odd, at, :] = arrived[-1][slot]
            held_ref[odd ^ 1, at, :] = handed[-1][slot]

        for index, pair in enumerate(pairs_of(chips)):
            for core, step in enumerate(pair):

                @pl.when((away == step) & (odd == core))
                def _():
                    held_ref[odd, at, :] = arrived[index][slot]
                    held_ref[odd ^ 1, at, :] = arrived[index][slots + slot]

                @pl.when((away == step) & (odd != core))
                def _():
                    held_ref[odd ^ 1, at, :] = handed[index][slot]
                    held_ref[odd, at, :] = handed[index][slots + slot]

    first = pl.ds(0, chunk)

    @pl.when(needed <= slots)
    def _():
        keys = keys_ref[first, :]
        values = values_ref[first, :]
        slot_keys[...] = keys
        query = stacked(query_ref, heads)
        grad = stacked(grad_ref, heads)
        bias = jnp.concatenate([bias_ref[first, :]] * heads, axis=1)
        scores = dot_t(keys, query) * scale + bias
        dprobs = dot_t(values, grad)
        row_max = jnp.maximum(max_own[...], jnp.max(scores, axis=0, keepdims=True))
        shrink = jnp.exp2(max_own[...] - row_max)
        terms = jnp.exp2(scores - row_max)
        inverse = 1.0 / (total_own[...] * shrink + jnp.sum(terms, axis=0, keepdims=True))
        weighted = weighted_own[...] * shrink + dot(values.T, terms.astype(jnp.bfloat16))
        out = (weighted * inverse).astype(jnp.bfloat16)
        delta = jnp.sum(
            grad_t_ref[...].astype(jnp.float32) * out.astype(jnp.float32), axis=0, keepdims=True
        )
        probs = terms * inverse
        dscores = (probs * (dprobs - delta)).astype(jnp.bfloat16)
        value_sum[first, :] = dot(probs.astype(jnp.bfloat16), grad)
        key_sum[first, :] = dot(dscores, query)
        out_t_ref[...] = out
        max_ref[...] = row_max
        inverse_ref[...] = inverse
        delta_ref[...] = delta
        dscores_ref[...] = dscores

    @pl.when(needed > slots)
    def _():
        used = (needed + slots - 1) // slots
        own_first = pl.multiple_of(used * chunk, chunk)
        own_rows = pl.ds(own_first, rows)
        copy = pltpu.make_async_copy(table_any, table_ref, copy_sem)
        copy.start()
        copy.wait()

        def ids(position):
            return table_ref[tile_total, position]

        def allowed(a, b):
            return table_ref[ids(rank * tiles + b), ids(rank * tiles + a)]

        own_bias(tiles, bias_ref.at[own_rows, :], allowed)
        keys_ref[own_rows, :] = key_ref[...]
        values_ref[own_rows, :] = value_ref[...]

        def fetch(index, carry):
            copy = pltpu.make_async_copy(more_ref.at[index - 1], staged_ref, copy_sem)
            copy.start()
            copy.wait()
            first_row = pl.multiple_of(index * chunk, chunk)
            for slot in range(slots):
                for part in range(2):
                    held_ref[odd ^ part, tile_rows(first_row, slot), :] = staged_ref[part, slot]
                listed = index * slots + slot
                position = info_ref[1 + listed]
                usable = (listed < needed) & (position // tiles != rank)
                for b in range(tiles):
                    seen = table_ref[ids(rank * tiles + b), ids(position)] == 1
                    bias_ref[tile_rows(first_row, slot), pl.ds(b * TILE, TILE)] = block_bias(
                        usable & seen
                    )
            return carry

        lax.fori_loop(1, used, fetch, 0)
        key_sum[...] = jnp.zeros_like(key_sum)
        value_sum[...] = jnp.zeros_like(value_sum)
        blocks = used * slots + tiles

        for h in range(heads):
            query = query_ref[:, columns[h]]
            grad = grad_ref[:, columns[h]]

            def score(index, row_max):
                at = tile_rows(0, index)
                scores = dot_t(keys_ref[at, :], query) * scale + bias_ref[at, :]
                score_ref[at, :] = scores
                return jnp.maximum(row_max, jnp.max(scores, axis=0, keepdims=True))

            row_max = lax.fori_loop(0, blocks, score, jnp.full((1, rows), FAR_BELOW, jnp.float32))

            def forward(index, carry):
                total, weighted = carry
                at = tile_rows(0, index)
                terms = jnp.exp2(score_ref[at, :] - row_max)
                score_ref[at, :] = terms
                weighted = weighted + dot(values_ref[at, :].T, terms.astype(jnp.bfloat16))
                return total + jnp.sum(terms, axis=0, keepdims=True), weighted

            zeros = jnp.zeros((HD, rows), jnp.float32)
            start = (jnp.zeros((1, rows), jnp.float32), zeros)
            total, weighted = lax.fori_loop(0, blocks, forward, start)
            inverse = 1.0 / total
            out = (weighted * inverse).astype(jnp.bfloat16)
            attended_ref[:, columns[h]] = out.T
            grad_t = grad_t_ref[:, pl.ds(h * rows, rows)].astype(jnp.float32)
            delta = jnp.sum(grad_t * out.astype(jnp.float32), axis=0, keepdims=True)

            def backward(index, query_t):
                at = tile_rows(0, index)
                probs = score_ref[at, :] * inverse
                dprobs = dot_t(values_ref[at, :], grad)
                dscores = (probs * (dprobs - delta)).astype(jnp.bfloat16)
                key_sum[at, :] += dot(dscores, query)
                value_sum[at, :] += dot(probs.astype(jnp.bfloat16), grad)
                return query_t + dot(keys_ref[at, :].T, dscores)

            query_t = lax.fori_loop(0, blocks, backward, zeros)
            query_out[:, columns[h]] = (query_t * factor).T

        key_sum[own_rows, :] = key_sum[own_rows, :] * factor
        for source, target in (
            (attended_ref, attended_full),
            (query_out, query_full),
            (key_sum.at[own_rows, :], key_full),
            (value_sum.at[own_rows, :], value_full),
        ):
            copy = pltpu.make_async_copy(source, target, copy_sem)
            copy.start()
            copy.wait()

        def store(index, carry):
            for part in range(2):
                repack(staged_ref.at[part], part, pl.multiple_of(index * chunk, chunk))
            copy = pltpu.make_async_copy(staged_ref, more_out.at[index - 1], copy_sem)
            copy.start()
            copy.wait()
            return carry

        lax.fori_loop(1, used, store, 0)

    for part in range(2):
        repack(parts_ref.at[pl.ds(part * slots, slots)], part, 0)


def fetch_full(copy_sem, *pairs):
    for source, target in pairs:
        copy = pltpu.make_async_copy(source, target, copy_sem)
        copy.start()
        copy.wait()


def own_grads_kernel(
    tiles,
    slots,
    heads,
    tile_total,
    info_ref,
    query_ref,
    grad_ref,
    key_ref,
    value_ref,
    max_ref,
    inverse_ref,
    delta_ref,
    key_full,
    value_full,
    order_ref,
    dscores_ref,
    key_out,
    value_out,
    order_out,
    bias_ref,
    copy_sem,
):
    del order_ref, order_out

    @pl.when(info_ref[0] <= slots)
    def _():
        query = stacked(query_ref, heads)
        grad = stacked(grad_ref, heads)
        scores = own_scores(
            tiles, slots, heads, tile_total, info_ref, bias_ref, key_ref[...], query
        )
        probs = jnp.exp2(scores - max_ref[...]) * inverse_ref[...]
        dprobs = dot_t(value_ref[...], grad)
        dscores = (probs * (dprobs - delta_ref[...])).astype(jnp.bfloat16)
        dscores_ref[...] = dscores
        value_out[...] = dot(probs.astype(jnp.bfloat16), grad)
        key_out[...] = dot(dscores, query) * HD**-0.5

    @pl.when(info_ref[0] > slots)
    def _():
        fetch_full(copy_sem, (key_full, key_out), (value_full, value_out))


def queries_kernel(
    slots,
    heads,
    info_ref,
    key_ref,
    own_dscores,
    slot_dscores,
    slot_keys,
    out_t_ref,
    attended_full,
    query_full,
    order_ref,
    attended_ref,
    query_out,
    copy_sem,
):
    del order_ref
    rows = query_out.shape[0]

    @pl.when(info_ref[0] <= slots)
    def _():
        query_t = dot(key_ref[...].T, own_dscores[...])
        query_t = (query_t + dot(slot_keys[...].T, slot_dscores[...])) * HD**-0.5
        for h in range(heads):
            columns = pl.ds(h * HD, HD)
            attended_ref[:, columns] = out_t_ref[:, pl.ds(h * rows, rows)].T
            query_out[:, columns] = query_t[:, h * rows : (h + 1) * rows].T

    @pl.when(info_ref[0] > slots)
    def _():
        fetch_full(copy_sem, (attended_full, attended_ref), (query_full, query_out))


def per_device(queries, key_rows, value_rows, out_grad, tile_ids, tile_mask):
    row_count = queries.shape[0]
    heads = queries.shape[1] // HD
    ranks = lax.axis_size("seq")
    chips = ranks // 2
    assert key_rows.shape[1] == HD and ranks > 1 and ranks & (ranks - 1) == 0
    tiles = row_count // TILE
    tile_total = tile_ids.shape[0]
    slots = tiles
    rounds = math.ceil(tile_total / slots)
    slot_shape = (slots, TILE, HD)
    buffer = (rounds - 1, 2) + slot_shape
    shape = jax.ShapeDtypeStruct
    bf16, f32 = jnp.bfloat16, jnp.float32

    def swap(values, step):
        return lax.ppermute(values, "seq", [(source, source ^ step) for source in range(ranks)])

    def across(values):
        return [swap(values, 2 * step) for step in range(1, chips)]

    def trade(full, half):
        got = []
        for pair in pairs_of(chips):
            routes = [(source, source ^ 2 * pair[source % 2]) for source in range(ranks)]
            got.append(lax.ppermute(full, "seq", routes))
        return got + [swap(half, 2 * (chips - 1))]

    def add(*values):
        total = values[0].astype(f32)
        for value in values[1:]:
            total = total + value.astype(f32)
        return total.astype(bf16)

    table = jnp.pad(tile_mask, ((0, 1), (0, 0)))
    table = table + jnp.pad(tile_ids[None], ((tile_total, 0), (0, 0)))
    key_other, value_other = swap(key_rows, 1), swap(value_rows, 1)
    chip_rows = (key_rows, value_rows, key_other, value_other)
    info, chosen, chosen_half, spare = call(
        functools.partial(list_kernel, tile_total, tiles, slots),
        [SMEM_SPEC] + [ANY_SPEC] * 4,
        (
            shape((info_size(tile_total, tiles, slots),), jnp.int32),
            shape((2 * slots, TILE, HD), bf16),
            shape(slot_shape, bf16),
            shape(buffer, bf16),
        ),
        (SMEM_SPEC, VMEM_SPEC, VMEM_SPEC, ANY_SPEC),
        scratch=(
            pltpu.SMEM((tile_total,), jnp.int32),
            *[pltpu.VMEM(key_rows.shape, bf16)] * 4,
            *[pltpu.SemaphoreType.DMA] * 4,
        ),
        moved=4 * 1024 * 1024,
    )(table, *chip_rows)
    used = (info[0] + slots - 1) // slots

    def select(index):
        return call(
            functools.partial(select_kernel, tiles, slots),
            [SMEM_SPEC] * 2 + [VMEM_SPEC] * 4,
            shape(slot_shape, bf16),
            VMEM_SPEC,
            moved=5 * row_count * HD * 2,
        )(info, index.reshape(1), *chip_rows)

    arrived = trade(chosen, chosen_half)
    handed = [swap(values, 1) for values in arrived]

    def gather_more(index, buffered):
        chosen = select(index)
        total = add(chosen, *across(chosen))
        pair = jnp.stack([total, swap(total, 1)])
        return lax.dynamic_update_index_in_dim(buffered, pair, index - 1, 0)

    more = lax.fori_loop(1, used, gather_more, spare)

    all_rows = row_count + rounds * slots * TILE
    columns = heads * row_count
    line = shape((1, columns), f32)
    work = 2 * columns * row_count * HD
    max_own, total_own, weighted, grad_t = call(
        functools.partial(own_kernel, tiles, slots, heads, tile_total),
        [SMEM_SPEC] + [VMEM_SPEC] * 4,
        (line, line, shape((HD, columns), f32), shape((HD, columns), bf16)),
        (VMEM_SPEC,) * 4,
        scratch=(pltpu.VMEM((row_count, row_count), f32),),
        flops=24 * work,
        moved=4 * row_count * heads * HD,
    )(info, queries, out_grad, key_rows, value_rows)

    full = (
        shape(queries.shape, bf16),
        shape(queries.shape, f32),
        shape(key_rows.shape, f32),
        shape(value_rows.shape, f32),
    )
    parts, row_max, inverse, delta, out_t, dscores, slot_keys, more_terms, *full_values = call(
        functools.partial(gathered_kernel, chips, tiles, slots, heads, tile_total),
        [SMEM_SPEC, ANY_SPEC] + [VMEM_SPEC] * 10 + [ANY_SPEC] + [VMEM_SPEC] * (2 * len(arrived)),
        (
            shape((2 * slots, TILE, HD), bf16),
            line,
            line,
            line,
            shape((HD, columns), bf16),
            shape((slots * TILE, columns), bf16),
            shape((slots * TILE, HD), bf16),
            shape(buffer, bf16),
        )
        + full,
        (VMEM_SPEC,) * 7 + (ANY_SPEC,) * 5,
        scratch=(
            pltpu.VMEM((all_rows, row_count), f32),
            pltpu.VMEM((2, all_rows, HD), bf16),
            pltpu.VMEM((2, all_rows, HD), f32),
            pltpu.VMEM((all_rows, row_count), f32),
            pltpu.VMEM((2,) + slot_shape, bf16),
            pltpu.VMEM(queries.shape, bf16),
            pltpu.VMEM(queries.shape, f32),
            pltpu.SMEM(table.shape, jnp.int32),
            pltpu.SemaphoreType.DMA,
        ),
        flops=24 * work,
        moved=4 * row_count * heads * HD,
    )(
        info,
        table,
        queries,
        out_grad,
        *chip_rows,
        max_own,
        total_own,
        weighted,
        grad_t,
        more,
        *arrived,
        *handed,
    )

    partner = swap(parts, 1)
    half_sum = add(parts[:slots], partner[slots:])
    chip_sum = jnp.concatenate([half_sum, add(parts[slots:], partner[:slots])])
    own_dscores, key_own, value_own, half_sum = call(
        functools.partial(own_grads_kernel, tiles, slots, heads, tile_total),
        [SMEM_SPEC] + [VMEM_SPEC] * 7 + [ANY_SPEC] * 3,
        (shape((row_count, columns), bf16), *full[2:], shape(slot_shape, bf16)),
        (VMEM_SPEC,) * 3 + (ANY_SPEC,),
        scratch=(pltpu.VMEM((row_count, row_count), f32), pltpu.SemaphoreType.DMA),
        flops=18 * work,
        moved=4 * row_count * heads * HD,
        aliases={10: 3},
    )(
        info,
        queries,
        out_grad,
        key_rows,
        value_rows,
        row_max,
        inverse,
        delta,
        *full_values[2:],
        half_sum,
    )
    back = trade(chip_sum, half_sum)
    attended, query_grad = call(
        functools.partial(queries_kernel, slots, heads),
        [SMEM_SPEC] + [VMEM_SPEC] * 5 + [ANY_SPEC] * 3,
        full[:2],
        (VMEM_SPEC,) * 2,
        scratch=(pltpu.SemaphoreType.DMA,),
        flops=16 * work,
        moved=8 * row_count * heads * HD,
    )(info, key_rows, own_dscores, dscores, slot_keys, out_t, *full_values[:2], back[0])
    sums = [chip_sum] + back + [swap(values, 1) for values in back]

    def close(kernel, lead, grads, sums):
        return call(
            kernel,
            [SMEM_SPEC] * len(lead) + [VMEM_SPEC] * (2 + len(sums)),
            (shape(key_rows.shape, f32), shape(value_rows.shape, f32)),
            (VMEM_SPEC,) * 2,
            moved=5 * row_count * HD * 4,
        )(*lead, *grads, *sums)

    def reduce_more(index, grads):
        terms = lax.dynamic_index_in_dim(more_terms, index - 1, 0, keepdims=False)
        part = add(terms[0], swap(terms[1], 1))
        total = add(part, *across(part))
        kernel = functools.partial(later_kernel, tiles, slots, tile_total)
        return tuple(close(kernel, (info, index.reshape(1)), grads, (total, swap(total, 1))))

    kernel = functools.partial(close_kernel, tiles, slots, chips, tile_total)
    grads = tuple(close(kernel, (info,), (key_own, value_own), sums))
    key_grad, value_grad = lax.fori_loop(1, used, reduce_more, grads)
    return attended, query_grad, key_grad, value_grad


def solution(mesh):
    return jax.shard_map(
        per_device,
        mesh=mesh,
        in_specs=(
            P(("batch", "seq"), "head"),
            P(("batch", "seq"), "head"),
            P(("batch", "seq"), "head"),
            P(("batch", "seq"), "head"),
            P("batch"),
            P("batch", None),
        ),
        out_specs=(P(("batch", "seq"), "head"),) * 4,
        check_vma=False,
    )
```

```python
import functools
import math

import jax
import jax.numpy as jnp
from jax import lax
from jax.experimental import pallas as pl
from jax.experimental.pallas import tpu as pltpu
from jax.sharding import PartitionSpec as P

HD = 128
TILE = 128
FAR_BELOW = -1e30
LOG2E = 1.4426950408889634
NT_DIMS = (((1,), (1,)), ((), ()))
VMEM_LIMIT = 32 * 1024 * 1024

SMEM_SPEC = pl.BlockSpec(memory_space=pltpu.SMEM)
VMEM_SPEC = pl.BlockSpec(memory_space=pltpu.VMEM)
ANY_SPEC = pl.BlockSpec(memory_space=pl.ANY)


def call(kernel, in_specs, out_shape, out_specs, scratch=(), flops=0, moved=0, aliases=None):
    return pl.pallas_call(
        kernel,
        in_specs=in_specs,
        out_shape=out_shape,
        out_specs=out_specs,
        scratch_shapes=list(scratch),
        input_output_aliases=aliases or {},
        compiler_params=pltpu.CompilerParams(vmem_limit_bytes=VMEM_LIMIT),
        cost_estimate=pl.CostEstimate(flops=flops, bytes_accessed=moved, transcendentals=0),
    )


def tile_rows(first_row, tile):
    return pl.ds(pl.multiple_of(first_row + tile * TILE, TILE), TILE)


def info_size(tile_total, tiles, slots):
    return 2 * tile_total + 2 + (slots + tiles) * tiles


def pairs_of(chips):
    return [(step, step + 1) for step in range(1, chips - 1, 2)]


def list_kernel(tile_total, tiles, slots, table_ref, *refs):
    sources, (info_ref, full_ref, half_ref, spare_ref, *refs) = refs[:4], refs[4:]
    any_ref, loaded, sems = refs[0], refs[1:5], refs[5:]
    del spare_ref
    rank = lax.axis_index("seq")
    copies = [
        pltpu.make_async_copy(source, target, sem)
        for source, target, sem in zip(sources, loaded, sems)
    ]
    for copy in copies:
        copy.start()

    def ids(position):
        return table_ref[tile_total, position]

    def mask(query_tile, key_tile):
        return table_ref[query_tile, key_tile]

    for place in range(1, tile_total + 2):
        info_ref[place] = 0
    for tile in range(tile_total):
        users = mask(0, tile)
        for other in range(1, tile_total):
            users = users + mask(other, tile)
        any_ref[tile] = users
    count = jnp.int32(0)
    for position in range(tile_total):
        key_tile = ids(position)
        away = any_ref[key_tile]
        for local in range(tiles):
            away = away - mask(ids(position // tiles * tiles + local), key_tile)
        info_ref[1 + count] = position
        info_ref[tile_total + 2 + position] = jnp.where(away > 0, count, -1)
        count = count + jnp.where(away > 0, 1, 0)
    info_ref[0] = count
    my_tiles = [ids(rank * tiles + b) for b in range(tiles)]
    place = 2 * tile_total + 2
    for slot in range(slots):
        position = info_ref[1 + slot]
        usable = ((slot < count) & (position // tiles != rank)).astype(jnp.int32)
        for b in range(tiles):
            info_ref[place] = usable * mask(my_tiles[b], ids(position))
            place += 1
    for a in range(tiles):
        for b in range(tiles):
            info_ref[place] = mask(my_tiles[b], my_tiles[a])
            place += 1
    for copy in copies:
        copy.wait()
    odd = rank % 2
    for kind in range(2):
        part = odd ^ kind
        target = full_ref.at[pl.ds(part * slots, slots)]
        pick(tiles, slots, 0, info_ref, loaded[kind], loaded[2 + kind], target)
    half_ref[...] = full_ref[:slots]


def pick(tiles, slots, base, info_ref, own_ref, other_ref, out_ref):
    rank = lax.axis_index("seq")
    for slot in range(slots):
        position = info_ref[1 + base + slot]
        home = position // tiles
        rows = tile_rows(0, position % tiles)
        out_ref[slot] = jnp.zeros_like(out_ref[slot])

        @pl.when(home == rank)
        def _():
            out_ref[slot] = own_ref[rows, :]

        @pl.when(home == rank ^ 1)
        def _():
            out_ref[slot] = other_ref[rows, :]


def select_kernel(tiles, slots, info_ref, round_ref, *refs):
    key_ref, value_ref, key_other, value_other, out_ref = refs
    rank = lax.axis_index("seq")
    for kind, own, other in ((0, key_ref, key_other), (1, value_ref, value_other)):

        @pl.when(rank % 2 == kind)
        def _():
            pick(tiles, slots, round_ref[0] * slots, info_ref, own, other, out_ref)


def add_sums(tiles, slots, tile_total, base, info_ref, grads, outs, sums_of):
    rank = lax.axis_index("seq")
    odd = rank % 2
    for grad, out in zip(grads, outs):
        out[...] = grad[...]
    for tile in range(tiles):
        slot = info_ref[tile_total + 2 + rank * tiles + tile] - base
        rows = tile_rows(0, tile)

        @pl.when((slot >= 0) & (slot < slots))
        def _():
            totals = []
            for part in range(2):
                total = None
                for source in sums_of(part, slot):
                    source = source.astype(jnp.float32)
                    total = source if total is None else total + source
                totals.append(total)
            for kind, out in enumerate(outs):
                out[rows, :] += jnp.where(odd == kind, totals[0], totals[1])


def close_kernel(tiles, slots, chips, tile_total, info_ref, *refs):
    grads, (chip_ref, *sums), outs = refs[:2], refs[2:-2], refs[-2:]
    half = len(sums) // 2
    arrived, handed = sums[:half], sums[half:]

    def sums_of(part, slot):
        yield chip_ref[part * slots + slot]
        for own, other in zip(arrived[:-1], handed[:-1]):
            yield own[part * slots + slot]
            yield other[(1 - part) * slots + slot]
        yield (handed if part else arrived)[-1][slot]

    add_sums(tiles, slots, tile_total, 0, info_ref, grads, outs, sums_of)


def later_kernel(tiles, slots, tile_total, info_ref, round_ref, *refs):
    grads, sums, outs = refs[:2], refs[2:-2], refs[-2:]

    def sums_of(part, slot):
        yield sums[part][slot]

    base = round_ref[0] * slots
    add_sums(tiles, slots, tile_total, base, info_ref, grads, outs, sums_of)


def causal_bias():
    later = lax.broadcasted_iota(jnp.int32, (TILE, TILE), 1)
    return jnp.where(lax.broadcasted_iota(jnp.int32, (TILE, TILE), 0) <= later, 0.0, FAR_BELOW)


def block_bias(allowed):
    return jnp.full((TILE, TILE), jnp.where(allowed, 0.0, FAR_BELOW), jnp.float32)


def own_bias(tiles, bias_ref, allowed):
    for a in range(tiles):
        for b in range(tiles):
            bias = causal_bias() if a == b else block_bias(allowed(a, b) == 1)
            bias_ref[pl.ds(a * TILE, TILE), pl.ds(b * TILE, TILE)] = bias


def stacked(ref, heads):
    return jnp.concatenate([ref[:, h * HD : (h + 1) * HD] for h in range(heads)], axis=0)


def dot(one, other):
    return jnp.dot(one, other, preferred_element_type=jnp.float32)


def dot_t(one, other):
    return lax.dot_general(one, other, NT_DIMS, preferred_element_type=jnp.float32)


def own_scores(tiles, slots, heads, tile_total, info_ref, bias_ref, keys, query):
    place = 2 * tile_total + 2 + slots * tiles
    own_bias(tiles, bias_ref, lambda a, b: info_ref[place + a * tiles + b])
    bias = jnp.concatenate([bias_ref[...]] * heads, axis=1)
    return dot_t(keys, query) * (HD**-0.5 * LOG2E) + bias


def own_kernel(
    tiles,
    slots,
    heads,
    tile_total,
    info_ref,
    query_ref,
    grad_ref,
    key_ref,
    value_ref,
    max_ref,
    total_ref,
    weighted_ref,
    grad_t_ref,
    bias_ref,
):
    query = stacked(query_ref, heads)
    scores = own_scores(tiles, slots, heads, tile_total, info_ref, bias_ref, key_ref[...], query)
    row_max = jnp.max(scores, axis=0, keepdims=True)
    terms = jnp.exp2(scores - row_max)
    max_ref[...] = row_max
    total_ref[...] = jnp.sum(terms, axis=0, keepdims=True)
    weighted_ref[...] = dot(value_ref[...].T, terms.astype(jnp.bfloat16))
    grad_t_ref[...] = stacked(grad_ref, heads).T


def gathered_kernel(
    chips,
    tiles,
    slots,
    heads,
    tile_total,
    info_ref,
    table_any,
    query_ref,
    grad_ref,
    key_any,
    value_any,
    key_other,
    value_other,
    max_own,
    total_own,
    weighted_own,
    grad_t_ref,
    more_ref,
    *refs,
):
    count = len(pairs_of(chips)) + 1
    arrived, handed, refs = refs[:count], refs[count : 2 * count], refs[2 * count :]
    parts_ref, max_ref, inverse_ref, delta_ref, out_t_ref, dscores_ref, *refs = refs
    slot_keys, *refs = refs
    more_out, attended_full, query_full, key_full, value_full, *refs = refs
    bias_ref, held_ref, sum_ref, score_ref, staged_ref, *refs = refs
    attended_ref, query_out, table_ref, copy_sem = refs
    keys_ref, values_ref = held_ref.at[0], held_ref.at[1]
    key_sum, value_sum = sum_ref.at[0], sum_ref.at[1]
    rank = lax.axis_index("seq")
    odd = rank % 2
    rows = tiles * TILE
    chunk = slots * TILE
    factor = HD**-0.5
    scale = factor * LOG2E
    needed = info_ref[0]
    columns = [pl.ds(h * HD, HD) for h in range(heads)]

    def repack(target, part, first_row):
        kind = odd ^ part
        for slot in range(slots):
            total = sum_ref[kind, tile_rows(first_row, slot), :]
            target[slot] = (total * jnp.where(kind == 0, factor, 1.0)).astype(jnp.bfloat16)

    for slot in range(slots):
        for b in range(tiles):
            allowed = info_ref[2 * tile_total + 2 + slot * tiles + b] == 1
            bias_ref[pl.ds(slot * TILE, TILE), pl.ds(b * TILE, TILE)] = block_bias(allowed)
        position = info_ref[1 + slot]
        away = (position // (2 * tiles)) ^ (rank // 2)
        at = tile_rows(0, slot)

        @pl.when(away == 0)
        def _():
            source = tile_rows(0, position % tiles)
            keys_ref[at, :] = key_other[source, :]
            values_ref[at, :] = value_other[source, :]

        @pl.when(away == chips - 1)
        def _():
            held_ref[odd, at, :] = arrived[-1][slot]
            held_ref[odd ^ 1, at, :] = handed[-1][slot]

        for index, pair in enumerate(pairs_of(chips)):
            for core, step in enumerate(pair):

                @pl.when((away == step) & (odd == core))
                def _():
                    held_ref[odd, at, :] = arrived[index][slot]
                    held_ref[odd ^ 1, at, :] = arrived[index][slots + slot]

                @pl.when((away == step) & (odd != core))
                def _():
                    held_ref[odd ^ 1, at, :] = handed[index][slot]
                    held_ref[odd, at, :] = handed[index][slots + slot]

    first = pl.ds(0, chunk)

    @pl.when(needed <= slots)
    def _():
        keys = keys_ref[first, :]
        values = values_ref[first, :]
        slot_keys[...] = keys
        query = stacked(query_ref, heads)
        grad = stacked(grad_ref, heads)
        bias = jnp.concatenate([bias_ref[first, :]] * heads, axis=1)
        scores = dot_t(keys, query) * scale + bias
        dprobs = dot_t(values, grad)
        row_max = jnp.maximum(max_own[...], jnp.max(scores, axis=0, keepdims=True))
        shrink = jnp.exp2(max_own[...] - row_max)
        terms = jnp.exp2(scores - row_max)
        inverse = 1.0 / (total_own[...] * shrink + jnp.sum(terms, axis=0, keepdims=True))
        weighted = weighted_own[...] * shrink + dot(values.T, terms.astype(jnp.bfloat16))
        out = (weighted * inverse).astype(jnp.bfloat16)
        delta = jnp.sum(
            grad_t_ref[...].astype(jnp.float32) * out.astype(jnp.float32), axis=0, keepdims=True
        )
        probs = terms * inverse
        dscores = (probs * (dprobs - delta)).astype(jnp.bfloat16)
        value_sum[first, :] = dot(probs.astype(jnp.bfloat16), grad)
        key_sum[first, :] = dot(dscores, query)
        out_t_ref[...] = out
        max_ref[...] = row_max
        inverse_ref[...] = inverse
        delta_ref[...] = delta
        dscores_ref[...] = dscores

    @pl.when(needed > slots)
    def _():
        used = (needed + slots - 1) // slots
        own_first = pl.multiple_of(used * chunk, chunk)
        own_rows = pl.ds(own_first, rows)
        copy = pltpu.make_async_copy(table_any, table_ref, copy_sem)
        copy.start()
        copy.wait()

        def ids(position):
            return table_ref[tile_total, position]

        def allowed(a, b):
            return table_ref[ids(rank * tiles + b), ids(rank * tiles + a)]

        own_bias(tiles, bias_ref.at[own_rows, :], allowed)
        for source, target in ((key_any, keys_ref), (value_any, values_ref)):
            copy = pltpu.make_async_copy(source, target.at[own_rows, :], copy_sem)
            copy.start()
            copy.wait()

        def fetch(index, carry):
            copy = pltpu.make_async_copy(more_ref.at[index - 1], staged_ref, copy_sem)
            copy.start()
            copy.wait()
            first_row = pl.multiple_of(index * chunk, chunk)
            for slot in range(slots):
                for part in range(2):
                    held_ref[odd ^ part, tile_rows(first_row, slot), :] = staged_ref[part, slot]
                listed = index * slots + slot
                position = info_ref[1 + listed]
                usable = (listed < needed) & (position // tiles != rank)
                for b in range(tiles):
                    seen = table_ref[ids(rank * tiles + b), ids(position)] == 1
                    bias_ref[tile_rows(first_row, slot), pl.ds(b * TILE, TILE)] = block_bias(
                        usable & seen
                    )
            return carry

        lax.fori_loop(1, used, fetch, 0)
        key_sum[...] = jnp.zeros_like(key_sum)
        value_sum[...] = jnp.zeros_like(value_sum)
        blocks = used * slots + tiles

        for h in range(heads):
            query = query_ref[:, columns[h]]
            grad = grad_ref[:, columns[h]]

            def score(index, row_max):
                at = tile_rows(0, index)
                scores = dot_t(keys_ref[at, :], query) * scale + bias_ref[at, :]
                score_ref[at, :] = scores
                return jnp.maximum(row_max, jnp.max(scores, axis=0, keepdims=True))

            row_max = lax.fori_loop(0, blocks, score, jnp.full((1, rows), FAR_BELOW, jnp.float32))

            def forward(index, carry):
                total, weighted = carry
                at = tile_rows(0, index)
                terms = jnp.exp2(score_ref[at, :] - row_max)
                score_ref[at, :] = terms
                weighted = weighted + dot(values_ref[at, :].T, terms.astype(jnp.bfloat16))
                return total + jnp.sum(terms, axis=0, keepdims=True), weighted

            zeros = jnp.zeros((HD, rows), jnp.float32)
            start = (jnp.zeros((1, rows), jnp.float32), zeros)
            total, weighted = lax.fori_loop(0, blocks, forward, start)
            inverse = 1.0 / total
            out = (weighted * inverse).astype(jnp.bfloat16)
            attended_ref[:, columns[h]] = out.T
            grad_t = grad_t_ref[:, pl.ds(h * rows, rows)].astype(jnp.float32)
            delta = jnp.sum(grad_t * out.astype(jnp.float32), axis=0, keepdims=True)

            def backward(index, query_t):
                at = tile_rows(0, index)
                probs = score_ref[at, :] * inverse
                dprobs = dot_t(values_ref[at, :], grad)
                dscores = (probs * (dprobs - delta)).astype(jnp.bfloat16)
                key_sum[at, :] += dot(dscores, query)
                value_sum[at, :] += dot(probs.astype(jnp.bfloat16), grad)
                return query_t + dot(keys_ref[at, :].T, dscores)

            query_t = lax.fori_loop(0, blocks, backward, zeros)
            query_out[:, columns[h]] = (query_t * factor).T

        key_sum[own_rows, :] = key_sum[own_rows, :] * factor
        for source, target in (
            (attended_ref, attended_full),
            (query_out, query_full),
            (key_sum.at[own_rows, :], key_full),
            (value_sum.at[own_rows, :], value_full),
        ):
            copy = pltpu.make_async_copy(source, target, copy_sem)
            copy.start()
            copy.wait()

        def store(index, carry):
            for part in range(2):
                repack(staged_ref.at[part], part, pl.multiple_of(index * chunk, chunk))
            copy = pltpu.make_async_copy(staged_ref, more_out.at[index - 1], copy_sem)
            copy.start()
            copy.wait()
            return carry

        lax.fori_loop(1, used, store, 0)

    for part in range(2):
        repack(parts_ref.at[pl.ds(part * slots, slots)], part, 0)


def fetch_full(copy_sem, *pairs):
    for source, target in pairs:
        copy = pltpu.make_async_copy(source, target, copy_sem)
        copy.start()
        copy.wait()


def own_grads_kernel(
    tiles,
    slots,
    heads,
    tile_total,
    info_ref,
    query_ref,
    grad_ref,
    key_ref,
    value_ref,
    max_ref,
    inverse_ref,
    delta_ref,
    key_full,
    value_full,
    order_ref,
    dscores_ref,
    key_out,
    value_out,
    order_out,
    bias_ref,
    copy_sem,
):
    del order_ref, order_out

    @pl.when(info_ref[0] <= slots)
    def _():
        query = stacked(query_ref, heads)
        grad = stacked(grad_ref, heads)
        scores = own_scores(
            tiles, slots, heads, tile_total, info_ref, bias_ref, key_ref[...], query
        )
        probs = jnp.exp2(scores - max_ref[...]) * inverse_ref[...]
        dprobs = dot_t(value_ref[...], grad)
        dscores = (probs * (dprobs - delta_ref[...])).astype(jnp.bfloat16)
        dscores_ref[...] = dscores
        value_out[...] = dot(probs.astype(jnp.bfloat16), grad)
        key_out[...] = dot(dscores, query) * HD**-0.5

    @pl.when(info_ref[0] > slots)
    def _():
        fetch_full(copy_sem, (key_full, key_out), (value_full, value_out))


def queries_kernel(
    slots,
    heads,
    info_ref,
    key_ref,
    own_dscores,
    slot_dscores,
    slot_keys,
    out_t_ref,
    attended_full,
    query_full,
    order_ref,
    attended_ref,
    query_out,
    order_out,
    copy_sem,
):
    del order_ref, order_out
    rows = query_out.shape[0]

    @pl.when(info_ref[0] <= slots)
    def _():
        query_t = dot(key_ref[...].T, own_dscores[...])
        query_t = (query_t + dot(slot_keys[...].T, slot_dscores[...])) * HD**-0.5
        for h in range(heads):
            columns = pl.ds(h * HD, HD)
            attended_ref[:, columns] = out_t_ref[:, pl.ds(h * rows, rows)].T
            query_out[:, columns] = query_t[:, h * rows : (h + 1) * rows].T

    @pl.when(info_ref[0] > slots)
    def _():
        fetch_full(copy_sem, (attended_full, attended_ref), (query_full, query_out))


def per_device(queries, key_rows, value_rows, out_grad, tile_ids, tile_mask):
    row_count = queries.shape[0]
    heads = queries.shape[1] // HD
    ranks = lax.axis_size("seq")
    chips = ranks // 2
    assert key_rows.shape[1] == HD and ranks > 1 and ranks & (ranks - 1) == 0
    tiles = row_count // TILE
    tile_total = tile_ids.shape[0]
    slots = tiles
    rounds = math.ceil(tile_total / slots)
    slot_shape = (slots, TILE, HD)
    buffer = (rounds - 1, 2) + slot_shape
    shape = jax.ShapeDtypeStruct
    bf16, f32 = jnp.bfloat16, jnp.float32

    def swap(values, step):
        return lax.ppermute(values, "seq", [(source, source ^ step) for source in range(ranks)])

    def across(values):
        return [swap(values, 2 * step) for step in range(1, chips)]

    def trade(full, half):
        got = []
        for pair in pairs_of(chips):
            routes = [(source, source ^ 2 * pair[source % 2]) for source in range(ranks)]
            got.append(lax.ppermute(full, "seq", routes))
        return got + [swap(half, 2 * (chips - 1))]

    def add(*values):
        total = values[0].astype(f32)
        for value in values[1:]:
            total = total + value.astype(f32)
        return total.astype(bf16)

    table = jnp.pad(tile_mask, ((0, 1), (0, 0)))
    table = table + jnp.pad(tile_ids[None], ((tile_total, 0), (0, 0)))
    key_other, value_other = swap(key_rows, 1), swap(value_rows, 1)
    chip_rows = (key_rows, value_rows, key_other, value_other)
    info, chosen, chosen_half, spare = call(
        functools.partial(list_kernel, tile_total, tiles, slots),
        [SMEM_SPEC] + [ANY_SPEC] * 4,
        (
            shape((info_size(tile_total, tiles, slots),), jnp.int32),
            shape((2 * slots, TILE, HD), bf16),
            shape(slot_shape, bf16),
            shape(buffer, bf16),
        ),
        (SMEM_SPEC, VMEM_SPEC, VMEM_SPEC, ANY_SPEC),
        scratch=(
            pltpu.SMEM((tile_total,), jnp.int32),
            *[pltpu.VMEM(key_rows.shape, bf16)] * 4,
            *[pltpu.SemaphoreType.DMA] * 4,
        ),
        moved=4 * 1024 * 1024,
    )(table, *chip_rows)
    used = (info[0] + slots - 1) // slots

    def select(index):
        return call(
            functools.partial(select_kernel, tiles, slots),
            [SMEM_SPEC] * 2 + [VMEM_SPEC] * 4,
            shape(slot_shape, bf16),
            VMEM_SPEC,
            moved=5 * row_count * HD * 2,
        )(info, index.reshape(1), *chip_rows)

    arrived = trade(chosen, chosen_half)
    handed = [swap(values, 1) for values in arrived]

    def gather_more(index, buffered):
        chosen = select(index)
        total = add(chosen, *across(chosen))
        pair = jnp.stack([total, swap(total, 1)])
        return lax.dynamic_update_index_in_dim(buffered, pair, index - 1, 0)

    more = lax.fori_loop(1, used, gather_more, spare)

    all_rows = row_count + rounds * slots * TILE
    columns = heads * row_count
    line = shape((1, columns), f32)
    work = 2 * columns * row_count * HD
    max_own, total_own, weighted, grad_t = call(
        functools.partial(own_kernel, tiles, slots, heads, tile_total),
        [SMEM_SPEC] + [VMEM_SPEC] * 4,
        (line, line, shape((HD, columns), f32), shape((HD, columns), bf16)),
        (VMEM_SPEC,) * 4,
        scratch=(pltpu.VMEM((row_count, row_count), f32),),
        flops=24 * work,
        moved=4 * row_count * heads * HD,
    )(info, queries, out_grad, key_rows, value_rows)

    full = (
        shape(queries.shape, bf16),
        shape(queries.shape, f32),
        shape(key_rows.shape, f32),
        shape(value_rows.shape, f32),
    )
    parts, row_max, inverse, delta, out_t, dscores, slot_keys, more_terms, *full_values = call(
        functools.partial(gathered_kernel, chips, tiles, slots, heads, tile_total),
        [SMEM_SPEC, ANY_SPEC]
        + [VMEM_SPEC] * 2
        + [ANY_SPEC] * 2
        + [VMEM_SPEC] * 6
        + [ANY_SPEC]
        + [VMEM_SPEC] * (2 * len(arrived)),
        (
            shape((2 * slots, TILE, HD), bf16),
            line,
            line,
            line,
            shape((HD, columns), bf16),
            shape((slots * TILE, columns), bf16),
            shape((slots * TILE, HD), bf16),
            shape(buffer, bf16),
        )
        + full,
        (VMEM_SPEC,) * 7 + (ANY_SPEC,) * 5,
        scratch=(
            pltpu.VMEM((all_rows, row_count), f32),
            pltpu.VMEM((2, all_rows, HD), bf16),
            pltpu.VMEM((2, all_rows, HD), f32),
            pltpu.VMEM((all_rows, row_count), f32),
            pltpu.VMEM((2,) + slot_shape, bf16),
            pltpu.VMEM(queries.shape, bf16),
            pltpu.VMEM(queries.shape, f32),
            pltpu.SMEM(table.shape, jnp.int32),
            pltpu.SemaphoreType.DMA,
        ),
        flops=24 * work,
        moved=4 * row_count * heads * HD,
    )(
        info,
        table,
        queries,
        out_grad,
        *chip_rows,
        max_own,
        total_own,
        weighted,
        grad_t,
        more,
        *arrived,
        *handed,
    )

    partner = swap(parts, 1)
    half_sum = add(parts[:slots], partner[slots:])
    chip_sum = jnp.concatenate([half_sum, add(parts[slots:], partner[:slots])])
    own_dscores, key_own, value_own, half_sum = call(
        functools.partial(own_grads_kernel, tiles, slots, heads, tile_total),
        [SMEM_SPEC] + [VMEM_SPEC] * 7 + [ANY_SPEC] * 3,
        (shape((row_count, columns), bf16), *full[2:], shape(slot_shape, bf16)),
        (VMEM_SPEC,) * 3 + (ANY_SPEC,),
        scratch=(pltpu.VMEM((row_count, row_count), f32), pltpu.SemaphoreType.DMA),
        flops=18 * work,
        moved=4 * row_count * heads * HD,
        aliases={10: 3},
    )(
        info,
        queries,
        out_grad,
        key_rows,
        value_rows,
        row_max,
        inverse,
        delta,
        *full_values[2:],
        half_sum,
    )
    back = trade(chip_sum, half_sum)
    attended, query_grad, back[0] = call(
        functools.partial(queries_kernel, slots, heads),
        [SMEM_SPEC] + [VMEM_SPEC] * 5 + [ANY_SPEC] * 3,
        (*full[:2], shape(back[0].shape, bf16)),
        (VMEM_SPEC,) * 2 + (ANY_SPEC,),
        scratch=(pltpu.SemaphoreType.DMA,),
        flops=16 * work,
        moved=8 * row_count * heads * HD,
        aliases={8: 2},
    )(info, key_rows, own_dscores, dscores, slot_keys, out_t, *full_values[:2], back[0])
    sums = [chip_sum] + back + [swap(values, 1) for values in back]

    def close(kernel, lead, grads, sums):
        return call(
            kernel,
            [SMEM_SPEC] * len(lead) + [VMEM_SPEC] * (2 + len(sums)),
            (shape(key_rows.shape, f32), shape(value_rows.shape, f32)),
            (VMEM_SPEC,) * 2,
            moved=5 * row_count * HD * 4,
        )(*lead, *grads, *sums)

    def reduce_more(index, grads):
        terms = lax.dynamic_index_in_dim(more_terms, index - 1, 0, keepdims=False)
        part = add(terms[0], swap(terms[1], 1))
        total = add(part, *across(part))
        kernel = functools.partial(later_kernel, tiles, slots, tile_total)
        return tuple(close(kernel, (info, index.reshape(1)), grads, (total, swap(total, 1))))

    kernel = functools.partial(close_kernel, tiles, slots, chips, tile_total)
    grads = tuple(close(kernel, (info,), (key_own, value_own), sums))
    key_grad, value_grad = lax.fori_loop(1, used, reduce_more, grads)
    return attended, query_grad, key_grad, value_grad


def solution(mesh):
    return jax.shard_map(
        per_device,
        mesh=mesh,
        in_specs=(
            P(("batch", "seq"), "head"),
            P(("batch", "seq"), "head"),
            P(("batch", "seq"), "head"),
            P(("batch", "seq"), "head"),
            P("batch"),
            P("batch", None),
        ),
        out_specs=(P(("batch", "seq"), "head"),) * 4,
        check_vma=False,
    )
```

```python
import functools
import math

import jax
import jax.numpy as jnp
from jax import lax
from jax.experimental import pallas as pl
from jax.experimental.pallas import tpu as pltpu
from jax.sharding import PartitionSpec as P

HD = 128
TILE = 128
FAR_BELOW = -1e30
LOG2E = 1.4426950408889634
NT_DIMS = (((1,), (1,)), ((), ()))
VMEM_LIMIT = 32 * 1024 * 1024

SMEM_SPEC = pl.BlockSpec(memory_space=pltpu.SMEM)
VMEM_SPEC = pl.BlockSpec(memory_space=pltpu.VMEM)
ANY_SPEC = pl.BlockSpec(memory_space=pl.ANY)


def call(kernel, in_specs, out_shape, out_specs, scratch=(), flops=0, moved=0, aliases=None):
    return pl.pallas_call(
        kernel,
        in_specs=in_specs,
        out_shape=out_shape,
        out_specs=out_specs,
        scratch_shapes=list(scratch),
        input_output_aliases=aliases or {},
        compiler_params=pltpu.CompilerParams(vmem_limit_bytes=VMEM_LIMIT),
        cost_estimate=pl.CostEstimate(flops=flops, bytes_accessed=moved, transcendentals=0),
    )


def tile_rows(first_row, tile):
    return pl.ds(pl.multiple_of(first_row + tile * TILE, TILE), TILE)


def info_size(tile_total, tiles, slots):
    return 2 * tile_total + 2 + (slots + tiles) * tiles


def pairs_of(chips):
    return [(step, step + 1) for step in range(1, chips - 1, 2)]


def list_kernel(tile_total, tiles, slots, table_ref, info_ref, spare_ref, any_ref):
    del spare_ref
    rank = lax.axis_index("seq")

    def ids(position):
        return table_ref[tile_total, position]

    def mask(query_tile, key_tile):
        return table_ref[query_tile, key_tile]

    for place in range(1, tile_total + 2):
        info_ref[place] = 0
    for tile in range(tile_total):
        users = mask(0, tile)
        for other in range(1, tile_total):
            users = users + mask(other, tile)
        any_ref[tile] = users
    count = jnp.int32(0)
    for position in range(tile_total):
        key_tile = ids(position)
        away = any_ref[key_tile]
        for local in range(tiles):
            away = away - mask(ids(position // tiles * tiles + local), key_tile)
        info_ref[1 + count] = position
        info_ref[tile_total + 2 + position] = jnp.where(away > 0, count, -1)
        count = count + jnp.where(away > 0, 1, 0)
    info_ref[0] = count
    my_tiles = [ids(rank * tiles + b) for b in range(tiles)]
    place = 2 * tile_total + 2
    for slot in range(slots):
        position = info_ref[1 + slot]
        usable = ((slot < count) & (position // tiles != rank)).astype(jnp.int32)
        for b in range(tiles):
            info_ref[place] = usable * mask(my_tiles[b], ids(position))
            place += 1
    for a in range(tiles):
        for b in range(tiles):
            info_ref[place] = mask(my_tiles[b], my_tiles[a])
            place += 1

def first_kernel(tiles, slots, info_ref, *refs):
    sources, (full_ref, half_ref) = refs[:4], refs[4:]
    odd = lax.axis_index("seq") % 2
    for kind in range(2):
        part = odd ^ kind
        target = full_ref.at[pl.ds(part * slots, slots)]
        pick(tiles, slots, 0, info_ref, sources[kind], sources[2 + kind], target)
    half_ref[...] = full_ref[:slots]


def pick(tiles, slots, base, info_ref, own_ref, other_ref, out_ref):
    rank = lax.axis_index("seq")
    for slot in range(slots):
        position = info_ref[1 + base + slot]
        home = position // tiles
        rows = tile_rows(0, position % tiles)
        out_ref[slot] = jnp.zeros_like(out_ref[slot])

        @pl.when(home == rank)
        def _():
            out_ref[slot] = own_ref[rows, :]

        @pl.when(home == rank ^ 1)
        def _():
            out_ref[slot] = other_ref[rows, :]


def select_kernel(tiles, slots, info_ref, round_ref, *refs):
    key_ref, value_ref, key_other, value_other, out_ref = refs
    rank = lax.axis_index("seq")
    for kind, own, other in ((0, key_ref, key_other), (1, value_ref, value_other)):

        @pl.when(rank % 2 == kind)
        def _():
            pick(tiles, slots, round_ref[0] * slots, info_ref, own, other, out_ref)


def add_sums(tiles, slots, tile_total, base, info_ref, grads, outs, sums_of):
    rank = lax.axis_index("seq")
    odd = rank % 2
    for grad, out in zip(grads, outs):
        out[...] = grad[...]
    for tile in range(tiles):
        slot = info_ref[tile_total + 2 + rank * tiles + tile] - base
        rows = tile_rows(0, tile)

        @pl.when((slot >= 0) & (slot < slots))
        def _():
            totals = []
            for part in range(2):
                total = None
                for source in sums_of(part, slot):
                    source = source.astype(jnp.float32)
                    total = source if total is None else total + source
                totals.append(total)
            for kind, out in enumerate(outs):
                out[rows, :] += jnp.where(odd == kind, totals[0], totals[1])


def close_kernel(tiles, slots, chips, tile_total, info_ref, *refs):
    grads, (chip_ref, *sums), outs = refs[:2], refs[2:-2], refs[-2:]
    half = len(sums) // 2
    arrived, handed = sums[:half], sums[half:]

    def sums_of(part, slot):
        yield chip_ref[part * slots + slot]
        for own, other in zip(arrived[:-1], handed[:-1]):
            yield own[part * slots + slot]
            yield other[(1 - part) * slots + slot]
        yield (handed if part else arrived)[-1][slot]

    add_sums(tiles, slots, tile_total, 0, info_ref, grads, outs, sums_of)


def later_kernel(tiles, slots, tile_total, info_ref, round_ref, *refs):
    grads, sums, outs = refs[:2], refs[2:-2], refs[-2:]

    def sums_of(part, slot):
        yield sums[part][slot]

    base = round_ref[0] * slots
    add_sums(tiles, slots, tile_total, base, info_ref, grads, outs, sums_of)


def causal_bias():
    later = lax.broadcasted_iota(jnp.int32, (TILE, TILE), 1)
    return jnp.where(lax.broadcasted_iota(jnp.int32, (TILE, TILE), 0) <= later, 0.0, FAR_BELOW)


def block_bias(allowed):
    return jnp.full((TILE, TILE), jnp.where(allowed, 0.0, FAR_BELOW), jnp.float32)


def own_bias(tiles, bias_ref, allowed):
    for a in range(tiles):
        for b in range(tiles):
            bias = causal_bias() if a == b else block_bias(allowed(a, b) == 1)
            bias_ref[pl.ds(a * TILE, TILE), pl.ds(b * TILE, TILE)] = bias


def stacked(ref, heads):
    return jnp.concatenate([ref[:, h * HD : (h + 1) * HD] for h in range(heads)], axis=0)


def dot(one, other):
    return jnp.dot(one, other, preferred_element_type=jnp.float32)


def dot_t(one, other):
    return lax.dot_general(one, other, NT_DIMS, preferred_element_type=jnp.float32)


def own_scores(tiles, slots, heads, tile_total, info_ref, bias_ref, keys, query):
    place = 2 * tile_total + 2 + slots * tiles
    own_bias(tiles, bias_ref, lambda a, b: info_ref[place + a * tiles + b])
    bias = jnp.concatenate([bias_ref[...]] * heads, axis=1)
    return dot_t(keys, query) * (HD**-0.5 * LOG2E) + bias


def own_kernel(
    tiles,
    slots,
    heads,
    tile_total,
    info_ref,
    query_ref,
    grad_ref,
    key_ref,
    value_ref,
    max_ref,
    total_ref,
    weighted_ref,
    grad_t_ref,
    bias_ref,
):
    query = stacked(query_ref, heads)
    scores = own_scores(tiles, slots, heads, tile_total, info_ref, bias_ref, key_ref[...], query)
    row_max = jnp.max(scores, axis=0, keepdims=True)
    terms = jnp.exp2(scores - row_max)
    max_ref[...] = row_max
    total_ref[...] = jnp.sum(terms, axis=0, keepdims=True)
    weighted_ref[...] = dot(value_ref[...].T, terms.astype(jnp.bfloat16))
    grad_t_ref[...] = stacked(grad_ref, heads).T


def gathered_kernel(
    chips,
    tiles,
    slots,
    heads,
    tile_total,
    info_ref,
    table_any,
    query_ref,
    grad_ref,
    key_any,
    value_any,
    key_other,
    value_other,
    max_own,
    total_own,
    weighted_own,
    grad_t_ref,
    more_ref,
    *refs,
):
    count = len(pairs_of(chips)) + 1
    arrived, handed, refs = refs[:count], refs[count : 2 * count], refs[2 * count :]
    parts_ref, max_ref, inverse_ref, delta_ref, out_t_ref, dscores_ref, *refs = refs
    slot_keys, *refs = refs
    more_out, attended_full, query_full, key_full, value_full, *refs = refs
    bias_ref, held_ref, sum_ref, score_ref, staged_ref, *refs = refs
    attended_ref, query_out, table_ref, copy_sem = refs
    keys_ref, values_ref = held_ref.at[0], held_ref.at[1]
    key_sum, value_sum = sum_ref.at[0], sum_ref.at[1]
    rank = lax.axis_index("seq")
    odd = rank % 2
    rows = tiles * TILE
    chunk = slots * TILE
    factor = HD**-0.5
    scale = factor * LOG2E
    needed = info_ref[0]
    columns = [pl.ds(h * HD, HD) for h in range(heads)]

    def repack(target, part, first_row):
        kind = odd ^ part
        for slot in range(slots):
            total = sum_ref[kind, tile_rows(first_row, slot), :]
            target[slot] = (total * jnp.where(kind == 0, factor, 1.0)).astype(jnp.bfloat16)

    for slot in range(slots):
        for b in range(tiles):
            allowed = info_ref[2 * tile_total + 2 + slot * tiles + b] == 1
            bias_ref[pl.ds(slot * TILE, TILE), pl.ds(b * TILE, TILE)] = block_bias(allowed)
        position = info_ref[1 + slot]
        away = (position // (2 * tiles)) ^ (rank // 2)
        at = tile_rows(0, slot)

        @pl.when(away == 0)
        def _():
            source = tile_rows(0, position % tiles)
            keys_ref[at, :] = key_other[source, :]
            values_ref[at, :] = value_other[source, :]

        @pl.when(away == chips - 1)
        def _():
            held_ref[odd, at, :] = arrived[-1][slot]
            held_ref[odd ^ 1, at, :] = handed[-1][slot]

        for index, pair in enumerate(pairs_of(chips)):
            for core, step in enumerate(pair):

                @pl.when((away == step) & (odd == core))
                def _():
                    held_ref[odd, at, :] = arrived[index][slot]
                    held_ref[odd ^ 1, at, :] = arrived[index][slots + slot]

                @pl.when((away == step) & (odd != core))
                def _():
                    held_ref[odd ^ 1, at, :] = handed[index][slot]
                    held_ref[odd, at, :] = handed[index][slots + slot]

    first = pl.ds(0, chunk)

    @pl.when(needed <= slots)
    def _():
        keys = keys_ref[first, :]
        values = values_ref[first, :]
        slot_keys[...] = keys
        values_t = values.T
        per_block = heads // 2 if heads % 2 == 0 else heads
        width = per_block * rows
        blocks = range(heads // per_block)
        bias = jnp.concatenate([bias_ref[first, :]] * per_block, axis=1)
        spans = [pl.ds(block * width, width) for block in blocks]
        query_all = stacked(query_ref, heads)
        grad_all = stacked(grad_ref, heads)
        query = [query_all[block * width : (block + 1) * width] for block in blocks]
        grad = [grad_all[block * width : (block + 1) * width] for block in blocks]
        scores = [dot_t(keys, query[block]) * scale + bias for block in blocks]
        dprobs, probs, outs = [], [], []
        for block, span in zip(blocks, spans):
            dprobs.append(dot_t(values, grad[block]))
            old_max = max_own[:, span]
            row_max = jnp.maximum(old_max, jnp.max(scores[block], axis=0, keepdims=True))
            shrink = jnp.exp2(old_max - row_max)
            terms = jnp.exp2(scores[block] - row_max)
            total = total_own[:, span] * shrink + jnp.sum(terms, axis=0, keepdims=True)
            inverse = 1.0 / total
            weighted = dot(values_t, terms.astype(jnp.bfloat16))
            outs.append((shrink * inverse, inverse, weighted))
            probs.append(terms * inverse)
            max_ref[:, span] = row_max
            inverse_ref[:, span] = inverse
        key_total, value_total = None, None
        for block, span in zip(blocks, spans):
            part = dot(probs[block].astype(jnp.bfloat16), grad[block])
            value_total = part if value_total is None else value_total + part
            shrunk, inverse, weighted = outs[block]
            out = (weighted_own[:, span] * shrunk + weighted * inverse).astype(jnp.bfloat16)
            out_t_ref[:, span] = out
            delta = jnp.sum(
                grad_t_ref[:, span].astype(jnp.float32) * out.astype(jnp.float32),
                axis=0,
                keepdims=True,
            )
            delta_ref[:, span] = delta
            dscores = (probs[block] * (dprobs[block] - delta)).astype(jnp.bfloat16)
            dscores_ref[:, span] = dscores
            part = dot(dscores, query[block])
            key_total = part if key_total is None else key_total + part
        key_sum[first, :] = key_total
        value_sum[first, :] = value_total

    @pl.when(needed > slots)
    def _():
        used = (needed + slots - 1) // slots
        own_first = pl.multiple_of(used * chunk, chunk)
        own_rows = pl.ds(own_first, rows)
        copy = pltpu.make_async_copy(table_any, table_ref, copy_sem)
        copy.start()
        copy.wait()

        def ids(position):
            return table_ref[tile_total, position]

        def allowed(a, b):
            return table_ref[ids(rank * tiles + b), ids(rank * tiles + a)]

        own_bias(tiles, bias_ref.at[own_rows, :], allowed)
        for source, target in ((key_any, keys_ref), (value_any, values_ref)):
            copy = pltpu.make_async_copy(source, target.at[own_rows, :], copy_sem)
            copy.start()
            copy.wait()

        def fetch(index, carry):
            copy = pltpu.make_async_copy(more_ref.at[index - 1], staged_ref, copy_sem)
            copy.start()
            copy.wait()
            first_row = pl.multiple_of(index * chunk, chunk)
            for slot in range(slots):
                for part in range(2):
                    held_ref[odd ^ part, tile_rows(first_row, slot), :] = staged_ref[part, slot]
                listed = index * slots + slot
                position = info_ref[1 + listed]
                usable = (listed < needed) & (position // tiles != rank)
                for b in range(tiles):
                    seen = table_ref[ids(rank * tiles + b), ids(position)] == 1
                    bias_ref[tile_rows(first_row, slot), pl.ds(b * TILE, TILE)] = block_bias(
                        usable & seen
                    )
            return carry

        lax.fori_loop(1, used, fetch, 0)
        key_sum[...] = jnp.zeros_like(key_sum)
        value_sum[...] = jnp.zeros_like(value_sum)
        blocks = used * slots + tiles

        for h in range(heads):
            query = query_ref[:, columns[h]]
            grad = grad_ref[:, columns[h]]

            def score(index, row_max):
                at = tile_rows(0, index)
                scores = dot_t(keys_ref[at, :], query) * scale + bias_ref[at, :]
                score_ref[at, :] = scores
                return jnp.maximum(row_max, jnp.max(scores, axis=0, keepdims=True))

            row_max = lax.fori_loop(0, blocks, score, jnp.full((1, rows), FAR_BELOW, jnp.float32))

            def forward(index, carry):
                total, weighted = carry
                at = tile_rows(0, index)
                terms = jnp.exp2(score_ref[at, :] - row_max)
                score_ref[at, :] = terms
                weighted = weighted + dot(values_ref[at, :].T, terms.astype(jnp.bfloat16))
                return total + jnp.sum(terms, axis=0, keepdims=True), weighted

            zeros = jnp.zeros((HD, rows), jnp.float32)
            start = (jnp.zeros((1, rows), jnp.float32), zeros)
            total, weighted = lax.fori_loop(0, blocks, forward, start)
            inverse = 1.0 / total
            out = (weighted * inverse).astype(jnp.bfloat16)
            attended_ref[:, columns[h]] = out.T
            grad_t = grad_t_ref[:, pl.ds(h * rows, rows)].astype(jnp.float32)
            delta = jnp.sum(grad_t * out.astype(jnp.float32), axis=0, keepdims=True)

            def backward(index, query_t):
                at = tile_rows(0, index)
                probs = score_ref[at, :] * inverse
                dprobs = dot_t(values_ref[at, :], grad)
                dscores = (probs * (dprobs - delta)).astype(jnp.bfloat16)
                key_sum[at, :] += dot(dscores, query)
                value_sum[at, :] += dot(probs.astype(jnp.bfloat16), grad)
                return query_t + dot(keys_ref[at, :].T, dscores)

            query_t = lax.fori_loop(0, blocks, backward, zeros)
            query_out[:, columns[h]] = (query_t * factor).T

        key_sum[own_rows, :] = key_sum[own_rows, :] * factor
        for source, target in (
            (attended_ref, attended_full),
            (query_out, query_full),
            (key_sum.at[own_rows, :], key_full),
            (value_sum.at[own_rows, :], value_full),
        ):
            copy = pltpu.make_async_copy(source, target, copy_sem)
            copy.start()
            copy.wait()

        def store(index, carry):
            for part in range(2):
                repack(staged_ref.at[part], part, pl.multiple_of(index * chunk, chunk))
            copy = pltpu.make_async_copy(staged_ref, more_out.at[index - 1], copy_sem)
            copy.start()
            copy.wait()
            return carry

        lax.fori_loop(1, used, store, 0)

    for part in range(2):
        repack(parts_ref.at[pl.ds(part * slots, slots)], part, 0)


def fetch_full(copy_sem, *pairs):
    for source, target in pairs:
        copy = pltpu.make_async_copy(source, target, copy_sem)
        copy.start()
        copy.wait()


def own_grads_kernel(
    tiles,
    slots,
    heads,
    tile_total,
    info_ref,
    query_ref,
    grad_ref,
    key_ref,
    value_ref,
    max_ref,
    inverse_ref,
    delta_ref,
    key_full,
    value_full,
    order_ref,
    dscores_ref,
    key_out,
    value_out,
    order_out,
    bias_ref,
    copy_sem,
):
    del order_ref, order_out

    @pl.when(info_ref[0] <= slots)
    def _():
        query = stacked(query_ref, heads)
        grad = stacked(grad_ref, heads)
        scores = own_scores(
            tiles, slots, heads, tile_total, info_ref, bias_ref, key_ref[...], query
        )
        probs = jnp.exp2(scores - max_ref[...]) * inverse_ref[...]
        dprobs = dot_t(value_ref[...], grad)
        dscores = (probs * (dprobs - delta_ref[...])).astype(jnp.bfloat16)
        dscores_ref[...] = dscores
        value_out[...] = dot(probs.astype(jnp.bfloat16), grad)
        key_out[...] = dot(dscores, query) * HD**-0.5

    @pl.when(info_ref[0] > slots)
    def _():
        fetch_full(copy_sem, (key_full, key_out), (value_full, value_out))


def queries_kernel(
    slots,
    heads,
    info_ref,
    key_ref,
    own_dscores,
    slot_dscores,
    slot_keys,
    out_t_ref,
    attended_full,
    query_full,
    order_ref,
    attended_ref,
    query_out,
    order_out,
    copy_sem,
):
    del order_ref, order_out
    rows = query_out.shape[0]

    @pl.when(info_ref[0] <= slots)
    def _():
        query_t = dot(key_ref[...].T, own_dscores[...])
        query_t = (query_t + dot(slot_keys[...].T, slot_dscores[...])) * HD**-0.5
        for h in range(heads):
            columns = pl.ds(h * HD, HD)
            attended_ref[:, columns] = out_t_ref[:, pl.ds(h * rows, rows)].T
            query_out[:, columns] = query_t[:, h * rows : (h + 1) * rows].T

    @pl.when(info_ref[0] > slots)
    def _():
        fetch_full(copy_sem, (attended_full, attended_ref), (query_full, query_out))


def per_device(queries, key_rows, value_rows, out_grad, tile_ids, tile_mask):
    row_count = queries.shape[0]
    heads = queries.shape[1] // HD
    ranks = lax.axis_size("seq")
    chips = ranks // 2
    assert key_rows.shape[1] == HD and ranks > 1 and ranks & (ranks - 1) == 0
    tiles = row_count // TILE
    tile_total = tile_ids.shape[0]
    slots = tiles
    rounds = math.ceil(tile_total / slots)
    slot_shape = (slots, TILE, HD)
    buffer = (rounds - 1, 2) + slot_shape
    shape = jax.ShapeDtypeStruct
    bf16, f32 = jnp.bfloat16, jnp.float32

    def swap(values, step):
        return lax.ppermute(values, "seq", [(source, source ^ step) for source in range(ranks)])

    def across(values):
        return [swap(values, 2 * step) for step in range(1, chips)]

    def trade(full, half):
        got = []
        for pair in pairs_of(chips):
            routes = [(source, source ^ 2 * pair[source % 2]) for source in range(ranks)]
            got.append(lax.ppermute(full, "seq", routes))
        return got + [swap(half, 2 * (chips - 1))]

    def add(*values):
        total = values[0].astype(f32)
        for value in values[1:]:
            total = total + value.astype(f32)
        return total.astype(bf16)

    table = jnp.pad(tile_mask, ((0, 1), (0, 0)))
    table = table + jnp.pad(tile_ids[None], ((tile_total, 0), (0, 0)))
    key_other, value_other = swap(key_rows, 1), swap(value_rows, 1)
    chip_rows = (key_rows, value_rows, key_other, value_other)
    info, spare = call(
        functools.partial(list_kernel, tile_total, tiles, slots),
        [SMEM_SPEC],
        (shape((info_size(tile_total, tiles, slots),), jnp.int32), shape(buffer, bf16)),
        (SMEM_SPEC, ANY_SPEC),
        scratch=(pltpu.SMEM((tile_total,), jnp.int32),),
        moved=4 * 1024 * 1024,
    )(table)
    chosen, chosen_half = call(
        functools.partial(first_kernel, tiles, slots),
        [SMEM_SPEC] + [VMEM_SPEC] * 4,
        (shape((2 * slots, TILE, HD), bf16), shape(slot_shape, bf16)),
        (VMEM_SPEC,) * 2,
        moved=5 * row_count * HD * 2,
    )(info, *chip_rows)
    used = (info[0] + slots - 1) // slots

    def select(index):
        return call(
            functools.partial(select_kernel, tiles, slots),
            [SMEM_SPEC] * 2 + [VMEM_SPEC] * 4,
            shape(slot_shape, bf16),
            VMEM_SPEC,
            moved=5 * row_count * HD * 2,
        )(info, index.reshape(1), *chip_rows)

    arrived = trade(chosen, chosen_half)
    handed = [swap(values, 1) for values in arrived]

    def gather_more(index, buffered):
        chosen = select(index)
        total = add(chosen, *across(chosen))
        pair = jnp.stack([total, swap(total, 1)])
        return lax.dynamic_update_index_in_dim(buffered, pair, index - 1, 0)

    more = lax.fori_loop(1, used, gather_more, spare)

    all_rows = row_count + rounds * slots * TILE
    columns = heads * row_count
    line = shape((1, columns), f32)
    work = 2 * columns * row_count * HD
    max_own, total_own, weighted, grad_t = call(
        functools.partial(own_kernel, tiles, slots, heads, tile_total),
        [SMEM_SPEC] + [VMEM_SPEC] * 4,
        (line, line, shape((HD, columns), f32), shape((HD, columns), bf16)),
        (VMEM_SPEC,) * 4,
        scratch=(pltpu.VMEM((row_count, row_count), f32),),
        flops=24 * work,
        moved=4 * row_count * heads * HD,
    )(info, queries, out_grad, key_rows, value_rows)

    full = (
        shape(queries.shape, bf16),
        shape(queries.shape, f32),
        shape(key_rows.shape, f32),
        shape(value_rows.shape, f32),
    )
    parts, row_max, inverse, delta, out_t, dscores, slot_keys, more_terms, *full_values = call(
        functools.partial(gathered_kernel, chips, tiles, slots, heads, tile_total),
        [SMEM_SPEC, ANY_SPEC]
        + [VMEM_SPEC] * 2
        + [ANY_SPEC] * 2
        + [VMEM_SPEC] * 6
        + [ANY_SPEC]
        + [VMEM_SPEC] * (2 * len(arrived)),
        (
            shape((2 * slots, TILE, HD), bf16),
            line,
            line,
            line,
            shape((HD, columns), bf16),
            shape((slots * TILE, columns), bf16),
            shape((slots * TILE, HD), bf16),
            shape(buffer, bf16),
        )
        + full,
        (VMEM_SPEC,) * 7 + (ANY_SPEC,) * 5,
        scratch=(
            pltpu.VMEM((all_rows, row_count), f32),
            pltpu.VMEM((2, all_rows, HD), bf16),
            pltpu.VMEM((2, all_rows, HD), f32),
            pltpu.VMEM((all_rows, row_count), f32),
            pltpu.VMEM((2,) + slot_shape, bf16),
            pltpu.VMEM(queries.shape, bf16),
            pltpu.VMEM(queries.shape, f32),
            pltpu.SMEM(table.shape, jnp.int32),
            pltpu.SemaphoreType.DMA,
        ),
        flops=24 * work,
        moved=4 * row_count * heads * HD,
    )(
        info,
        table,
        queries,
        out_grad,
        *chip_rows,
        max_own,
        total_own,
        weighted,
        grad_t,
        more,
        *arrived,
        *handed,
    )

    partner = swap(parts, 1)
    half_sum = add(parts[:slots], partner[slots:])
    chip_sum = jnp.concatenate([half_sum, add(parts[slots:], partner[:slots])])
    own_dscores, key_own, value_own, half_sum = call(
        functools.partial(own_grads_kernel, tiles, slots, heads, tile_total),
        [SMEM_SPEC] + [VMEM_SPEC] * 7 + [ANY_SPEC] * 3,
        (shape((row_count, columns), bf16), *full[2:], shape(slot_shape, bf16)),
        (VMEM_SPEC,) * 3 + (ANY_SPEC,),
        scratch=(pltpu.VMEM((row_count, row_count), f32), pltpu.SemaphoreType.DMA),
        flops=18 * work,
        moved=4 * row_count * heads * HD,
        aliases={10: 3},
    )(
        info,
        queries,
        out_grad,
        key_rows,
        value_rows,
        row_max,
        inverse,
        delta,
        *full_values[2:],
        half_sum,
    )
    back = trade(chip_sum, half_sum)
    attended, query_grad, back[0] = call(
        functools.partial(queries_kernel, slots, heads),
        [SMEM_SPEC] + [VMEM_SPEC] * 5 + [ANY_SPEC] * 3,
        (*full[:2], shape(back[0].shape, bf16)),
        (VMEM_SPEC,) * 2 + (ANY_SPEC,),
        scratch=(pltpu.SemaphoreType.DMA,),
        flops=16 * work,
        moved=8 * row_count * heads * HD,
        aliases={8: 2},
    )(info, key_rows, own_dscores, dscores, slot_keys, out_t, *full_values[:2], back[0])
    sums = [chip_sum] + back + [swap(values, 1) for values in back]

    def close(kernel, lead, grads, sums):
        return call(
            kernel,
            [SMEM_SPEC] * len(lead) + [VMEM_SPEC] * (2 + len(sums)),
            (shape(key_rows.shape, f32), shape(value_rows.shape, f32)),
            (VMEM_SPEC,) * 2,
            moved=5 * row_count * HD * 4,
        )(*lead, *grads, *sums)

    def reduce_more(index, grads):
        terms = lax.dynamic_index_in_dim(more_terms, index - 1, 0, keepdims=False)
        part = add(terms[0], swap(terms[1], 1))
        total = add(part, *across(part))
        kernel = functools.partial(later_kernel, tiles, slots, tile_total)
        return tuple(close(kernel, (info, index.reshape(1)), grads, (total, swap(total, 1))))

    kernel = functools.partial(close_kernel, tiles, slots, chips, tile_total)
    grads = tuple(close(kernel, (info,), (key_own, value_own), sums))
    key_grad, value_grad = lax.fori_loop(1, used, reduce_more, grads)
    return attended, query_grad, key_grad, value_grad


def solution(mesh):
    return jax.shard_map(
        per_device,
        mesh=mesh,
        in_specs=(
            P(("batch", "seq"), "head"),
            P(("batch", "seq"), "head"),
            P(("batch", "seq"), "head"),
            P(("batch", "seq"), "head"),
            P("batch"),
            P("batch", None),
        ),
        out_specs=(P(("batch", "seq"), "head"),) * 4,
        check_vma=False,
    )
```

```python
import functools
import math

import jax
import jax.numpy as jnp
from jax import lax
from jax.experimental import pallas as pl
from jax.experimental.pallas import tpu as pltpu
from jax.sharding import PartitionSpec as P

HD = 128
TILE = 128
FAR_BELOW = -1e30
LOG2E = 1.4426950408889634
NT_DIMS = (((1,), (1,)), ((), ()))
VMEM_LIMIT = 32 * 1024 * 1024

SMEM_SPEC = pl.BlockSpec(memory_space=pltpu.SMEM)
VMEM_SPEC = pl.BlockSpec(memory_space=pltpu.VMEM)
ANY_SPEC = pl.BlockSpec(memory_space=pl.ANY)


def call(kernel, in_specs, out_shape, out_specs, scratch=(), flops=0, moved=0, aliases=None):
    return pl.pallas_call(
        kernel,
        in_specs=in_specs,
        out_shape=out_shape,
        out_specs=out_specs,
        scratch_shapes=list(scratch),
        input_output_aliases=aliases or {},
        compiler_params=pltpu.CompilerParams(vmem_limit_bytes=VMEM_LIMIT),
        cost_estimate=pl.CostEstimate(flops=flops, bytes_accessed=moved, transcendentals=0),
    )


def tile_rows(first_row, tile):
    return pl.ds(pl.multiple_of(first_row + tile * TILE, TILE), TILE)


def info_size(tile_total, tiles, slots):
    return 2 * tile_total + 2 + (slots + tiles) * tiles


def pairs_of(chips):
    return [(step, step + 1) for step in range(1, chips - 1, 2)]


def list_kernel(tile_total, tiles, slots, table_ref, key_any, value_any, *refs):
    info_ref, spare_ref, key_out, value_out, key_sem, value_sem = refs
    del spare_ref
    copies = [
        pltpu.make_async_copy(key_any, key_out, key_sem),
        pltpu.make_async_copy(value_any, value_out, value_sem),
    ]
    for copy in copies:
        copy.start()
    rank = lax.axis_index("seq")
    for place in range(1, tile_total + 2):
        info_ref[place] = 0
    ids = [table_ref[1, position] for position in range(tile_total)]
    rows = [table_ref[0, tile] for tile in ids]
    wants = [
        functools.reduce(jnp.bitwise_or, rows[first : first + tiles])
        for first in range(0, tile_total, tiles)
    ]
    before, behind = [jnp.int32(0)], [jnp.int32(0)]
    for want in wants:
        before.append(before[-1] | want)
    for want in wants[::-1]:
        behind.append(behind[-1] | want)
    behind = behind[::-1]
    count = jnp.int32(0)
    for position in range(tile_total):
        home = position // tiles
        wanted = ((before[home] | behind[home + 1]) >> ids[position]) & 1
        info_ref[1 + count] = position
        info_ref[tile_total + 2 + position] = jnp.where(wanted == 1, count, -1)
        count = count + wanted
    info_ref[0] = count
    my_tiles = [table_ref[1, rank * tiles + b] for b in range(tiles)]
    my_rows = [table_ref[0, tile] for tile in my_tiles]
    place = 2 * tile_total + 2
    for slot in range(slots):
        position = info_ref[1 + slot]
        usable = ((slot < count) & (position // tiles != rank)).astype(jnp.int32)
        for b in range(tiles):
            info_ref[place] = usable & (my_rows[b] >> table_ref[1, position])
            place += 1
    for a in range(tiles):
        for b in range(tiles):
            info_ref[place] = (my_rows[b] >> my_tiles[a]) & 1
            place += 1
    for copy in copies:
        copy.wait()


def first_kernel(tiles, slots, info_ref, *refs):
    sources, (full_ref, half_ref) = refs[:4], refs[4:]
    odd = lax.axis_index("seq") % 2
    for kind in range(2):
        part = odd ^ kind
        target = full_ref.at[pl.ds(part * slots, slots)]
        pick(tiles, slots, 0, info_ref, sources[kind], sources[2 + kind], target)
    half_ref[...] = full_ref[:slots]


def pick(tiles, slots, base, info_ref, own_ref, other_ref, out_ref):
    rank = lax.axis_index("seq")
    for slot in range(slots):
        position = info_ref[1 + base + slot]
        home = position // tiles
        rows = tile_rows(0, position % tiles)
        out_ref[slot] = jnp.zeros_like(out_ref[slot])

        @pl.when(home == rank)
        def _():
            out_ref[slot] = own_ref[rows, :]

        @pl.when(home == rank ^ 1)
        def _():
            out_ref[slot] = other_ref[rows, :]


def select_kernel(tiles, slots, info_ref, round_ref, *refs):
    key_ref, value_ref, key_other, value_other, out_ref = refs
    rank = lax.axis_index("seq")
    for kind, own, other in ((0, key_ref, key_other), (1, value_ref, value_other)):

        @pl.when(rank % 2 == kind)
        def _():
            pick(tiles, slots, round_ref[0] * slots, info_ref, own, other, out_ref)


def add_sums(tiles, slots, tile_total, base, info_ref, grads, outs, sums_of):
    rank = lax.axis_index("seq")
    odd = rank % 2
    for grad, out in zip(grads, outs):
        out[...] = grad[...]
    for tile in range(tiles):
        slot = info_ref[tile_total + 2 + rank * tiles + tile] - base
        rows = tile_rows(0, tile)

        @pl.when((slot >= 0) & (slot < slots))
        def _():
            totals = []
            for part in range(2):
                total = None
                for source in sums_of(part, slot):
                    source = source.astype(jnp.float32)
                    total = source if total is None else total + source
                totals.append(total)
            for kind, out in enumerate(outs):
                out[rows, :] += jnp.where(odd == kind, totals[0], totals[1])


def close_kernel(tiles, slots, chips, tile_total, info_ref, *refs):
    grads, (chip_ref, *sums), outs = refs[:2], refs[2:-2], refs[-2:]
    half = len(sums) // 2
    arrived, handed = sums[:half], sums[half:]

    def sums_of(part, slot):
        yield chip_ref[part * slots + slot]
        for own, other in zip(arrived[:-1], handed[:-1]):
            yield own[part * slots + slot]
            yield other[(1 - part) * slots + slot]
        yield (handed if part else arrived)[-1][slot]

    add_sums(tiles, slots, tile_total, 0, info_ref, grads, outs, sums_of)


def later_kernel(tiles, slots, tile_total, info_ref, round_ref, *refs):
    grads, sums, outs = refs[:2], refs[2:-2], refs[-2:]

    def sums_of(part, slot):
        yield sums[part][slot]

    base = round_ref[0] * slots
    add_sums(tiles, slots, tile_total, base, info_ref, grads, outs, sums_of)


def causal_bias():
    later = lax.broadcasted_iota(jnp.int32, (TILE, TILE), 1)
    return jnp.where(lax.broadcasted_iota(jnp.int32, (TILE, TILE), 0) <= later, 0.0, FAR_BELOW)


def block_bias(allowed):
    return jnp.full((TILE, TILE), jnp.where(allowed, 0.0, FAR_BELOW), jnp.float32)


def own_bias(tiles, bias_ref, allowed):
    for a in range(tiles):
        for b in range(tiles):
            bias = causal_bias() if a == b else block_bias(allowed(a, b) == 1)
            bias_ref[pl.ds(a * TILE, TILE), pl.ds(b * TILE, TILE)] = bias


def stacked(ref, heads):
    return jnp.concatenate([ref[:, h * HD : (h + 1) * HD] for h in range(heads)], axis=0)


def dot(one, other):
    return jnp.dot(one, other, preferred_element_type=jnp.float32)


def dot_t(one, other):
    return lax.dot_general(one, other, NT_DIMS, preferred_element_type=jnp.float32)


def own_scores(tiles, slots, heads, tile_total, info_ref, bias_ref, keys, query):
    place = 2 * tile_total + 2 + slots * tiles
    own_bias(tiles, bias_ref, lambda a, b: info_ref[place + a * tiles + b])
    bias = jnp.concatenate([bias_ref[...]] * heads, axis=1)
    return dot_t(keys, query) * (HD**-0.5 * LOG2E) + bias


def own_kernel(
    tiles,
    slots,
    heads,
    tile_total,
    info_ref,
    query_ref,
    grad_ref,
    key_ref,
    value_ref,
    max_ref,
    total_ref,
    weighted_ref,
    grad_t_ref,
    bias_ref,
):
    query = stacked(query_ref, heads)
    scores = own_scores(tiles, slots, heads, tile_total, info_ref, bias_ref, key_ref[...], query)
    row_max = jnp.max(scores, axis=0, keepdims=True)
    terms = jnp.exp2(scores - row_max)
    max_ref[...] = row_max
    total_ref[...] = jnp.sum(terms, axis=0, keepdims=True)
    weighted_ref[...] = dot(value_ref[...].T, terms.astype(jnp.bfloat16))
    grad_t_ref[...] = stacked(grad_ref, heads).T


def gathered_kernel(
    chips,
    tiles,
    slots,
    heads,
    tile_total,
    info_ref,
    table_any,
    query_ref,
    grad_ref,
    key_any,
    value_any,
    key_other,
    value_other,
    max_own,
    total_own,
    weighted_own,
    grad_t_ref,
    more_ref,
    *refs,
):
    count = len(pairs_of(chips)) + 1
    arrived, handed, refs = refs[:count], refs[count : 2 * count], refs[2 * count :]
    parts_ref, max_ref, inverse_ref, delta_ref, out_t_ref, dscores_ref, *refs = refs
    slot_keys, *refs = refs
    more_out, attended_full, query_full, key_full, value_full, *refs = refs
    bias_ref, held_ref, sum_ref, score_ref, staged_ref, *refs = refs
    attended_ref, query_out, table_ref, copy_sem = refs
    keys_ref, values_ref = held_ref.at[0], held_ref.at[1]
    key_sum, value_sum = sum_ref.at[0], sum_ref.at[1]
    rank = lax.axis_index("seq")
    odd = rank % 2
    rows = tiles * TILE
    chunk = slots * TILE
    factor = HD**-0.5
    scale = factor * LOG2E
    needed = info_ref[0]
    columns = [pl.ds(h * HD, HD) for h in range(heads)]

    def repack(target, part, first_row):
        kind = odd ^ part
        for slot in range(slots):
            total = sum_ref[kind, tile_rows(first_row, slot), :]
            target[slot] = (total * jnp.where(kind == 0, factor, 1.0)).astype(jnp.bfloat16)

    for slot in range(slots):
        for b in range(tiles):
            allowed = info_ref[2 * tile_total + 2 + slot * tiles + b] == 1
            bias_ref[pl.ds(slot * TILE, TILE), pl.ds(b * TILE, TILE)] = block_bias(allowed)
        position = info_ref[1 + slot]
        away = (position // (2 * tiles)) ^ (rank // 2)
        at = tile_rows(0, slot)

        @pl.when(away == 0)
        def _():
            source = tile_rows(0, position % tiles)
            keys_ref[at, :] = key_other[source, :]
            values_ref[at, :] = value_other[source, :]

        @pl.when(away == chips - 1)
        def _():
            held_ref[odd, at, :] = arrived[-1][slot]
            held_ref[odd ^ 1, at, :] = handed[-1][slot]

        for index, pair in enumerate(pairs_of(chips)):
            for core, step in enumerate(pair):

                @pl.when((away == step) & (odd == core))
                def _():
                    held_ref[odd, at, :] = arrived[index][slot]
                    held_ref[odd ^ 1, at, :] = arrived[index][slots + slot]

                @pl.when((away == step) & (odd != core))
                def _():
                    held_ref[odd ^ 1, at, :] = handed[index][slot]
                    held_ref[odd, at, :] = handed[index][slots + slot]

    first = pl.ds(0, chunk)

    @pl.when(needed <= slots)
    def _():
        keys = keys_ref[first, :]
        values = values_ref[first, :]
        slot_keys[...] = keys
        values_t = values.T
        per_block = heads // 2 if heads % 2 == 0 else heads
        width = per_block * rows
        blocks = range(heads // per_block)
        bias = jnp.concatenate([bias_ref[first, :]] * per_block, axis=1)
        spans = [pl.ds(block * width, width) for block in blocks]
        query_all = stacked(query_ref, heads)
        grad_all = stacked(grad_ref, heads)
        query = [query_all[block * width : (block + 1) * width] for block in blocks]
        grad = [grad_all[block * width : (block + 1) * width] for block in blocks]
        scores = [dot_t(keys, query[block]) * scale + bias for block in blocks]
        dprobs, probs, outs = [], [], []
        for block, span in zip(blocks, spans):
            dprobs.append(dot_t(values, grad[block]))
            old_max = max_own[:, span]
            row_max = jnp.maximum(old_max, jnp.max(scores[block], axis=0, keepdims=True))
            shrink = jnp.exp2(old_max - row_max)
            terms = jnp.exp2(scores[block] - row_max)
            total = total_own[:, span] * shrink + jnp.sum(terms, axis=0, keepdims=True)
            inverse = 1.0 / total
            weighted = dot(values_t, terms.astype(jnp.bfloat16))
            outs.append((shrink * inverse, inverse, weighted))
            probs.append(terms * inverse)
            max_ref[:, span] = row_max
            inverse_ref[:, span] = inverse
        key_total, value_total = None, None
        for block, span in zip(blocks, spans):
            part = dot(probs[block].astype(jnp.bfloat16), grad[block])
            value_total = part if value_total is None else value_total + part
            shrunk, inverse, weighted = outs[block]
            out = (weighted_own[:, span] * shrunk + weighted * inverse).astype(jnp.bfloat16)
            out_t_ref[:, span] = out
            delta = jnp.sum(
                grad_t_ref[:, span].astype(jnp.float32) * out.astype(jnp.float32),
                axis=0,
                keepdims=True,
            )
            delta_ref[:, span] = delta
            dscores = (probs[block] * (dprobs[block] - delta)).astype(jnp.bfloat16)
            dscores_ref[:, span] = dscores
            part = dot(dscores, query[block])
            key_total = part if key_total is None else key_total + part
        key_sum[first, :] = key_total
        value_sum[first, :] = value_total

    @pl.when(needed > slots)
    def _():
        used = (needed + slots - 1) // slots
        own_first = pl.multiple_of(used * chunk, chunk)
        own_rows = pl.ds(own_first, rows)
        copy = pltpu.make_async_copy(table_any, table_ref, copy_sem)
        copy.start()
        copy.wait()

        def seen(query_position, key_position):
            return (table_ref[0, table_ref[1, query_position]] >> table_ref[1, key_position]) & 1

        def allowed(a, b):
            return seen(rank * tiles + b, rank * tiles + a)

        own_bias(tiles, bias_ref.at[own_rows, :], allowed)
        for source, target in ((key_any, keys_ref), (value_any, values_ref)):
            copy = pltpu.make_async_copy(source, target.at[own_rows, :], copy_sem)
            copy.start()
            copy.wait()

        def fetch(index, carry):
            copy = pltpu.make_async_copy(more_ref.at[index - 1], staged_ref, copy_sem)
            copy.start()
            copy.wait()
            first_row = pl.multiple_of(index * chunk, chunk)
            for slot in range(slots):
                for part in range(2):
                    held_ref[odd ^ part, tile_rows(first_row, slot), :] = staged_ref[part, slot]
                listed = index * slots + slot
                position = info_ref[1 + listed]
                usable = (listed < needed) & (position // tiles != rank)
                for b in range(tiles):
                    bias_ref[tile_rows(first_row, slot), pl.ds(b * TILE, TILE)] = block_bias(
                        usable & (seen(rank * tiles + b, position) == 1)
                    )
            return carry

        lax.fori_loop(1, used, fetch, 0)
        key_sum[...] = jnp.zeros_like(key_sum)
        value_sum[...] = jnp.zeros_like(value_sum)
        blocks = used * slots + tiles

        for h in range(heads):
            query = query_ref[:, columns[h]]
            grad = grad_ref[:, columns[h]]

            def score(index, row_max):
                at = tile_rows(0, index)
                scores = dot_t(keys_ref[at, :], query) * scale + bias_ref[at, :]
                score_ref[at, :] = scores
                return jnp.maximum(row_max, jnp.max(scores, axis=0, keepdims=True))

            row_max = lax.fori_loop(0, blocks, score, jnp.full((1, rows), FAR_BELOW, jnp.float32))

            def forward(index, carry):
                total, weighted = carry
                at = tile_rows(0, index)
                terms = jnp.exp2(score_ref[at, :] - row_max)
                score_ref[at, :] = terms
                weighted = weighted + dot(values_ref[at, :].T, terms.astype(jnp.bfloat16))
                return total + jnp.sum(terms, axis=0, keepdims=True), weighted

            zeros = jnp.zeros((HD, rows), jnp.float32)
            start = (jnp.zeros((1, rows), jnp.float32), zeros)
            total, weighted = lax.fori_loop(0, blocks, forward, start)
            inverse = 1.0 / total
            out = (weighted * inverse).astype(jnp.bfloat16)
            attended_ref[:, columns[h]] = out.T
            grad_t = grad_t_ref[:, pl.ds(h * rows, rows)].astype(jnp.float32)
            delta = jnp.sum(grad_t * out.astype(jnp.float32), axis=0, keepdims=True)

            def backward(index, query_t):
                at = tile_rows(0, index)
                probs = score_ref[at, :] * inverse
                dprobs = dot_t(values_ref[at, :], grad)
                dscores = (probs * (dprobs - delta)).astype(jnp.bfloat16)
                key_sum[at, :] += dot(dscores, query)
                value_sum[at, :] += dot(probs.astype(jnp.bfloat16), grad)
                return query_t + dot(keys_ref[at, :].T, dscores)

            query_t = lax.fori_loop(0, blocks, backward, zeros)
            query_out[:, columns[h]] = (query_t * factor).T

        key_sum[own_rows, :] = key_sum[own_rows, :] * factor
        for source, target in (
            (attended_ref, attended_full),
            (query_out, query_full),
            (key_sum.at[own_rows, :], key_full),
            (value_sum.at[own_rows, :], value_full),
        ):
            copy = pltpu.make_async_copy(source, target, copy_sem)
            copy.start()
            copy.wait()

        def store(index, carry):
            for part in range(2):
                repack(staged_ref.at[part], part, pl.multiple_of(index * chunk, chunk))
            copy = pltpu.make_async_copy(staged_ref, more_out.at[index - 1], copy_sem)
            copy.start()
            copy.wait()
            return carry

        lax.fori_loop(1, used, store, 0)

    for part in range(2):
        repack(parts_ref.at[pl.ds(part * slots, slots)], part, 0)


def fetch_full(copy_sem, *pairs):
    for source, target in pairs:
        copy = pltpu.make_async_copy(source, target, copy_sem)
        copy.start()
        copy.wait()


def own_grads_kernel(
    tiles,
    slots,
    heads,
    tile_total,
    info_ref,
    query_ref,
    grad_ref,
    key_ref,
    value_ref,
    max_ref,
    inverse_ref,
    delta_ref,
    key_full,
    value_full,
    order_ref,
    dscores_ref,
    key_out,
    value_out,
    order_out,
    bias_ref,
    copy_sem,
):
    del order_ref, order_out

    @pl.when(info_ref[0] <= slots)
    def _():
        query = stacked(query_ref, heads)
        grad = stacked(grad_ref, heads)
        scores = own_scores(
            tiles, slots, heads, tile_total, info_ref, bias_ref, key_ref[...], query
        )
        probs = jnp.exp2(scores - max_ref[...]) * inverse_ref[...]
        dprobs = dot_t(value_ref[...], grad)
        dscores = (probs * (dprobs - delta_ref[...])).astype(jnp.bfloat16)
        dscores_ref[...] = dscores
        value_out[...] = dot(probs.astype(jnp.bfloat16), grad)
        key_out[...] = dot(dscores, query) * HD**-0.5

    @pl.when(info_ref[0] > slots)
    def _():
        fetch_full(copy_sem, (key_full, key_out), (value_full, value_out))


def queries_kernel(
    slots,
    heads,
    info_ref,
    key_ref,
    own_dscores,
    slot_dscores,
    slot_keys,
    out_t_ref,
    attended_full,
    query_full,
    order_ref,
    attended_ref,
    query_out,
    order_out,
    copy_sem,
):
    del order_ref, order_out
    rows = query_out.shape[0]

    @pl.when(info_ref[0] <= slots)
    def _():
        query_t = dot(key_ref[...].T, own_dscores[...])
        query_t = (query_t + dot(slot_keys[...].T, slot_dscores[...])) * HD**-0.5
        for h in range(heads):
            columns = pl.ds(h * HD, HD)
            attended_ref[:, columns] = out_t_ref[:, pl.ds(h * rows, rows)].T
            query_out[:, columns] = query_t[:, h * rows : (h + 1) * rows].T

    @pl.when(info_ref[0] > slots)
    def _():
        fetch_full(copy_sem, (attended_full, attended_ref), (query_full, query_out))


def per_device(queries, key_rows, value_rows, out_grad, tile_ids, tile_mask):
    row_count = queries.shape[0]
    heads = queries.shape[1] // HD
    ranks = lax.axis_size("seq")
    chips = ranks // 2
    assert key_rows.shape[1] == HD and ranks > 1 and ranks & (ranks - 1) == 0
    tiles = row_count // TILE
    tile_total = tile_ids.shape[0]
    slots = tiles
    rounds = math.ceil(tile_total / slots)
    slot_shape = (slots, TILE, HD)
    buffer = (rounds - 1, 2) + slot_shape
    shape = jax.ShapeDtypeStruct
    bf16, f32 = jnp.bfloat16, jnp.float32

    def swap(values, step):
        return lax.ppermute(values, "seq", [(source, source ^ step) for source in range(ranks)])

    def across(values):
        return [swap(values, 2 * step) for step in range(1, chips)]

    def trade(full, half):
        got = []
        for pair in pairs_of(chips):
            routes = [(source, source ^ 2 * pair[source % 2]) for source in range(ranks)]
            got.append(lax.ppermute(full, "seq", routes))
        return got + [swap(half, 2 * (chips - 1))]

    def add(*values):
        total = values[0].astype(f32)
        for value in values[1:]:
            total = total + value.astype(f32)
        return total.astype(bf16)

    assert tile_total <= 32
    bits = jnp.where(tile_mask == 1, 1 << jnp.arange(tile_total, dtype=jnp.int32), 0)
    table = jnp.stack([jnp.sum(bits, axis=1, dtype=jnp.int32), tile_ids])
    key_other, value_other = swap(key_rows, 1), swap(value_rows, 1)
    chip_rows = (key_rows, value_rows, key_other, value_other)
    info, spare, key_here, value_here = call(
        functools.partial(list_kernel, tile_total, tiles, slots),
        [SMEM_SPEC] + [ANY_SPEC] * 2,
        (
            shape((info_size(tile_total, tiles, slots),), jnp.int32),
            shape(buffer, bf16),
            shape(key_rows.shape, bf16),
            shape(value_rows.shape, bf16),
        ),
        (SMEM_SPEC, ANY_SPEC, VMEM_SPEC, VMEM_SPEC),
        scratch=(pltpu.SemaphoreType.DMA, pltpu.SemaphoreType.DMA),
        moved=4 * 1024 * 1024,
    )(table, key_rows, value_rows)
    chosen, chosen_half = call(
        functools.partial(first_kernel, tiles, slots),
        [SMEM_SPEC] + [VMEM_SPEC] * 4,
        (shape((2 * slots, TILE, HD), bf16), shape(slot_shape, bf16)),
        (VMEM_SPEC,) * 2,
        moved=5 * row_count * HD * 2,
    )(info, key_here, value_here, key_other, value_other)
    used = (info[0] + slots - 1) // slots

    def select(index):
        return call(
            functools.partial(select_kernel, tiles, slots),
            [SMEM_SPEC] * 2 + [VMEM_SPEC] * 4,
            shape(slot_shape, bf16),
            VMEM_SPEC,
            moved=5 * row_count * HD * 2,
        )(info, index.reshape(1), *chip_rows)

    arrived = trade(chosen, chosen_half)
    handed = [swap(values, 1) for values in arrived]

    def gather_more(index, buffered):
        chosen = select(index)
        total = add(chosen, *across(chosen))
        pair = jnp.stack([total, swap(total, 1)])
        return lax.dynamic_update_index_in_dim(buffered, pair, index - 1, 0)

    more = lax.fori_loop(1, used, gather_more, spare)

    all_rows = row_count + rounds * slots * TILE
    columns = heads * row_count
    line = shape((1, columns), f32)
    work = 2 * columns * row_count * HD
    max_own, total_own, weighted, grad_t = call(
        functools.partial(own_kernel, tiles, slots, heads, tile_total),
        [SMEM_SPEC] + [VMEM_SPEC] * 4,
        (line, line, shape((HD, columns), f32), shape((HD, columns), bf16)),
        (VMEM_SPEC,) * 4,
        scratch=(pltpu.VMEM((row_count, row_count), f32),),
        flops=24 * work,
        moved=4 * row_count * heads * HD,
    )(info, queries, out_grad, key_rows, value_rows)

    full = (
        shape(queries.shape, bf16),
        shape(queries.shape, f32),
        shape(key_rows.shape, f32),
        shape(value_rows.shape, f32),
    )
    parts, row_max, inverse, delta, out_t, dscores, slot_keys, more_terms, *full_values = call(
        functools.partial(gathered_kernel, chips, tiles, slots, heads, tile_total),
        [SMEM_SPEC, ANY_SPEC]
        + [VMEM_SPEC] * 2
        + [ANY_SPEC] * 2
        + [VMEM_SPEC] * 6
        + [ANY_SPEC]
        + [VMEM_SPEC] * (2 * len(arrived)),
        (
            shape((2 * slots, TILE, HD), bf16),
            line,
            line,
            line,
            shape((HD, columns), bf16),
            shape((slots * TILE, columns), bf16),
            shape((slots * TILE, HD), bf16),
            shape(buffer, bf16),
        )
        + full,
        (VMEM_SPEC,) * 7 + (ANY_SPEC,) * 5,
        scratch=(
            pltpu.VMEM((all_rows, row_count), f32),
            pltpu.VMEM((2, all_rows, HD), bf16),
            pltpu.VMEM((2, all_rows, HD), f32),
            pltpu.VMEM((all_rows, row_count), f32),
            pltpu.VMEM((2,) + slot_shape, bf16),
            pltpu.VMEM(queries.shape, bf16),
            pltpu.VMEM(queries.shape, f32),
            pltpu.SMEM(table.shape, jnp.int32),
            pltpu.SemaphoreType.DMA,
        ),
        flops=24 * work,
        moved=4 * row_count * heads * HD,
    )(
        info,
        table,
        queries,
        out_grad,
        *chip_rows,
        max_own,
        total_own,
        weighted,
        grad_t,
        more,
        *arrived,
        *handed,
    )

    partner = swap(parts, 1)
    half_sum = add(parts[:slots], partner[slots:])
    chip_sum = jnp.concatenate([half_sum, add(parts[slots:], partner[:slots])])
    own_dscores, key_own, value_own, half_sum = call(
        functools.partial(own_grads_kernel, tiles, slots, heads, tile_total),
        [SMEM_SPEC] + [VMEM_SPEC] * 7 + [ANY_SPEC] * 3,
        (shape((row_count, columns), bf16), *full[2:], shape(slot_shape, bf16)),
        (VMEM_SPEC,) * 3 + (ANY_SPEC,),
        scratch=(pltpu.VMEM((row_count, row_count), f32), pltpu.SemaphoreType.DMA),
        flops=18 * work,
        moved=4 * row_count * heads * HD,
        aliases={10: 3},
    )(
        info,
        queries,
        out_grad,
        key_rows,
        value_rows,
        row_max,
        inverse,
        delta,
        *full_values[2:],
        half_sum,
    )
    back = trade(chip_sum, half_sum)
    attended, query_grad, back[0] = call(
        functools.partial(queries_kernel, slots, heads),
        [SMEM_SPEC] + [VMEM_SPEC] * 5 + [ANY_SPEC] * 3,
        (*full[:2], shape(back[0].shape, bf16)),
        (VMEM_SPEC,) * 2 + (ANY_SPEC,),
        scratch=(pltpu.SemaphoreType.DMA,),
        flops=16 * work,
        moved=8 * row_count * heads * HD,
        aliases={8: 2},
    )(info, key_rows, own_dscores, dscores, slot_keys, out_t, *full_values[:2], back[0])
    sums = [chip_sum] + back + [swap(values, 1) for values in back]

    def close(kernel, lead, grads, sums):
        return call(
            kernel,
            [SMEM_SPEC] * len(lead) + [VMEM_SPEC] * (2 + len(sums)),
            (shape(key_rows.shape, f32), shape(value_rows.shape, f32)),
            (VMEM_SPEC,) * 2,
            moved=5 * row_count * HD * 4,
        )(*lead, *grads, *sums)

    def reduce_more(index, grads):
        terms = lax.dynamic_index_in_dim(more_terms, index - 1, 0, keepdims=False)
        part = add(terms[0], swap(terms[1], 1))
        total = add(part, *across(part))
        kernel = functools.partial(later_kernel, tiles, slots, tile_total)
        return tuple(close(kernel, (info, index.reshape(1)), grads, (total, swap(total, 1))))

    kernel = functools.partial(close_kernel, tiles, slots, chips, tile_total)
    grads = tuple(close(kernel, (info,), (key_own, value_own), sums))
    key_grad, value_grad = lax.fori_loop(1, used, reduce_more, grads)
    return attended, query_grad, key_grad, value_grad


def solution(mesh):
    return jax.shard_map(
        per_device,
        mesh=mesh,
        in_specs=(
            P(("batch", "seq"), "head"),
            P(("batch", "seq"), "head"),
            P(("batch", "seq"), "head"),
            P(("batch", "seq"), "head"),
            P("batch"),
            P("batch", None),
        ),
        out_specs=(P(("batch", "seq"), "head"),) * 4,
        check_vma=False,
    )
```

```python
import functools
import math

import jax
import jax.numpy as jnp
from jax import lax
from jax.experimental import pallas as pl
from jax.experimental.pallas import tpu as pltpu
from jax.sharding import PartitionSpec as P

HD = 128
TILE = 128
FAR_BELOW = -1e30
LOG2E = 1.4426950408889634
NT_DIMS = (((1,), (1,)), ((), ()))
VMEM_LIMIT = 32 * 1024 * 1024

SMEM_SPEC = pl.BlockSpec(memory_space=pltpu.SMEM)
VMEM_SPEC = pl.BlockSpec(memory_space=pltpu.VMEM)
ANY_SPEC = pl.BlockSpec(memory_space=pl.ANY)


def call(kernel, in_specs, out_shape, out_specs, scratch=(), flops=0, moved=0, aliases=None):
    return pl.pallas_call(
        kernel,
        in_specs=in_specs,
        out_shape=out_shape,
        out_specs=out_specs,
        scratch_shapes=list(scratch),
        input_output_aliases=aliases or {},
        compiler_params=pltpu.CompilerParams(vmem_limit_bytes=VMEM_LIMIT),
        cost_estimate=pl.CostEstimate(flops=flops, bytes_accessed=moved, transcendentals=0),
    )


def tile_rows(first_row, tile):
    return pl.ds(pl.multiple_of(first_row + tile * TILE, TILE), TILE)


def info_size(tile_total, tiles, slots):
    return 2 * tile_total + 2 + (slots + tiles) * tiles


def pairs_of(chips):
    return [(step, step + 1) for step in range(1, chips - 1, 2)]


def list_kernel(tile_total, tiles, slots, table_ref, info_ref, spare_ref, any_ref):
    del spare_ref
    rank = lax.axis_index("seq")

    def ids(position):
        return table_ref[tile_total, position]

    def mask(query_tile, key_tile):
        return table_ref[query_tile, key_tile]

    for place in range(1, tile_total + 2):
        info_ref[place] = 0
    for tile in range(tile_total):
        users = mask(0, tile)
        for other in range(1, tile_total):
            users = users + mask(other, tile)
        any_ref[tile] = users
    count = jnp.int32(0)
    for position in range(tile_total):
        key_tile = ids(position)
        away = any_ref[key_tile]
        for local in range(tiles):
            away = away - mask(ids(position // tiles * tiles + local), key_tile)
        info_ref[1 + count] = position
        info_ref[tile_total + 2 + position] = jnp.where(away > 0, count, -1)
        count = count + jnp.where(away > 0, 1, 0)
    info_ref[0] = count
    my_tiles = [ids(rank * tiles + b) for b in range(tiles)]
    place = 2 * tile_total + 2
    for slot in range(slots):
        position = info_ref[1 + slot]
        usable = ((slot < count) & (position // tiles != rank)).astype(jnp.int32)
        for b in range(tiles):
            info_ref[place] = usable * mask(my_tiles[b], ids(position))
            place += 1
    for a in range(tiles):
        for b in range(tiles):
            info_ref[place] = mask(my_tiles[b], my_tiles[a])
            place += 1

def first_kernel(tiles, slots, info_ref, *refs):
    sources, (full_ref, half_ref) = refs[:4], refs[4:]
    odd = lax.axis_index("seq") % 2
    for kind in range(2):
        part = odd ^ kind
        target = full_ref.at[pl.ds(part * slots, slots)]
        pick(tiles, slots, 0, info_ref, sources[kind], sources[2 + kind], target)
    half_ref[...] = full_ref[:slots]


def pick(tiles, slots, base, info_ref, own_ref, other_ref, out_ref):
    rank = lax.axis_index("seq")
    for slot in range(slots):
        position = info_ref[1 + base + slot]
        home = position // tiles
        rows = tile_rows(0, position % tiles)
        out_ref[slot] = jnp.zeros_like(out_ref[slot])

        @pl.when(home == rank)
        def _():
            out_ref[slot] = own_ref[rows, :]

        @pl.when(home == rank ^ 1)
        def _():
            out_ref[slot] = other_ref[rows, :]


def select_kernel(tiles, slots, info_ref, round_ref, *refs):
    key_ref, value_ref, key_other, value_other, out_ref = refs
    rank = lax.axis_index("seq")
    for kind, own, other in ((0, key_ref, key_other), (1, value_ref, value_other)):

        @pl.when(rank % 2 == kind)
        def _():
            pick(tiles, slots, round_ref[0] * slots, info_ref, own, other, out_ref)


def add_sums(tiles, slots, tile_total, base, info_ref, grads, outs, sums_of):
    rank = lax.axis_index("seq")
    odd = rank % 2
    for grad, out in zip(grads, outs):
        out[...] = grad[...]
    for tile in range(tiles):
        slot = info_ref[tile_total + 2 + rank * tiles + tile] - base
        rows = tile_rows(0, tile)

        @pl.when((slot >= 0) & (slot < slots))
        def _():
            totals = []
            for part in range(2):
                total = None
                for source in sums_of(part, slot):
                    source = source.astype(jnp.float32)
                    total = source if total is None else total + source
                totals.append(total)
            for kind, out in enumerate(outs):
                out[rows, :] += jnp.where(odd == kind, totals[0], totals[1])


def close_kernel(tiles, slots, chips, tile_total, info_ref, *refs):
    grads, (chip_ref, *sums), outs = refs[:2], refs[2:-2], refs[-2:]
    half = len(sums) // 2
    arrived, handed = sums[:half], sums[half:]

    def sums_of(part, slot):
        yield chip_ref[part * slots + slot]
        for own, other in zip(arrived[:-1], handed[:-1]):
            yield own[part * slots + slot]
            yield other[(1 - part) * slots + slot]
        yield (handed if part else arrived)[-1][slot]

    add_sums(tiles, slots, tile_total, 0, info_ref, grads, outs, sums_of)


def later_kernel(tiles, slots, tile_total, info_ref, round_ref, *refs):
    grads, sums, outs = refs[:2], refs[2:-2], refs[-2:]

    def sums_of(part, slot):
        yield sums[part][slot]

    base = round_ref[0] * slots
    add_sums(tiles, slots, tile_total, base, info_ref, grads, outs, sums_of)


def causal_bias():
    later = lax.broadcasted_iota(jnp.int32, (TILE, TILE), 1)
    return jnp.where(lax.broadcasted_iota(jnp.int32, (TILE, TILE), 0) <= later, 0.0, FAR_BELOW)


def block_bias(allowed):
    return jnp.full((TILE, TILE), jnp.where(allowed, 0.0, FAR_BELOW), jnp.float32)


def own_bias(tiles, bias_ref, allowed):
    for a in range(tiles):
        for b in range(tiles):
            bias = causal_bias() if a == b else block_bias(allowed(a, b) == 1)
            bias_ref[pl.ds(a * TILE, TILE), pl.ds(b * TILE, TILE)] = bias


def stacked(ref, heads):
    return jnp.concatenate([ref[:, h * HD : (h + 1) * HD] for h in range(heads)], axis=0)


def dot(one, other):
    return jnp.dot(one, other, preferred_element_type=jnp.float32)


def dot_t(one, other):
    return lax.dot_general(one, other, NT_DIMS, preferred_element_type=jnp.float32)


def own_scores(tiles, slots, heads, tile_total, info_ref, bias_ref, keys, query):
    place = 2 * tile_total + 2 + slots * tiles
    own_bias(tiles, bias_ref, lambda a, b: info_ref[place + a * tiles + b])
    bias = jnp.concatenate([bias_ref[...]] * heads, axis=1)
    return dot_t(keys, query) * (HD**-0.5 * LOG2E) + bias


def own_kernel(
    tiles,
    slots,
    heads,
    tile_total,
    info_ref,
    query_ref,
    grad_ref,
    key_ref,
    value_ref,
    max_ref,
    total_ref,
    weighted_ref,
    grad_t_ref,
    bias_ref,
):
    query = stacked(query_ref, heads)
    scores = own_scores(tiles, slots, heads, tile_total, info_ref, bias_ref, key_ref[...], query)
    row_max = jnp.max(scores, axis=0, keepdims=True)
    terms = jnp.exp2(scores - row_max)
    max_ref[...] = row_max
    total_ref[...] = jnp.sum(terms, axis=0, keepdims=True)
    weighted_ref[...] = dot(value_ref[...].T, terms.astype(jnp.bfloat16))
    grad_t_ref[...] = stacked(grad_ref, heads).T


def gathered_kernel(
    chips,
    tiles,
    slots,
    heads,
    tile_total,
    info_ref,
    table_any,
    query_ref,
    grad_ref,
    key_any,
    value_any,
    key_other,
    value_other,
    max_own,
    total_own,
    weighted_own,
    grad_t_ref,
    more_ref,
    *refs,
):
    count = len(pairs_of(chips)) + 1
    arrived, handed, refs = refs[:count], refs[count : 2 * count], refs[2 * count :]
    parts_ref, kept_ref, max_ref, inverse_ref, delta_ref, out_t_ref, dscores_ref, *refs = refs
    slot_keys, *refs = refs
    more_out, attended_full, query_full, key_full, value_full, *refs = refs
    bias_ref, held_ref, sum_ref, score_ref, staged_ref, *refs = refs
    attended_ref, query_out, table_ref, copy_sem = refs
    keys_ref, values_ref = held_ref.at[0], held_ref.at[1]
    key_sum, value_sum = sum_ref.at[0], sum_ref.at[1]
    rank = lax.axis_index("seq")
    odd = rank % 2
    rows = tiles * TILE
    chunk = slots * TILE
    factor = HD**-0.5
    scale = factor * LOG2E
    needed = info_ref[0]
    columns = [pl.ds(h * HD, HD) for h in range(heads)]

    def repack(target, part, first_row):
        kind = odd ^ part
        for slot in range(slots):
            total = sum_ref[kind, tile_rows(first_row, slot), :]
            target[slot] = (total * jnp.where(kind == 0, factor, 1.0)).astype(jnp.bfloat16)

    for slot in range(slots):
        for b in range(tiles):
            allowed = info_ref[2 * tile_total + 2 + slot * tiles + b] == 1
            bias_ref[pl.ds(slot * TILE, TILE), pl.ds(b * TILE, TILE)] = block_bias(allowed)
        position = info_ref[1 + slot]
        away = (position // (2 * tiles)) ^ (rank // 2)
        at = tile_rows(0, slot)

        @pl.when(away == 0)
        def _():
            source = tile_rows(0, position % tiles)
            keys_ref[at, :] = key_other[source, :]
            values_ref[at, :] = value_other[source, :]

        @pl.when(away == chips - 1)
        def _():
            held_ref[odd, at, :] = arrived[-1][slot]
            held_ref[odd ^ 1, at, :] = handed[-1][slot]

        for index, pair in enumerate(pairs_of(chips)):
            for core, step in enumerate(pair):

                @pl.when((away == step) & (odd == core))
                def _():
                    held_ref[odd, at, :] = arrived[index][slot]
                    held_ref[odd ^ 1, at, :] = arrived[index][slots + slot]

                @pl.when((away == step) & (odd != core))
                def _():
                    held_ref[odd ^ 1, at, :] = handed[index][slot]
                    held_ref[odd, at, :] = handed[index][slots + slot]

    first = pl.ds(0, chunk)

    @pl.when(needed <= slots)
    def _():
        keys = keys_ref[first, :]
        values = values_ref[first, :]
        slot_keys[...] = keys
        values_t = values.T
        per_block = heads // 2 if heads % 2 == 0 else heads
        width = per_block * rows
        blocks = range(heads // per_block)
        bias = jnp.concatenate([bias_ref[first, :]] * per_block, axis=1)
        spans = [pl.ds(block * width, width) for block in blocks]
        query_all = stacked(query_ref, heads)
        grad_all = stacked(grad_ref, heads)
        query = [query_all[block * width : (block + 1) * width] for block in blocks]
        grad = [grad_all[block * width : (block + 1) * width] for block in blocks]
        scores = [dot_t(keys, query[block]) * scale + bias for block in blocks]
        dprobs, probs, outs = [], [], []
        for block, span in zip(blocks, spans):
            dprobs.append(dot_t(values, grad[block]))
            old_max = max_own[:, span]
            row_max = jnp.maximum(old_max, jnp.max(scores[block], axis=0, keepdims=True))
            shrink = jnp.exp2(old_max - row_max)
            terms = jnp.exp2(scores[block] - row_max)
            total = total_own[:, span] * shrink + jnp.sum(terms, axis=0, keepdims=True)
            inverse = 1.0 / total
            weighted = dot(values_t, terms.astype(jnp.bfloat16))
            outs.append((shrink * inverse, inverse, weighted))
            probs.append(terms * inverse)
            max_ref[:, span] = row_max
            inverse_ref[:, span] = inverse
        key_total, value_total = None, None
        for block, span in zip(blocks, spans):
            part = dot(probs[block].astype(jnp.bfloat16), grad[block])
            value_total = part if value_total is None else value_total + part
            shrunk, inverse, weighted = outs[block]
            out = (weighted_own[:, span] * shrunk + weighted * inverse).astype(jnp.bfloat16)
            out_t_ref[:, span] = out
            delta = jnp.sum(
                grad_t_ref[:, span].astype(jnp.float32) * out.astype(jnp.float32),
                axis=0,
                keepdims=True,
            )
            delta_ref[:, span] = delta
            dscores = (probs[block] * (dprobs[block] - delta)).astype(jnp.bfloat16)
            dscores_ref[:, span] = dscores
            part = dot(dscores, query[block])
            key_total = part if key_total is None else key_total + part
        key_sum[first, :] = key_total
        value_sum[first, :] = value_total

    @pl.when(needed > slots)
    def _():
        used = (needed + slots - 1) // slots
        own_first = pl.multiple_of(used * chunk, chunk)
        own_rows = pl.ds(own_first, rows)
        copy = pltpu.make_async_copy(table_any, table_ref, copy_sem)
        copy.start()
        copy.wait()

        def ids(position):
            return table_ref[tile_total, position]

        def allowed(a, b):
            return table_ref[ids(rank * tiles + b), ids(rank * tiles + a)]

        own_bias(tiles, bias_ref.at[own_rows, :], allowed)
        for source, target in ((key_any, keys_ref), (value_any, values_ref)):
            copy = pltpu.make_async_copy(source, target.at[own_rows, :], copy_sem)
            copy.start()
            copy.wait()

        def fetch(index, carry):
            copy = pltpu.make_async_copy(more_ref.at[index - 1], staged_ref, copy_sem)
            copy.start()
            copy.wait()
            first_row = pl.multiple_of(index * chunk, chunk)
            for slot in range(slots):
                for part in range(2):
                    held_ref[odd ^ part, tile_rows(first_row, slot), :] = staged_ref[part, slot]
                listed = index * slots + slot
                position = info_ref[1 + listed]
                usable = (listed < needed) & (position // tiles != rank)
                for b in range(tiles):
                    seen = table_ref[ids(rank * tiles + b), ids(position)] == 1
                    bias_ref[tile_rows(first_row, slot), pl.ds(b * TILE, TILE)] = block_bias(
                        usable & seen
                    )
            return carry

        lax.fori_loop(1, used, fetch, 0)
        key_sum[...] = jnp.zeros_like(key_sum)
        value_sum[...] = jnp.zeros_like(value_sum)
        blocks = used * slots + tiles

        for h in range(heads):
            query = query_ref[:, columns[h]]
            grad = grad_ref[:, columns[h]]

            def score(index, row_max):
                at = tile_rows(0, index)
                scores = dot_t(keys_ref[at, :], query) * scale + bias_ref[at, :]
                score_ref[at, :] = scores
                return jnp.maximum(row_max, jnp.max(scores, axis=0, keepdims=True))

            row_max = lax.fori_loop(0, blocks, score, jnp.full((1, rows), FAR_BELOW, jnp.float32))

            def forward(index, carry):
                total, weighted = carry
                at = tile_rows(0, index)
                terms = jnp.exp2(score_ref[at, :] - row_max)
                score_ref[at, :] = terms
                weighted = weighted + dot(values_ref[at, :].T, terms.astype(jnp.bfloat16))
                return total + jnp.sum(terms, axis=0, keepdims=True), weighted

            zeros = jnp.zeros((HD, rows), jnp.float32)
            start = (jnp.zeros((1, rows), jnp.float32), zeros)
            total, weighted = lax.fori_loop(0, blocks, forward, start)
            inverse = 1.0 / total
            out = (weighted * inverse).astype(jnp.bfloat16)
            attended_ref[:, columns[h]] = out.T
            grad_t = grad_t_ref[:, pl.ds(h * rows, rows)].astype(jnp.float32)
            delta = jnp.sum(grad_t * out.astype(jnp.float32), axis=0, keepdims=True)

            def backward(index, query_t):
                at = tile_rows(0, index)
                probs = score_ref[at, :] * inverse
                dprobs = dot_t(values_ref[at, :], grad)
                dscores = (probs * (dprobs - delta)).astype(jnp.bfloat16)
                key_sum[at, :] += dot(dscores, query)
                value_sum[at, :] += dot(probs.astype(jnp.bfloat16), grad)
                return query_t + dot(keys_ref[at, :].T, dscores)

            query_t = lax.fori_loop(0, blocks, backward, zeros)
            query_out[:, columns[h]] = (query_t * factor).T

        key_sum[own_rows, :] = key_sum[own_rows, :] * factor
        for source, target in (
            (attended_ref, attended_full),
            (query_out, query_full),
            (key_sum.at[own_rows, :], key_full),
            (value_sum.at[own_rows, :], value_full),
        ):
            copy = pltpu.make_async_copy(source, target, copy_sem)
            copy.start()
            copy.wait()

        def store(index, carry):
            for part in range(2):
                repack(staged_ref.at[part], part, pl.multiple_of(index * chunk, chunk))
            copy = pltpu.make_async_copy(staged_ref, more_out.at[index - 1], copy_sem)
            copy.start()
            copy.wait()
            return carry

        lax.fori_loop(1, used, store, 0)

    for part in range(2):
        repack(parts_ref.at[pl.ds(part * slots, slots)], part, 0)
    kept_ref[...] = parts_ref[...]


def fetch_full(copy_sem, *pairs):
    for source, target in pairs:
        copy = pltpu.make_async_copy(source, target, copy_sem)
        copy.start()
        copy.wait()


def own_grads_kernel(
    tiles,
    slots,
    heads,
    tile_total,
    info_ref,
    query_ref,
    grad_ref,
    key_ref,
    value_ref,
    max_ref,
    inverse_ref,
    delta_ref,
    key_full,
    value_full,
    order_ref,
    dscores_ref,
    key_out,
    value_out,
    order_out,
    bias_ref,
    copy_sem,
):
    del order_ref, order_out

    @pl.when(info_ref[0] <= slots)
    def _():
        query = stacked(query_ref, heads)
        grad = stacked(grad_ref, heads)
        scores = own_scores(
            tiles, slots, heads, tile_total, info_ref, bias_ref, key_ref[...], query
        )
        probs = jnp.exp2(scores - max_ref[...]) * inverse_ref[...]
        dprobs = dot_t(value_ref[...], grad)
        dscores = (probs * (dprobs - delta_ref[...])).astype(jnp.bfloat16)
        dscores_ref[...] = dscores
        value_out[...] = dot(probs.astype(jnp.bfloat16), grad)
        key_out[...] = dot(dscores, query) * HD**-0.5

    @pl.when(info_ref[0] > slots)
    def _():
        fetch_full(copy_sem, (key_full, key_out), (value_full, value_out))


def queries_kernel(
    slots,
    heads,
    info_ref,
    key_ref,
    own_dscores,
    slot_dscores,
    slot_keys,
    out_t_ref,
    attended_full,
    query_full,
    order_ref,
    attended_ref,
    query_out,
    order_out,
    copy_sem,
):
    del order_ref, order_out
    rows = query_out.shape[0]

    @pl.when(info_ref[0] <= slots)
    def _():
        query_t = dot(key_ref[...].T, own_dscores[...])
        query_t = (query_t + dot(slot_keys[...].T, slot_dscores[...])) * HD**-0.5
        for h in range(heads):
            columns = pl.ds(h * HD, HD)
            attended_ref[:, columns] = out_t_ref[:, pl.ds(h * rows, rows)].T
            query_out[:, columns] = query_t[:, h * rows : (h + 1) * rows].T

    @pl.when(info_ref[0] > slots)
    def _():
        fetch_full(copy_sem, (attended_full, attended_ref), (query_full, query_out))


def per_device(queries, key_rows, value_rows, out_grad, tile_ids, tile_mask):
    row_count = queries.shape[0]
    heads = queries.shape[1] // HD
    ranks = lax.axis_size("seq")
    chips = ranks // 2
    assert key_rows.shape[1] == HD and ranks > 1 and ranks & (ranks - 1) == 0
    tiles = row_count // TILE
    tile_total = tile_ids.shape[0]
    slots = tiles
    rounds = math.ceil(tile_total / slots)
    slot_shape = (slots, TILE, HD)
    buffer = (rounds - 1, 2) + slot_shape
    shape = jax.ShapeDtypeStruct
    bf16, f32 = jnp.bfloat16, jnp.float32

    def swap(values, step):
        return lax.ppermute(values, "seq", [(source, source ^ step) for source in range(ranks)])

    def across(values):
        return [swap(values, 2 * step) for step in range(1, chips)]

    def trade(full, half):
        got = []
        for pair in pairs_of(chips):
            routes = [(source, source ^ 2 * pair[source % 2]) for source in range(ranks)]
            got.append(lax.ppermute(full, "seq", routes))
        return got + [swap(half, 2 * (chips - 1))]

    def add(*values):
        total = values[0].astype(f32)
        for value in values[1:]:
            total = total + value.astype(f32)
        return total.astype(bf16)

    table = jnp.pad(tile_mask, ((0, 1), (0, 0)))
    table = table + jnp.pad(tile_ids[None], ((tile_total, 0), (0, 0)))
    key_other, value_other = swap(key_rows, 1), swap(value_rows, 1)
    chip_rows = (key_rows, value_rows, key_other, value_other)
    info, spare = call(
        functools.partial(list_kernel, tile_total, tiles, slots),
        [SMEM_SPEC],
        (shape((info_size(tile_total, tiles, slots),), jnp.int32), shape(buffer, bf16)),
        (SMEM_SPEC, ANY_SPEC),
        scratch=(pltpu.SMEM((tile_total,), jnp.int32),),
        moved=4 * 1024 * 1024,
    )(table)
    chosen, chosen_half = call(
        functools.partial(first_kernel, tiles, slots),
        [SMEM_SPEC] + [VMEM_SPEC] * 4,
        (shape((2 * slots, TILE, HD), bf16), shape(slot_shape, bf16)),
        (VMEM_SPEC,) * 2,
        moved=5 * row_count * HD * 2,
    )(info, *chip_rows)
    used = (info[0] + slots - 1) // slots

    def select(index):
        return call(
            functools.partial(select_kernel, tiles, slots),
            [SMEM_SPEC] * 2 + [VMEM_SPEC] * 4,
            shape(slot_shape, bf16),
            VMEM_SPEC,
            moved=5 * row_count * HD * 2,
        )(info, index.reshape(1), *chip_rows)

    arrived = trade(chosen, chosen_half)
    handed = [swap(values, 1) for values in arrived]

    def gather_more(index, buffered):
        chosen = select(index)
        total = add(chosen, *across(chosen))
        pair = jnp.stack([total, swap(total, 1)])
        return lax.dynamic_update_index_in_dim(buffered, pair, index - 1, 0)

    more = lax.fori_loop(1, used, gather_more, spare)

    all_rows = row_count + rounds * slots * TILE
    columns = heads * row_count
    line = shape((1, columns), f32)
    work = 2 * columns * row_count * HD
    max_own, total_own, weighted, grad_t = call(
        functools.partial(own_kernel, tiles, slots, heads, tile_total),
        [SMEM_SPEC] + [VMEM_SPEC] * 4,
        (line, line, shape((HD, columns), f32), shape((HD, columns), bf16)),
        (VMEM_SPEC,) * 4,
        scratch=(pltpu.VMEM((row_count, row_count), f32),),
        flops=24 * work,
        moved=4 * row_count * heads * HD,
    )(info, queries, out_grad, key_rows, value_rows)

    full = (
        shape(queries.shape, bf16),
        shape(queries.shape, f32),
        shape(key_rows.shape, f32),
        shape(value_rows.shape, f32),
    )
    parts, kept, row_max, inverse, delta, out_t, dscores, slot_keys, more_terms, *full_values = call(
        functools.partial(gathered_kernel, chips, tiles, slots, heads, tile_total),
        [SMEM_SPEC, ANY_SPEC]
        + [VMEM_SPEC] * 2
        + [ANY_SPEC] * 2
        + [VMEM_SPEC] * 6
        + [ANY_SPEC]
        + [VMEM_SPEC] * (2 * len(arrived)),
        (
            shape((2 * slots, TILE, HD), bf16),
            shape((2 * slots, TILE, HD), bf16),
            line,
            line,
            line,
            shape((HD, columns), bf16),
            shape((slots * TILE, columns), bf16),
            shape((slots * TILE, HD), bf16),
            shape(buffer, bf16),
        )
        + full,
        (VMEM_SPEC,) * 8 + (ANY_SPEC,) * 5,
        scratch=(
            pltpu.VMEM((all_rows, row_count), f32),
            pltpu.VMEM((2, all_rows, HD), bf16),
            pltpu.VMEM((2, all_rows, HD), f32),
            pltpu.VMEM((all_rows, row_count), f32),
            pltpu.VMEM((2,) + slot_shape, bf16),
            pltpu.VMEM(queries.shape, bf16),
            pltpu.VMEM(queries.shape, f32),
            pltpu.SMEM(table.shape, jnp.int32),
            pltpu.SemaphoreType.DMA,
        ),
        flops=24 * work,
        moved=4 * row_count * heads * HD,
    )(
        info,
        table,
        queries,
        out_grad,
        *chip_rows,
        max_own,
        total_own,
        weighted,
        grad_t,
        more,
        *arrived,
        *handed,
    )

    partner = swap(parts, 1)
    own_dscores, key_own, value_own, kept = call(
        functools.partial(own_grads_kernel, tiles, slots, heads, tile_total),
        [SMEM_SPEC] + [VMEM_SPEC] * 7 + [ANY_SPEC] * 3,
        (shape((row_count, columns), bf16), *full[2:], shape(kept.shape, bf16)),
        (VMEM_SPEC,) * 3 + (ANY_SPEC,),
        scratch=(pltpu.VMEM((row_count, row_count), f32), pltpu.SemaphoreType.DMA),
        flops=18 * work,
        moved=4 * row_count * heads * HD,
        aliases={10: 3},
    )(
        info,
        queries,
        out_grad,
        key_rows,
        value_rows,
        row_max,
        inverse,
        delta,
        *full_values[2:],
        kept,
    )
    half_sum = add(kept[:slots], partner[slots:])
    chip_sum = jnp.concatenate([half_sum, add(kept[slots:], partner[:slots])])
    back = trade(chip_sum, half_sum)
    attended, query_grad, back[0] = call(
        functools.partial(queries_kernel, slots, heads),
        [SMEM_SPEC] + [VMEM_SPEC] * 5 + [ANY_SPEC] * 3,
        (*full[:2], shape(back[0].shape, bf16)),
        (VMEM_SPEC,) * 2 + (ANY_SPEC,),
        scratch=(pltpu.SemaphoreType.DMA,),
        flops=16 * work,
        moved=8 * row_count * heads * HD,
        aliases={8: 2},
    )(info, key_rows, own_dscores, dscores, slot_keys, out_t, *full_values[:2], back[0])
    sums = [chip_sum] + back + [swap(values, 1) for values in back]

    def close(kernel, lead, grads, sums):
        return call(
            kernel,
            [SMEM_SPEC] * len(lead) + [VMEM_SPEC] * (2 + len(sums)),
            (shape(key_rows.shape, f32), shape(value_rows.shape, f32)),
            (VMEM_SPEC,) * 2,
            moved=5 * row_count * HD * 4,
        )(*lead, *grads, *sums)

    def reduce_more(index, grads):
        terms = lax.dynamic_index_in_dim(more_terms, index - 1, 0, keepdims=False)
        part = add(terms[0], swap(terms[1], 1))
        total = add(part, *across(part))
        kernel = functools.partial(later_kernel, tiles, slots, tile_total)
        return tuple(close(kernel, (info, index.reshape(1)), grads, (total, swap(total, 1))))

    kernel = functools.partial(close_kernel, tiles, slots, chips, tile_total)
    grads = tuple(close(kernel, (info,), (key_own, value_own), sums))
    key_grad, value_grad = lax.fori_loop(1, used, reduce_more, grads)
    return attended, query_grad, key_grad, value_grad


def solution(mesh):
    return jax.shard_map(
        per_device,
        mesh=mesh,
        in_specs=(
            P(("batch", "seq"), "head"),
            P(("batch", "seq"), "head"),
            P(("batch", "seq"), "head"),
            P(("batch", "seq"), "head"),
            P("batch"),
            P("batch", None),
        ),
        out_specs=(P(("batch", "seq"), "head"),) * 4,
        check_vma=False,
    )
```

```python
import functools
import math

import jax
import jax.numpy as jnp
from jax import lax
from jax.experimental import pallas as pl
from jax.experimental.pallas import tpu as pltpu
from jax.sharding import PartitionSpec as P

HD = 128
TILE = 128
FAR_BELOW = -1e30
LOG2E = 1.4426950408889634
NT_DIMS = (((1,), (1,)), ((), ()))
VMEM_LIMIT = 32 * 1024 * 1024

SMEM_SPEC = pl.BlockSpec(memory_space=pltpu.SMEM)
VMEM_SPEC = pl.BlockSpec(memory_space=pltpu.VMEM)
ANY_SPEC = pl.BlockSpec(memory_space=pl.ANY)


def call(kernel, in_specs, out_shape, out_specs, scratch=(), flops=0, moved=0, aliases=None):
    return pl.pallas_call(
        kernel,
        in_specs=in_specs,
        out_shape=out_shape,
        out_specs=out_specs,
        scratch_shapes=list(scratch),
        input_output_aliases=aliases or {},
        compiler_params=pltpu.CompilerParams(vmem_limit_bytes=VMEM_LIMIT),
        cost_estimate=pl.CostEstimate(flops=flops, bytes_accessed=moved, transcendentals=0),
    )


def tile_rows(first_row, tile):
    return pl.ds(pl.multiple_of(first_row + tile * TILE, TILE), TILE)


def info_size(tile_total, tiles, slots):
    return 2 * tile_total + 2 + (slots + tiles) * tiles


def pairs_of(chips):
    return [(step, step + 1) for step in range(1, chips - 1, 2)]


def list_kernel(tile_total, tiles, slots, table_ref, info_ref, spare_ref, spare_sums_ref, any_ref):
    del spare_ref, spare_sums_ref
    rank = lax.axis_index("seq")

    def ids(position):
        return table_ref[tile_total, position]

    def mask(query_tile, key_tile):
        return table_ref[query_tile, key_tile]

    for place in range(1, tile_total + 2):
        info_ref[place] = 0
    for tile in range(tile_total):
        users = mask(0, tile)
        for other in range(1, tile_total):
            users = users + mask(other, tile)
        any_ref[tile] = users
    count = jnp.int32(0)
    for position in range(tile_total):
        key_tile = ids(position)
        away = any_ref[key_tile]
        for local in range(tiles):
            away = away - mask(ids(position // tiles * tiles + local), key_tile)
        info_ref[1 + count] = position
        info_ref[tile_total + 2 + position] = jnp.where(away > 0, count, -1)
        count = count + jnp.where(away > 0, 1, 0)
    info_ref[0] = count
    my_tiles = [ids(rank * tiles + b) for b in range(tiles)]
    place = 2 * tile_total + 2
    for slot in range(slots):
        position = info_ref[1 + slot]
        usable = ((slot < count) & (position // tiles != rank)).astype(jnp.int32)
        for b in range(tiles):
            info_ref[place] = usable * mask(my_tiles[b], ids(position))
            place += 1
    for a in range(tiles):
        for b in range(tiles):
            info_ref[place] = mask(my_tiles[b], my_tiles[a])
            place += 1

def first_kernel(tiles, slots, info_ref, *refs):
    sources, (full_ref, half_ref) = refs[:4], refs[4:]
    odd = lax.axis_index("seq") % 2
    for kind in range(2):
        part = odd ^ kind
        target = full_ref.at[pl.ds(part * slots, slots)]
        pick(tiles, slots, 0, info_ref, sources[kind], sources[2 + kind], target)
    half_ref[...] = full_ref[:slots]


def pick(tiles, slots, base, info_ref, own_ref, other_ref, out_ref):
    rank = lax.axis_index("seq")
    for slot in range(slots):
        position = info_ref[1 + base + slot]
        home = position // tiles
        rows = tile_rows(0, position % tiles)
        out_ref[slot] = jnp.zeros_like(out_ref[slot])

        @pl.when(home == rank)
        def _():
            out_ref[slot] = own_ref[rows, :]

        @pl.when(home == rank ^ 1)
        def _():
            out_ref[slot] = other_ref[rows, :]


def select_kernel(tiles, slots, info_ref, round_ref, *refs):
    key_ref, value_ref, key_other, value_other, out_ref = refs
    rank = lax.axis_index("seq")
    for kind, own, other in ((0, key_ref, key_other), (1, value_ref, value_other)):

        @pl.when(rank % 2 == kind)
        def _():
            pick(tiles, slots, round_ref[0] * slots, info_ref, own, other, out_ref)


def close_kernel(tiles, slots, chips, tile_total, info_ref, extra_ref, *refs):
    grads, (chip_ref, *sums) = refs[:2], refs[2:-8]
    outs, staged_ref, late_ref, sems = refs[-6:-4], refs[-4], refs[-3], refs[-2:]
    half = len(sums) // 2
    arrived, handed = sums[:half], sums[half:]
    rank = lax.axis_index("seq")
    odd = rank % 2

    def total_of(part, slot):
        total = chip_ref[part * slots + slot].astype(jnp.float32)
        for own, other in zip(arrived[:-1], handed[:-1]):
            total = total + own[part * slots + slot].astype(jnp.float32)
            total = total + other[(1 - part) * slots + slot].astype(jnp.float32)
        return total + (handed if part else arrived)[-1][slot].astype(jnp.float32)

    for tile in range(tiles):
        slot = info_ref[tile_total + 2 + rank * tiles + tile]
        rows = pl.ds(tile * TILE, TILE)

        def place(totals):
            copies = []
            for kind in range(2):
                total = jnp.where(odd == kind, totals[0], totals[1])
                staged_ref[kind] = grads[kind][rows, :] + total
                copies.append(
                    pltpu.make_async_copy(staged_ref.at[kind], outs[kind].at[rows, :], sems[kind])
                )
            for copy in copies:
                copy.start()
            for copy in copies:
                copy.wait()

        @pl.when((slot >= 0) & (slot < slots))
        def _():
            place([total_of(part, slot) for part in range(2)])

        @pl.when(slot >= slots)
        def _():
            for part in range(2):
                source = extra_ref.at[slot // slots - 1, part, slot % slots]
                copy = pltpu.make_async_copy(source, late_ref.at[part], sems[part])
                copy.start()
                copy.wait()
            place([late_ref[part].astype(jnp.float32) for part in range(2)])


def causal_bias():
    later = lax.broadcasted_iota(jnp.int32, (TILE, TILE), 1)
    return jnp.where(lax.broadcasted_iota(jnp.int32, (TILE, TILE), 0) <= later, 0.0, FAR_BELOW)


def block_bias(allowed):
    return jnp.full((TILE, TILE), jnp.where(allowed, 0.0, FAR_BELOW), jnp.float32)


def own_bias(tiles, bias_ref, allowed):
    for a in range(tiles):
        for b in range(tiles):
            bias = causal_bias() if a == b else block_bias(allowed(a, b) == 1)
            bias_ref[pl.ds(a * TILE, TILE), pl.ds(b * TILE, TILE)] = bias


def stacked(ref, heads):
    return jnp.concatenate([ref[:, h * HD : (h + 1) * HD] for h in range(heads)], axis=0)


def dot(one, other):
    return jnp.dot(one, other, preferred_element_type=jnp.float32)


def dot_t(one, other):
    return lax.dot_general(one, other, NT_DIMS, preferred_element_type=jnp.float32)


def own_scores(tiles, slots, heads, tile_total, info_ref, bias_ref, keys, query):
    place = 2 * tile_total + 2 + slots * tiles
    own_bias(tiles, bias_ref, lambda a, b: info_ref[place + a * tiles + b])
    bias = jnp.concatenate([bias_ref[...]] * heads, axis=1)
    return dot_t(keys, query) * (HD**-0.5 * LOG2E) + bias


def own_kernel(
    tiles,
    slots,
    heads,
    tile_total,
    info_ref,
    query_ref,
    grad_ref,
    key_ref,
    value_ref,
    max_ref,
    total_ref,
    weighted_ref,
    grad_t_ref,
    bias_ref,
):
    query = stacked(query_ref, heads)
    scores = own_scores(tiles, slots, heads, tile_total, info_ref, bias_ref, key_ref[...], query)
    row_max = jnp.max(scores, axis=0, keepdims=True)
    terms = jnp.exp2(scores - row_max)
    max_ref[...] = row_max
    total_ref[...] = jnp.sum(terms, axis=0, keepdims=True)
    weighted_ref[...] = dot(value_ref[...].T, terms.astype(jnp.bfloat16))
    grad_t_ref[...] = stacked(grad_ref, heads).T


def gathered_kernel(
    chips,
    tiles,
    slots,
    heads,
    tile_total,
    info_ref,
    table_any,
    query_ref,
    grad_ref,
    key_any,
    value_any,
    key_other,
    value_other,
    max_own,
    total_own,
    weighted_own,
    grad_t_ref,
    more_ref,
    *refs,
):
    count = len(pairs_of(chips)) + 1
    arrived, handed, refs = refs[:count], refs[count : 2 * count], refs[2 * count :]
    parts_ref, max_ref, inverse_ref, delta_ref, out_t_ref, dscores_ref, *refs = refs
    slot_keys, *refs = refs
    more_out, attended_full, query_full, key_full, value_full, *refs = refs
    bias_ref, held_ref, sum_ref, score_ref, staged_ref, *refs = refs
    attended_ref, query_out, table_ref, copy_sem = refs
    keys_ref, values_ref = held_ref.at[0], held_ref.at[1]
    key_sum, value_sum = sum_ref.at[0], sum_ref.at[1]
    rank = lax.axis_index("seq")
    odd = rank % 2
    rows = tiles * TILE
    chunk = slots * TILE
    factor = HD**-0.5
    scale = factor * LOG2E
    needed = info_ref[0]
    columns = [pl.ds(h * HD, HD) for h in range(heads)]

    def repack(target, part, first_row):
        kind = odd ^ part
        for slot in range(slots):
            total = sum_ref[kind, tile_rows(first_row, slot), :]
            target[slot] = (total * jnp.where(kind == 0, factor, 1.0)).astype(jnp.bfloat16)

    for slot in range(slots):
        for b in range(tiles):
            allowed = info_ref[2 * tile_total + 2 + slot * tiles + b] == 1
            bias_ref[pl.ds(slot * TILE, TILE), pl.ds(b * TILE, TILE)] = block_bias(allowed)
        position = info_ref[1 + slot]
        away = (position // (2 * tiles)) ^ (rank // 2)
        at = tile_rows(0, slot)

        @pl.when(away == 0)
        def _():
            source = tile_rows(0, position % tiles)
            keys_ref[at, :] = key_other[source, :]
            values_ref[at, :] = value_other[source, :]

        @pl.when(away == chips - 1)
        def _():
            held_ref[odd, at, :] = arrived[-1][slot]
            held_ref[odd ^ 1, at, :] = handed[-1][slot]

        for index, pair in enumerate(pairs_of(chips)):
            for core, step in enumerate(pair):

                @pl.when((away == step) & (odd == core))
                def _():
                    held_ref[odd, at, :] = arrived[index][slot]
                    held_ref[odd ^ 1, at, :] = arrived[index][slots + slot]

                @pl.when((away == step) & (odd != core))
                def _():
                    held_ref[odd ^ 1, at, :] = handed[index][slot]
                    held_ref[odd, at, :] = handed[index][slots + slot]

    first = pl.ds(0, chunk)

    @pl.when(needed <= slots)
    def _():
        keys = keys_ref[first, :]
        values = values_ref[first, :]
        slot_keys[...] = keys
        values_t = values.T
        per_block = heads // 2 if heads % 2 == 0 else heads
        width = per_block * rows
        blocks = range(heads // per_block)
        bias = jnp.concatenate([bias_ref[first, :]] * per_block, axis=1)
        spans = [pl.ds(block * width, width) for block in blocks]
        query_all = stacked(query_ref, heads)
        grad_all = stacked(grad_ref, heads)
        query = [query_all[block * width : (block + 1) * width] for block in blocks]
        grad = [grad_all[block * width : (block + 1) * width] for block in blocks]
        scores = [dot_t(keys, query[block]) * scale + bias for block in blocks]
        dprobs, probs, outs = [], [], []
        for block, span in zip(blocks, spans):
            dprobs.append(dot_t(values, grad[block]))
            old_max = max_own[:, span]
            row_max = jnp.maximum(old_max, jnp.max(scores[block], axis=0, keepdims=True))
            shrink = jnp.exp2(old_max - row_max)
            terms = jnp.exp2(scores[block] - row_max)
            total = total_own[:, span] * shrink + jnp.sum(terms, axis=0, keepdims=True)
            inverse = 1.0 / total
            weighted = dot(values_t, terms.astype(jnp.bfloat16))
            outs.append((shrink * inverse, inverse, weighted))
            probs.append(terms * inverse)
            max_ref[:, span] = row_max
            inverse_ref[:, span] = inverse
        key_total, value_total = None, None
        for block, span in zip(blocks, spans):
            part = dot(probs[block].astype(jnp.bfloat16), grad[block])
            value_total = part if value_total is None else value_total + part
            shrunk, inverse, weighted = outs[block]
            out = (weighted_own[:, span] * shrunk + weighted * inverse).astype(jnp.bfloat16)
            out_t_ref[:, span] = out
            delta = jnp.sum(
                grad_t_ref[:, span].astype(jnp.float32) * out.astype(jnp.float32),
                axis=0,
                keepdims=True,
            )
            delta_ref[:, span] = delta
            dscores = (probs[block] * (dprobs[block] - delta)).astype(jnp.bfloat16)
            dscores_ref[:, span] = dscores
            part = dot(dscores, query[block])
            key_total = part if key_total is None else key_total + part
        key_sum[first, :] = key_total
        value_sum[first, :] = value_total

    @pl.when(needed > slots)
    def _():
        used = (needed + slots - 1) // slots
        own_first = pl.multiple_of(used * chunk, chunk)
        own_rows = pl.ds(own_first, rows)
        copy = pltpu.make_async_copy(table_any, table_ref, copy_sem)
        copy.start()
        copy.wait()

        def ids(position):
            return table_ref[tile_total, position]

        def allowed(a, b):
            return table_ref[ids(rank * tiles + b), ids(rank * tiles + a)]

        own_bias(tiles, bias_ref.at[own_rows, :], allowed)
        for source, target in ((key_any, keys_ref), (value_any, values_ref)):
            copy = pltpu.make_async_copy(source, target.at[own_rows, :], copy_sem)
            copy.start()
            copy.wait()

        def fetch(index, carry):
            copy = pltpu.make_async_copy(more_ref.at[index - 1], staged_ref, copy_sem)
            copy.start()
            copy.wait()
            first_row = pl.multiple_of(index * chunk, chunk)
            for slot in range(slots):
                for part in range(2):
                    held_ref[odd ^ part, tile_rows(first_row, slot), :] = staged_ref[part, slot]
                listed = index * slots + slot
                position = info_ref[1 + listed]
                usable = (listed < needed) & (position // tiles != rank)
                for b in range(tiles):
                    seen = table_ref[ids(rank * tiles + b), ids(position)] == 1
                    bias_ref[tile_rows(first_row, slot), pl.ds(b * TILE, TILE)] = block_bias(
                        usable & seen
                    )
            return carry

        lax.fori_loop(1, used, fetch, 0)
        key_sum[...] = jnp.zeros_like(key_sum)
        value_sum[...] = jnp.zeros_like(value_sum)
        blocks = used * slots + tiles

        for h in range(heads):
            query = query_ref[:, columns[h]]
            grad = grad_ref[:, columns[h]]

            def score(index, row_max):
                at = tile_rows(0, index)
                scores = dot_t(keys_ref[at, :], query) * scale + bias_ref[at, :]
                score_ref[at, :] = scores
                return jnp.maximum(row_max, jnp.max(scores, axis=0, keepdims=True))

            row_max = lax.fori_loop(0, blocks, score, jnp.full((1, rows), FAR_BELOW, jnp.float32))

            def forward(index, carry):
                total, weighted = carry
                at = tile_rows(0, index)
                terms = jnp.exp2(score_ref[at, :] - row_max)
                score_ref[at, :] = terms
                weighted = weighted + dot(values_ref[at, :].T, terms.astype(jnp.bfloat16))
                return total + jnp.sum(terms, axis=0, keepdims=True), weighted

            zeros = jnp.zeros((HD, rows), jnp.float32)
            start = (jnp.zeros((1, rows), jnp.float32), zeros)
            total, weighted = lax.fori_loop(0, blocks, forward, start)
            inverse = 1.0 / total
            out = (weighted * inverse).astype(jnp.bfloat16)
            attended_ref[:, columns[h]] = out.T
            grad_t = grad_t_ref[:, pl.ds(h * rows, rows)].astype(jnp.float32)
            delta = jnp.sum(grad_t * out.astype(jnp.float32), axis=0, keepdims=True)

            def backward(index, query_t):
                at = tile_rows(0, index)
                probs = score_ref[at, :] * inverse
                dprobs = dot_t(values_ref[at, :], grad)
                dscores = (probs * (dprobs - delta)).astype(jnp.bfloat16)
                key_sum[at, :] += dot(dscores, query)
                value_sum[at, :] += dot(probs.astype(jnp.bfloat16), grad)
                return query_t + dot(keys_ref[at, :].T, dscores)

            query_t = lax.fori_loop(0, blocks, backward, zeros)
            query_out[:, columns[h]] = (query_t * factor).T

        key_sum[own_rows, :] = key_sum[own_rows, :] * factor
        for source, target in (
            (attended_ref, attended_full),
            (query_out, query_full),
            (key_sum.at[own_rows, :], key_full),
            (value_sum.at[own_rows, :], value_full),
        ):
            copy = pltpu.make_async_copy(source, target, copy_sem)
            copy.start()
            copy.wait()

        def store(index, carry):
            for part in range(2):
                repack(staged_ref.at[part], part, pl.multiple_of(index * chunk, chunk))
            copy = pltpu.make_async_copy(staged_ref, more_out.at[index - 1], copy_sem)
            copy.start()
            copy.wait()
            return carry

        lax.fori_loop(1, used, store, 0)

    for part in range(2):
        repack(parts_ref.at[pl.ds(part * slots, slots)], part, 0)


def fetch_full(copy_sem, *pairs):
    for source, target in pairs:
        copy = pltpu.make_async_copy(source, target, copy_sem)
        copy.start()
        copy.wait()


def own_grads_kernel(
    tiles,
    slots,
    heads,
    tile_total,
    info_ref,
    query_ref,
    grad_ref,
    key_ref,
    value_ref,
    max_ref,
    inverse_ref,
    delta_ref,
    key_full,
    value_full,
    order_ref,
    dscores_ref,
    key_out,
    value_out,
    order_out,
    bias_ref,
    copy_sem,
):
    del order_ref, order_out

    @pl.when(info_ref[0] <= slots)
    def _():
        query = stacked(query_ref, heads)
        grad = stacked(grad_ref, heads)
        scores = own_scores(
            tiles, slots, heads, tile_total, info_ref, bias_ref, key_ref[...], query
        )
        probs = jnp.exp2(scores - max_ref[...]) * inverse_ref[...]
        dprobs = dot_t(value_ref[...], grad)
        dscores = (probs * (dprobs - delta_ref[...])).astype(jnp.bfloat16)
        dscores_ref[...] = dscores
        value_out[...] = dot(probs.astype(jnp.bfloat16), grad)
        key_out[...] = dot(dscores, query) * HD**-0.5

    @pl.when(info_ref[0] > slots)
    def _():
        fetch_full(copy_sem, (key_full, key_out), (value_full, value_out))


def queries_kernel(
    slots,
    heads,
    info_ref,
    key_ref,
    own_dscores,
    slot_dscores,
    slot_keys,
    out_t_ref,
    attended_full,
    query_full,
    attended_ref,
    query_out,
    copy_sem,
):
    rows = query_out.shape[0]

    @pl.when(info_ref[0] <= slots)
    def _():
        query_t = dot(key_ref[...].T, own_dscores[...])
        query_t = (query_t + dot(slot_keys[...].T, slot_dscores[...])) * HD**-0.5
        for h in range(heads):
            columns = pl.ds(h * HD, HD)
            attended_ref[:, columns] = out_t_ref[:, pl.ds(h * rows, rows)].T
            query_out[:, columns] = query_t[:, h * rows : (h + 1) * rows].T

    @pl.when(info_ref[0] > slots)
    def _():
        fetch_full(copy_sem, (attended_full, attended_ref), (query_full, query_out))


def place_kernel(key_own, value_own, key_placed, value_placed, key_sem, value_sem):
    copies = [
        pltpu.make_async_copy(key_own, key_placed, key_sem),
        pltpu.make_async_copy(value_own, value_placed, value_sem),
    ]
    for copy in copies:
        copy.start()
    for copy in copies:
        copy.wait()


def per_device(queries, key_rows, value_rows, out_grad, tile_ids, tile_mask):
    row_count = queries.shape[0]
    heads = queries.shape[1] // HD
    ranks = lax.axis_size("seq")
    chips = ranks // 2
    assert key_rows.shape[1] == HD and ranks > 1 and ranks & (ranks - 1) == 0
    tiles = row_count // TILE
    tile_total = tile_ids.shape[0]
    slots = tiles
    rounds = math.ceil(tile_total / slots)
    slot_shape = (slots, TILE, HD)
    buffer = (rounds - 1, 2) + slot_shape
    shape = jax.ShapeDtypeStruct
    bf16, f32 = jnp.bfloat16, jnp.float32

    def swap(values, step):
        return lax.ppermute(values, "seq", [(source, source ^ step) for source in range(ranks)])

    def across(values):
        return [swap(values, 2 * step) for step in range(1, chips)]

    def trade(full, half):
        got = []
        for pair in pairs_of(chips):
            routes = [(source, source ^ 2 * pair[source % 2]) for source in range(ranks)]
            got.append(lax.ppermute(full, "seq", routes))
        return got + [swap(half, 2 * (chips - 1))]

    def add(*values):
        total = values[0].astype(f32)
        for value in values[1:]:
            total = total + value.astype(f32)
        return total.astype(bf16)

    table = jnp.pad(tile_mask, ((0, 1), (0, 0)))
    table = table + jnp.pad(tile_ids[None], ((tile_total, 0), (0, 0)))
    key_other, value_other = swap(key_rows, 1), swap(value_rows, 1)
    chip_rows = (key_rows, value_rows, key_other, value_other)
    info, spare, spare_sums = call(
        functools.partial(list_kernel, tile_total, tiles, slots),
        [SMEM_SPEC],
        (
            shape((info_size(tile_total, tiles, slots),), jnp.int32),
            shape(buffer, bf16),
            shape(buffer, bf16),
        ),
        (SMEM_SPEC, ANY_SPEC, ANY_SPEC),
        scratch=(pltpu.SMEM((tile_total,), jnp.int32),),
        moved=4 * 1024 * 1024,
    )(table)
    chosen, chosen_half = call(
        functools.partial(first_kernel, tiles, slots),
        [SMEM_SPEC] + [VMEM_SPEC] * 4,
        (shape((2 * slots, TILE, HD), bf16), shape(slot_shape, bf16)),
        (VMEM_SPEC,) * 2,
        moved=5 * row_count * HD * 2,
    )(info, *chip_rows)
    used = (info[0] + slots - 1) // slots

    def select(index):
        return call(
            functools.partial(select_kernel, tiles, slots),
            [SMEM_SPEC] * 2 + [VMEM_SPEC] * 4,
            shape(slot_shape, bf16),
            VMEM_SPEC,
            moved=5 * row_count * HD * 2,
        )(info, index.reshape(1), *chip_rows)

    arrived = trade(chosen, chosen_half)
    handed = [swap(values, 1) for values in arrived]

    def gather_more(index, buffered):
        chosen = select(index)
        total = add(chosen, *across(chosen))
        pair = jnp.stack([total, swap(total, 1)])
        return lax.dynamic_update_index_in_dim(buffered, pair, index - 1, 0)

    more = lax.fori_loop(1, used, gather_more, spare)

    all_rows = row_count + rounds * slots * TILE
    columns = heads * row_count
    line = shape((1, columns), f32)
    work = 2 * columns * row_count * HD
    max_own, total_own, weighted, grad_t = call(
        functools.partial(own_kernel, tiles, slots, heads, tile_total),
        [SMEM_SPEC] + [VMEM_SPEC] * 4,
        (line, line, shape((HD, columns), f32), shape((HD, columns), bf16)),
        (VMEM_SPEC,) * 4,
        scratch=(pltpu.VMEM((row_count, row_count), f32),),
        flops=24 * work,
        moved=4 * row_count * heads * HD,
    )(info, queries, out_grad, key_rows, value_rows)

    full = (
        shape(queries.shape, bf16),
        shape(queries.shape, f32),
        shape(key_rows.shape, f32),
        shape(value_rows.shape, f32),
    )
    parts, row_max, inverse, delta, out_t, dscores, slot_keys, more_terms, *full_values = call(
        functools.partial(gathered_kernel, chips, tiles, slots, heads, tile_total),
        [SMEM_SPEC, ANY_SPEC]
        + [VMEM_SPEC] * 2
        + [ANY_SPEC] * 2
        + [VMEM_SPEC] * 6
        + [ANY_SPEC]
        + [VMEM_SPEC] * (2 * len(arrived)),
        (
            shape((2 * slots, TILE, HD), bf16),
            line,
            line,
            line,
            shape((HD, columns), bf16),
            shape((slots * TILE, columns), bf16),
            shape((slots * TILE, HD), bf16),
            shape(buffer, bf16),
        )
        + full,
        (VMEM_SPEC,) * 7 + (ANY_SPEC,) * 5,
        scratch=(
            pltpu.VMEM((all_rows, row_count), f32),
            pltpu.VMEM((2, all_rows, HD), bf16),
            pltpu.VMEM((2, all_rows, HD), f32),
            pltpu.VMEM((all_rows, row_count), f32),
            pltpu.VMEM((2,) + slot_shape, bf16),
            pltpu.VMEM(queries.shape, bf16),
            pltpu.VMEM(queries.shape, f32),
            pltpu.SMEM(table.shape, jnp.int32),
            pltpu.SemaphoreType.DMA,
        ),
        flops=24 * work,
        moved=4 * row_count * heads * HD,
    )(
        info,
        table,
        queries,
        out_grad,
        *chip_rows,
        max_own,
        total_own,
        weighted,
        grad_t,
        more,
        *arrived,
        *handed,
    )

    partner = swap(parts, 1)
    half_sum = add(parts[:slots], partner[slots:])
    chip_sum = jnp.concatenate([half_sum, add(parts[slots:], partner[:slots])])
    own_dscores, key_own, value_own, half_sum = call(
        functools.partial(own_grads_kernel, tiles, slots, heads, tile_total),
        [SMEM_SPEC] + [VMEM_SPEC] * 7 + [ANY_SPEC] * 3,
        (shape((row_count, columns), bf16), *full[2:], shape(slot_shape, bf16)),
        (VMEM_SPEC,) * 3 + (ANY_SPEC,),
        scratch=(pltpu.VMEM((row_count, row_count), f32), pltpu.SemaphoreType.DMA),
        flops=18 * work,
        moved=4 * row_count * heads * HD,
        aliases={10: 3},
    )(
        info,
        queries,
        out_grad,
        key_rows,
        value_rows,
        row_max,
        inverse,
        delta,
        *full_values[2:],
        half_sum,
    )
    back = trade(chip_sum, half_sum)
    key_placed, value_placed = call(
        place_kernel,
        [VMEM_SPEC] * 2,
        tuple(full[2:]),
        (ANY_SPEC,) * 2,
        scratch=(pltpu.SemaphoreType.DMA,) * 2,
        moved=2 * 1024 * 1024,
    )(key_own, value_own)
    attended, query_grad = call(
        functools.partial(queries_kernel, slots, heads),
        [SMEM_SPEC] + [VMEM_SPEC] * 5 + [ANY_SPEC] * 2,
        full[:2],
        (VMEM_SPEC,) * 2,
        scratch=(pltpu.SemaphoreType.DMA,),
        flops=16 * work,
        moved=8 * row_count * heads * HD,
    )(
        info,
        key_rows,
        own_dscores,
        dscores,
        slot_keys,
        out_t,
        *full_values[:2],
    )
    sums = [chip_sum] + back + [swap(values, 1) for values in back]

    def reduce_more(index, totals):
        terms = lax.dynamic_index_in_dim(more_terms, index - 1, 0, keepdims=False)
        part = add(terms[0], swap(terms[1], 1))
        total = add(part, *across(part))
        pair = jnp.stack([total, swap(total, 1)])
        return lax.dynamic_update_index_in_dim(totals, pair, index - 1, 0)

    extra = lax.fori_loop(1, used, reduce_more, spare_sums)
    key_grad, value_grad = call(
        functools.partial(close_kernel, tiles, slots, chips, tile_total),
        [SMEM_SPEC, ANY_SPEC] + [VMEM_SPEC] * (2 + len(sums)) + [ANY_SPEC] * 2,
        tuple(full[2:]),
        (ANY_SPEC,) * 2,
        scratch=(
            pltpu.VMEM((2, TILE, HD), f32),
            pltpu.VMEM((2, TILE, HD), bf16),
            pltpu.SemaphoreType.DMA,
            pltpu.SemaphoreType.DMA,
        ),
        moved=5 * row_count * HD * 4,
        aliases={4 + len(sums): 0, 5 + len(sums): 1},
    )(info, extra, key_own, value_own, *sums, key_placed, value_placed)
    return attended, query_grad, key_grad, value_grad


def solution(mesh):
    return jax.shard_map(
        per_device,
        mesh=mesh,
        in_specs=(
            P(("batch", "seq"), "head"),
            P(("batch", "seq"), "head"),
            P(("batch", "seq"), "head"),
            P(("batch", "seq"), "head"),
            P("batch"),
            P("batch", None),
        ),
        out_specs=(P(("batch", "seq"), "head"),) * 4,
        check_vma=False,
    )
```

```python
import functools
import math

import jax
import jax.numpy as jnp
from jax import lax
from jax.experimental import pallas as pl
from jax.experimental.pallas import tpu as pltpu
from jax.sharding import PartitionSpec as P

HD = 128
TILE = 128
FAR_BELOW = -1e30
LOG2E = 1.4426950408889634
NT_DIMS = (((1,), (1,)), ((), ()))
VMEM_LIMIT = 32 * 1024 * 1024

SMEM_SPEC = pl.BlockSpec(memory_space=pltpu.SMEM)
VMEM_SPEC = pl.BlockSpec(memory_space=pltpu.VMEM)
ANY_SPEC = pl.BlockSpec(memory_space=pl.ANY)


def call(kernel, in_specs, out_shape, out_specs, scratch=(), flops=0, moved=0, aliases=None):
    return pl.pallas_call(
        kernel,
        in_specs=in_specs,
        out_shape=out_shape,
        out_specs=out_specs,
        scratch_shapes=list(scratch),
        input_output_aliases=aliases or {},
        compiler_params=pltpu.CompilerParams(vmem_limit_bytes=VMEM_LIMIT),
        cost_estimate=pl.CostEstimate(flops=flops, bytes_accessed=moved, transcendentals=0),
    )


def tile_rows(first_row, tile):
    return pl.ds(pl.multiple_of(first_row + tile * TILE, TILE), TILE)


def info_size(tile_total, tiles, slots):
    return 2 * tile_total + 2 + (slots + tiles) * tiles


def pairs_of(chips):
    return [(step, step + 1) for step in range(1, chips - 1, 2)]


def list_kernel(tile_total, tiles, slots, table_ref, info_ref, spare_ref, any_ref):
    del spare_ref
    rank = lax.axis_index("seq")

    def ids(position):
        return table_ref[tile_total, position]

    def mask(query_tile, key_tile):
        return table_ref[query_tile, key_tile]

    for place in range(1, tile_total + 2):
        info_ref[place] = 0
    for tile in range(tile_total):
        users = mask(0, tile)
        for other in range(1, tile_total):
            users = users + mask(other, tile)
        any_ref[tile] = users
    count = jnp.int32(0)
    for position in range(tile_total):
        key_tile = ids(position)
        away = any_ref[key_tile]
        for local in range(tiles):
            away = away - mask(ids(position // tiles * tiles + local), key_tile)
        info_ref[1 + count] = position
        info_ref[tile_total + 2 + position] = jnp.where(away > 0, count, -1)
        count = count + jnp.where(away > 0, 1, 0)
    info_ref[0] = count
    my_tiles = [ids(rank * tiles + b) for b in range(tiles)]
    place = 2 * tile_total + 2
    for slot in range(slots):
        position = info_ref[1 + slot]
        usable = ((slot < count) & (position // tiles != rank)).astype(jnp.int32)
        for b in range(tiles):
            info_ref[place] = usable * mask(my_tiles[b], ids(position))
            place += 1
    for a in range(tiles):
        for b in range(tiles):
            info_ref[place] = mask(my_tiles[b], my_tiles[a])
            place += 1

def first_kernel(tiles, slots, info_ref, *refs):
    sources, (full_ref, half_ref) = refs[:4], refs[4:]
    odd = lax.axis_index("seq") % 2
    for kind in range(2):
        part = odd ^ kind
        target = full_ref.at[pl.ds(part * slots, slots)]
        pick(tiles, slots, 0, info_ref, sources[kind], sources[2 + kind], target)
    half_ref[...] = full_ref[:slots]


def pick(tiles, slots, base, info_ref, own_ref, other_ref, out_ref):
    rank = lax.axis_index("seq")
    for slot in range(slots):
        position = info_ref[1 + base + slot]
        home = position // tiles
        rows = tile_rows(0, position % tiles)
        out_ref[slot] = jnp.zeros_like(out_ref[slot])

        @pl.when(home == rank)
        def _():
            out_ref[slot] = own_ref[rows, :]

        @pl.when(home == rank ^ 1)
        def _():
            out_ref[slot] = other_ref[rows, :]


def select_kernel(tiles, slots, info_ref, round_ref, *refs):
    key_ref, value_ref, key_other, value_other, out_ref = refs
    rank = lax.axis_index("seq")
    for kind, own, other in ((0, key_ref, key_other), (1, value_ref, value_other)):

        @pl.when(rank % 2 == kind)
        def _():
            pick(tiles, slots, round_ref[0] * slots, info_ref, own, other, out_ref)


def close_kernel(tiles, slots, chips, tile_total, info_ref, extra_ref, *refs):
    grads, (chip_ref, *sums) = refs[:2], refs[2:-8]
    outs, staged_ref, late_ref, sems = refs[-6:-4], refs[-4], refs[-3], refs[-2:]
    half = len(sums) // 2
    arrived, handed = sums[:half], sums[half:]
    rank = lax.axis_index("seq")
    odd = rank % 2

    def total_of(part, slot):
        total = chip_ref[part * slots + slot].astype(jnp.float32)
        for own, other in zip(arrived[:-1], handed[:-1]):
            total = total + own[part * slots + slot].astype(jnp.float32)
            total = total + other[(1 - part) * slots + slot].astype(jnp.float32)
        return total + (handed if part else arrived)[-1][slot].astype(jnp.float32)

    for tile in range(tiles):
        slot = info_ref[tile_total + 2 + rank * tiles + tile]
        rows = pl.ds(tile * TILE, TILE)

        def place(totals):
            copies = []
            for kind in range(2):
                total = jnp.where(odd == kind, totals[0], totals[1])
                staged_ref[kind] = grads[kind][rows, :] + total
                copies.append(
                    pltpu.make_async_copy(staged_ref.at[kind], outs[kind].at[rows, :], sems[kind])
                )
            for copy in copies:
                copy.start()
            for copy in copies:
                copy.wait()

        @pl.when((slot >= 0) & (slot < slots))
        def _():
            place([total_of(part, slot) for part in range(2)])

        @pl.when(slot >= slots)
        def _():
            for part in range(2):
                source = extra_ref.at[slot // slots - 1, part, slot % slots]
                copy = pltpu.make_async_copy(source, late_ref.at[part], sems[part])
                copy.start()
                copy.wait()
            place([late_ref[part].astype(jnp.float32) for part in range(2)])


def causal_bias():
    later = lax.broadcasted_iota(jnp.int32, (TILE, TILE), 1)
    return jnp.where(lax.broadcasted_iota(jnp.int32, (TILE, TILE), 0) <= later, 0.0, FAR_BELOW)


def block_bias(allowed):
    return jnp.full((TILE, TILE), jnp.where(allowed, 0.0, FAR_BELOW), jnp.float32)


def own_bias(tiles, bias_ref, allowed):
    for a in range(tiles):
        for b in range(tiles):
            bias = causal_bias() if a == b else block_bias(allowed(a, b) == 1)
            bias_ref[pl.ds(a * TILE, TILE), pl.ds(b * TILE, TILE)] = bias


def stacked(ref, heads):
    return jnp.concatenate([ref[:, h * HD : (h + 1) * HD] for h in range(heads)], axis=0)


def dot(one, other):
    return jnp.dot(one, other, preferred_element_type=jnp.float32)


def dot_t(one, other):
    return lax.dot_general(one, other, NT_DIMS, preferred_element_type=jnp.float32)


def own_scores(tiles, slots, heads, tile_total, info_ref, bias_ref, keys, query):
    place = 2 * tile_total + 2 + slots * tiles
    own_bias(tiles, bias_ref, lambda a, b: info_ref[place + a * tiles + b])
    bias = jnp.concatenate([bias_ref[...]] * heads, axis=1)
    return dot_t(keys, query) * (HD**-0.5 * LOG2E) + bias


def own_kernel(
    tiles,
    slots,
    heads,
    tile_total,
    info_ref,
    query_ref,
    grad_ref,
    key_ref,
    value_ref,
    max_ref,
    total_ref,
    weighted_ref,
    grad_t_ref,
    bias_ref,
):
    query = stacked(query_ref, heads)
    scores = own_scores(tiles, slots, heads, tile_total, info_ref, bias_ref, key_ref[...], query)
    row_max = jnp.max(scores, axis=0, keepdims=True)
    terms = jnp.exp2(scores - row_max)
    max_ref[...] = row_max
    total_ref[...] = jnp.sum(terms, axis=0, keepdims=True)
    weighted_ref[...] = dot(value_ref[...].T, terms.astype(jnp.bfloat16))
    grad_t_ref[...] = stacked(grad_ref, heads).T


def gathered_kernel(
    chips,
    tiles,
    slots,
    heads,
    tile_total,
    info_ref,
    table_any,
    query_ref,
    grad_ref,
    key_any,
    value_any,
    key_other,
    value_other,
    max_own,
    total_own,
    weighted_own,
    grad_t_ref,
    more_ref,
    *refs,
):
    count = len(pairs_of(chips)) + 1
    arrived, handed, refs = refs[:count], refs[count : 2 * count], refs[2 * count :]
    parts_ref, max_ref, inverse_ref, delta_ref, out_t_ref, dscores_ref, *refs = refs
    slot_keys, *refs = refs
    more_out, attended_full, query_full, key_full, value_full, *refs = refs
    bias_ref, held_ref, sum_ref, score_ref, staged_ref, *refs = refs
    attended_ref, query_out, table_ref, copy_sem = refs
    keys_ref, values_ref = held_ref.at[0], held_ref.at[1]
    key_sum, value_sum = sum_ref.at[0], sum_ref.at[1]
    rank = lax.axis_index("seq")
    odd = rank % 2
    rows = tiles * TILE
    chunk = slots * TILE
    factor = HD**-0.5
    scale = factor * LOG2E
    needed = info_ref[0]
    columns = [pl.ds(h * HD, HD) for h in range(heads)]

    def repack(target, part, first_row):
        kind = odd ^ part
        for slot in range(slots):
            total = sum_ref[kind, tile_rows(first_row, slot), :]
            target[slot] = (total * jnp.where(kind == 0, factor, 1.0)).astype(jnp.bfloat16)

    for slot in range(slots):
        for b in range(tiles):
            allowed = info_ref[2 * tile_total + 2 + slot * tiles + b] == 1
            bias_ref[pl.ds(slot * TILE, TILE), pl.ds(b * TILE, TILE)] = block_bias(allowed)
        position = info_ref[1 + slot]
        away = (position // (2 * tiles)) ^ (rank // 2)
        at = tile_rows(0, slot)

        @pl.when(away == 0)
        def _():
            source = tile_rows(0, position % tiles)
            keys_ref[at, :] = key_other[source, :]
            values_ref[at, :] = value_other[source, :]

        @pl.when(away == chips - 1)
        def _():
            held_ref[odd, at, :] = arrived[-1][slot]
            held_ref[odd ^ 1, at, :] = handed[-1][slot]

        for index, pair in enumerate(pairs_of(chips)):
            for core, step in enumerate(pair):

                @pl.when((away == step) & (odd == core))
                def _():
                    held_ref[odd, at, :] = arrived[index][slot]
                    held_ref[odd ^ 1, at, :] = arrived[index][slots + slot]

                @pl.when((away == step) & (odd != core))
                def _():
                    held_ref[odd ^ 1, at, :] = handed[index][slot]
                    held_ref[odd, at, :] = handed[index][slots + slot]

    first = pl.ds(0, chunk)

    @pl.when(needed <= slots)
    def _():
        keys = keys_ref[first, :]
        values = values_ref[first, :]
        slot_keys[...] = keys
        values_t = values.T
        per_block = heads // 2 if heads % 2 == 0 else heads
        width = per_block * rows
        blocks = range(heads // per_block)
        bias = jnp.concatenate([bias_ref[first, :]] * per_block, axis=1)
        spans = [pl.ds(block * width, width) for block in blocks]
        query_all = stacked(query_ref, heads)
        grad_all = stacked(grad_ref, heads)
        query = [query_all[block * width : (block + 1) * width] for block in blocks]
        grad = [grad_all[block * width : (block + 1) * width] for block in blocks]
        scores = [dot_t(keys, query[block]) * scale + bias for block in blocks]
        dprobs, probs, outs = [], [], []
        for block, span in zip(blocks, spans):
            dprobs.append(dot_t(values, grad[block]))
            old_max = max_own[:, span]
            row_max = jnp.maximum(old_max, jnp.max(scores[block], axis=0, keepdims=True))
            shrink = jnp.exp2(old_max - row_max)
            terms = jnp.exp2(scores[block] - row_max)
            total = total_own[:, span] * shrink + jnp.sum(terms, axis=0, keepdims=True)
            inverse = 1.0 / total
            weighted = dot(values_t, terms.astype(jnp.bfloat16))
            outs.append((shrink * inverse, inverse, weighted))
            probs.append(terms * inverse)
            max_ref[:, span] = row_max
            inverse_ref[:, span] = inverse
        key_total, value_total = None, None
        for block, span in zip(blocks, spans):
            part = dot(probs[block].astype(jnp.bfloat16), grad[block])
            value_total = part if value_total is None else value_total + part
            shrunk, inverse, weighted = outs[block]
            out = (weighted_own[:, span] * shrunk + weighted * inverse).astype(jnp.bfloat16)
            out_t_ref[:, span] = out
            delta = jnp.sum(
                grad_t_ref[:, span].astype(jnp.float32) * out.astype(jnp.float32),
                axis=0,
                keepdims=True,
            )
            delta_ref[:, span] = delta
            dscores = (probs[block] * (dprobs[block] - delta)).astype(jnp.bfloat16)
            dscores_ref[:, span] = dscores
            part = dot(dscores, query[block])
            key_total = part if key_total is None else key_total + part
        key_sum[first, :] = key_total
        value_sum[first, :] = value_total

    @pl.when(needed > slots)
    def _():
        used = (needed + slots - 1) // slots
        own_first = pl.multiple_of(used * chunk, chunk)
        own_rows = pl.ds(own_first, rows)
        copy = pltpu.make_async_copy(table_any, table_ref, copy_sem)
        copy.start()
        copy.wait()

        def ids(position):
            return table_ref[tile_total, position]

        def allowed(a, b):
            return table_ref[ids(rank * tiles + b), ids(rank * tiles + a)]

        own_bias(tiles, bias_ref.at[own_rows, :], allowed)
        for source, target in ((key_any, keys_ref), (value_any, values_ref)):
            copy = pltpu.make_async_copy(source, target.at[own_rows, :], copy_sem)
            copy.start()
            copy.wait()

        def fetch(index, carry):
            copy = pltpu.make_async_copy(more_ref.at[index - 1], staged_ref, copy_sem)
            copy.start()
            copy.wait()
            first_row = pl.multiple_of(index * chunk, chunk)
            for slot in range(slots):
                for part in range(2):
                    held_ref[odd ^ part, tile_rows(first_row, slot), :] = staged_ref[part, slot]
                listed = index * slots + slot
                position = info_ref[1 + listed]
                usable = (listed < needed) & (position // tiles != rank)
                for b in range(tiles):
                    seen = table_ref[ids(rank * tiles + b), ids(position)] == 1
                    bias_ref[tile_rows(first_row, slot), pl.ds(b * TILE, TILE)] = block_bias(
                        usable & seen
                    )
            return carry

        lax.fori_loop(1, used, fetch, 0)
        key_sum[...] = jnp.zeros_like(key_sum)
        value_sum[...] = jnp.zeros_like(value_sum)
        blocks = used * slots + tiles

        for h in range(heads):
            query = query_ref[:, columns[h]]
            grad = grad_ref[:, columns[h]]

            def score(index, row_max):
                at = tile_rows(0, index)
                scores = dot_t(keys_ref[at, :], query) * scale + bias_ref[at, :]
                score_ref[at, :] = scores
                return jnp.maximum(row_max, jnp.max(scores, axis=0, keepdims=True))

            row_max = lax.fori_loop(0, blocks, score, jnp.full((1, rows), FAR_BELOW, jnp.float32))

            def forward(index, carry):
                total, weighted = carry
                at = tile_rows(0, index)
                terms = jnp.exp2(score_ref[at, :] - row_max)
                score_ref[at, :] = terms
                weighted = weighted + dot(values_ref[at, :].T, terms.astype(jnp.bfloat16))
                return total + jnp.sum(terms, axis=0, keepdims=True), weighted

            zeros = jnp.zeros((HD, rows), jnp.float32)
            start = (jnp.zeros((1, rows), jnp.float32), zeros)
            total, weighted = lax.fori_loop(0, blocks, forward, start)
            inverse = 1.0 / total
            out = (weighted * inverse).astype(jnp.bfloat16)
            attended_ref[:, columns[h]] = out.T
            grad_t = grad_t_ref[:, pl.ds(h * rows, rows)].astype(jnp.float32)
            delta = jnp.sum(grad_t * out.astype(jnp.float32), axis=0, keepdims=True)

            def backward(index, query_t):
                at = tile_rows(0, index)
                probs = score_ref[at, :] * inverse
                dprobs = dot_t(values_ref[at, :], grad)
                dscores = (probs * (dprobs - delta)).astype(jnp.bfloat16)
                key_sum[at, :] += dot(dscores, query)
                value_sum[at, :] += dot(probs.astype(jnp.bfloat16), grad)
                return query_t + dot(keys_ref[at, :].T, dscores)

            query_t = lax.fori_loop(0, blocks, backward, zeros)
            query_out[:, columns[h]] = (query_t * factor).T

        key_sum[own_rows, :] = key_sum[own_rows, :] * factor
        for source, target in (
            (attended_ref, attended_full),
            (query_out, query_full),
            (key_sum.at[own_rows, :], key_full),
            (value_sum.at[own_rows, :], value_full),
        ):
            copy = pltpu.make_async_copy(source, target, copy_sem)
            copy.start()
            copy.wait()

        def store(index, carry):
            for part in range(2):
                repack(staged_ref.at[part], part, pl.multiple_of(index * chunk, chunk))
            copy = pltpu.make_async_copy(staged_ref, more_out.at[index - 1], copy_sem)
            copy.start()
            copy.wait()
            return carry

        lax.fori_loop(1, used, store, 0)

    for part in range(2):
        repack(parts_ref.at[pl.ds(part * slots, slots)], part, 0)


def fetch_full(copy_sem, *pairs):
    for source, target in pairs:
        copy = pltpu.make_async_copy(source, target, copy_sem)
        copy.start()
        copy.wait()


def own_grads_kernel(
    tiles,
    slots,
    heads,
    tile_total,
    info_ref,
    query_ref,
    grad_ref,
    key_ref,
    value_ref,
    max_ref,
    inverse_ref,
    delta_ref,
    key_full,
    value_full,
    order_ref,
    dscores_ref,
    key_out,
    value_out,
    order_out,
    bias_ref,
    copy_sem,
):
    del order_ref, order_out

    @pl.when(info_ref[0] <= slots)
    def _():
        query = stacked(query_ref, heads)
        grad = stacked(grad_ref, heads)
        scores = own_scores(
            tiles, slots, heads, tile_total, info_ref, bias_ref, key_ref[...], query
        )
        probs = jnp.exp2(scores - max_ref[...]) * inverse_ref[...]
        dprobs = dot_t(value_ref[...], grad)
        dscores = (probs * (dprobs - delta_ref[...])).astype(jnp.bfloat16)
        dscores_ref[...] = dscores
        value_out[...] = dot(probs.astype(jnp.bfloat16), grad)
        key_out[...] = dot(dscores, query) * HD**-0.5

    @pl.when(info_ref[0] > slots)
    def _():
        fetch_full(copy_sem, (key_full, key_out), (value_full, value_out))


def queries_kernel(
    slots,
    heads,
    info_ref,
    key_ref,
    own_dscores,
    slot_dscores,
    slot_keys,
    out_t_ref,
    attended_full,
    query_full,
    attended_ref,
    query_out,
    copy_sem,
):
    rows = query_out.shape[0]

    @pl.when(info_ref[0] <= slots)
    def _():
        query_t = dot(key_ref[...].T, own_dscores[...])
        query_t = (query_t + dot(slot_keys[...].T, slot_dscores[...])) * HD**-0.5
        for h in range(heads):
            columns = pl.ds(h * HD, HD)
            attended_ref[:, columns] = out_t_ref[:, pl.ds(h * rows, rows)].T
            query_out[:, columns] = query_t[:, h * rows : (h + 1) * rows].T

    @pl.when(info_ref[0] > slots)
    def _():
        fetch_full(copy_sem, (attended_full, attended_ref), (query_full, query_out))


def place_kernel(key_own, value_own, key_placed, value_placed, key_sem, value_sem):
    copies = [
        pltpu.make_async_copy(key_own, key_placed, key_sem),
        pltpu.make_async_copy(value_own, value_placed, value_sem),
    ]
    for copy in copies:
        copy.start()
    for copy in copies:
        copy.wait()


def per_device(queries, key_rows, value_rows, out_grad, tile_ids, tile_mask):
    row_count = queries.shape[0]
    heads = queries.shape[1] // HD
    ranks = lax.axis_size("seq")
    chips = ranks // 2
    assert key_rows.shape[1] == HD and ranks > 1 and ranks & (ranks - 1) == 0
    tiles = row_count // TILE
    tile_total = tile_ids.shape[0]
    slots = tiles
    rounds = math.ceil(tile_total / slots)
    slot_shape = (slots, TILE, HD)
    buffer = (rounds - 1, 2) + slot_shape
    shape = jax.ShapeDtypeStruct
    bf16, f32 = jnp.bfloat16, jnp.float32

    def swap(values, step):
        return lax.ppermute(values, "seq", [(source, source ^ step) for source in range(ranks)])

    def across(values):
        return [swap(values, 2 * step) for step in range(1, chips)]

    def trade(full, half):
        got = []
        for pair in pairs_of(chips):
            routes = [(source, source ^ 2 * pair[source % 2]) for source in range(ranks)]
            got.append(lax.ppermute(full, "seq", routes))
        return got + [swap(half, 2 * (chips - 1))]

    def add(*values):
        total = values[0].astype(f32)
        for value in values[1:]:
            total = total + value.astype(f32)
        return total.astype(bf16)

    table = jnp.pad(tile_mask, ((0, 1), (0, 0)))
    table = table + jnp.pad(tile_ids[None], ((tile_total, 0), (0, 0)))
    key_other, value_other = swap(key_rows, 1), swap(value_rows, 1)
    chip_rows = (key_rows, value_rows, key_other, value_other)
    info, spare = call(
        functools.partial(list_kernel, tile_total, tiles, slots),
        [SMEM_SPEC],
        (
            shape((info_size(tile_total, tiles, slots),), jnp.int32),
            shape(buffer, bf16),
        ),
        (SMEM_SPEC, ANY_SPEC),
        scratch=(pltpu.SMEM((tile_total,), jnp.int32),),
        moved=4 * 1024 * 1024,
    )(table)
    chosen, chosen_half = call(
        functools.partial(first_kernel, tiles, slots),
        [SMEM_SPEC] + [VMEM_SPEC] * 4,
        (shape((2 * slots, TILE, HD), bf16), shape(slot_shape, bf16)),
        (VMEM_SPEC,) * 2,
        moved=5 * row_count * HD * 2,
    )(info, *chip_rows)
    used = (info[0] + slots - 1) // slots

    def select(index):
        return call(
            functools.partial(select_kernel, tiles, slots),
            [SMEM_SPEC] * 2 + [VMEM_SPEC] * 4,
            shape(slot_shape, bf16),
            VMEM_SPEC,
            moved=5 * row_count * HD * 2,
        )(info, index.reshape(1), *chip_rows)

    arrived = trade(chosen, chosen_half)
    handed = [swap(values, 1) for values in arrived]

    def gather_more(index, buffered):
        chosen = select(index)
        total = add(chosen, *across(chosen))
        pair = jnp.stack([total, swap(total, 1)])
        return lax.dynamic_update_index_in_dim(buffered, pair, index - 1, 0)

    more = lax.fori_loop(1, used, gather_more, spare)

    all_rows = row_count + rounds * slots * TILE
    columns = heads * row_count
    line = shape((1, columns), f32)
    work = 2 * columns * row_count * HD
    max_own, total_own, weighted, grad_t = call(
        functools.partial(own_kernel, tiles, slots, heads, tile_total),
        [SMEM_SPEC] + [VMEM_SPEC] * 4,
        (line, line, shape((HD, columns), f32), shape((HD, columns), bf16)),
        (VMEM_SPEC,) * 4,
        scratch=(pltpu.VMEM((row_count, row_count), f32),),
        flops=24 * work,
        moved=4 * row_count * heads * HD,
    )(info, queries, out_grad, key_rows, value_rows)

    full = (
        shape(queries.shape, bf16),
        shape(queries.shape, f32),
        shape(key_rows.shape, f32),
        shape(value_rows.shape, f32),
    )
    parts, row_max, inverse, delta, out_t, dscores, slot_keys, more_terms, *full_values = call(
        functools.partial(gathered_kernel, chips, tiles, slots, heads, tile_total),
        [SMEM_SPEC, ANY_SPEC]
        + [VMEM_SPEC] * 2
        + [ANY_SPEC] * 2
        + [VMEM_SPEC] * 6
        + [ANY_SPEC]
        + [VMEM_SPEC] * (2 * len(arrived)),
        (
            shape((2 * slots, TILE, HD), bf16),
            line,
            line,
            line,
            shape((HD, columns), bf16),
            shape((slots * TILE, columns), bf16),
            shape((slots * TILE, HD), bf16),
            shape(buffer, bf16),
        )
        + full,
        (VMEM_SPEC,) * 7 + (ANY_SPEC,) * 5,
        scratch=(
            pltpu.VMEM((all_rows, row_count), f32),
            pltpu.VMEM((2, all_rows, HD), bf16),
            pltpu.VMEM((2, all_rows, HD), f32),
            pltpu.VMEM((all_rows, row_count), f32),
            pltpu.VMEM((2,) + slot_shape, bf16),
            pltpu.VMEM(queries.shape, bf16),
            pltpu.VMEM(queries.shape, f32),
            pltpu.SMEM(table.shape, jnp.int32),
            pltpu.SemaphoreType.DMA,
        ),
        flops=24 * work,
        moved=4 * row_count * heads * HD,
    )(
        info,
        table,
        queries,
        out_grad,
        *chip_rows,
        max_own,
        total_own,
        weighted,
        grad_t,
        more,
        *arrived,
        *handed,
    )

    partner = swap(parts, 1)
    half_sum = add(parts[:slots], partner[slots:])
    chip_sum = jnp.concatenate([half_sum, add(parts[slots:], partner[:slots])])
    own_dscores, key_own, value_own, half_sum = call(
        functools.partial(own_grads_kernel, tiles, slots, heads, tile_total),
        [SMEM_SPEC] + [VMEM_SPEC] * 7 + [ANY_SPEC] * 3,
        (shape((row_count, columns), bf16), *full[2:], shape(slot_shape, bf16)),
        (VMEM_SPEC,) * 3 + (ANY_SPEC,),
        scratch=(pltpu.VMEM((row_count, row_count), f32), pltpu.SemaphoreType.DMA),
        flops=18 * work,
        moved=4 * row_count * heads * HD,
        aliases={10: 3},
    )(
        info,
        queries,
        out_grad,
        key_rows,
        value_rows,
        row_max,
        inverse,
        delta,
        *full_values[2:],
        half_sum,
    )
    back = trade(chip_sum, half_sum)
    key_placed, value_placed = call(
        place_kernel,
        [VMEM_SPEC] * 2,
        tuple(full[2:]),
        (ANY_SPEC,) * 2,
        scratch=(pltpu.SemaphoreType.DMA,) * 2,
        moved=2 * 1024 * 1024,
    )(key_own, value_own)
    attended, query_grad = call(
        functools.partial(queries_kernel, slots, heads),
        [SMEM_SPEC] + [VMEM_SPEC] * 5 + [ANY_SPEC] * 2,
        full[:2],
        (VMEM_SPEC,) * 2,
        scratch=(pltpu.SemaphoreType.DMA,),
        flops=16 * work,
        moved=8 * row_count * heads * HD,
    )(
        info,
        key_rows,
        own_dscores,
        dscores,
        slot_keys,
        out_t,
        *full_values[:2],
    )
    sums = [chip_sum] + back + [swap(values, 1) for values in back]

    def reduce_more(index, totals):
        terms = lax.dynamic_index_in_dim(more_terms, index - 1, 0, keepdims=False)
        part = add(terms[0], swap(terms[1], 1))
        total = add(part, *across(part))
        pair = jnp.stack([total, swap(total, 1)])
        return lax.dynamic_update_index_in_dim(totals, pair, index - 1, 0)

    extra = lax.fori_loop(1, used, reduce_more, more)
    key_grad, value_grad = call(
        functools.partial(close_kernel, tiles, slots, chips, tile_total),
        [SMEM_SPEC, ANY_SPEC] + [VMEM_SPEC] * (2 + len(sums)) + [ANY_SPEC] * 2,
        tuple(full[2:]),
        (ANY_SPEC,) * 2,
        scratch=(
            pltpu.VMEM((2, TILE, HD), f32),
            pltpu.VMEM((2, TILE, HD), bf16),
            pltpu.SemaphoreType.DMA,
            pltpu.SemaphoreType.DMA,
        ),
        moved=5 * row_count * HD * 4,
        aliases={4 + len(sums): 0, 5 + len(sums): 1},
    )(info, extra, key_own, value_own, *sums, key_placed, value_placed)
    return attended, query_grad, key_grad, value_grad


def solution(mesh):
    return jax.shard_map(
        per_device,
        mesh=mesh,
        in_specs=(
            P(("batch", "seq"), "head"),
            P(("batch", "seq"), "head"),
            P(("batch", "seq"), "head"),
            P(("batch", "seq"), "head"),
            P("batch"),
            P("batch", None),
        ),
        out_specs=(P(("batch", "seq"), "head"),) * 4,
        check_vma=False,
    )
```
